32 devices in a mesh: dp: 8 (over y, x, core), tensor: 4 (over z).
Axes of the slice: x: 2, y: 2, z: 4, core: 2. Of those that a mesh axis runs over, the one named last changes fastest.
Arguments:
- tokens: bfloat16 [64, 256, 768], P('dp'), may hold values from -6 to 6
- lengths: int32 [64], P('dp'), may hold values from 64 to 256, as said below
- adapter_mask: int32 [64], P('dp'), may hold values from 1 to 65535, as said below
- cotangent: bfloat16 [64, 256, 768], P(('dp', 'tensor')), may hold values from -6 to 6
- att_query: bfloat16 [768, 768], P(None, 'tensor'), may hold values from -0.3125 to 0.3125
- att_key: bfloat16 [768, 768], P(None, 'tensor'), may hold values from -0.3125 to 0.3125
- att_value: bfloat16 [768, 768], P(None, 'tensor'), may hold values from -0.21875 to 0.21875
- att_out: bfloat16 [768, 768], P('tensor'), may hold values from -0.875 to 0.875
- norm1_gain: float32 [768], replicated, may hold values from 0.5 to 1.5
- norm1_bias: float32 [768], replicated, may hold values from -1.25 to 1.25
- ffn_in: bfloat16 [768, 3072], P(None, 'tensor'), may hold values from -0.21875 to 0.21875
- ffn_bias: float32 [3072], replicated, may hold values from -1.75 to 1.75
- ffn_out: bfloat16 [3072, 768], P('tensor'), may hold values from -0.109375 to 0.109375
- adapt_down: bfloat16 [768, 768], replicated, may hold values from -0.21875 to 0.21875
- adapt_up: bfloat16 [16, 48, 768], replicated, may hold values from -1.5 to 1.5
- norm2_gain: float32 [768], replicated, may hold values from 0.5 to 1.5
- norm2_bias: float32 [768], replicated, may hold values from -1.25 to 1.25
- joining_query: bfloat16 [768, 768], P(('dp', 'tensor')), may hold values from -0.4375 to 0.4375
- joining_key: bfloat16 [768, 768], P(('dp', 'tensor')), may hold values from -0.4375 to 0.4375
- joining_value: bfloat16 [768, 768], P(('dp', 'tensor')), may hold values from -0.21875 to 0.21875
- joining_qbias: bfloat16 [768], P(('dp', 'tensor')), may hold values from -1.75 to 1.75
- joining_vbias: bfloat16 [768], P(('dp', 'tensor')), may hold values from -1.75 to 1.75
Outputs:
- layer_out: bfloat16 [64, 256, 768], P(('dp', 'tensor'))
- input_grad: bfloat16 [64, 256, 768], P(('dp', 'tensor'))
- grad_joining_query: float32 [768, 768], P(('dp', 'tensor'))
- grad_joining_key: float32 [768, 768], P(('dp', 'tensor'))
- grad_joining_value: float32 [768, 768], P(('dp', 'tensor'))
- grad_joining_qbias: float32 [768], P(('dp', 'tensor'))
- grad_joining_vbias: float32 [768], P(('dp', 'tensor'))
The draws below stay inside these ranges and needn't reach their ends.
Inputs may be any that keep to these rules, and one draw needn't show every extreme that they name: Padding lengths; some sequence is full and some has exactly 64 tokens. `adapter_mask`: bit m (m below 16) tells whether adapter m is available to the sequence; every sequence has one available adapter or more, some sequence all of them, some only adapter 0.
All inputs are finite; a program needn't handle non-finite values.
Results may differ from the reference program's by a relative error of at most 0.039.
Values may be sent and summed in bfloat16 or wider, within the bound.
No kernel may reach another device: no remote copies, remote signals or barrier semaphores. Data moves between devices by JAX's collectives and lax.ppermute only.
A program may use at most 256 MiB of HBM per device.

```python
import math
import jax
import jax.numpy as jnp
from jax import lax

D = 768
HEADS = 12
FF = 3072
ADAPTERS = 16
BOTTLENECK = 48
LEN = 256
SEQS = 64


def draw_lengths(key, part):
    drawn = jax.random.randint(key, (SEQS,), LEN // 4, LEN + 1, dtype=jnp.int32)
    drawn = drawn.at[0].set(LEN)
    return drawn.at[1].set(LEN // 4)


def draw_adapter_mask(key, part):
    first_key, second_key = jax.random.split(jax.random.fold_in(key, 17))
    drawn = jax.random.randint(first_key, (SEQS,), 0, 2 ** ADAPTERS, dtype=jnp.int32)
    single = jax.random.randint(second_key, (SEQS,), 0, ADAPTERS, dtype=jnp.int32)
    drawn = jnp.bitwise_or(drawn, jnp.left_shift(jnp.ones_like(single), single))
    drawn = drawn.at[0].set(2 ** ADAPTERS - 1)
    return drawn.at[1].set(1)


def steps_of(own_key, shape, shards, low, top_value):
    factor_of, own = 1.0, jax.random.fold_in(own_key, 6)
    for axis_at, shards_of in shards:
        heights = jnp.exp(jax.random.uniform(jax.random.fold_in(own, axis_at), (shards_of,), jnp.float32, low / len(shards), top_value / len(shards)))
        factor_of = factor_of * jnp.repeat(heights, shape[axis_at] // shards_of).reshape([-1 if axis == axis_at else 1 for axis in range(len(shape))])
    return factor_of


def noise(key, shape, spread, limit, shards=(), held_as=jnp.bfloat16):
    result = jax.random.normal(key, shape, jnp.float32) * spread
    if len(shards) > 0:
        result = steps_of(key, shape, shards, -0.22, 0.18) * result
    return jnp.clip(result, min=-limit, max=limit).astype(held_as)


def setup_inputs(seed: int = 0) -> dict:
    key_list = jax.random.split(jax.random.key(seed), 23)
    tokens = noise(key_list[0], (SEQS, LEN, D), 1.0, 6.0, ((0, 8),))
    lengths = draw_lengths(jax.random.fold_in(key_list[22], 71), 0)
    adapter_mask = draw_adapter_mask(jax.random.fold_in(key_list[22], 71), 0)
    cotangent = noise(key_list[3], (SEQS, LEN, D), 1.0, 6.0, ((0, 32),))
    att_query = noise(key_list[4], (D, D), (D // 2) ** -0.5, 0.3125, ((1, 4),))
    att_key = noise(key_list[5], (D, D), (D // 2) ** -0.5, 0.3125, ((1, 4),))
    att_value = noise(key_list[6], (D, D), D ** -0.5, 0.21875, ((1, 4),))
    att_out = noise(key_list[7], (D, D), (D // 16) ** -0.5, 0.875, ((0, 4),))
    norm1_gain = jnp.clip(1.0 + 0.1 * jax.random.normal(key_list[8], (D,), jnp.float32), 0.5, 1.5)
    norm1_bias = noise(key_list[9], (D,), 0.2, 1.25, (), jnp.float32)
    ffn_in = noise(key_list[10], (D, FF), D ** -0.5, 0.21875, ((1, 4),))
    ffn_bias = noise(key_list[11], (FF,), 0.3, 1.75, (), jnp.float32)
    ffn_out = noise(key_list[12], (FF, D), FF ** -0.5, 0.109375, ((0, 4),))
    adapt_down = noise(key_list[13], (D, ADAPTERS * BOTTLENECK), D ** -0.5, 0.21875)
    adapt_up = noise(key_list[14], (ADAPTERS, BOTTLENECK, D), (BOTTLENECK // 3) ** -0.5, 1.5)
    norm2_gain = jnp.clip(1.0 + 0.1 * jax.random.normal(key_list[15], (D,), jnp.float32), 0.5, 1.5)
    norm2_bias = noise(key_list[16], (D,), 0.2, 1.25, (), jnp.float32)
    joining_query = noise(key_list[17], (D, D), (D // 4) ** -0.5, 0.4375, ((0, 32),))
    joining_key = noise(key_list[18], (D, D), (D // 4) ** -0.5, 0.4375, ((0, 32),))
    joining_value = noise(key_list[19], (D, D), D ** -0.5, 0.21875, ((0, 32),))
    joining_qbias = noise(key_list[20], (D,), 0.3, 1.75, ((0, 32),))
    joining_vbias = noise(key_list[21], (D,), 0.3, 1.75, ((0, 32),))
    return dict(tokens=tokens, lengths=lengths, adapter_mask=adapter_mask, cotangent=cotangent, att_query=att_query, att_key=att_key, att_value=att_value, att_out=att_out, norm1_gain=norm1_gain, norm1_bias=norm1_bias, ffn_in=ffn_in, ffn_bias=ffn_bias, ffn_out=ffn_out, adapt_down=adapt_down, adapt_up=adapt_up, norm2_gain=norm2_gain, norm2_bias=norm2_bias, joining_query=joining_query, joining_key=joining_key, joining_value=joining_value, joining_qbias=joining_qbias, joining_vbias=joining_vbias)


@jax.custom_vjp
def low(v):
    return lax.optimization_barrier(v.astype(jnp.bfloat16)).astype(jnp.float32)

@jax.custom_vjp
def low_back(v):
    return v

def low_keep(v):
    return (low(v), None)

def low_pass(kept, grad):
    return (grad,)

def back_keep(v):
    return (v, None)

def back_low(kept, grad):
    return (low(grad),)
low.defvjp(low_keep, low_pass)
low_back.defvjp(back_keep, back_low)
norm_epsilon = 1e-05
highest = lax.Precision.HIGHEST

def layer_norm(values, gain_vec, bias_vec):
    average = lax.optimization_barrier(jnp.mean(values, axis=-1, keepdims=True))
    centered = values - average
    variance = lax.optimization_barrier(jnp.mean(centered * centered, axis=-1, keepdims=True))
    return centered * lax.rsqrt(variance + norm_epsilon) * gain_vec + bias_vec

def masked_softmax(scores):
    row_max = lax.optimization_barrier(jnp.max(scores, axis=-1, keepdims=True))
    weights_exp = jnp.exp(scores - row_max)
    return weights_exp / lax.optimization_barrier(jnp.sum(weights_exp, axis=-1, keepdims=True))

def forward(frozen, trained, tokens, lengths, adapter_mask):
    att_query, att_key, att_value, att_out, norm1_gain, norm1_bias, ffn_in, ffn_bias, ffn_out, adapt_down, adapt_up, norm2_gain, norm2_bias = frozen
    joining_query, joining_key, joining_value, joining_qbias, joining_vbias = trained
    seq_count, seq_len, model_dim = tokens.shape
    head_dim = model_dim // HEADS
    row_count = seq_count * seq_len
    flat_tokens = tokens.reshape(row_count, model_dim)

    def project(weight):
        raw_out = jnp.dot(flat_tokens, weight, precision=highest)
        return low(low_back(raw_out)).reshape(seq_count, seq_len, HEADS, head_dim)
    queries = project(att_query)
    att_keys = project(att_key)
    att_values = project(att_value)
    raw_scores = jnp.einsum('sqhe,skhe->shqk', queries, att_keys, precision=highest) * (1.0 / math.sqrt(head_dim))
    positions = jnp.arange(seq_len, dtype=jnp.int32)
    valid_keys = (positions[None, :] < lengths[:, None])[:, None, None, :]
    scores = jnp.where(valid_keys, low_back(raw_scores), -1e+30)
    att_probs = low(masked_softmax(scores))
    context = jnp.einsum('shqk,skhe->sqhe', att_probs, att_values, precision=highest).reshape(row_count, model_dim)
    context = low(low_back(context))
    attended = low_back(jnp.dot(context, att_out, precision=highest))
    normed1 = layer_norm(flat_tokens + attended, norm1_gain, norm1_bias)
    pre_act = low_back(jnp.dot(low(normed1), ffn_in, precision=highest) + ffn_bias)
    activated = low(jax.nn.gelu(pre_act, approximate=False))
    ffn_output = low_back(jnp.dot(activated, ffn_out, precision=highest))
    ffn_low = low(ffn_output)
    down_act = low(jax.nn.gelu(low_back(jnp.dot(ffn_low, adapt_down, precision=highest)), approximate=False))
    down_act = down_act.reshape(row_count, ADAPTERS, BOTTLENECK)
    branch = low_back(jnp.einsum('rmb,mbd->rmd', down_act, adapt_up, precision=highest))
    adapted = low(ffn_output[:, None, :] + branch)
    joining_q = low_back(jnp.dot(ffn_low, joining_query, precision=highest) + joining_qbias)
    adapter_keys = low_back(jnp.einsum('rmd,de->rme', adapted, joining_key, precision=highest))
    adapter_vals = low_back(jnp.einsum('rmd,de->rme', adapted, joining_value, precision=highest) + joining_vbias)
    mask_bits = jnp.right_shift(adapter_mask[:, None], jnp.arange(ADAPTERS, dtype=jnp.int32)[None, :]) % 2
    available = jnp.broadcast_to((mask_bits == 1)[:, None, :], (seq_count, seq_len, ADAPTERS)).reshape(row_count, ADAPTERS)
    fscores = lax.optimization_barrier(jnp.sum(joining_q[:, None, :] * adapter_keys, axis=-1)) * (1.0 / math.sqrt(model_dim))
    fprobs = masked_softmax(jnp.where(available, fscores, -1e+30))
    mixture = lax.optimization_barrier(jnp.sum(fprobs[:, :, None] * adapter_vals, axis=1))
    return layer_norm(normed1 + mixture, norm2_gain, norm2_bias)

def widen(array_in):
    return array_in.astype(jnp.float32)

def reference(tokens, lengths, adapter_mask, cotangent, att_query, att_key, att_value, att_out, norm1_gain, norm1_bias, ffn_in, ffn_bias, ffn_out, adapt_down, adapt_up, norm2_gain, norm2_bias, joining_query, joining_key, joining_value, joining_qbias, joining_vbias):
    frozen = jax.tree.map(widen, (att_query, att_key, att_value, att_out, norm1_gain, norm1_bias, ffn_in, ffn_bias, ffn_out, adapt_down, adapt_up, norm2_gain, norm2_bias))
    trained = jax.tree.map(widen, (joining_query, joining_key, joining_value, joining_qbias, joining_vbias))
    seq_total = tokens.shape[0]
    group_size = math.gcd(seq_total, 8)
    group_count = seq_total // group_size

    def split_groups(array_in):
        return array_in.reshape((group_count, group_size) + array_in.shape[1:])
    group_inputs = (split_groups(widen(tokens)), split_groups(lengths), split_groups(adapter_mask), split_groups(widen(cotangent)))

    def one_group(grad_sums, group_data):
        group_tokens, group_lengths, group_mask, group_cot = group_data

        def run_layer(token_in, trained_in):
            return forward(frozen, trained_in, token_in, group_lengths, group_mask)
        output, pullback = jax.vjp(run_layer, group_tokens, trained)
        token_grad, trained_grad = pullback(group_cot.reshape(output.shape))
        grad_sums = jax.tree.map(jnp.add, grad_sums, trained_grad)
        return (grad_sums, (output.reshape(group_tokens.shape).astype(jnp.bfloat16), token_grad.astype(jnp.bfloat16)))
    zero_sums = jax.tree.map(jnp.zeros_like, trained)
    grad_sums, (outputs, input_grads) = lax.scan(one_group, zero_sums, group_inputs)
    layer_out = outputs.reshape(tokens.shape)
    input_grad = input_grads.reshape(tokens.shape)
    return (layer_out, input_grad, grad_sums[0], grad_sums[1], grad_sums[2], grad_sums[3], grad_sums[4])
```

```python
import math

import jax
import jax.numpy as jnp
from jax import lax
from jax.sharding import PartitionSpec as P

HEADS = 12
EPS = 1e-05
MASKED = -1e30
ALL = ("dp", "tensor")
BF = jnp.bfloat16
F32 = jnp.float32


def mm(left, right):
    return jnp.dot(left, right, preferred_element_type=F32)


def mm_t(left, right):
    return lax.dot_general(left, right, (((1,), (1,)), ((), ())), preferred_element_type=F32)


def t_mm(left, right):
    return lax.dot_general(left, right, (((0,), (0,)), ((), ())), preferred_element_type=F32)


def norm_parts(values):
    average = jnp.mean(values, axis=-1, keepdims=True)
    centered = values - average
    variance = jnp.mean(centered * centered, axis=-1, keepdims=True)
    rstd = lax.rsqrt(variance + EPS)
    return centered * rstd, rstd


def norm_back(grad, gain, xhat, rstd):
    scaled = grad * gain
    return rstd * (
        scaled
        - jnp.mean(scaled, axis=-1, keepdims=True)
        - xhat * jnp.mean(scaled * xhat, axis=-1, keepdims=True)
    )


def gelu_parts(pre):
    cdf = 0.5 * (1.0 + lax.erf(pre * (1.0 / math.sqrt(2.0))))
    pdf = jnp.exp(-0.5 * pre * pre) * (1.0 / math.sqrt(2.0 * math.pi))
    return pre * cdf, cdf + pre * pdf


def shards(
    tokens, lengths, adapter_mask, cotangent, att_query, att_key, att_value, att_out,
    norm1_gain, norm1_bias, ffn_in, ffn_bias, ffn_out, adapt_down, adapt_up, norm2_gain,
    norm2_bias, joining_query, joining_key, joining_value, joining_qbias, joining_vbias,
):
    groups = lax.axis_size("tensor")
    dp_size = lax.axis_size("dp")
    t_rank = lax.axis_index("tensor")
    d_rank = lax.axis_index("dp")
    seq_local, seq_len, dim = tokens.shape
    mine = seq_local // groups
    rows = mine * seq_len
    head_dim = dim // HEADS
    adapters, neck = adapt_up.shape[0], adapt_up.shape[1]

    def my_slice(array):
        return lax.dynamic_slice_in_dim(array, t_rank * mine, mine, 0)

    def my_part(weight):
        part = weight.shape[0] // dp_size
        return lax.dynamic_slice_in_dim(weight, d_rank * part, part, 0)

    def gather(part):
        return lax.all_gather(part, ALL, axis=0, tiled=False).reshape((dp_size, groups) + part.shape)

    def cols_whole(weight):
        g = gather(my_part(weight))
        return g.transpose(0, 2, 1, 3).reshape(weight.shape[0], groups * weight.shape[1])

    def rows_whole(weight):
        g = gather(my_part(weight))
        return g.transpose(1, 0, 2, 3).reshape(groups * weight.shape[0], weight.shape[1])

    w_q, w_k, w_v = cols_whole(att_query), cols_whole(att_key), cols_whole(att_value)
    w_o = rows_whole(att_out)
    w_in = cols_whole(ffn_in)
    w_out = rows_whole(ffn_out)
    j_q = lax.all_gather(joining_query, ALL, axis=0, tiled=True)
    j_k = lax.all_gather(joining_key, ALL, axis=0, tiled=True)
    j_v = lax.all_gather(joining_value, ALL, axis=0, tiled=True)
    j_qb = lax.all_gather(joining_qbias, ALL, axis=0, tiled=True).astype(F32)
    j_vb = lax.all_gather(joining_vbias, ALL, axis=0, tiled=True).astype(F32)

    x_low = my_slice(tokens).reshape(rows, dim)
    x_mine = x_low.astype(F32)
    len_mine = my_slice(lengths)
    mask_mine = my_slice(adapter_mask)
    shifts = jnp.arange(adapters, dtype=jnp.int32)
    bits = jnp.right_shift(mask_mine[:, None], shifts[None, :]) % 2
    available = jnp.broadcast_to((bits == 1)[:, None, :], (mine, seq_len, adapters)).reshape(rows, adapters)
    cot = cotangent.reshape(rows, dim).astype(F32)

    def heads_of(weight):
        return mm(x_low, weight).astype(BF).reshape(mine, seq_len, HEADS, head_dim)

    q, k, v = heads_of(w_q), heads_of(w_k), heads_of(w_v)
    scale = 1.0 / math.sqrt(head_dim)
    valid = (jnp.arange(seq_len, dtype=jnp.int32)[None, :] < len_mine[:, None])[:, None, None, :]
    scores = jnp.einsum("sqhe,skhe->shqk", q, k, preferred_element_type=F32) * scale
    scores = jnp.where(valid, scores, MASKED)
    row_max = jnp.max(scores, axis=-1, keepdims=True)
    exps = jnp.exp(scores - row_max)
    probs = exps / jnp.sum(exps, axis=-1, keepdims=True)
    probs_low = probs.astype(BF)
    ctx = jnp.einsum("shqk,skhe->sqhe", probs_low, v, preferred_element_type=F32)
    ctx = ctx.astype(BF).reshape(rows, dim)
    xhat1, rstd1 = norm_parts(x_mine + mm(ctx, w_o))
    normed1 = xhat1 * norm1_gain + norm1_bias

    act, act_slope = gelu_parts(mm(normed1.astype(BF), w_in) + ffn_bias)
    ffn = mm(act.astype(BF), w_out)

    up = adapt_up.reshape(adapters * neck, dim)
    x_ffn = ffn.astype(BF)
    down, down_slope = gelu_parts(mm(x_ffn, adapt_down))
    down_low = down.astype(BF).astype(F32)
    jq = mm(x_ffn, j_q) + j_qb
    jq_low = jq.astype(BF)
    u = mm_t(jq_low, j_k)
    big_u = mm_t(u.astype(BF), up)

    def per_adapter(values):
        return jnp.sum(values.reshape(rows, adapters, neck), axis=-1)

    def spread(values):
        return jnp.broadcast_to(values[:, :, None], (rows, adapters, neck)).reshape(rows, adapters * neck)

    fscale = 1.0 / math.sqrt(dim)
    fscores = (per_adapter(down_low * big_u) + jnp.sum(ffn * u, axis=-1, keepdims=True)) * fscale
    fscores = jnp.where(available, fscores, MASKED)
    fexp = jnp.exp(fscores - jnp.max(fscores, axis=-1, keepdims=True))
    fprobs = fexp / jnp.sum(fexp, axis=-1, keepdims=True)
    p_wide = spread(fprobs)
    mixed = ffn + mm((p_wide * down_low).astype(BF), up)
    mixed_low = mixed.astype(BF)
    xhat2, rstd2 = norm_parts(normed1 + mm(mixed_low, j_v) + j_vb)
    layer_out = (xhat2 * norm2_gain + norm2_bias).astype(BF)

    g2 = norm_back(cot, norm2_gain, xhat2, rstd2)
    g2_low = g2.astype(BF)
    w = mm_t(g2_low, j_v)
    big_w = mm_t(w.astype(BF), up)
    gvals = per_adapter(down_low * big_w) + jnp.sum(ffn * w, axis=-1, keepdims=True) + jnp.sum(g2 * j_vb, axis=-1, keepdims=True)
    gs = fprobs * (gvals - jnp.sum(gvals * fprobs, axis=-1, keepdims=True)) * fscale
    gs_wide = spread(gs)
    gs_sum = jnp.sum(gs, axis=-1, keepdims=True)
    t = mm((gs_wide * down_low).astype(BF), up) + gs_sum * ffn
    t_low = t.astype(BF)
    gq_low = mm(t_low, j_k).astype(BF)
    d_jq = t_mm(x_ffn, gq_low)
    d_jk = t_mm(t_low, jq_low)
    d_jv = t_mm(mixed_low, g2_low)
    d_qb = jnp.sum(gq_low.astype(F32), axis=0)
    d_vb = jnp.sum(g2, axis=0)
    g_down = ((gs_wide * big_u + p_wide * big_w) * down_slope).astype(BF)
    g_ffn = (gs_sum * u + w + mm_t(g_down, adapt_down) + mm_t(gq_low, j_q)).astype(BF)

    g_pre = (mm_t(g_ffn, w_out) * act_slope).astype(BF)
    g_norm1 = mm_t(g_pre, w_in) + g2
    g1 = norm_back(g_norm1, norm1_gain, xhat1, rstd1)

    g_ctx = mm_t(g1.astype(BF), w_o).astype(BF).reshape(mine, seq_len, HEADS, head_dim)
    g_probs = jnp.einsum("sqhe,skhe->shqk", g_ctx, v, preferred_element_type=F32)
    g_v = jnp.einsum("shqk,sqhe->skhe", probs_low, g_ctx, preferred_element_type=F32)
    g_scores = (probs * (g_probs - jnp.sum(g_probs * probs, axis=-1, keepdims=True))).astype(BF)
    g_q = jnp.einsum("shqk,skhe->sqhe", g_scores, k, preferred_element_type=F32) * scale
    g_k = jnp.einsum("shqk,sqhe->skhe", g_scores, q, preferred_element_type=F32) * scale
    total = g1
    for grad, weight in ((g_q, w_q), (g_k, w_k), (g_v, w_v)):
        total = total + mm_t(grad.astype(BF).reshape(rows, dim), weight)
    input_grad = total.astype(BF)

    def scatter(value):
        return lax.psum_scatter(value, ALL, scatter_dimension=0, tiled=True)

    return (
        layer_out.reshape(mine, seq_len, dim),
        input_grad.reshape(mine, seq_len, dim),
        scatter(d_jq), scatter(d_jk), scatter(d_jv), scatter(d_qb), scatter(d_vb),
    )


def solution(mesh):
    both = P(ALL, None)
    return jax.shard_map(
        shards,
        mesh=mesh,
        in_specs=(
            P("dp", None, None), P("dp"), P("dp"), P(ALL, None, None),
            P(None, "tensor"), P(None, "tensor"), P(None, "tensor"), P("tensor", None),
            P(), P(), P(None, "tensor"), P(), P("tensor", None), P(), P(), P(), P(),
            both, both, both, P(ALL), P(ALL),
        ),
        out_specs=(P(ALL, None, None), P(ALL, None, None), both, both, both, P(ALL), P(ALL)),
        check_vma=False,
    )
```

```python
from functools import partial
import math

import jax
import jax.numpy as jnp
from jax import lax
from jax.experimental import pallas as pl
from jax.experimental.pallas import tpu as pltpu
from jax.sharding import PartitionSpec as P

HEADS = 12
EPS = 1e-05
MASKED = -1e30
ALL = ("dp", "tensor")
BF = jnp.bfloat16
F32 = jnp.float32


def mm(left, right):
    return jnp.dot(left, right, preferred_element_type=F32)


def mm_t(left, right):
    return lax.dot_general(left, right, (((1,), (1,)), ((), ())), preferred_element_type=F32)


def t_mm(left, right):
    return lax.dot_general(left, right, (((0,), (0,)), ((), ())), preferred_element_type=F32)


def norm_parts(values):
    average = jnp.mean(values, axis=-1, keepdims=True)
    centered = values - average
    variance = jnp.mean(centered * centered, axis=-1, keepdims=True)
    rstd = lax.rsqrt(variance + EPS)
    return centered * rstd, rstd


def norm_back(grad, gain, xhat, rstd):
    scaled = grad * gain
    return rstd * (
        scaled
        - jnp.mean(scaled, axis=-1, keepdims=True)
        - xhat * jnp.mean(scaled * xhat, axis=-1, keepdims=True)
    )


def gelu_parts(pre):
    cdf = 0.5 * (1.0 + lax.erf(pre * (1.0 / math.sqrt(2.0))))
    pdf = jnp.exp(-0.5 * pre * pre) * (1.0 / math.sqrt(2.0 * math.pi))
    return pre * cdf, cdf + pre * pdf


CORE = [(i, i ^ 1) for i in range(8)]
ALONG_X = [(i, i ^ 2) for i in range(8)]
ALONG_Y = [(i, i ^ 4) for i in range(8)]
SPLIT_XY = [(i, i ^ (4 if i & 1 else 2)) for i in range(8)]
CROSS_XY = [(i, i ^ (3 if i & 1 else 5)) for i in range(8)]


def send(array, pairs):
    return lax.ppermute(array, "dp", pairs)


def shift(array, by, groups):
    return lax.ppermute(array, "tensor", [(i, (i + by) % groups) for i in range(groups)])


def place_kernel(spots_ref, *refs, first_item, item_count, groups):
    pieces, out, sems = refs[:-2], refs[-2], refs[-1]
    copies = []
    if first_item:
        pieces, own = pieces[:-1], pieces[-1]
        copies.append(pltpu.make_async_copy(own, out.at[spots_ref[8]], sems.at[0]))
    for k, piece in enumerate(pieces):
        for i in range(item_count):
            plane = lax.rem(spots_ref[8] + (groups - first_item - i), groups)
            copies.append(
                pltpu.make_async_copy(piece.at[i], out.at[plane, spots_ref[k]], sems.at[len(copies)])
            )
    for copy in copies:
        copy.start()
    for copy in copies:
        copy.wait()


def place(pieces, own, spots, groups):
    item_count = pieces[0].shape[0]
    first_item = 0 if own is None else 1
    arrays = list(pieces) + ([] if own is None else [own])
    return pl.pallas_call(
        partial(place_kernel, first_item=first_item, item_count=item_count, groups=groups),
        out_shape=jax.ShapeDtypeStruct((groups, 8) + pieces[0].shape[1:], BF),
        in_specs=[pl.BlockSpec(memory_space=pltpu.SMEM)] + [pl.BlockSpec(memory_space=pl.ANY)] * len(arrays),
        out_specs=pl.BlockSpec(memory_space=pltpu.VMEM),
        scratch_shapes=[pltpu.SemaphoreType.DMA((8 * item_count + first_item,))],
        compiler_params=pltpu.CompilerParams(vmem_limit_bytes=32 * 2**20),
    )(spots, *arrays)


class Gather:
    def __init__(self, dp_size, groups, my_d, my_z):
        self.dp_size, self.groups, self.my_d, self.my_z = dp_size, groups, my_d, my_z
        self.paired = dp_size == 8 and groups == 4
        core = lax.rem(my_d, 2)
        even = [0, 1, 2, 3, 7, 5, 4, 6]
        odd = [0, 1, 4, 5, 7, 3, 2, 6]
        flips = jnp.where(core == 0, jnp.array(even, jnp.int32), jnp.array(odd, jnp.int32))
        self.spots = jnp.concatenate([jnp.bitwise_xor(my_d, flips), my_z[None]]).astype(jnp.int32)

    def spread(self, items):
        other = send(items, CORE)
        near0, near1 = send(items, SPLIT_XY), send(other, SPLIT_XY)
        far = send(near0, CROSS_XY)
        return [items, other, near0, near1, far, send(near0, CORE), send(near1, CORE), send(far, CORE)]

    def frozen(self, shard):
        rows = shard.shape[0] // self.dp_size
        part = lax.dynamic_slice_in_dim(shard, self.my_d * rows, rows, 0)
        if not self.paired:
            return lax.all_gather(part, ("dp", "tensor"), axis=0).reshape(
                (self.dp_size, self.groups) + part.shape
            ).transpose(1, 0, 2, 3)
        items = jnp.stack([shift(part, i, self.groups) for i in range(1, self.groups)])
        return place(self.spread(items), shard.reshape(self.dp_size, rows, -1), self.spots, self.groups)

    def joining(self, part):
        if not self.paired:
            return lax.all_gather(part, ("dp", "tensor"), axis=0).reshape(
                (self.dp_size, self.groups) + part.shape
            ).transpose(1, 0, 2, 3)
        items = jnp.stack([part] + [shift(part, i, self.groups) for i in range(1, self.groups)])
        return place(self.spread(items), None, self.spots, self.groups)


def reduce_grads(grads, dp_size, groups, my_d, my_z, own_rows):
    part = own_rows * groups
    dim = grads.shape[-1]
    if dp_size == 8 and groups == 4:
        core, quarter = lax.rem(my_d, 2), my_d // 2
        by_core = grads.reshape(4, 2, *grads.shape[1:])
        away = lax.dynamic_index_in_dim(by_core, 1 - core, 1, keepdims=False).astype(BF)
        half = lax.dynamic_index_in_dim(by_core, core, 1, keepdims=False)
        half = half + send(away, CORE).astype(F32)

        def block(flip):
            return lax.dynamic_index_in_dim(half, jnp.bitwise_xor(quarter, flip), 0, keepdims=False)

        passed = send(block(3).astype(BF), SPLIT_XY).astype(F32)
        to_x = block(1) + jnp.where(core == 1, passed, 0.0)
        to_y = block(2) + jnp.where(core == 0, passed, 0.0)
        total = block(0) + send(to_x.astype(BF), ALONG_X).astype(F32) + send(to_y.astype(BF), ALONG_Y).astype(F32)
    else:
        total = lax.psum_scatter(grads, "dp", scatter_dimension=0, tiled=False)
    mats = total[: 3 * part].reshape(3, groups, own_rows, dim).transpose(1, 0, 2, 3).reshape(groups, 3 * own_rows, dim)
    extra = jnp.pad(total[3 * part : 3 * part + groups][:, None, :], ((0, 0), (0, 7), (0, 0)))
    blocks = jnp.concatenate([mats, extra], axis=1)
    if dp_size == 8 and groups == 4:
        mine = lax.dynamic_index_in_dim(blocks, my_z, 0, keepdims=False)
        for i in range(1, groups):
            goes = lax.dynamic_index_in_dim(blocks, lax.rem(my_z + i, groups), 0, keepdims=False)
            mine = mine + shift(goes.astype(BF), i, groups).astype(F32)
    else:
        mine = lax.psum_scatter(blocks, "tensor", scatter_dimension=0, tiled=False)
    return mine[: 3 * own_rows].reshape(3, own_rows, dim), mine[3 * own_rows]


def shards(
    tokens, lengths, adapter_mask, cotangent, att_query, att_key, att_value, att_out,
    norm1_gain, norm1_bias, ffn_in, ffn_bias, ffn_out, adapt_down, adapt_up, norm2_gain,
    norm2_bias, joining_query, joining_key, joining_value, joining_qbias, joining_vbias,
):
    groups = lax.axis_size("tensor")
    dp_size = lax.axis_size("dp")
    t_rank = lax.axis_index("tensor")
    d_rank = lax.axis_index("dp")
    seq_local, seq_len, dim = tokens.shape
    mine = seq_local // groups
    rows = mine * seq_len
    head_dim = dim // HEADS
    adapters, neck = adapt_up.shape[0], adapt_up.shape[1]

    def my_slice(array):
        return lax.dynamic_slice_in_dim(array, t_rank * mine, mine, 0)

    my_z, my_d = t_rank, d_rank
    att_pack = jnp.concatenate([att_query.T, att_key.T, att_value.T, att_out], axis=0)
    gather = Gather(dp_size, groups, my_d, my_z)
    att_all = gather.frozen(att_pack)
    in_all = gather.frozen(ffn_in)
    out_all = gather.frozen(ffn_out)
    own_rows = joining_query.shape[0]
    bias_row = jnp.zeros((8, dim), BF)
    bias_row = bias_row.at[0, :own_rows].set(joining_qbias).at[0, own_rows : 2 * own_rows].set(joining_vbias)
    join_all = gather.joining(jnp.concatenate([joining_query, joining_key, joining_value, bias_row], axis=0))

    att_all = att_all.reshape(groups, 4, dim // groups, dim)
    w_q, w_k, w_v, w_o = (att_all[:, i].reshape(dim, dim) for i in range(4))
    w_q, w_k, w_v = w_q.T, w_k.T, w_v.T
    w_in = in_all.reshape(groups, dim, -1).transpose(1, 0, 2).reshape(dim, -1)
    w_out = out_all.reshape(-1, dim)
    join_all = join_all.transpose(1, 0, 2, 3)

    def joined(lo, hi):
        return join_all[:, :, lo:hi].reshape(-1, dim)

    j_q, j_k, j_v = (joined(i * own_rows, (i + 1) * own_rows) for i in range(3))
    biases = join_all[:, :, 3 * own_rows, : 2 * own_rows].astype(F32)
    j_qb = biases[:, :, :own_rows].reshape(-1)
    j_vb = biases[:, :, own_rows:].reshape(-1)

    x_low = my_slice(tokens).reshape(rows, dim)
    x_mine = x_low.astype(F32)
    len_mine = my_slice(lengths)
    mask_mine = my_slice(adapter_mask)
    shifts = jnp.arange(adapters, dtype=jnp.int32)
    bits = jnp.right_shift(mask_mine[:, None], shifts[None, :]) % 2
    available = jnp.broadcast_to((bits == 1)[:, None, :], (mine, seq_len, adapters)).reshape(rows, adapters)
    cot = cotangent.reshape(rows, dim).astype(F32)

    def heads_of(weight):
        return mm(x_low, weight).astype(BF).reshape(mine, seq_len, HEADS, head_dim)

    q, k, v = heads_of(w_q), heads_of(w_k), heads_of(w_v)
    scale = 1.0 / math.sqrt(head_dim)
    valid = (jnp.arange(seq_len, dtype=jnp.int32)[None, :] < len_mine[:, None])[:, None, None, :]
    scores = jnp.einsum("sqhe,skhe->shqk", q, k, preferred_element_type=F32) * scale
    scores = jnp.where(valid, scores, MASKED)
    row_max = jnp.max(scores, axis=-1, keepdims=True)
    exps = jnp.exp(scores - row_max)
    probs = exps / jnp.sum(exps, axis=-1, keepdims=True)
    probs_low = probs.astype(BF)
    ctx = jnp.einsum("shqk,skhe->sqhe", probs_low, v, preferred_element_type=F32)
    ctx = ctx.astype(BF).reshape(rows, dim)
    xhat1, rstd1 = norm_parts(x_mine + mm(ctx, w_o))
    normed1 = xhat1 * norm1_gain + norm1_bias

    act, act_slope = gelu_parts(mm(normed1.astype(BF), w_in) + ffn_bias)
    ffn = mm(act.astype(BF), w_out)

    up = adapt_up.reshape(adapters * neck, dim)
    x_ffn = ffn.astype(BF)
    down, down_slope = gelu_parts(mm(x_ffn, adapt_down))
    down_low = down.astype(BF).astype(F32)
    jq = mm(x_ffn, j_q) + j_qb
    jq_low = jq.astype(BF)
    u = mm_t(jq_low, j_k)
    big_u = mm_t(u.astype(BF), up)

    def per_adapter(values):
        return jnp.sum(values.reshape(rows, adapters, neck), axis=-1)

    def spread(values):
        return jnp.broadcast_to(values[:, :, None], (rows, adapters, neck)).reshape(rows, adapters * neck)

    fscale = 1.0 / math.sqrt(dim)
    fscores = (per_adapter(down_low * big_u) + jnp.sum(ffn * u, axis=-1, keepdims=True)) * fscale
    fscores = jnp.where(available, fscores, MASKED)
    fexp = jnp.exp(fscores - jnp.max(fscores, axis=-1, keepdims=True))
    fprobs = fexp / jnp.sum(fexp, axis=-1, keepdims=True)
    p_wide = spread(fprobs)
    mixed = ffn + mm((p_wide * down_low).astype(BF), up)
    mixed_low = mixed.astype(BF)
    xhat2, rstd2 = norm_parts(normed1 + mm(mixed_low, j_v) + j_vb)
    layer_out = (xhat2 * norm2_gain + norm2_bias).astype(BF)

    g2 = norm_back(cot, norm2_gain, xhat2, rstd2)
    g2_low = g2.astype(BF)
    w = mm_t(g2_low, j_v)
    big_w = mm_t(w.astype(BF), up)
    gvals = per_adapter(down_low * big_w) + jnp.sum(ffn * w, axis=-1, keepdims=True) + jnp.sum(g2 * j_vb, axis=-1, keepdims=True)
    gs = fprobs * (gvals - jnp.sum(gvals * fprobs, axis=-1, keepdims=True)) * fscale
    gs_wide = spread(gs)
    gs_sum = jnp.sum(gs, axis=-1, keepdims=True)
    t = mm((gs_wide * down_low).astype(BF), up) + gs_sum * ffn
    t_low = t.astype(BF)
    gq_low = mm(t_low, j_k).astype(BF)
    d_jq = t_mm(x_ffn, gq_low)
    d_jk = t_mm(t_low, jq_low)
    d_jv = t_mm(mixed_low, g2_low)
    d_qb = jnp.sum(gq_low.astype(F32), axis=0)
    d_vb = jnp.sum(g2, axis=0)
    g_down = ((gs_wide * big_u + p_wide * big_w) * down_slope).astype(BF)
    g_ffn = (gs_sum * u + w + mm_t(g_down, adapt_down) + mm_t(gq_low, j_q)).astype(BF)

    g_pre = (mm_t(g_ffn, w_out) * act_slope).astype(BF)
    g_norm1 = mm_t(g_pre, w_in) + g2
    g1 = norm_back(g_norm1, norm1_gain, xhat1, rstd1)

    g_ctx = mm_t(g1.astype(BF), w_o).astype(BF).reshape(mine, seq_len, HEADS, head_dim)
    g_probs = jnp.einsum("sqhe,skhe->shqk", g_ctx, v, preferred_element_type=F32)
    g_v = jnp.einsum("shqk,sqhe->skhe", probs_low, g_ctx, preferred_element_type=F32)
    g_scores = (probs * (g_probs - jnp.sum(g_probs * probs, axis=-1, keepdims=True))).astype(BF)
    g_q = jnp.einsum("shqk,skhe->sqhe", g_scores, k, preferred_element_type=F32) * scale
    g_k = jnp.einsum("shqk,sqhe->skhe", g_scores, q, preferred_element_type=F32) * scale
    total = g1
    for grad, weight in ((g_q, w_q), (g_k, w_k), (g_v, w_v)):
        total = total + mm_t(grad.astype(BF).reshape(rows, dim), weight)
    input_grad = total.astype(BF)

    part = dim // dp_size
    bias_grads = jnp.stack([d_qb.reshape(dp_size, groups, own_rows), d_vb.reshape(dp_size, groups, own_rows)], axis=2)
    bias_grads = jnp.pad(
        bias_grads.reshape(dp_size, groups, 2 * own_rows), ((0, 0), (0, 16 - groups), (0, dim - 2 * own_rows))
    )
    grads = jnp.concatenate(
        [d_jq.reshape(dp_size, part, dim), d_jk.reshape(dp_size, part, dim), d_jv.reshape(dp_size, part, dim), bias_grads],
        axis=1,
    )
    mats, bias_sum = reduce_grads(grads, dp_size, groups, my_d, my_z, own_rows)
    return (
        layer_out.reshape(mine, seq_len, dim),
        input_grad.reshape(mine, seq_len, dim),
        mats[0], mats[1], mats[2],
        bias_sum[:own_rows], bias_sum[own_rows : 2 * own_rows],
    )


def solution(mesh):
    both = P(ALL, None)
    return jax.shard_map(
        shards,
        mesh=mesh,
        in_specs=(
            P("dp", None, None), P("dp"), P("dp"), P(ALL, None, None),
            P(None, "tensor"), P(None, "tensor"), P(None, "tensor"), P("tensor", None),
            P(), P(), P(None, "tensor"), P(), P("tensor", None), P(), P(), P(), P(),
            both, both, both, P(ALL), P(ALL),
        ),
        out_specs=(P(ALL, None, None), P(ALL, None, None), both, both, both, P(ALL), P(ALL)),
        check_vma=False,
    )
```

```python
from functools import partial
import math

import jax
import jax.numpy as jnp
from jax import lax
from jax.experimental import pallas as pl
from jax.experimental.pallas import tpu as pltpu
from jax.sharding import PartitionSpec as P

HEADS = 12
EPS = 1e-05
MASKED = -1e30
ALL = ("dp", "tensor")
BF = jnp.bfloat16
F32 = jnp.float32


def mm(left, right):
    return jnp.dot(left, right, preferred_element_type=F32)


def mm_t(left, right):
    return lax.dot_general(left, right, (((1,), (1,)), ((), ())), preferred_element_type=F32)


def t_mm(left, right):
    return lax.dot_general(left, right, (((0,), (0,)), ((), ())), preferred_element_type=F32)


def norm_parts(values):
    average = jnp.mean(values, axis=-1, keepdims=True)
    centered = values - average
    variance = jnp.mean(centered * centered, axis=-1, keepdims=True)
    rstd = lax.rsqrt(variance + EPS)
    return centered * rstd, rstd


def norm_back(grad, gain, xhat, rstd):
    scaled = grad * gain
    return rstd * (
        scaled
        - jnp.mean(scaled, axis=-1, keepdims=True)
        - xhat * jnp.mean(scaled * xhat, axis=-1, keepdims=True)
    )


def gelu_parts(pre):
    cdf = 0.5 * (1.0 + lax.erf(pre * (1.0 / math.sqrt(2.0))))
    pdf = jnp.exp(-0.5 * pre * pre) * (1.0 / math.sqrt(2.0 * math.pi))
    return pre * cdf, cdf + pre * pdf


SMALL_PARAMS = pltpu.CompilerParams(vmem_limit_bytes=60 * 2**20)
VMEM = pl.BlockSpec(memory_space=pltpu.VMEM)
SMEM = pl.BlockSpec(memory_space=pltpu.SMEM)
LITTLE = pltpu.CompilerParams(vmem_limit_bytes=24 * 2**20)
FAR_XY = [(i, i ^ 6) for i in range(8)]
CORE = [(i, i ^ 1) for i in range(8)]
ALONG_X = [(i, i ^ 2) for i in range(8)]
ALONG_Y = [(i, i ^ 4) for i in range(8)]
SPLIT_XY = [(i, i ^ (4 if i & 1 else 2)) for i in range(8)]
CROSS_XY = [(i, i ^ (3 if i & 1 else 5)) for i in range(8)]


def send(array, pairs):
    return lax.ppermute(array, "dp", pairs)


def shift(array, by, groups):
    return lax.ppermute(array, "tensor", [(i, (i + by) % groups) for i in range(groups)])


def scoped(name, step, *args):
    with jax.named_scope(name):
        return step(*args)


def tie(array, *others):
    return lax.optimization_barrier((array,) + others)[0]


def order_kernel(spots_ref, *refs, groups):
    pieces, (join_ref, bias_ref, stage_ref, sems) = refs[:-4], refs[-4:]
    copies = []
    for k, piece in enumerate(pieces):
        for i in range(groups):
            plane = lax.rem(spots_ref[8] + (groups - i), groups)
            copies.append(
                pltpu.make_async_copy(piece.at[i], stage_ref.at[spots_ref[k] * groups + plane], sems.at[len(copies)])
            )
    for copy in copies:
        copy.start()
    for copy in copies:
        copy.wait()
    rows = join_ref.shape[1] // stage_ref.shape[0]
    for b in range(0, stage_ref.shape[0], 2):
        pair = [stage_ref[b + i].astype(F32) for i in range(2)]
        for m in range(3):
            both = jnp.concatenate([block[m * rows : (m + 1) * rows] for block in pair], axis=0)
            join_ref[m, b * rows : (b + 2) * rows, :] = both.astype(BF)
        for i in range(2):
            bias_ref[b + i] = pair[i][3 * rows :]


def order(pieces, spots, groups):
    height, dim = pieces[0].shape[1:]
    blocks = 8 * groups
    return pl.pallas_call(
        partial(order_kernel, groups=groups),
        out_shape=[jax.ShapeDtypeStruct((3, dim, dim), BF), jax.ShapeDtypeStruct((blocks, 8, dim), F32)],
        in_specs=[SMEM] + [ANY] * 8,
        out_specs=[VMEM] * 2,
        scratch_shapes=[pltpu.VMEM((blocks, height, dim), BF), pltpu.SemaphoreType.DMA((blocks,))],
        compiler_params=SMALL_PARAMS,
    )(spots, *pieces)


COPIES = 32


def fetch(spots_ref, sources, out_ref, sems, stacked=False):
    if len(sources) == 1:
        copies = [pltpu.make_async_copy(sources[0], out_ref, sems.at[0])]
    else:
        pieces, own = sources[:-1], sources[-1]
        groups, dim = out_ref.shape[0], out_ref.shape[1]
        rows, width = pieces[0].shape[1], dim // groups
        copies = []

        def add(source, target):
            copies.append(pltpu.make_async_copy(source, target, sems.at[len(copies)]))

        my_z = spots_ref[8]
        if stacked:
            for m in range(groups):
                add(own.at[pl.ds(m * width, width)], out_ref.at[m, pl.ds(pl.multiple_of(my_z * width, width), width)])
        else:
            add(own, out_ref.at[my_z])
        per = width // rows
        for k, piece in enumerate(pieces):
            e = spots_ref[k]
            for i in range(groups - 1):
                plane = lax.rem(my_z + (groups - 1 - i), groups)
                if stacked:
                    at = pl.multiple_of(plane * width + lax.rem(e, per) * rows, rows)
                    add(piece.at[i], out_ref.at[lax.div(e, per), pl.ds(at, rows)])
                else:
                    add(piece.at[i], out_ref.at[plane, pl.ds(pl.multiple_of(e * rows, rows), rows)])
    for copy in copies:
        copy.start()
    return copies


ANY = pl.BlockSpec(memory_space=pl.ANY)


class Gather:
    def __init__(self, dp_size, groups, my_d, my_z):
        self.dp_size, self.groups, self.my_d, self.my_z = dp_size, groups, my_d, my_z
        self.paired = dp_size == 8 and groups == 4
        core = lax.rem(my_d, 2)
        even = [0, 1, 2, 3, 7, 5, 4, 6]
        odd = [0, 1, 4, 5, 7, 3, 2, 6]
        flips = jnp.where(core == 0, jnp.array(even, jnp.int32), jnp.array(odd, jnp.int32))
        self.spots = jnp.concatenate([jnp.bitwise_xor(my_d, flips), my_z[None]]).astype(jnp.int32)

    def all_parts(self, part):
        whole = lax.all_gather(part, ("dp", "tensor"), axis=0)
        return whole.reshape((self.dp_size, self.groups) + part.shape).transpose(1, 0, 2, 3)

    def part_of(self, shard):
        rows = shard.shape[0] // self.dp_size
        return lax.dynamic_slice_in_dim(shard, self.my_d * rows, rows, 0)

    def all_rounds(self, parts, steps):
        count = len(parts)
        gathered, spread = [], []
        ahead, done = self.planes(parts[0][0], 0), []
        for r in range(count + 2):
            with jax.named_scope("round%d" % r):
                if r < count:
                    part, with_own = parts[r]
                    items = jnp.stack(([part] if with_own else []) + [ahead[i] for i in (1, 2, 3)])
                    items = tie(items, *done)
                    mark = [items]
                    other = scoped("other", send, items, CORE)
                    if r + 1 < count:
                        ahead = self.planes(tie(parts[r + 1][0], items), r + 1)
                else:
                    mark = done
                if 1 <= r <= count:
                    last = spread[r - 1]
                    last.append(scoped("far", send, tie(last[2], *mark), CROSS_XY))
                if r < count:
                    near0, near1 = scoped("near0", send, items, SPLIT_XY), scoped("near1", send, other, SPLIT_XY)
                if 1 <= r <= count:
                    last += [scoped("swap%d" % i, send, tie(last[2 + i], *mark), CORE) for i in range(2)]
                if r >= 2:
                    whole = spread[r - 2]
                    gathered.append(whole + [scoped("swap2", send, tie(whole[4], *mark), CORE)])
                if r < count:
                    spread.append([items, other, near0, near1])
                done = steps[r](gathered)
        return gathered

    def planes(self, part, g):
        with jax.named_scope("planes%d" % g):
            return {i: scoped("by%d" % i, shift, part, i, self.groups) for i in (1, 3, 2)}

    def whole(self, part, stacked=False):
        whole = self.all_parts(part)
        dim = part.shape[1]
        if stacked:
            whole = whole.reshape(self.groups, 4, -1, dim).transpose(1, 0, 2, 3)
        return [whole.reshape(4, -1, dim)]


def reduce_grads(gather, grads, own_rows):
    groups, spots = gather.groups, gather.spots
    if not gather.paired:
        mats, bias = grads
        mats = lax.psum_scatter(mats, ("dp", "tensor"), scatter_dimension=1, tiled=True)
        return mats[0], mats[1], mats[2], lax.psum(bias, ("dp", "tensor"))
    keep, away = grads
    rows, dim = keep.shape[1:]
    low = jax.ShapeDtypeStruct((rows, dim), BF)
    come = scoped("cores", send, away, CORE)
    own, bias, to_x, to_y, to_far = pl.pallas_call(
        add_cores_kernel,
        out_shape=[jax.ShapeDtypeStruct((rows - 16, dim), F32), jax.ShapeDtypeStruct((8, dim), F32), low, low, low],
        in_specs=[SMEM, VMEM, VMEM],
        out_specs=[VMEM] * 5,
        compiler_params=LITTLE,
    )(spots, keep, come)
    from_far = scoped("far", send, to_far, FAR_XY)
    from_x = scoped("x", send, to_x, ALONG_X)
    from_y = scoped("y", send, to_y, ALONG_Y)
    block = jax.ShapeDtypeStruct((3 * own_rows + 24, dim), BF)
    mine, *goes = pl.pallas_call(
        add_plane_kernel,
        out_shape=[jax.ShapeDtypeStruct((3 * own_rows + 8, dim), F32)] + [block] * (groups - 1),
        in_specs=[SMEM] + [VMEM] * 5,
        out_specs=[VMEM] * groups,
        scratch_shapes=[pltpu.VMEM((rows - 16, dim), F32)],
        compiler_params=LITTLE,
    )(spots, own, bias, from_x, from_y, from_far)
    comes = [scoped("stack%d" % i, shift, go, i + 1, groups) for i, go in enumerate(goes)]
    part = jax.ShapeDtypeStruct((own_rows, dim), F32)
    return pl.pallas_call(
        add_stack_kernel,
        out_shape=[part, part, part, jax.ShapeDtypeStruct((8, dim), F32)],
        in_specs=[VMEM] * groups,
        out_specs=[VMEM] * 4,
        compiler_params=LITTLE,
    )(mine, *comes)


def cost(flops, moved, exps=0):
    return pl.CostEstimate(flops=int(flops), bytes_accessed=int(moved), transcendentals=int(exps))


def head_masks():
    lane = lax.broadcasted_iota(jnp.int32, (1, 128), 1)
    first = (lane < 64).astype(F32)
    return [first.astype(BF), (1.0 - first).astype(BF)], lane < 64


def attention_kernel(spots_ref, len_ref, x_ref, gain_ref, bias_ref, *refs):
    sources = refs[:-10]
    q_ref, k_ref, v_ref, p_ref, low_ref, xhat_ref, rstd_ref, w_ref, ctx_ref, sems = refs[-10:]
    copies = fetch(spots_ref, sources, w_ref, sems, True)
    rows, dim = x_ref.shape
    for copy in copies:
        copy.wait()
    seq_len = p_ref.shape[1]
    x = x_ref[...]
    q_ref[...] = (mm_t(x, w_ref[0]).astype(BF).astype(F32) * (1.0 / math.sqrt(dim // HEADS))).astype(BF)
    k_ref[...] = mm_t(x, w_ref[1]).astype(BF)
    v_ref[...] = mm_t(x, w_ref[2]).astype(BF)
    masks, first = head_masks()
    key_at = lax.broadcasted_iota(jnp.int32, (seq_len, 1), 0)

    def one_seq(s, _):
        at = pl.ds(pl.multiple_of(s * seq_len, seq_len), seq_len)
        valid = key_at < len_ref[s]
        for j in range(HEADS // 2):
            cols = slice(128 * j, 128 * (j + 1))
            q, k, v = q_ref[at, cols], k_ref[at, cols], v_ref[at, cols]
            parts = []
            for h in range(2):
                scores = jnp.where(valid, mm_t(k, q * masks[h]), MASKED)
                exps = jnp.exp(scores - jnp.max(scores, axis=0, keepdims=True))
                probs = (exps * (1.0 / jnp.sum(exps, axis=0, keepdims=True))).astype(BF)
                p_ref[s * HEADS + 2 * j + h] = probs
                parts.append(t_mm(probs, v))
            ctx_ref[at, cols] = jnp.where(first, parts[0], parts[1]).astype(BF)
        return 0

    lax.fori_loop(0, rows // seq_len, one_seq, 0)
    xhat, rstd = norm_parts(x.astype(F32) + mm(ctx_ref[...], w_ref[3]))
    xhat_ref[...] = xhat
    rstd_ref[...] = rstd
    low_ref[...] = (xhat * gain_ref[...] + bias_ref[...]).astype(BF)


def attention_forward(spots, lengths, x, sources, gain, bias, seq_len):
    rows, dim = x.shape
    seqs = rows // seq_len
    low = jax.ShapeDtypeStruct((rows, dim), BF)
    return pl.pallas_call(
        attention_kernel,
        out_shape=[low, low, low,
                   jax.ShapeDtypeStruct((seqs * HEADS, seq_len, seq_len), BF), low,
                   jax.ShapeDtypeStruct((rows, dim), F32), jax.ShapeDtypeStruct((rows, 1), F32)],
        in_specs=[SMEM] * 2 + [VMEM] * 3 + [ANY] * len(sources),
        out_specs=[VMEM] * 7,
        scratch_shapes=[pltpu.VMEM((4, dim, dim), BF), pltpu.VMEM((rows, dim), BF), pltpu.SemaphoreType.DMA((COPIES,))],
        compiler_params=SMALL_PARAMS,
        cost_estimate=cost(2 * rows * dim * (4 * dim + 2 * seq_len), 2 * (4 * dim * dim + 8 * rows * dim), rows * seq_len * HEADS),
    )(spots, lengths, x, gain, bias, *sources)


def gelu_rows(pre_ref, act_ref, slope_ref, step=32):
    def some(i, _):
        at = pl.ds(pl.multiple_of(i * step, step), step)
        act, slope = gelu_parts(pre_ref[at, :])
        act_ref[at, :] = act.astype(act_ref.dtype)
        slope_ref[at, :] = slope.astype(slope_ref.dtype)
        return 0

    lax.fori_loop(0, pre_ref.shape[0] // step, some, 0)


def ffn_in_kernel(spots_ref, x_ref, bias_ref, *refs):
    sources = refs[:-5]
    act_ref, slope_ref, w_ref, pre_ref, sems = refs[-5:]
    for copy in fetch(spots_ref, sources, w_ref, sems):
        copy.wait()
    for p in range(w_ref.shape[0]):
        pre_ref[...] = mm(x_ref[...], w_ref[p]) + bias_ref[p]
        gelu_rows(pre_ref, act_ref.at[p], slope_ref.at[p])


def ffn_forward(spots, x, sources, bias, units):
    rows, dim = x.shape
    planes = bias.shape[0] // units
    out = jax.ShapeDtypeStruct((planes, rows, units), BF)
    return pl.pallas_call(
        ffn_in_kernel,
        out_shape=[out, out],
        in_specs=[SMEM] + [VMEM] * 2 + [ANY] * len(sources),
        out_specs=[VMEM] * 2,
        scratch_shapes=[
            pltpu.VMEM((planes, dim, units), BF), pltpu.VMEM((rows, units), F32), pltpu.SemaphoreType.DMA((COPIES,)),
        ],
        compiler_params=SMALL_PARAMS,
        cost_estimate=cost(2 * rows * dim * units * planes, 2 * planes * units * (dim + 2 * rows), 2 * rows * units * planes),
    )(spots, x, bias.reshape(planes, 1, units), *sources)


def two_pass(values, table):
    high = values.astype(BF)
    return mm(high, table) + mm((values - high.astype(F32)).astype(BF), table)


def put_rows(ref, mats, bias):
    at = 0
    for mat in mats:
        ref[at : at + mat.shape[0], :] = mat.astype(BF)
        at += mat.shape[0]
    high = bias.astype(BF).astype(F32)
    ref[at : at + 16, :] = jnp.concatenate([high, bias - high], axis=0).astype(BF)


def sum_rows(arrays):
    total = arrays[0].astype(F32)
    for array in arrays[1:]:
        total = total + array.astype(F32)
    rows = total.shape[0] - 16
    return total[:rows], total[rows : rows + 8] + total[rows + 8 :]


def add_cores_kernel(spots_ref, keep_ref, come_ref, own_ref, bias_ref, x_ref, y_ref, far_ref):
    quarter = lax.div(spots_ref[0], 2)
    own_ref[...], bias_ref[...] = sum_rows([keep_ref[quarter], come_ref[quarter]])
    for flip, ref in ((1, x_ref), (2, y_ref), (3, far_ref)):
        q = jnp.bitwise_xor(quarter, flip)
        mats, bias = sum_rows([keep_ref[q], come_ref[q]])
        put_rows(ref, [mats], bias)


def add_plane_kernel(spots_ref, own_ref, bias_ref, x_ref, y_ref, far_ref, mine_ref, *refs):
    go_refs, total_ref = refs[:-1], refs[-1]
    mats, bias = sum_rows([x_ref[...], y_ref[...], far_ref[...]])
    total_ref[...] = own_ref[...] + mats
    bias = bias + bias_ref[...]
    groups = len(go_refs) + 1
    width = total_ref.shape[0] // 3
    rows = width // groups

    def block(plane):
        at = [pl.multiple_of(i * width + plane * rows, 8) for i in range(3)]
        return jnp.concatenate([total_ref[pl.ds(a, rows), :] for a in at], axis=0)

    my_z = spots_ref[8]
    mine_ref[...] = jnp.concatenate([block(my_z), bias], axis=0)
    high = bias.astype(BF).astype(F32)
    for i, ref in enumerate(go_refs):
        there = block(lax.rem(my_z + i + 1, groups))
        ref[...] = jnp.concatenate([there, high, bias - high, jnp.zeros_like(bias)], axis=0).astype(BF)


def add_stack_kernel(mine_ref, *refs):
    come_refs, (q_ref, k_ref, v_ref, bias_ref) = refs[:-4], refs[-4:]
    total = mine_ref[...]
    rows = q_ref.shape[0]
    for ref in come_refs:
        come = ref[...].astype(F32)
        bias = come[3 * rows : 3 * rows + 8] + come[3 * rows + 8 : 3 * rows + 16]
        total = total + jnp.concatenate([come[: 3 * rows], bias], axis=0)
    q_ref[...], k_ref[...], v_ref[...] = (total[i * rows : (i + 1) * rows] for i in range(3))
    bias_ref[...] = total[3 * rows :]


def joining_kernel(
    spots_ref, act_ref, member_ref, member_t_ref, qb_ref, vb_ref, avail_ref,
    xhat1_ref, gain1_ref, bias1_ref, cot_ref, gain2_ref, bias2_ref, *refs, halves
):
    *refs, w_out_ref, down_ref, up_ref, join_ref, pre_ref, down_act_ref, slope_ref, sums_ref, bias_sums_ref, out_sems, sems = refs
    *sources, down_hbm, up_hbm, join_hbm, out_ref, g2_ref, g_ffn_ref, grad_ref0, grad_ref1 = refs
    grad_refs = [grad_ref0, grad_ref1]
    s = pl.program_id(0)
    loads = [
        pltpu.make_async_copy(source, target, sems.at[i])
        for i, (source, target) in enumerate(((down_hbm, down_ref), (join_hbm, join_ref), (up_hbm, up_ref)))
    ]

    @pl.when(s == 0)
    def _():
        copies = fetch(spots_ref, sources, w_out_ref, out_sems)
        for load in loads:
            load.start()
        for copy in copies:
            copy.wait()

    dim = out_ref.shape[-1]
    fscale = 1.0 / math.sqrt(dim)
    member, member_t = member_ref[...], member_t_ref[...]
    ffn = mm(act_ref[0], w_out_ref[0])
    for p in range(1, act_ref.shape[0]):
        ffn = ffn + mm(act_ref[p], w_out_ref[p])
    x_low = ffn.astype(BF)

    @pl.when(s == 0)
    def _():
        for load in loads:
            load.wait()

    up = up_ref[...]
    pre_ref[...] = mm(x_low, down_ref[...])
    gelu_rows(pre_ref, down_act_ref, slope_ref)
    q_low = (mm(x_low, join_ref[0]) + qb_ref[...]).astype(BF)
    u = mm_t(q_low, join_ref[1])
    big_u = mm_t(u.astype(BF), up)
    down = down_act_ref[...].astype(F32)
    fscores = (two_pass(down * big_u, member) + jnp.sum(ffn * u, axis=-1, keepdims=True)) * fscale
    fscores = jnp.where(avail_ref[0] > 0, fscores, MASKED)
    fexp = jnp.exp(fscores - jnp.max(fscores, axis=-1, keepdims=True))
    fprobs = fexp / jnp.sum(fexp, axis=-1, keepdims=True)
    p_wide = two_pass(fprobs, member_t)
    mixed_low = (ffn + mm((p_wide * down).astype(BF), up)).astype(BF)
    normed1 = xhat1_ref[...] * gain1_ref[...] + bias1_ref[...]
    xhat2, rstd2 = norm_parts(normed1 + mm(mixed_low, join_ref[2]) + vb_ref[...])
    out_ref[...] = (xhat2 * gain2_ref[...] + bias2_ref[...]).astype(BF)

    g2 = norm_back(cot_ref[...].astype(F32), gain2_ref[...], xhat2, rstd2)
    g2_ref[...] = g2
    g2_low = g2.astype(BF)
    w = mm_t(g2_low, join_ref[2])
    big_w = mm_t(w.astype(BF), up)
    gvals = two_pass(down * big_w, member) + jnp.sum(ffn * w, axis=-1, keepdims=True) + jnp.sum(g2 * vb_ref[...], axis=-1, keepdims=True)
    gs = fprobs * (gvals - jnp.sum(gvals * fprobs, axis=-1, keepdims=True)) * fscale
    gs_sum = jnp.sum(gs, axis=-1, keepdims=True)
    gs_wide = two_pass(gs, member_t)
    t_low = (mm((gs_wide * down).astype(BF), up) + gs_sum * ffn).astype(BF)
    gq_low = mm(t_low, join_ref[1]).astype(BF)
    g_down = ((gs_wide * big_u + p_wide * big_w) * slope_ref[...]).astype(BF)
    g_ffn = gs_sum * u + w + mm_t(g_down, down_ref[...]) + mm_t(gq_low, join_ref[0])
    g_ffn_ref[...] = g_ffn.astype(BF)

    first, last = s == 0, s == pl.num_programs(0) - 1
    pairs = ((x_low, gq_low), (t_low, q_low), (mixed_low, g2_low))
    d_qb = jnp.sum(gq_low.astype(F32), axis=0, keepdims=True)
    d_vb = jnp.sum(g2, axis=0, keepdims=True)
    row = lax.broadcasted_iota(jnp.int32, (8, 1), 0)
    d_bias = jnp.where(row == 0, d_qb, jnp.where(row == 1, d_vb, 0.0))

    @pl.when(first)
    def _():
        bias_sums_ref[...] = d_bias
        for i, (left, right) in enumerate(pairs):
            sums_ref[i] = t_mm(left, right)

    @pl.when(jnp.logical_not(first))
    def _():
        bias_sums_ref[...] += d_bias
        for i, (left, right) in enumerate(pairs):
            sums_ref[i] += t_mm(left, right)

    @pl.when(last)
    def _():
        if not halves:
            grad_refs[0][...] = sums_ref[...]
            grad_refs[1][...] = bias_sums_ref[...]
            return
        core = lax.rem(spots_ref[0], 2)
        part = dim // 8
        for ref, side in zip(grad_refs, (core, 1 - core)):
            for q in range(4):
                at = pl.ds(pl.multiple_of((2 * q + side) * part, part), part)
                put_rows(ref.at[q], [sums_ref[i, at, :] for i in range(3)], bias_sums_ref[...])


def joining(spots, halves, act, sources, adapt_down, up, join, qb, vb, avail, xhat1, gain1, bias1, cot, gain2, bias2, seq_len, neck):
    planes, rows, units = act.shape
    dim = xhat1.shape[1]
    seqs = rows // seq_len
    owner = jnp.arange(up.shape[0], dtype=jnp.int32) // neck
    member = (owner[:, None] == jnp.arange(128, dtype=jnp.int32)[None, :]).astype(BF)
    row_block = pl.BlockSpec((seq_len, dim), lambda s: (s, 0))

    def whole(array):
        return pl.BlockSpec(array.shape, lambda s: (0,) * array.ndim, pipeline_mode=pl.Buffered(1))

    member_t = member.T
    if halves:
        grads = [jax.ShapeDtypeStruct((4, 3 * dim // 8 + 16, dim), BF)] * 2
    else:
        grads = [jax.ShapeDtypeStruct((3, dim, dim), F32), jax.ShapeDtypeStruct((8, dim), F32)]
    return pl.pallas_call(
        partial(joining_kernel, halves=halves),
        grid=(seqs,),
        out_shape=[
            jax.ShapeDtypeStruct((rows, dim), BF),
            jax.ShapeDtypeStruct((rows, dim), F32),
            jax.ShapeDtypeStruct((rows, dim), BF),
        ] + grads,
        in_specs=[
            SMEM, pl.BlockSpec((planes, seq_len, units), lambda s: (0, s, 0)),
            whole(member), whole(member_t), whole(qb), whole(vb),
            pl.BlockSpec((1, 1, 128), lambda s: (s, 0, 0)),
            row_block, whole(gain1), whole(bias1), row_block, whole(gain2), whole(bias2),
        ] + [ANY] * (len(sources) + 3),
        out_specs=[row_block, row_block, row_block] + [whole(grad) for grad in grads],
        scratch_shapes=[
            pltpu.VMEM((planes, units, dim), BF),
            pltpu.VMEM(adapt_down.shape, BF),
            pltpu.VMEM(up.shape, BF),
            pltpu.VMEM(join.shape, BF),
            pltpu.VMEM((seq_len, dim), F32),
            pltpu.VMEM((seq_len, dim), BF),
            pltpu.VMEM((seq_len, dim), F32),
            pltpu.VMEM((3, dim, dim), F32),
            pltpu.VMEM((8, dim), F32),
            pltpu.SemaphoreType.DMA((COPIES,)),
            pltpu.SemaphoreType.DMA((3,)),
        ],
        compiler_params=SMALL_PARAMS,
        cost_estimate=cost(2 * rows * dim * (15 * dim + planes * units), 2 * dim * (8 * dim + 10 * rows), 2 * rows * dim),
    )(spots, act, member, member_t, qb, vb, avail, xhat1, gain1, bias1, cot, gain2, bias2, *sources, adapt_down, up, join)


def ffn_back_kernel(spots_ref, g_ref, rstd_ref, gain_ref, *refs, count):
    out_sources, in_sources = refs[:count], refs[count : 2 * count]
    slope_hbm, g2_hbm, xhat_hbm, g1_ref = refs[2 * count : 2 * count + 4]
    w_out_ref, w_in_ref, slope_ref, g2_ref, xhat_ref, pre_ref, out_sems, in_sems, sems = refs[2 * count + 4 :]
    out_copies = fetch(spots_ref, out_sources, w_out_ref, out_sems)
    loads = [
        pltpu.make_async_copy(source, target, sems.at[i])
        for i, (source, target) in enumerate(((slope_hbm, slope_ref), (g2_hbm, g2_ref), (xhat_hbm, xhat_ref)))
    ]
    loads[0].start()
    in_copies = fetch(spots_ref, in_sources, w_in_ref, in_sems)
    loads[1].start()
    loads[2].start()
    for copy in out_copies:
        copy.wait()
    loads[0].wait()
    planes = slope_ref.shape[0]
    for p in range(planes):
        pre_ref[p] = (mm_t(g_ref[...], w_out_ref[p]) * slope_ref[p].astype(F32)).astype(BF)
    for copy in in_copies:
        copy.wait()
    total = mm_t(pre_ref[0], w_in_ref[0])
    for p in range(1, planes):
        total = total + mm_t(pre_ref[p], w_in_ref[p])
    loads[1].wait()
    loads[2].wait()
    g1_ref[...] = norm_back(total + g2_ref[...], gain_ref[...], xhat_ref[...], rstd_ref[...])


def ffn_backward(spots, g_ffn, slope, out_sources, in_sources, g2, xhat, rstd, gain):
    planes, rows, units = slope.shape
    dim = xhat.shape[1]
    return pl.pallas_call(
        partial(ffn_back_kernel, count=len(out_sources)),
        out_shape=jax.ShapeDtypeStruct((rows, dim), F32),
        in_specs=[SMEM] + [VMEM] * 3 + [ANY] * (2 * len(out_sources) + 3),
        out_specs=VMEM,
        scratch_shapes=[
            pltpu.VMEM((planes, units, dim), BF), pltpu.VMEM((planes, dim, units), BF), pltpu.VMEM((planes, rows, units), BF),
            pltpu.VMEM((rows, dim), F32), pltpu.VMEM((rows, dim), F32), pltpu.VMEM((planes, rows, units), BF),
            pltpu.SemaphoreType.DMA((COPIES,)), pltpu.SemaphoreType.DMA((COPIES,)), pltpu.SemaphoreType.DMA((3,)),
        ],
        compiler_params=SMALL_PARAMS,
        cost_estimate=cost(4 * rows * dim * units * planes, 2 * planes * units * (2 * dim + rows)),
    )(spots, g_ffn, rstd, gain, *out_sources, *in_sources, slope, g2, xhat)


def attention_back_kernel(spots_ref, g1_ref, *refs):
    *refs, out_ref, w_ref, q_ref, k_ref, v_ref, p_ref, ctx_ref, dq_ref, dk_ref, dv_ref, w_sems, sems = refs
    *sources, q_hbm, k_hbm, v_hbm, p_hbm = refs
    copies = fetch(spots_ref, sources, w_ref, w_sems, True)
    loads = [
        pltpu.make_async_copy(source, target, sems.at[i])
        for i, (source, target) in enumerate(((q_hbm, q_ref), (k_hbm, k_ref), (v_hbm, v_ref), (p_hbm, p_ref)))
    ]
    for load in loads:
        load.start()
    for copy in copies:
        copy.wait()
    rows, dim = g1_ref.shape
    seq_len = p_ref.shape[1]
    scale = 1.0 / math.sqrt(dim // HEADS)
    ctx_ref[...] = mm_t(g1_ref[...].astype(BF), w_ref[3]).astype(BF)
    for load in loads:
        load.wait()
    masks, first = head_masks()

    def one_seq(s, _):
        at = pl.ds(pl.multiple_of(s * seq_len, seq_len), seq_len)
        for j in range(HEADS // 2):
            cols = slice(128 * j, 128 * (j + 1))
            q, k, v, g = q_ref[at, cols], k_ref[at, cols], v_ref[at, cols], ctx_ref[at, cols]
            dq, dk, dv = [], [], []
            for h in range(2):
                probs_low = p_ref[s * HEADS + 2 * j + h]
                probs = probs_low.astype(F32)
                g_probs = mm_t(v, g * masks[h])
                g_scores = (probs * (g_probs - jnp.sum(g_probs * probs, axis=0, keepdims=True))).astype(BF)
                dv.append(mm(probs_low, g))
                dk.append(mm(g_scores, q))
                dq.append(t_mm(g_scores, k))
            dq_ref[at, cols] = (jnp.where(first, dq[0], dq[1]) * scale).astype(BF)
            dk_ref[at, cols] = jnp.where(first, dk[0], dk[1]).astype(BF)
            dv_ref[at, cols] = jnp.where(first, dv[0], dv[1]).astype(BF)
        return 0

    lax.fori_loop(0, rows // seq_len, one_seq, 0)
    total = g1_ref[...] + mm(dq_ref[...], w_ref[0])
    total = total + mm(dk_ref[...], w_ref[1])
    out_ref[...] = (total + mm(dv_ref[...], w_ref[2])).astype(BF)


def attention_backward(spots, g1, sources, q, k, v, probs):
    rows, dim = g1.shape
    seq_len = probs.shape[1]
    low = pltpu.VMEM((rows, dim), BF)
    return pl.pallas_call(
        attention_back_kernel,
        out_shape=jax.ShapeDtypeStruct((rows, dim), BF),
        in_specs=[SMEM, VMEM] + [ANY] * (len(sources) + 4),
        out_specs=VMEM,
        scratch_shapes=[pltpu.VMEM((4, dim, dim), BF), low, low, low, pltpu.VMEM(probs.shape, BF), low, low, low, low,
                        pltpu.SemaphoreType.DMA((COPIES,)), pltpu.SemaphoreType.DMA((4,))],
        compiler_params=SMALL_PARAMS,
        cost_estimate=cost(2 * rows * dim * (4 * dim + 4 * seq_len), 2 * (4 * dim * dim + 8 * rows * dim)),
    )(spots, g1, *sources, q, k, v, probs)


def shards(
    tokens, lengths, adapter_mask, cotangent, att_query, att_key, att_value, att_out,
    norm1_gain, norm1_bias, ffn_in, ffn_bias, ffn_out, adapt_down, adapt_up, norm2_gain,
    norm2_bias, joining_query, joining_key, joining_value, joining_qbias, joining_vbias,
):
    groups = lax.axis_size("tensor")
    dp_size = lax.axis_size("dp")
    my_z = lax.axis_index("tensor")
    my_d = lax.axis_index("dp")
    seq_local, seq_len, dim = tokens.shape
    mine = seq_local // groups
    rows = mine * seq_len
    adapters, neck = adapt_up.shape[0], adapt_up.shape[1]
    own_rows = joining_query.shape[0]

    gather = Gather(dp_size, groups, my_d, my_z)
    spots = gather.spots
    biases = jnp.pad(jnp.stack([joining_qbias, joining_vbias]), ((0, 6), (0, dim - own_rows)))
    att_pack = jnp.concatenate([att_query.T, att_key.T, att_value.T, att_out], axis=0)
    join_part = jnp.concatenate([joining_query, joining_key, joining_value, biases], axis=0)
    parts = [gather.part_of(att_pack), gather.part_of(ffn_in), join_part, gather.part_of(ffn_out)]

    def my_slice(array):
        return lax.dynamic_slice_in_dim(array, my_z * mine, mine, 0)

    x = my_slice(tokens).reshape(rows, dim)
    shifts = jnp.arange(128, dtype=jnp.int32)
    bits = jnp.right_shift(my_slice(adapter_mask)[:, None], jnp.minimum(shifts, adapters)[None, :]) % 2
    avail = jnp.where(shifts[None, :] < adapters, bits, 0)[:, None, :]
    gain1, bias1, gain2, bias2 = (v.reshape(1, dim) for v in (norm1_gain, norm1_bias, norm2_gain, norm2_bias))
    kept = {}

    def attend(sources):
        kept["att"] = attention_forward(spots, my_slice(lengths), x, sources, gain1, bias1, seq_len)
        return [kept["att"][4]]

    def feed(sources):
        kept["ffn"] = ffn_forward(spots, kept["att"][4], sources, ffn_bias, ffn_in.shape[1])
        return [kept["ffn"][0]]

    def join_of(join, rows_of_bias):
        kept["join"] = join
        kept["bias"] = [rows_of_bias[:, i, :own_rows].reshape(1, dim) for i in range(2)]
        return [join] + kept["bias"]

    if gather.paired:
        own = [att_pack, ffn_in, None, ffn_out]
        steps = [
            lambda got: [],
            lambda got: [],
            lambda got: attend(got[0] + own[:1]),
            lambda got: feed(got[1] + own[1:2]),
            lambda got: join_of(*order(got[2], spots, groups)),
            lambda got: [],
        ]
        got = gather.all_rounds([(part, shard is None) for part, shard in zip(parts, own)], steps)
        att_sources, in_sources, out_sources = (got[i] + [own[i]] for i in (0, 1, 3))
    else:
        att_sources, in_sources, out_sources = (gather.whole(parts[i], i == 0) for i in (0, 1, 3))
        attend(att_sources)
        feed(in_sources)
        join_all = gather.all_parts(parts[2]).transpose(1, 0, 2, 3)
        mats = [join_all[:, :, i * own_rows : (i + 1) * own_rows].reshape(dim, dim) for i in range(3)]
        join_of(jnp.stack(mats), join_all[:, :, 3 * own_rows :].reshape(-1, 8, dim).astype(F32))
    q, k, v, probs, low1, xhat1, rstd1 = kept["att"]
    act, slope = kept["ffn"]
    up = adapt_up.reshape(adapters * neck, dim)
    layer_out, g2, g_ffn, *grads = joining(
        spots, gather.paired, act, out_sources, adapt_down, up, kept["join"], *kept["bias"], avail, xhat1, gain1, bias1,
        cotangent.reshape(rows, dim), gain2, bias2, seq_len, neck,
    )
    g1 = ffn_backward(spots, g_ffn, slope, out_sources, in_sources, g2, xhat1, rstd1, gain1)
    input_grad = attention_backward(spots, g1, att_sources, q, k, v, probs)
    d_q, d_k, d_v, d_bias = reduce_grads(gather, grads, own_rows)
    d_bias = lax.dynamic_slice_in_dim(d_bias[:2], (my_d * groups + my_z) * own_rows, own_rows, 1)
    return (
        layer_out.reshape(mine, seq_len, dim),
        input_grad.reshape(mine, seq_len, dim),
        d_q, d_k, d_v, d_bias[0], d_bias[1],
    )


def solution(mesh):
    both = P(ALL, None)
    return jax.shard_map(
        shards,
        mesh=mesh,
        in_specs=(
            P("dp", None, None), P("dp"), P("dp"), P(ALL, None, None),
            P(None, "tensor"), P(None, "tensor"), P(None, "tensor"), P("tensor", None),
            P(), P(), P(None, "tensor"), P(), P("tensor", None), P(), P(), P(), P(),
            both, both, both, P(ALL), P(ALL),
        ),
        out_specs=(P(ALL, None, None), P(ALL, None, None), both, both, both, P(ALL), P(ALL)),
        check_vma=False,
    )
```

```python
from functools import partial
import math

import jax
import jax.numpy as jnp
from jax import lax
from jax.experimental import pallas as pl
from jax.experimental.pallas import tpu as pltpu
from jax.sharding import PartitionSpec as P

HEADS = 12
EPS = 1e-05
MASKED = -1e30
ALL = ("dp", "tensor")
BF = jnp.bfloat16
F32 = jnp.float32


def mm(left, right):
    return jnp.dot(left, right, preferred_element_type=F32)


def mm_t(left, right):
    return lax.dot_general(left, right, (((1,), (1,)), ((), ())), preferred_element_type=F32)


def t_mm(left, right):
    return lax.dot_general(left, right, (((0,), (0,)), ((), ())), preferred_element_type=F32)


def norm_parts(values):
    average = jnp.mean(values, axis=-1, keepdims=True)
    centered = values - average
    variance = jnp.mean(centered * centered, axis=-1, keepdims=True)
    rstd = lax.rsqrt(variance + EPS)
    return centered * rstd, rstd


def norm_back(grad, gain, xhat, rstd):
    scaled = grad * gain
    return rstd * (
        scaled
        - jnp.mean(scaled, axis=-1, keepdims=True)
        - xhat * jnp.mean(scaled * xhat, axis=-1, keepdims=True)
    )


def gelu_parts(pre):
    cdf = 0.5 * (1.0 + lax.erf(pre * (1.0 / math.sqrt(2.0))))
    pdf = jnp.exp(-0.5 * pre * pre) * (1.0 / math.sqrt(2.0 * math.pi))
    return pre * cdf, cdf + pre * pdf


def limit(mebibytes):
    return pltpu.CompilerParams(vmem_limit_bytes=mebibytes * 2**20)


VMEM = pl.BlockSpec(memory_space=pltpu.VMEM)
SMEM = pl.BlockSpec(memory_space=pltpu.SMEM)
LITTLE = limit(24)
FAR_XY = [(i, i ^ 6) for i in range(8)]
CORE = [(i, i ^ 1) for i in range(8)]
ALONG_X = [(i, i ^ 2) for i in range(8)]
ALONG_Y = [(i, i ^ 4) for i in range(8)]
SPLIT_XY = [(i, i ^ (4 if i & 1 else 2)) for i in range(8)]
CROSS_XY = [(i, i ^ (3 if i & 1 else 5)) for i in range(8)]


def send(array, pairs):
    return lax.ppermute(array, "dp", pairs)


def shift(array, by, groups):
    return lax.ppermute(array, "tensor", [(i, (i + by) % groups) for i in range(groups)])


def scoped(name, step, *args):
    with jax.named_scope(name):
        return step(*args)


def tie(array, *others):
    return lax.optimization_barrier((array,) + others)[0]


def fetch_blocks(spots_ref, sources, stage_ref, sem):
    if len(sources) == 1:
        pltpu.make_async_copy(sources[0], stage_ref, sem).start()
        return
    planes = planes_in_order(spots_ref)
    for k, (ref, first) in enumerate(views(sources)):
        for i, plane in enumerate(planes[1:] + planes[:1]):
            pltpu.make_async_copy(ref.at[first + i], stage_ref.at[spots_ref[k] * len(planes) + plane], sem).start()


def order_rows(stage_ref, join_ref, biases_ref):
    blocks = stage_ref.shape[0]
    rows = join_ref.shape[1] // blocks
    total = 0.0
    for b in range(0, blocks, 2):
        pair = [stage_ref[b + i].astype(F32) for i in range(2)]
        for m in range(3):
            both = jnp.concatenate([block[m * rows : (m + 1) * rows] for block in pair], axis=0)
            join_ref[m, b * rows : (b + 2) * rows, :] = both.astype(BF)
        total = total + pair[0][3 * rows :] + pair[1][3 * rows :]
    biases_ref[...] = total


def fetch(spots_ref, sources, out_ref, sems, stacked=False):
    groups, dim = out_ref.shape[0], out_ref.shape[1]

    def copy(source, index, target):
        pltpu.make_async_copy(source, target, sems.at[index]).start()

    if len(sources) == 1:
        for m in range(groups):
            copy(sources[0].at[m], m, out_ref.at[m])
        return
    pieces, own = views(sources[:-1]), sources[-1]
    rows, width = sources[0].shape[1], dim // groups
    my_z = spots_ref[8]
    if stacked:
        for m in range(groups):
            copy(own.at[pl.ds(m * width, width)], m, out_ref.at[m, pl.ds(pl.multiple_of(my_z * width, width), width)])
    else:
        copy(own, my_z, out_ref.at[my_z])
    per = width // rows
    for i, plane in enumerate(planes_in_order(spots_ref)[1:]):
        for k, (ref, first) in enumerate(pieces):
            e = spots_ref[k]
            if stacked:
                at = pl.multiple_of(plane * width + lax.rem(e, per) * rows, rows)
                copy(ref.at[first + i], lax.div(e, per), out_ref.at[lax.div(e, per), pl.ds(at, rows)])
            else:
                copy(ref.at[first + i], plane, out_ref.at[plane, pl.ds(pl.multiple_of(e * rows, rows), rows)])


def views(sources):
    if len(sources) == 8:
        return [(source, 0) for source in sources]
    both, near, far, swapped, swapped_far = sources
    count = far.shape[0]
    return [(both, 0), (both, count), (near, 0), (near, count), (far, 0), (swapped, 0), (swapped, count), (swapped_far, 0)]


def merge_kernel(spots_ref, *refs, count):
    beside, across, beside2, across2, *own = refs[:count]
    outs = refs[count:]
    core = lax.rem(spots_ref[0], 2)
    rows = across.shape[0]
    blocks = 3 + len(own) // 2
    sides = [outs[0], outs[1]] if len(outs) == 2 else [outs[0].at[pl.ds(i * blocks, blocks)] for i in range(2)]
    parts = [pl.ds(pl.multiple_of(at * rows, rows), rows) for at in (core, 1 - core)]
    for side, at, last, mine in zip(sides, parts, (across, across2), own or (None, None)):
        side[core] = beside[at, :]
        side[1 - core] = beside2[at, :]
        side[2] = last[...]
        if mine is not None:
            side[3] = mine[...]


def merge(spots, arrays, split):
    rows, dim = arrays[1].shape
    blocks = 3 + (len(arrays) - 4) // 2
    outs = [blocks, blocks] if split else [2 * blocks]
    return pl.pallas_call(
        partial(merge_kernel, count=len(arrays)),
        out_shape=[jax.ShapeDtypeStruct((out, rows, dim), BF) for out in outs],
        in_specs=[SMEM] + [VMEM] * len(arrays),
        out_specs=[VMEM] * len(outs),
        compiler_params=limit(8),
    )(spots, *arrays)


def arrive(out_ref, sems, m):
    pltpu.make_async_copy(out_ref.at[m], out_ref.at[m], sems.at[m]).wait()


def planes_in_order(spots_ref, groups=4):
    return [lax.rem(spots_ref[8] + step, groups) for step in (0, 1, groups - 1, 2)]


def begin(pairs, sems):
    copies = [pltpu.make_async_copy(source, target, sems.at[i]) for i, (source, target) in enumerate(pairs)]
    for one in copies:
        one.start()
    return copies


WEIGHT_SEMS = pltpu.SemaphoreType.DMA((4,))
ANY = pl.BlockSpec(memory_space=pltpu.HBM)


class Gather:
    def __init__(self, dp_size, groups, my_d, my_z, seqs):
        self.dp_size, self.groups, self.my_d, self.my_z = dp_size, groups, my_d, my_z
        self.paired = dp_size == 8 and groups == 4 and seqs == 2
        core = lax.rem(my_d, 2)
        even = [0, 1, 2, 3, 7, 5, 4, 6]
        odd = [0, 1, 4, 5, 7, 3, 2, 6]
        flips = jnp.where(core == 0, jnp.array(even, jnp.int32), jnp.array(odd, jnp.int32))
        self.spots = jnp.concatenate([jnp.bitwise_xor(my_d, flips), my_z[None]]).astype(jnp.int32)

    def all_parts(self, part):
        whole = lax.all_gather(part, ("dp", "tensor"), axis=0)
        return whole.reshape((self.dp_size, self.groups) + part.shape).transpose(1, 0, 2, 3)

    def part_of(self, shard):
        rows = shard.shape[0] // self.dp_size
        return lax.dynamic_slice_in_dim(shard, self.my_d * rows, rows, 0)

    def all_rounds(self, parts, steps):
        count = len(parts)
        gathered, spread = [], []
        ahead, done = self.planes(parts[0], 0), [rows for part in parts[1:] for rows in part[:2]]
        for r in range(count + 2):
            with jax.named_scope("round%d" % r):
                ready = list(lax.optimization_barrier((*ahead, *done)))
                ahead = ready[: len(ahead)]
                if r >= 1:
                    at = len(ahead)
                    if r <= count:
                        last = spread[r - 1]
                        last[1] = ready[at : at + len(last[1])]
                        at += len(last[1])
                    if r >= 2:
                        spread[r - 2][2] = ready[at]
                done = []
                if 1 <= r <= count:
                    near_half = last[1][0] if len(last[1]) == 2 else last[1][0][: last[1][0].shape[0] // 2]
                    last.append(scoped("far", send, near_half, CROSS_XY))
                if r < count:
                    beside, across = ahead
                    others = [scoped("others", send, beside, CORE), scoped("others", send, across, CORE)]
                    both = merge(self.spots, [beside, across, *others, *parts[r][2:]], r == count - 1)
                    near = [scoped("near", send, side, SPLIT_XY) for side in both]
                    spread.append([both, near])
                    done += near
                    ahead = []
                    if r + 1 < count:
                        ahead = self.planes([tie(rows, both[0]) for rows in parts[r + 1]], r + 1)
                else:
                    ahead = []
                if 1 <= r <= count:
                    last.append([scoped("swap", send, array, CORE) for array in last[1]])
                    done += last[2:3] + last[3]
                if r >= 2:
                    whole = spread[r - 2]
                    gathered.append([*whole[0], *whole[1], whole[2], *whole[3], scoped("swapfar", send, whole[2], CORE)])
                done += steps[r](gathered)
        return gathered

    def planes(self, part, r):
        with jax.named_scope("planes%d" % r):
            groups = self.groups
            pairs = [
                (d * groups + z, d * groups + (z + (1 if d & 1 else groups - 1)) % groups)
                for d in range(self.dp_size)
                for z in range(groups)
            ]
            beside = scoped("beside", lax.ppermute, part[1], ("dp", "tensor"), pairs)
            return beside, scoped("across", shift, part[0], 2, groups)

    def half_of(self, quarter):
        rows = quarter.shape[0] // 2
        return jnp.where(lax.rem(self.my_d, 2) == 0, quarter[:rows], quarter[rows:])

    def quarter_of(self, shard):
        rows = 2 * shard.shape[0] // self.dp_size
        return lax.dynamic_slice_in_dim(shard, self.my_d // 2 * rows, rows, 0)

    def whole(self, part, stacked=False):
        whole = self.all_parts(part)
        dim = part.shape[1]
        if stacked:
            whole = whole.reshape(self.groups, 4, -1, dim).transpose(1, 0, 2, 3)
        return [whole.reshape(4, -1, dim)]


def reduce_grads(gather, grads, own_rows):
    groups, spots = gather.groups, gather.spots
    if not gather.paired:
        mats, bias = grads
        mats = lax.psum_scatter(mats, ("dp", "tensor"), scatter_dimension=1, tiled=True)
        return mats[0], mats[1], mats[2], lax.psum(bias, ("dp", "tensor"))
    keep, away = grads
    rows, dim = keep.shape[1:]
    low = jax.ShapeDtypeStruct((rows, dim), BF)
    come = scoped("cores", send, away, CORE)
    own, bias, to_x, to_y, to_far = pl.pallas_call(
        add_cores_kernel,
        out_shape=[jax.ShapeDtypeStruct((rows - 16, dim), F32), jax.ShapeDtypeStruct((8, dim), F32), low, low, low],
        in_specs=[SMEM, VMEM, VMEM],
        out_specs=[VMEM] * 5,
        compiler_params=LITTLE,
    )(spots, keep, come)
    from_far = scoped("far", send, to_far, FAR_XY)
    from_x = scoped("x", send, to_x, ALONG_X)
    from_y = scoped("y", send, to_y, ALONG_Y)
    block = jax.ShapeDtypeStruct((3 * own_rows + 24, dim), BF)
    mine, *goes = pl.pallas_call(
        add_plane_kernel,
        out_shape=[jax.ShapeDtypeStruct((3 * own_rows + 8, dim), F32)] + [block] * (groups - 1),
        in_specs=[SMEM] + [VMEM] * 5,
        out_specs=[VMEM] * groups,
        scratch_shapes=[pltpu.VMEM((rows - 16, dim), F32)],
        compiler_params=LITTLE,
    )(spots, own, bias, from_x, from_y, from_far)
    comes = [scoped("stack%d" % i, shift, go, i + 1, groups) for i, go in enumerate(goes)]
    part = jax.ShapeDtypeStruct((own_rows, dim), F32)
    return pl.pallas_call(
        add_stack_kernel,
        out_shape=[part, part, part, jax.ShapeDtypeStruct((8, dim), F32)],
        in_specs=[VMEM] * groups,
        out_specs=[VMEM] * 4,
        compiler_params=LITTLE,
    )(mine, *comes)


def cost(flops, moved, exps=0):
    return pl.CostEstimate(flops=int(flops), bytes_accessed=int(moved), transcendentals=int(exps))


def head_masks():
    lane = lax.broadcasted_iota(jnp.int32, (1, 128), 1)
    first = (lane < 64).astype(F32)
    return [first.astype(BF), (1.0 - first).astype(BF)], lane < 64


def attention_kernel(spots_ref, len_ref, x_ref, norms_ref, *refs):
    *sources, q_hbm, k_hbm, v_hbm, p_hbm, low_ref, xhat_hbm, rstd_ref, w_ref, ctx_ref, q_ref, k_ref, v_ref, p_ref, xhat_ref, sems, store_sems = refs
    fetch(spots_ref, sources, w_ref, sems, True)
    rows, dim = x_ref.shape
    for m in range(4):
        arrive(w_ref, sems, m)
    seq_len = p_ref.shape[1]
    x = x_ref[...]
    q_ref[...] = (mm_t(x, w_ref[0]).astype(BF).astype(F32) * (1.0 / math.sqrt(dim // HEADS))).astype(BF)
    k_ref[...] = mm_t(x, w_ref[1]).astype(BF)
    v_ref[...] = mm_t(x, w_ref[2]).astype(BF)
    masks, first = head_masks()
    key_at = lax.broadcasted_iota(jnp.int32, (seq_len, 1), 0)

    def one_seq(s, _):
        at = pl.ds(pl.multiple_of(s * seq_len, seq_len), seq_len)
        valid = key_at < len_ref[s]
        for j in range(HEADS // 2):
            cols = slice(128 * j, 128 * (j + 1))
            q, k, v = q_ref[at, cols], k_ref[at, cols], v_ref[at, cols]
            parts = []
            for h in range(2):
                scores = jnp.where(valid, mm_t(k, q * masks[h]), MASKED)
                exps = jnp.exp(scores - jnp.max(scores, axis=0, keepdims=True))
                probs = (exps * (1.0 / jnp.sum(exps, axis=0, keepdims=True))).astype(BF)
                p_ref[s * HEADS + 2 * j + h] = probs
                parts.append(t_mm(probs, v))
            ctx_ref[at, cols] = jnp.where(first, parts[0], parts[1]).astype(BF)
        return 0

    lax.fori_loop(0, rows // seq_len, one_seq, 0)
    stores = begin(((q_ref, q_hbm), (k_ref, k_hbm), (v_ref, v_hbm), (p_ref, p_hbm)), store_sems)
    xhat, rstd = norm_parts(x.astype(F32) + mm(ctx_ref[...], w_ref[3]))
    xhat_ref[...] = xhat
    stores += begin(((xhat_ref, xhat_hbm),), store_sems.at[pl.ds(4, 1)])
    rstd_ref[...] = rstd
    low_ref[...] = (xhat * norms_ref[0:1, :] + norms_ref[1:2, :]).astype(BF)
    for store in stores:
        store.wait()


def attention_forward(spots, lengths, x, sources, norms, seq_len):
    rows, dim = x.shape
    seqs = rows // seq_len
    low = jax.ShapeDtypeStruct((rows, dim), BF)
    return pl.pallas_call(
        attention_kernel,
        out_shape=[low, low, low,
                   jax.ShapeDtypeStruct((seqs * HEADS, seq_len, seq_len), BF), low,
                   jax.ShapeDtypeStruct((rows, dim), F32), jax.ShapeDtypeStruct((rows, 1), F32)],
        in_specs=[SMEM] * 2 + [VMEM] * 2 + [ANY] * len(sources),
        out_specs=[ANY] * 4 + [VMEM, ANY, VMEM],
        scratch_shapes=[pltpu.VMEM((4, dim, dim), BF)] + [pltpu.VMEM((rows, dim), BF)] * 4 + [
            pltpu.VMEM((seqs * HEADS, seq_len, seq_len), BF), pltpu.VMEM((rows, dim), F32),
            WEIGHT_SEMS, pltpu.SemaphoreType.DMA((5,)),
        ],
        compiler_params=limit(60),
        cost_estimate=cost(2 * rows * dim * (4 * dim + 2 * seq_len), 2 * (4 * dim * dim + 8 * rows * dim), rows * seq_len * HEADS),
    )(spots, lengths, x, norms, *sources)


def by_rows(rows, step, work, unroll=1):
    work(slice(0, rows))


def ffn_in_kernel(spots_ref, x_ref, bias_ref, *refs):
    *sources, act_hbm, slope_hbm, act_ref, slope_ref, w_ref, pre_ref, sems, store_sems = refs
    fetch(spots_ref, sources, w_ref, sems)
    units = pre_ref.shape[1]
    stores = []
    for i, p in enumerate(planes_in_order(spots_ref, w_ref.shape[0])):
        arrive(w_ref, sems, p)
        pre_ref[...] = mm(x_ref[...], w_ref[p])
        cols = pl.ds(pl.multiple_of(p * units, units), units)
        act, slope = gelu_parts(pre_ref[...] + bias_ref[p])
        act_ref[:, cols] = act.astype(BF)
        slope_ref[:, cols] = slope.astype(BF)
        pairs = [(act_ref, act_hbm), (slope_ref, slope_hbm)]
        stores += begin([(ref.at[:, cols], hbm.at[:, cols]) for ref, hbm in pairs], store_sems.at[pl.ds(2 * i, 2)])
    for store in stores:
        store.wait()


def ffn_forward(spots, x, sources, bias, units):
    rows, dim = x.shape
    planes = bias.shape[0] // units
    out = jax.ShapeDtypeStruct((rows, planes * units), BF)
    return pl.pallas_call(
        ffn_in_kernel,
        out_shape=[out, out],
        in_specs=[SMEM] + [VMEM] * 2 + [ANY] * len(sources),
        out_specs=[ANY] * 2,
        scratch_shapes=[
            pltpu.VMEM((rows, planes * units), BF), pltpu.VMEM((rows, planes * units), BF),
            pltpu.VMEM((planes, dim, units), BF), pltpu.VMEM((rows, units), F32), WEIGHT_SEMS, pltpu.SemaphoreType.DMA((8,)),
        ],
        compiler_params=limit(60),
        cost_estimate=cost(2 * rows * dim * units * planes, 2 * planes * units * (dim + 2 * rows), 2 * rows * units * planes),
    )(spots, x, bias.reshape(planes, 1, units), *sources)


def two_pass(values, table):
    high = values.astype(BF)
    return mm(high, table) + mm((values - high.astype(F32)).astype(BF), table)


def put_rows(ref, mats, bias):
    at = 0
    for mat in mats:
        ref[at : at + mat.shape[0], :] = mat.astype(BF)
        at += mat.shape[0]
    high = bias.astype(BF).astype(F32)
    ref[at : at + 16, :] = jnp.concatenate([high, bias - high], axis=0).astype(BF)


def sum_rows(arrays):
    total = arrays[0].astype(F32)
    for array in arrays[1:]:
        total = total + array.astype(F32)
    rows = total.shape[0] - 16
    return total[:rows], total[rows : rows + 8] + total[rows + 8 :]


def add_cores_kernel(spots_ref, keep_ref, come_ref, own_ref, bias_ref, x_ref, y_ref, far_ref):
    quarter = lax.div(spots_ref[0], 2)
    own_ref[...], bias_ref[...] = sum_rows([keep_ref[quarter], come_ref[quarter]])
    for flip, ref in ((1, x_ref), (2, y_ref), (3, far_ref)):
        q = jnp.bitwise_xor(quarter, flip)
        mats, bias = sum_rows([keep_ref[q], come_ref[q]])
        put_rows(ref, [mats], bias)


def add_plane_kernel(spots_ref, own_ref, bias_ref, x_ref, y_ref, far_ref, mine_ref, *refs):
    go_refs, total_ref = refs[:-1], refs[-1]
    mats, bias = sum_rows([x_ref[...], y_ref[...], far_ref[...]])
    total_ref[...] = own_ref[...] + mats
    bias = bias + bias_ref[...]
    groups = len(go_refs) + 1
    width = total_ref.shape[0] // 3
    rows = width // groups

    def block(plane):
        at = [pl.multiple_of(i * width + plane * rows, 8) for i in range(3)]
        return jnp.concatenate([total_ref[pl.ds(a, rows), :] for a in at], axis=0)

    my_z = spots_ref[8]
    mine_ref[...] = jnp.concatenate([block(my_z), bias], axis=0)
    high = bias.astype(BF).astype(F32)
    for i, ref in enumerate(go_refs):
        there = block(lax.rem(my_z + i + 1, groups))
        ref[...] = jnp.concatenate([there, high, bias - high, jnp.zeros_like(bias)], axis=0).astype(BF)


def add_stack_kernel(mine_ref, *refs):
    come_refs, (q_ref, k_ref, v_ref, bias_ref) = refs[:-4], refs[-4:]
    total = mine_ref[...]
    rows = q_ref.shape[0]
    for ref in come_refs:
        come = ref[...].astype(F32)
        bias = come[3 * rows : 3 * rows + 8] + come[3 * rows + 8 : 3 * rows + 16]
        total = total + jnp.concatenate([come[: 3 * rows], bias], axis=0)
    q_ref[...], k_ref[...], v_ref[...] = (total[i * rows : (i + 1) * rows] for i in range(3))
    bias_ref[...] = total[3 * rows :]


def joining_kernel(
    spots_ref, member_ref, member_t_ref, avail_ref, norms_ref, act_hbm, xhat1_hbm, cot_hbm, *refs, halves, count
):
    gain1, bias1, gain2, bias2 = (norms_ref[i : i + 1, :] for i in range(4))
    down_hbm, up_hbm, *refs = refs
    join_sources, sources, refs = refs[:count], refs[count:-43], refs[-43:]
    stage_ref, biases_ref, stage_sem, refs = refs[-3], refs[-2], refs[-1], refs[:-3]
    out_hbm, g2_hbm, g_ffn_ref, grad_hbm0, grad_hbm1 = refs[:5]
    act_ref, w_out_ref, down_ref, up_ref, join_ref, xhat1_ref, cot_ref, act_sems, out_sems, sems, store_sems = refs[5:16]
    ffn_ref, tmp_ref, u_ref, w_ref, big_u_ref, big_w_ref, p_wide_ref = refs[16:23]
    x_ref, act2_ref, slope_ref, q_ref, high_ref, low_ref, mixed_ref, t_ref = refs[23:31]
    sums_ref, bias_sums_ref, dot_ref, dot2_ref, out_ref, g2_ref, grad_ref0, grad_ref1, bias_ref = refs[31:40]
    rows, dim = out_ref.shape
    planes, units = w_out_ref.shape[:2]
    fetch(spots_ref, sources, w_out_ref, out_sems)
    act_loads = []
    for i, p in enumerate(planes_in_order(spots_ref, planes)):
        cols = pl.ds(pl.multiple_of(p * units, units), units)
        act_loads.append((p, cols, pltpu.make_async_copy(act_hbm.at[:, cols], act_ref.at[:, cols], act_sems.at[i])))
        act_loads[-1][2].start()
    fetch_blocks(spots_ref, join_sources, stage_ref, stage_sem)
    loads = begin(((down_hbm, down_ref), (up_hbm, up_ref), (xhat1_hbm, xhat1_ref), (cot_hbm, cot_ref)), sems)
    seqs = avail_ref.shape[0]
    fscale = 1.0 / math.sqrt(dim)
    member, member_t = member_ref[...], member_t_ref[...]
    for i, (p, cols, load) in enumerate(act_loads):
        load.wait()
        arrive(w_out_ref, out_sems, p)
        term = mm(act_ref[:, cols], w_out_ref[p])
        ffn_ref[...] = term if i == 0 else ffn_ref[...] + term

    def lower_ffn(at):
        x_ref[at, :] = ffn_ref[at, :].astype(BF)

    by_rows(rows, 64, lower_ffn)
    loads[0].wait()
    big_w_ref[...] = mm(x_ref[...], down_ref[...])

    def gelu(at):
        act, slope = gelu_parts(big_w_ref[at, :])
        act2_ref[at, :] = act.astype(BF)
        slope_ref[at, :] = slope.astype(BF)

    pltpu.make_async_copy(stage_ref, stage_ref, stage_sem).wait()
    order_rows(stage_ref, join_ref, biases_ref)
    qb, vb = biases_ref[0:1, :], biases_ref[1:2, :]
    tmp_ref[...] = mm(x_ref[...], join_ref[0])

    def lower_q(at):
        q_ref[at, :] = (tmp_ref[at, :] + qb).astype(BF)

    by_rows(rows, 64, lower_q)
    u_ref[...] = mm_t(q_ref[...], join_ref[1])

    def lower_u(at):
        u = u_ref[at, :]
        high_ref[at, :] = u.astype(BF)
        dot_ref[at, :] = jnp.sum(ffn_ref[at, :] * u, axis=-1, keepdims=True)

    by_rows(rows, 64, lower_u)
    loads[1].wait()
    big_u_ref[...] = mm_t(high_ref[...], up_ref[...])
    by_rows(rows, 32, gelu)

    def product(source_ref):
        def work(at):
            both = act2_ref[at, :].astype(F32) * source_ref[at, :]
            high = both.astype(BF)
            high_ref[at, :] = high
            low_ref[at, :] = (both - high.astype(F32)).astype(BF)

        by_rows(rows, 64, work)
        return mm(high_ref[...], member) + mm(low_ref[...], member)

    avail = jnp.concatenate([jnp.broadcast_to(avail_ref[i], (rows // seqs, 128)) for i in range(seqs)], axis=0)
    fscores = (product(big_u_ref) + dot_ref[...]) * fscale
    fscores = jnp.where(avail > 0, fscores, MASKED)
    fexp = jnp.exp(fscores - jnp.max(fscores, axis=-1, keepdims=True))
    fprobs = fexp / jnp.sum(fexp, axis=-1, keepdims=True)
    p_wide_ref[...] = two_pass(fprobs, member_t)

    def weigh_p(at):
        high_ref[at, :] = (p_wide_ref[at, :] * act2_ref[at, :].astype(F32)).astype(BF)

    by_rows(rows, 64, weigh_p)
    tmp_ref[...] = mm(high_ref[...], up_ref[...])

    def mix(at):
        mixed_ref[at, :] = (ffn_ref[at, :] + tmp_ref[at, :]).astype(BF)

    by_rows(rows, 64, mix)
    tmp_ref[...] = mm(mixed_ref[...], join_ref[2])
    bias_sums_ref[...] = jnp.zeros_like(bias_sums_ref)
    loads[2].wait()
    loads[3].wait()

    def norm(at):
        normed1 = xhat1_ref[at, :] * gain1 + bias1
        xhat2, rstd2 = norm_parts(normed1 + tmp_ref[at, :] + vb)
        out_ref[at, :] = (xhat2 * gain2 + bias2).astype(BF)
        g2 = norm_back(cot_ref[at, :].astype(F32), gain2, xhat2, rstd2)
        g2_ref[at, :] = g2
        low_ref[at, :] = g2.astype(BF)
        dot2_ref[at, :] = jnp.sum(g2 * vb, axis=-1, keepdims=True)
        bias_sums_ref[1] += jnp.sum(g2.reshape(-1, 8, dim), axis=0)

    by_rows(rows, 32, norm)
    stores = begin(((out_ref, out_hbm), (g2_ref, g2_hbm)), store_sems)
    sums_ref[2] = t_mm(mixed_ref[...], low_ref[...])
    w_ref[...] = mm_t(low_ref[...], join_ref[2])

    def lower_w(at):
        w = w_ref[at, :]
        high_ref[at, :] = w.astype(BF)
        dot2_ref[at, :] += jnp.sum(ffn_ref[at, :] * w, axis=-1, keepdims=True)

    by_rows(rows, 64, lower_w)
    big_w_ref[...] = mm_t(high_ref[...], up_ref[...])
    gvals = product(big_w_ref) + dot2_ref[...]
    gs = fprobs * (gvals - jnp.sum(gvals * fprobs, axis=-1, keepdims=True)) * fscale
    dot_ref[...] = jnp.sum(gs, axis=-1, keepdims=True)
    tmp_ref[...] = two_pass(gs, member_t)

    def weigh_gs(at):
        wide = tmp_ref[at, :]
        high_ref[at, :] = (wide * act2_ref[at, :].astype(F32)).astype(BF)
        grad = wide * big_u_ref[at, :] + p_wide_ref[at, :] * big_w_ref[at, :]
        slope_ref[at, :] = (grad * slope_ref[at, :].astype(F32)).astype(BF)

    by_rows(rows, 64, weigh_gs)
    tmp_ref[...] = mm(high_ref[...], up_ref[...])

    def lower_t(at):
        t_ref[at, :] = (tmp_ref[at, :] + dot_ref[at, :] * ffn_ref[at, :]).astype(BF)

    by_rows(rows, 64, lower_t)
    tmp_ref[...] = mm(t_ref[...], join_ref[1])

    def lower_gq(at):
        gq = tmp_ref[at, :].astype(BF)
        high_ref[at, :] = gq
        bias_sums_ref[0] += jnp.sum(gq.astype(F32).reshape(-1, 8, dim), axis=0)

    by_rows(rows, 64, lower_gq)
    sums_ref[0] = t_mm(x_ref[...], high_ref[...])
    sums_ref[1] = t_mm(t_ref[...], q_ref[...])
    row = lax.broadcasted_iota(jnp.int32, (8, 1), 0)
    d_bias = [jnp.sum(bias_sums_ref[i], axis=0, keepdims=True) for i in range(2)]
    bias_ref[...] = jnp.where(row == 0, d_bias[0], jnp.where(row == 1, d_bias[1], 0.0))
    if halves:
        core = lax.rem(spots_ref[0], 2)
        part = dim // 8
        for i, (ref, side) in enumerate(((grad_ref1, 1 - core), (grad_ref0, core))):
            for q in range(4):
                at = pl.ds(pl.multiple_of((2 * q + side) * part, part), part)
                put_rows(ref.at[q], [sums_ref[i, at, :] for i in range(3)], bias_ref[...])
            hbm = grad_hbm0 if i else grad_hbm1
            stores += begin(((ref, hbm),), store_sems.at[pl.ds(2 + i, 1)])
    else:
        stores += begin(((sums_ref, grad_hbm0), (bias_ref, grad_hbm1)), store_sems.at[pl.ds(2, 2)])
    tmp_ref[...] = mm_t(slope_ref[...], down_ref[...]) + mm_t(high_ref[...], join_ref[0])

    def add_ffn(at):
        g_ffn_ref[at, :] = (dot_ref[at, :] * u_ref[at, :] + w_ref[at, :] + tmp_ref[at, :]).astype(BF)

    by_rows(rows, 64, add_ffn)
    for store in stores:
        store.wait()


def joining(spots, halves, act, sources, adapt_down, up, join_sources, member, member_t, avail, xhat1, norms, cot):
    rows, dim = xhat1.shape
    if halves:
        grads = [jax.ShapeDtypeStruct((4, 3 * dim // 8 + 16, dim), BF)] * 2
    else:
        grads = [jax.ShapeDtypeStruct((3, dim, dim), F32), jax.ShapeDtypeStruct((8, dim), F32)]
    wide, low = pltpu.VMEM((rows, dim), F32), pltpu.VMEM((rows, dim), BF)
    height, blocks = join_sources[-1].shape[-2:][0], 32
    stage_shape = join_sources[0].shape if len(join_sources) == 1 else (blocks, height, dim)
    return pl.pallas_call(
        partial(joining_kernel, halves=halves, count=len(join_sources)),
        out_shape=[
            jax.ShapeDtypeStruct((rows, dim), BF),
            jax.ShapeDtypeStruct((rows, dim), F32),
            jax.ShapeDtypeStruct((rows, dim), BF),
        ] + grads,
        in_specs=[SMEM] + [VMEM] * 4 + [ANY] * (len(sources) + len(join_sources) + 5),
        out_specs=[ANY, ANY, VMEM, ANY, ANY],
        scratch_shapes=[
            pltpu.VMEM(act.shape, BF),
            pltpu.VMEM((4, act.shape[1] // 4, dim), BF),
            pltpu.VMEM(adapt_down.shape, BF),
            pltpu.VMEM(up.shape, BF),
            pltpu.VMEM((3, dim, dim), BF),
            wide,
            low,
            WEIGHT_SEMS,
            WEIGHT_SEMS,
            pltpu.SemaphoreType.DMA((4,)),
            pltpu.SemaphoreType.DMA((4,)),
        ] + [wide] * 7 + [low] * 8 + [
            pltpu.VMEM((3, dim, dim), F32),
            pltpu.VMEM((2, 8, dim), F32),
            pltpu.VMEM((rows, 1), F32),
            pltpu.VMEM((rows, 1), F32),
            low,
            wide,
            pltpu.VMEM(grads[0].shape if halves else (8, 128), BF),
            pltpu.VMEM(grads[1].shape if halves else (8, 128), BF),
            pltpu.VMEM((8, dim), F32),
            pltpu.VMEM(stage_shape, BF),
            pltpu.VMEM((8, dim), F32),
            pltpu.SemaphoreType.DMA,
        ],
        compiler_params=limit(60),
        cost_estimate=cost(2 * rows * dim * (15 * dim + act.shape[1]), 2 * dim * (8 * dim + 10 * rows), 2 * rows * dim),
    )(spots, member, member_t, avail, norms, act, xhat1, cot, adapt_down, up, *join_sources, *sources)


def ffn_back_kernel(spots_ref, g_ref, rstd_ref, norms_ref, slope_hbm, g2_hbm, xhat_hbm, *refs, count):
    refs, (out_sources, in_sources) = refs[sum(count) :], (refs[: count[0]], refs[count[0] : sum(count)])
    g1_ref, slope_ref, g2_ref, xhat_ref, w_out_ref, w_in_ref, pre_ref, out_sems, in_sems, slope_sems, sems = refs
    planes, units = w_out_ref.shape[:2]
    fetch(spots_ref, out_sources, w_out_ref, out_sems)
    slopes = []
    for i, p in enumerate(planes_in_order(spots_ref, planes)):
        cols = pl.ds(pl.multiple_of(p * units, units), units)
        slopes.append((p, cols, pltpu.make_async_copy(slope_hbm.at[:, cols], slope_ref.at[:, cols], slope_sems.at[i])))
        slopes[-1][2].start()
    fetch(spots_ref, in_sources, w_in_ref, in_sems)
    loads = begin(((g2_hbm, g2_ref), (xhat_hbm, xhat_ref)), sems)
    for p, cols, load in slopes:
        arrive(w_out_ref, out_sems, p)
        load.wait()
        pre_ref[p] = (mm_t(g_ref[...], w_out_ref[p]) * slope_ref[:, cols].astype(F32)).astype(BF)
    total = None
    for p, _, _ in slopes:
        arrive(w_in_ref, in_sems, p)
        term = mm_t(pre_ref[p], w_in_ref[p])
        total = term if total is None else total + term
    for load in loads:
        load.wait()
    g1_ref[...] = norm_back(total + g2_ref[...], norms_ref[0:1, :], xhat_ref[...], rstd_ref[...])


def ffn_backward(spots, g_ffn, slope, out_sources, in_sources, g2, xhat, rstd, norms):
    rows, dim = xhat.shape
    planes = 4
    units = slope.shape[1] // planes
    return pl.pallas_call(
        partial(ffn_back_kernel, count=(len(out_sources), len(in_sources))),
        out_shape=jax.ShapeDtypeStruct((rows, dim), F32),
        in_specs=[SMEM] + [VMEM] * 3 + [ANY] * (len(out_sources) + len(in_sources) + 3),
        out_specs=VMEM,
        scratch_shapes=[
            pltpu.VMEM(slope.shape, BF), pltpu.VMEM((rows, dim), F32), pltpu.VMEM((rows, dim), F32),
            pltpu.VMEM((planes, units, dim), BF), pltpu.VMEM((planes, dim, units), BF), pltpu.VMEM((planes, rows, units), BF),
            WEIGHT_SEMS, WEIGHT_SEMS, WEIGHT_SEMS, pltpu.SemaphoreType.DMA((2,)),
        ],
        compiler_params=limit(60),
        cost_estimate=cost(4 * rows * dim * units * planes, 2 * planes * units * (2 * dim + rows)),
    )(spots, g_ffn, rstd, norms, slope, g2, xhat, *out_sources, *in_sources)


def attention_back_kernel(spots_ref, g1_ref, *refs):
    *refs, out_ref, w_ref, q_ref, k_ref, v_ref, p_ref, ctx_ref, dq_ref, dk_ref, dv_ref, w_sems, sems = refs
    *sources, q_hbm, k_hbm, v_hbm, p_hbm = refs
    rows, dim = g1_ref.shape
    seq_len = p_ref.shape[1]
    scale = 1.0 / math.sqrt(dim // HEADS)
    fetch(spots_ref, sources, w_ref, w_sems, True)
    half = p_ref.shape[0] // 2
    halves = [(p_hbm.at[pl.ds(i * half, half)], p_ref.at[pl.ds(i * half, half)]) for i in range(2)]
    loads = begin(((v_hbm, v_ref), (q_hbm, q_ref), (k_hbm, k_ref), *halves), sems)
    arrive(w_ref, w_sems, 3)
    ctx_ref[...] = mm_t(g1_ref[...].astype(BF), w_ref[3]).astype(BF)
    for load in loads:
        load.wait()
    masks, first = head_masks()

    def one_seq(s, _):
        at = pl.ds(pl.multiple_of(s * seq_len, seq_len), seq_len)
        for j in range(HEADS // 2):
            cols = slice(128 * j, 128 * (j + 1))
            q, k, v, g = q_ref[at, cols], k_ref[at, cols], v_ref[at, cols], ctx_ref[at, cols]
            dq, dk, dv = [], [], []
            for h in range(2):
                probs_low = p_ref[s * HEADS + 2 * j + h]
                probs = probs_low.astype(F32)
                g_probs = mm_t(v, g * masks[h])
                g_scores = (probs * (g_probs - jnp.sum(g_probs * probs, axis=0, keepdims=True))).astype(BF)
                dv.append(mm(probs_low, g))
                dk.append(mm(g_scores, q))
                dq.append(t_mm(g_scores, k))
            dq_ref[at, cols] = (jnp.where(first, dq[0], dq[1]) * scale).astype(BF)
            dk_ref[at, cols] = jnp.where(first, dk[0], dk[1]).astype(BF)
            dv_ref[at, cols] = jnp.where(first, dv[0], dv[1]).astype(BF)
        return 0

    lax.fori_loop(0, rows // seq_len, one_seq, 0)
    for m in range(3):
        arrive(w_ref, w_sems, m)
    total = g1_ref[...] + mm(dq_ref[...], w_ref[0])
    total = total + mm(dk_ref[...], w_ref[1])
    out_ref[...] = (total + mm(dv_ref[...], w_ref[2])).astype(BF)


def attention_backward(spots, g1, sources, q, k, v, probs):
    rows, dim = g1.shape
    seq_len = probs.shape[1]
    low = pltpu.VMEM((rows, dim), BF)
    return pl.pallas_call(
        attention_back_kernel,
        out_shape=jax.ShapeDtypeStruct((rows, dim), BF),
        in_specs=[SMEM, VMEM] + [ANY] * (len(sources) + 4),
        out_specs=VMEM,
        scratch_shapes=[pltpu.VMEM((4, dim, dim), BF), low, low, low, pltpu.VMEM(probs.shape, BF), low, low, low, low,
                        WEIGHT_SEMS, pltpu.SemaphoreType.DMA((5,))],
        compiler_params=limit(60),
        cost_estimate=cost(2 * rows * dim * (4 * dim + 4 * seq_len), 2 * (4 * dim * dim + 8 * rows * dim)),
    )(spots, g1, *sources, q, k, v, probs)


def shards(
    tokens, lengths, adapter_mask, cotangent, att_query, att_key, att_value, att_out,
    norm1_gain, norm1_bias, ffn_in, ffn_bias, ffn_out, adapt_down, adapt_up, norm2_gain,
    norm2_bias, joining_query, joining_key, joining_value, joining_qbias, joining_vbias,
):
    groups = lax.axis_size("tensor")
    dp_size = lax.axis_size("dp")
    my_z = lax.axis_index("tensor")
    my_d = lax.axis_index("dp")
    seq_local, seq_len, dim = tokens.shape
    mine = seq_local // groups
    rows = mine * seq_len
    adapters, neck = adapt_up.shape[0], adapt_up.shape[1]
    own_rows = joining_query.shape[0]

    gather = Gather(dp_size, groups, my_d, my_z, mine)
    spots = gather.spots
    biases = lax.dynamic_update_slice(
        jnp.zeros((8, dim), BF), jnp.stack([joining_qbias, joining_vbias]), (0, (my_d * groups + my_z) * own_rows)
    )
    att_mats = [att_query.T, att_key.T, att_value.T, att_out]
    att_pack = jnp.concatenate(att_mats, axis=0)
    join_part = jnp.concatenate([joining_query, joining_key, joining_value, biases], axis=0)
    parts = [gather.part_of(att_pack), gather.part_of(ffn_in), join_part, gather.part_of(ffn_out)]

    def my_slice(array):
        return lax.dynamic_slice_in_dim(array, my_z * mine, mine, 0)

    x = my_slice(tokens).reshape(rows, dim)
    shifts = jnp.arange(128, dtype=jnp.int32)
    bits = jnp.right_shift(my_slice(adapter_mask)[:, None], jnp.minimum(shifts, adapters)[None, :]) % 2
    avail = jnp.where(shifts[None, :] < adapters, bits, 0)[:, None, :]
    norms = jnp.stack([norm1_gain, norm1_bias, norm2_gain, norm2_bias])
    lens = my_slice(lengths)
    owner = jnp.arange(adapters * neck, dtype=jnp.int32) // neck
    member = (owner[:, None] == shifts[None, :]).astype(BF)
    member_t = (shifts[:, None] == owner[None, :]).astype(BF)
    kept = {}

    def attend(sources):
        kept["att"] = attention_forward(spots, lens, x, sources, norms, seq_len)
        return [kept["att"][4]]

    def feed(sources):
        kept["ffn"] = ffn_forward(spots, kept["att"][4], sources, ffn_bias, ffn_in.shape[1])
        return [kept["ffn"][0]]

    if gather.paired:
        own = [att_pack, ffn_in, None, ffn_out]
        steps = [
            lambda got: [x, norms, lens, avail, member, member_t, spots],
            lambda got: [],
            lambda got: attend(got[0] + own[:1]),
            lambda got: feed(got[1] + own[1:2]),
            lambda got: [],
            lambda got: [],
        ]
        quarter = att_mats[3]
        for i in range(3):
            quarter = jnp.where(my_d // 2 == i, att_mats[i], quarter)
        rounds = [(gather.half_of(quarter), quarter)]
        for shard in (ffn_in, ffn_out):
            shard = tie(shard, *rounds[0])
            rounds.append((gather.part_of(shard), gather.quarter_of(shard)))
        join_part = tie(join_part, *rounds[0])
        theirs = send(join_part, CORE)
        even = lax.rem(my_d, 2) == 0
        pair = jnp.concatenate([jnp.where(even, join_part, theirs), jnp.where(even, theirs, join_part)], axis=0)
        rounds.insert(2, (join_part, pair, join_part, theirs))
        got = gather.all_rounds(rounds, steps)
        att_sources, in_sources, out_sources = (got[i] + [own[i]] for i in (0, 1, 3))
        join_sources = got[2]
    else:
        att_sources, in_sources, out_sources = (gather.whole(parts[i], i == 0) for i in (0, 1, 3))
        join_sources = [lax.all_gather(parts[2], ("dp", "tensor"), axis=0)]
    up = adapt_up.reshape(adapters * neck, dim)
    cot = cotangent.reshape(rows, dim)

    def rest(att, ffn, avail, cot):
        q, k, v, probs, low1, xhat1, rstd1 = att
        act, slope = ffn
        layer_out, g2, g_ffn, *grads = joining(
            spots, gather.paired, act, out_sources, adapt_down, up, join_sources, member, member_t, avail, xhat1, norms, cot
        )
        g1 = ffn_backward(spots, g_ffn, slope, out_sources, in_sources, g2, xhat1, rstd1, norms)
        return layer_out, attention_backward(spots, g1, att_sources, q, k, v, probs), grads

    if gather.paired:
        layer_out, input_grad, grads = rest(kept["att"], kept["ffn"], avail, cot)
    else:
        step = 2 - mine % 2
        outs = []
        for first in range(0, mine, step):
            at = slice(first * seq_len, (first + step) * seq_len)
            att = attention_forward(spots, lens[first : first + step], x[at], att_sources, norms, seq_len)
            ffn = ffn_forward(spots, att[4], in_sources, ffn_bias, ffn_in.shape[1])
            outs.append(rest(att, ffn, avail[first : first + step], cot[at]))
        layer_out, input_grad = (jnp.concatenate([out[i] for out in outs]) for i in range(2))
        grads = [sum(out[2][i] for out in outs) for i in range(2)]
    d_q, d_k, d_v, d_bias = reduce_grads(gather, grads, own_rows)
    d_bias = lax.dynamic_slice_in_dim(d_bias[:2], (my_d * groups + my_z) * own_rows, own_rows, 1)
    return (
        layer_out.reshape(mine, seq_len, dim),
        input_grad.reshape(mine, seq_len, dim),
        d_q, d_k, d_v, d_bias[0], d_bias[1],
    )


def solution(mesh):
    both = P(ALL, None)
    return jax.shard_map(
        shards,
        mesh=mesh,
        in_specs=(
            P("dp", None, None), P("dp"), P("dp"), P(ALL, None, None),
            P(None, "tensor"), P(None, "tensor"), P(None, "tensor"), P("tensor", None),
            P(), P(), P(None, "tensor"), P(), P("tensor", None), P(), P(), P(), P(),
            both, both, both, P(ALL), P(ALL),
        ),
        out_specs=(P(ALL, None, None), P(ALL, None, None), both, both, both, P(ALL), P(ALL)),
        check_vma=False,
    )
```

```python
from functools import partial
import math

import jax
import jax.numpy as jnp
from jax import lax
from jax.experimental import pallas as pl
from jax.experimental.pallas import tpu as pltpu
from jax.sharding import PartitionSpec as P

HEADS = 12
EPS = 1e-05
MASKED = -1e30
ALL = ("dp", "tensor")
BF = jnp.bfloat16
F32 = jnp.float32


def mm(left, right):
    return jnp.dot(left, right, preferred_element_type=F32)


def mm_t(left, right):
    return lax.dot_general(left, right, (((1,), (1,)), ((), ())), preferred_element_type=F32)


def t_mm(left, right):
    return lax.dot_general(left, right, (((0,), (0,)), ((), ())), preferred_element_type=F32)


def norm_parts(values):
    average = jnp.mean(values, axis=-1, keepdims=True)
    centered = values - average
    variance = jnp.mean(centered * centered, axis=-1, keepdims=True)
    rstd = lax.rsqrt(variance + EPS)
    return centered * rstd, rstd


def norm_back(grad, gain, xhat, rstd):
    scaled = grad * gain
    return rstd * (
        scaled
        - jnp.mean(scaled, axis=-1, keepdims=True)
        - xhat * jnp.mean(scaled * xhat, axis=-1, keepdims=True)
    )


def gelu_parts(pre):
    cdf = 0.5 * (1.0 + lax.erf(pre * (1.0 / math.sqrt(2.0))))
    pdf = jnp.exp(-0.5 * pre * pre) * (1.0 / math.sqrt(2.0 * math.pi))
    return pre * cdf, cdf + pre * pdf


def limit(mebibytes):
    return pltpu.CompilerParams(vmem_limit_bytes=mebibytes * 2**20)


VMEM = pl.BlockSpec(memory_space=pltpu.VMEM)
SMEM = pl.BlockSpec(memory_space=pltpu.SMEM)
LITTLE = limit(24)
FAR_XY = [(i, i ^ 6) for i in range(8)]
CORE = [(i, i ^ 1) for i in range(8)]
ALONG_X = [(i, i ^ 2) for i in range(8)]
ALONG_Y = [(i, i ^ 4) for i in range(8)]
SPLIT_XY = [(i, i ^ (4 if i & 1 else 2)) for i in range(8)]
CROSS_XY = [(i, i ^ (3 if i & 1 else 5)) for i in range(8)]


def send(array, pairs):
    return lax.ppermute(array, "dp", pairs)


def shift(array, by, groups):
    return lax.ppermute(array, "tensor", [(i, (i + by) % groups) for i in range(groups)])


def scoped(name, step, *args):
    with jax.named_scope(name):
        return step(*args)


def tie(array, *others):
    return lax.optimization_barrier((array,) + others)[0]


def fetch_blocks(spots_ref, sources, stage_ref, sem):
    if len(sources) == 1:
        pltpu.make_async_copy(sources[0], stage_ref, sem).start()
        return
    planes = planes_in_order(spots_ref)
    for k, (ref, first) in enumerate(views(sources)):
        for i, plane in enumerate(planes[1:] + planes[:1]):
            pltpu.make_async_copy(ref.at[first + i], stage_ref.at[spots_ref[k] * len(planes) + plane], sem).start()


def order_rows(stage_ref, join_ref, biases_ref):
    blocks = stage_ref.shape[0]
    rows = join_ref.shape[1] // blocks
    total = 0.0
    for b in range(0, blocks, 2):
        pair = [stage_ref[b + i].astype(F32) for i in range(2)]
        for m in range(3):
            both = jnp.concatenate([block[m * rows : (m + 1) * rows] for block in pair], axis=0)
            join_ref[m, b * rows : (b + 2) * rows, :] = both.astype(BF)
        total = total + pair[0][3 * rows :] + pair[1][3 * rows :]
    biases_ref[...] = total


def fetch(spots_ref, sources, out_ref, sems, which, side_by_side=False):
    planes = planes_in_order(spots_ref)
    dim = sources[-1].shape[-1]
    rows = sources[-1].shape[-2]

    def copy(source, r, at):
        if side_by_side:
            target = out_ref.at[at, pl.ds(r * dim, dim)]
        else:
            target = out_ref.at[pl.ds(r * rows + at.start, at.size)]
        pltpu.make_async_copy(source, target, sems.at[r]).start()

    for r in which:
        if len(sources) == 1:
            copy(sources[0].at[planes[r]], r, pl.ds(0, rows))
        elif r == 0:
            copy(sources[-1], r, pl.ds(0, rows))
        else:
            for k, (ref, first) in enumerate(views(sources[:-1])):
                part = ref.shape[1]
                copy(ref.at[first + r - 1], r, pl.ds(pl.multiple_of(spots_ref[k] * part, part), part))


def arrive(out_ref, sems, r, side_by_side=False):
    dim = out_ref.shape[0] if side_by_side else out_ref.shape[1]
    block = out_ref.at[:, pl.ds(r * dim, dim)] if side_by_side else out_ref.at[pl.ds(r * out_ref.shape[0] // 4, out_ref.shape[0] // 4)]
    pltpu.make_async_copy(block, block, sems.at[r]).wait()


def fetch_stacked(spots_ref, sources, out_ref, sems, last):
    groups, dim = out_ref.shape[0], out_ref.shape[1]
    chosen = range(groups - 1, groups) if last else range(groups - 1)
    if len(sources) == 1:
        for m in chosen:
            pltpu.make_async_copy(sources[0].at[m], out_ref.at[m], sems.at[m]).start()
        return
    own = sources[-groups:]
    pieces = views(sources[:-groups])
    width, rows = dim // groups, pieces[0][0].shape[1]
    per = width // rows
    my_z = spots_ref[8]
    for m in chosen:
        at = pl.ds(pl.multiple_of(my_z * width, width), width)
        pltpu.make_async_copy(own[m], out_ref.at[m, at], sems.at[m]).start()
    for k, (ref, first) in enumerate(pieces):
        e = spots_ref[k]
        m = lax.div(e, per)

        @pl.when((m == groups - 1) == last)
        def _():
            for i, plane in enumerate(planes_in_order(spots_ref)[1:]):
                at = pl.ds(pl.multiple_of(plane * width + lax.rem(e, per) * rows, rows), rows)
                pltpu.make_async_copy(ref.at[first + i], out_ref.at[m, at], sems.at[m]).start()


def arrive_stacked(out_ref, sems, m):
    pltpu.make_async_copy(out_ref.at[m], out_ref.at[m], sems.at[m]).wait()


def views(sources):
    if len(sources) == 8:
        return [(source, 0) for source in sources]
    both, near, far, swapped, swapped_far = sources
    count = far.shape[0]
    return [(both, 0), (both, count), (near, 0), (near, count), (far, 0), (swapped, 0), (swapped, count), (swapped_far, 0)]


def cut_kernel(spots_ref, *refs):
    count = (len(refs) - 1) // 3
    shards, outs, sems = refs[:count], refs[count:-1], refs[-1]
    pairs = []
    for i, shard in enumerate(shards):
        rows = outs[2 * i].shape[0]
        at = pl.ds(pl.multiple_of(lax.div(spots_ref[0], 2) * rows, rows), rows)
        pairs.append((shard.at[at], outs[2 * i]))
        at = pl.ds(pl.multiple_of(spots_ref[0] * (rows // 2), rows // 2), rows // 2)
        pairs.append((shard.at[at], outs[2 * i + 1]))
    for copy in begin(pairs, sems):
        copy.wait()


def cut(spots, shards):
    outs = []
    for shard in shards:
        rows, dim = shard.shape
        outs += [jax.ShapeDtypeStruct((rows // 4, dim), BF), jax.ShapeDtypeStruct((rows // 8, dim), BF)]
    return pl.pallas_call(
        cut_kernel,
        out_shape=outs,
        in_specs=[SMEM] + [ANY] * len(shards),
        out_specs=[VMEM] * len(outs),
        scratch_shapes=[pltpu.SemaphoreType.DMA((len(outs),))],
        compiler_params=limit(60),
    )(spots, *shards)


def merge_kernel(spots_ref, *refs, count):
    beside, across, beside2, across2, *own = refs[:count]
    outs = refs[count:]
    core = lax.rem(spots_ref[0], 2)
    rows = across.shape[0]
    blocks = 3 + len(own) // 2
    sides = [outs[0], outs[1]] if len(outs) == 2 else [outs[0].at[pl.ds(i * blocks, blocks)] for i in range(2)]
    parts = [pl.ds(pl.multiple_of(at * rows, rows), rows) for at in (core, 1 - core)]
    for side, at, last, mine in zip(sides, parts, (across, across2), own or (None, None)):
        side[core] = beside[at, :]
        side[1 - core] = beside2[at, :]
        side[2] = last[...]
        if mine is not None:
            side[3] = mine[...]


def merge(spots, arrays, split):
    rows, dim = arrays[1].shape
    blocks = 3 + (len(arrays) - 4) // 2
    outs = [blocks, blocks] if split else [2 * blocks]
    return pl.pallas_call(
        partial(merge_kernel, count=len(arrays)),
        out_shape=[jax.ShapeDtypeStruct((out, rows, dim), BF) for out in outs],
        in_specs=[SMEM] + [VMEM] * len(arrays),
        out_specs=[VMEM] * len(outs),
        compiler_params=limit(8),
    )(spots, *arrays)


def planes_in_order(spots_ref, groups=4):
    return [lax.rem(spots_ref[8] + step, groups) for step in (0, 1, groups - 1, 2)]


def begin(pairs, sems):
    copies = [pltpu.make_async_copy(source, target, sems.at[i]) for i, (source, target) in enumerate(pairs)]
    for one in copies:
        one.start()
    return copies


WEIGHT_SEMS = pltpu.SemaphoreType.DMA((4,))
ANY = pl.BlockSpec(memory_space=pltpu.HBM)


class Gather:
    def __init__(self, dp_size, groups, my_d, my_z, seqs):
        self.dp_size, self.groups, self.my_d, self.my_z = dp_size, groups, my_d, my_z
        self.paired = dp_size == 8 and groups == 4 and seqs == 2
        core = lax.rem(my_d, 2)
        even = [0, 1, 2, 3, 7, 5, 4, 6]
        odd = [0, 1, 4, 5, 7, 3, 2, 6]
        flips = jnp.where(core == 0, jnp.array(even, jnp.int32), jnp.array(odd, jnp.int32))
        self.spots = jnp.concatenate([jnp.bitwise_xor(my_d, flips), my_z[None]]).astype(jnp.int32)

    def all_parts(self, part):
        whole = lax.all_gather(part, ("dp", "tensor"), axis=0)
        return whole.reshape((self.dp_size, self.groups) + part.shape).transpose(1, 0, 2, 3)

    def part_of(self, shard):
        rows = shard.shape[0] // self.dp_size
        return lax.dynamic_slice_in_dim(shard, self.my_d * rows, rows, 0)

    def all_rounds(self, parts, early, steps):
        count = len(parts)
        gathered, spread = [], []
        ahead, done = self.planes(parts[0], 0), [rows for part in parts[1:] for rows in part[:2]] + early
        for r in range(count + 2):
            with jax.named_scope("round%d" % r):
                ready = list(lax.optimization_barrier((*ahead, *done)))
                ahead = ready[: len(ahead)]
                if r >= 1:
                    at = len(ahead)
                    if r <= count:
                        last = spread[r - 1]
                        last[1] = ready[at : at + len(last[1])]
                        at += len(last[1])
                    if 2 <= r <= count:
                        spread[r - 2][2] = ready[at]
                done = []
                if 1 <= r < count:
                    near_half = last[1][0] if len(last[1]) == 2 else last[1][0][: last[1][0].shape[0] // 2]
                    last.append(scoped("far", send, near_half, CROSS_XY))
                if r < count:
                    beside, across = ahead
                    ahead = []
                    if r + 1 < count:
                        ahead = self.planes([tie(rows, beside) for rows in parts[r + 1]], r + 1)
                    others = [scoped("others", send, beside, CORE), scoped("others", send, across, CORE)]
                    both = merge(self.spots, [beside, across, *others, *parts[r][2:]], r == count - 1)
                    near = [scoped("near", send, side, SPLIT_XY) for side in both]
                    spread.append([both, near])
                    done += near
                else:
                    ahead = []
                if 1 <= r <= count:
                    late = last[2:] if r == count else []
                    last.append([scoped("swap", send, array, CORE) for array in last[1][:-1]])
                    last[3].append(scoped("swap", send, tie(last[1][-1], *late), CORE))
                    done += (last[2:3] if r < count else []) + last[3]
                if r >= 2:
                    whole = spread[r - 2]
                    gathered.append([*whole[0], *whole[1], whole[2], *whole[3], scoped("swapfar", send, whole[2], CORE)])
                done += steps[r](gathered)
                if r == count - 1:
                    spread[r].append(scoped("far", send, tie(near[0], *done[len(near) :]), CROSS_XY))
        return gathered

    def planes(self, part, r):
        with jax.named_scope("planes%d" % r):
            groups = self.groups
            pairs = [
                (d * groups + z, d * groups + (z + (1 if d & 1 else groups - 1)) % groups)
                for d in range(self.dp_size)
                for z in range(groups)
            ]
            beside = scoped("beside", lax.ppermute, part[1], ("dp", "tensor"), pairs)
            return beside, scoped("across", shift, part[0], 2, groups)

    def half_of(self, quarter):
        rows = quarter.shape[0] // 2
        return jnp.where(lax.rem(self.my_d, 2) == 0, quarter[:rows], quarter[rows:])

    def quarter_of(self, shard):
        rows = 2 * shard.shape[0] // self.dp_size
        return lax.dynamic_slice_in_dim(shard, self.my_d // 2 * rows, rows, 0)

    def whole(self, part, stacked=False):
        whole = self.all_parts(part)
        dim = part.shape[1]
        if stacked:
            whole = whole.reshape(self.groups, 4, -1, dim).transpose(1, 0, 2, 3)
        return [whole.reshape(4, -1, dim)]


def reduce_grads(gather, grads, own_rows, between, at_last):
    groups, spots = gather.groups, gather.spots
    if not gather.paired:
        mats, bias = grads
        mats = lax.psum_scatter(mats, ("dp", "tensor"), scatter_dimension=1, tiled=True)
        middle = between(None)
        return (mats[0], mats[1], mats[2], lax.psum(bias, ("dp", "tensor"))), at_last(None)
    keep, away = grads
    rows, dim = keep.shape[1:]
    low = jax.ShapeDtypeStruct((rows, dim), BF)
    come = scoped("cores", send, away, CORE)
    to_x, to_y, to_far = pl.pallas_call(
        add_cores_kernel,
        out_shape=[low, low, low],
        in_specs=[SMEM, ANY, ANY],
        out_specs=[VMEM] * 3,
        scratch_shapes=[pltpu.VMEM((3, rows, dim), BF), pltpu.VMEM((3, rows, dim), BF), pltpu.SemaphoreType.DMA((6,))],
        compiler_params=limit(60),
    )(spots, keep, come)
    from_far = scoped("far", send, to_far, FAR_XY)
    from_x = scoped("x", send, to_x, ALONG_X)
    from_y = scoped("y", send, to_y, ALONG_Y)
    block = jax.ShapeDtypeStruct((3 * own_rows + 24, dim), BF)
    middle = between(to_far)
    mine, *goes = pl.pallas_call(
        add_plane_kernel,
        out_shape=[jax.ShapeDtypeStruct((3 * own_rows + 8, dim), F32)] + [block] * (groups - 1),
        in_specs=[SMEM] + [VMEM] * 3 + [ANY] * 2,
        out_specs=[VMEM] * groups,
        scratch_shapes=[pltpu.VMEM((rows - 16, dim), F32), pltpu.VMEM((rows, dim), BF), pltpu.VMEM((rows, dim), BF),
                        pltpu.SemaphoreType.DMA((2,))],
        compiler_params=limit(60),
    )(spots, from_x, from_y, from_far, tie(keep, middle), come)
    after = at_last(mine)
    comes = [scoped("stack%d" % i, shift, go, i + 1, groups) for i, go in enumerate(goes)]
    part = jax.ShapeDtypeStruct((own_rows, dim), F32)
    sums = pl.pallas_call(
        add_stack_kernel,
        out_shape=[part, part, part, jax.ShapeDtypeStruct((8, dim), F32)],
        in_specs=[VMEM] * groups,
        out_specs=[VMEM] * 4,
        compiler_params=LITTLE,
    )(mine, *comes)
    return sums, after


def cost(flops, moved, exps=0):
    return pl.CostEstimate(flops=int(flops), bytes_accessed=int(moved), transcendentals=int(exps))


def head_masks():
    lane = lax.broadcasted_iota(jnp.int32, (1, 128), 1)
    first = (lane < 64).astype(F32)
    return [first.astype(BF), (1.0 - first).astype(BF)], lane < 64


def attention_kernel(spots_ref, len_ref, x_ref, norms_ref, *refs):
    *sources, q_hbm, k_hbm, v_hbm, p_hbm, low_ref, xhat_hbm, rstd_ref, w_ref, ctx_ref, q_ref, k_ref, v_ref, p_ref, xhat_ref, sems, store_sems = refs
    fetch_stacked(spots_ref, sources, w_ref, sems, False)
    fetch_stacked(spots_ref, sources, w_ref, sems, True)
    rows, dim = x_ref.shape
    for m in range(4):
        arrive_stacked(w_ref, sems, m)
    seq_len = p_ref.shape[1]
    x = x_ref[...]
    q_ref[...] = (mm_t(x, w_ref[0]).astype(BF).astype(F32) * (1.0 / math.sqrt(dim // HEADS))).astype(BF)
    k_ref[...] = mm_t(x, w_ref[1]).astype(BF)
    v_ref[...] = mm_t(x, w_ref[2]).astype(BF)
    stores = begin(((q_ref, q_hbm), (k_ref, k_hbm), (v_ref, v_hbm)), store_sems)
    masks, first = head_masks()
    key_at = lax.broadcasted_iota(jnp.int32, (seq_len, 1), 0)

    for s in range(rows // seq_len):
        at = slice(s * seq_len, (s + 1) * seq_len)
        valid = key_at < len_ref[s]
        for j in range(HEADS // 2):
            cols = slice(128 * j, 128 * (j + 1))
            q, k, v = q_ref[at, cols], k_ref[at, cols], v_ref[at, cols]
            parts = []
            for h in range(2):
                scores = jnp.where(valid, mm_t(k, q * masks[h]), MASKED)
                exps = jnp.exp(scores - jnp.max(scores, axis=0, keepdims=True))
                probs = (exps * (1.0 / jnp.sum(exps, axis=0, keepdims=True))).astype(BF)
                p_ref[s * HEADS + 2 * j + h] = probs
                parts.append(t_mm(probs, v))
            ctx_ref[at, cols] = jnp.where(first, parts[0], parts[1]).astype(BF)
        heads = pl.ds(s * HEADS, HEADS)
        stores += begin(((p_ref.at[heads], p_hbm.at[heads]),), store_sems.at[pl.ds(3 + s, 1)])
    xhat, rstd = norm_parts(x.astype(F32) + mm(ctx_ref[...], w_ref[3]))
    xhat_ref[...] = xhat
    stores += begin(((xhat_ref, xhat_hbm),), store_sems.at[pl.ds(3 + rows // seq_len, 1)])
    rstd_ref[...] = rstd
    low_ref[...] = (xhat * norms_ref[0:1, :] + norms_ref[1:2, :]).astype(BF)
    for store in stores:
        store.wait()


def attention_forward(spots, lengths, x, sources, norms, seq_len):
    rows, dim = x.shape
    seqs = rows // seq_len
    low = jax.ShapeDtypeStruct((rows, dim), BF)
    return pl.pallas_call(
        attention_kernel,
        out_shape=[low, low, low,
                   jax.ShapeDtypeStruct((seqs * HEADS, seq_len, seq_len), BF), low,
                   jax.ShapeDtypeStruct((rows, dim), F32), jax.ShapeDtypeStruct((rows, 1), F32)],
        in_specs=[SMEM] * 2 + [VMEM] * 2 + [ANY] * len(sources),
        out_specs=[ANY] * 4 + [VMEM, ANY, VMEM],
        scratch_shapes=[pltpu.VMEM((4, dim, dim), BF)] + [pltpu.VMEM((rows, dim), BF)] * 4 + [
            pltpu.VMEM((seqs * HEADS, seq_len, seq_len), BF), pltpu.VMEM((rows, dim), F32),
            WEIGHT_SEMS, pltpu.SemaphoreType.DMA((4 + seqs,)),
        ],
        compiler_params=limit(60),
        cost_estimate=cost(2 * rows * dim * (4 * dim + 2 * seq_len), 2 * (4 * dim * dim + 8 * rows * dim), rows * seq_len * HEADS),
    )(spots, lengths, x, norms, *sources)


def by_rows(rows, step, work, unroll=1):
    work(slice(0, rows))


def ffn_in_kernel(spots_ref, x_ref, bias_ref, *refs):
    *sources, act_hbm, slope_hbm, act_ref, slope_ref, w_ref, pre_ref, sems, store_sems = refs
    units = pre_ref.shape[1]
    order = planes_in_order(spots_ref)
    stores = []
    fetch(spots_ref, sources, w_ref, sems, [0, 1])
    for r in range(4):
        fetch(spots_ref, sources, w_ref, sems, [r + 2] if r < 2 else [])
        arrive(w_ref, sems, r)
        pre_ref[...] = mm(x_ref[...], w_ref[r * x_ref.shape[1] : (r + 1) * x_ref.shape[1], :])
        cols = slice(r * units, (r + 1) * units)
        act, slope = gelu_parts(pre_ref[...] + bias_ref[order[r]])
        act_ref[:, cols] = act.astype(BF)
        slope_ref[:, cols] = slope.astype(BF)
        pairs = [(act_ref, act_hbm), (slope_ref, slope_hbm)]
        stores += begin([(ref.at[:, cols], hbm.at[:, cols]) for ref, hbm in pairs], store_sems.at[pl.ds(2 * r, 2)])
    for store in stores:
        store.wait()


def ffn_forward(spots, x, sources, bias, units):
    rows, dim = x.shape
    planes = bias.shape[0] // units
    out = jax.ShapeDtypeStruct((rows, planes * units), BF)
    return pl.pallas_call(
        ffn_in_kernel,
        out_shape=[out, out],
        in_specs=[SMEM] + [VMEM] * 2 + [ANY] * len(sources),
        out_specs=[ANY] * 2,
        scratch_shapes=[
            pltpu.VMEM((rows, planes * units), BF), pltpu.VMEM((rows, planes * units), BF),
            pltpu.VMEM((planes * dim, units), BF), pltpu.VMEM((rows, units), F32), WEIGHT_SEMS, pltpu.SemaphoreType.DMA((8,)),
        ],
        compiler_params=limit(60),
        cost_estimate=cost(2 * rows * dim * units * planes, 2 * planes * units * (dim + 2 * rows), 2 * rows * units * planes),
    )(spots, x, bias.reshape(planes, 1, units), *sources)


def two_pass(values, table):
    high = values.astype(BF)
    return mm(high, table) + mm((values - high.astype(F32)).astype(BF), table)


def put_rows(ref, mats, bias):
    at = 0
    for mat in mats:
        ref[at : at + mat.shape[0], :] = mat.astype(BF)
        at += mat.shape[0]
    high = bias.astype(BF).astype(F32)
    ref[at : at + 16, :] = jnp.concatenate([high, bias - high], axis=0).astype(BF)


def sum_rows(arrays):
    total = arrays[0].astype(F32)
    for array in arrays[1:]:
        total = total + array.astype(F32)
    rows = total.shape[0] - 16
    return total[:rows], total[rows : rows + 8] + total[rows + 8 :]


def add_cores_kernel(spots_ref, keep_hbm, come_hbm, x_ref, y_ref, far_ref, keep_ref, come_ref, sems):
    quarter = lax.div(spots_ref[0], 2)
    pairs = []
    for i in range(3):
        q = jnp.bitwise_xor(quarter, i + 1)
        pairs += [(keep_hbm.at[q], keep_ref.at[i]), (come_hbm.at[q], come_ref.at[i])]
    copies = begin(pairs, sems)
    for i, ref in enumerate((x_ref, y_ref, far_ref)):
        copies[2 * i].wait()
        copies[2 * i + 1].wait()
        mats, bias = sum_rows([keep_ref[i], come_ref[i]])
        put_rows(ref, [mats], bias)


def add_plane_kernel(spots_ref, x_ref, y_ref, far_ref, keep_hbm, come_hbm, mine_ref, *refs):
    *go_refs, total_ref, keep_ref, come_ref, sems = refs
    quarter = lax.div(spots_ref[0], 2)
    for copy in begin(((keep_hbm.at[quarter], keep_ref), (come_hbm.at[quarter], come_ref)), sems):
        copy.wait()
    total_ref[...], bias = sum_rows([keep_ref[...], come_ref[...], x_ref[...], y_ref[...], far_ref[...]])
    groups = len(go_refs) + 1
    width = total_ref.shape[0] // 3
    rows = width // groups

    def block(plane):
        at = [pl.multiple_of(i * width + plane * rows, 8) for i in range(3)]
        return jnp.concatenate([total_ref[pl.ds(a, rows), :] for a in at], axis=0)

    my_z = spots_ref[8]
    mine_ref[...] = jnp.concatenate([block(my_z), bias], axis=0)
    high = bias.astype(BF).astype(F32)
    for i, ref in enumerate(go_refs):
        there = block(lax.rem(my_z + i + 1, groups))
        ref[...] = jnp.concatenate([there, high, bias - high, jnp.zeros_like(bias)], axis=0).astype(BF)


def add_stack_kernel(mine_ref, *refs):
    come_refs, (q_ref, k_ref, v_ref, bias_ref) = refs[:-4], refs[-4:]
    total = mine_ref[...]
    rows = q_ref.shape[0]
    for ref in come_refs:
        come = ref[...].astype(F32)
        bias = come[3 * rows : 3 * rows + 8] + come[3 * rows + 8 : 3 * rows + 16]
        total = total + jnp.concatenate([come[: 3 * rows], bias], axis=0)
    q_ref[...], k_ref[...], v_ref[...] = (total[i * rows : (i + 1) * rows] for i in range(3))
    bias_ref[...] = total[3 * rows :]


def joining_kernel(
    spots_ref, member_ref, member_t_ref, avail_ref, norms_ref, act_hbm, xhat1_hbm, cot_hbm, *refs, halves, count
):
    gain1, bias1, gain2, bias2 = (norms_ref[i : i + 1, :] for i in range(4))
    down_hbm, up_hbm, *refs = refs
    join_sources, sources, refs = refs[:count], refs[count:-39], refs[-39:]
    stage_ref, biases_ref, stage_sem, refs = refs[-3], refs[-2], refs[-1], refs[:-3]
    out_hbm, g2_hbm, g_ffn_ref, grad_hbm0, grad_hbm1 = refs[:5]
    act_ref, w_out_ref, down_ref, up_ref, join_ref, xhat1_ref, cot_ref, act_sems, out_sems, sems, store_sems = refs[5:16]
    ffn_ref, u_ref, w_ref, big_u_ref, big_w_ref, p_wide_ref, sums_ref = refs[16:23]
    x_ref, act2_ref, slope_ref, q_ref, gq_ref, low_ref, mixed_ref, t_ref = refs[23:31]
    out_ref, g2_ref, grad_ref0, grad_ref1, bias_ref = refs[31:36]
    rows, dim = out_ref.shape
    units = w_out_ref.shape[0] // 4
    seqs = avail_ref.shape[0]
    per = rows // seqs
    everyone = [slice(i * per, (i + 1) * per) for i in range(seqs)]
    fscale = 1.0 / math.sqrt(dim)
    member, member_t = member_ref[...], member_t_ref[...]
    loads = []

    def issue(r):
        if r < 4:
            fetch(spots_ref, sources, w_out_ref, out_sems, [r])
            cols = pl.ds(r * units, units)
            loads.extend(begin(((act_hbm.at[:, cols], act_ref.at[:, cols]),), act_sems.at[pl.ds(r, 1)]))
        elif r == 4:
            fetch_blocks(spots_ref, join_sources, stage_ref, stage_sem)
        elif r == 5:
            pairs = ((down_hbm, down_ref), (up_hbm, up_ref), (xhat1_hbm, xhat1_ref), (cot_hbm, cot_ref))
            loads.extend(begin(pairs, sems))

    issue(0)
    issue(1)
    for r in range(4):
        issue(r + 2)
        loads[r].wait()
        arrive(w_out_ref, out_sems, r)
        if r % 2 == 1:
            both = slice((r - 1) * units, (r + 1) * units)
            for at in everyone:
                term = mm(act_ref[at, both], w_out_ref[both, :])
                ffn_ref[at, :] = term if r == 1 else ffn_ref[at, :] + term
    loads = loads[4:]
    for at in everyone:
        x_ref[at, :] = ffn_ref[at, :].astype(BF)
    pltpu.make_async_copy(stage_ref, stage_ref, stage_sem).wait()
    order_rows(stage_ref, join_ref, biases_ref)
    qb, vb = biases_ref[0:1, :], biases_ref[1:2, :]
    for load in loads:
        load.wait()
    up = up_ref[...]
    halves_of = {}

    def narrow(i, name, value=None):
        if value is not None:
            halves_of[i, name] = value
        return halves_of[i, name]

    def per_adapter(values):
        high = values.astype(BF)
        return mm(high, member) + mm((values - high.astype(F32)).astype(BF), member)

    def to_q(i, at):
        q_ref[at, :] = (mm(x_ref[at, :], join_ref[0]) + qb).astype(BF)

    def down(i, at):
        act, slope = gelu_parts(mm(x_ref[at, :], down_ref[...]))
        act2_ref[at, :] = act.astype(BF)
        slope_ref[at, :] = slope.astype(BF)

    def to_u(i, at):
        u = mm_t(q_ref[at, :], join_ref[1])
        u_ref[at, :] = u
        narrow(i, "dot", jnp.sum(ffn_ref[at, :] * u, axis=-1, keepdims=True))

    def scores(i, at):
        big_u = mm_t(u_ref[at, :].astype(BF), up)
        big_u_ref[at, :] = big_u
        fscores = (per_adapter(act2_ref[at, :].astype(F32) * big_u) + narrow(i, "dot")) * fscale
        fscores = jnp.where(avail_ref[i] > 0, fscores, MASKED)
        fexp = jnp.exp(fscores - jnp.max(fscores, axis=-1, keepdims=True))
        narrow(i, "probs", fexp / jnp.sum(fexp, axis=-1, keepdims=True))

    def mix(i, at):
        p_wide = two_pass(narrow(i, "probs"), member_t)
        p_wide_ref[at, :] = p_wide
        weighed = (p_wide * act2_ref[at, :].astype(F32)).astype(BF)
        mixed_ref[at, :] = (ffn_ref[at, :] + mm(weighed, up)).astype(BF)

    def norm(i, at):
        normed1 = xhat1_ref[at, :] * gain1 + bias1
        xhat2, rstd2 = norm_parts(normed1 + mm(mixed_ref[at, :], join_ref[2]) + vb)
        out_ref[at, :] = (xhat2 * gain2 + bias2).astype(BF)
        g2 = norm_back(cot_ref[at, :].astype(F32), gain2, xhat2, rstd2)
        g2_ref[at, :] = g2
        low_ref[at, :] = g2.astype(BF)
        narrow(i, "dot2", jnp.sum(g2 * vb, axis=-1, keepdims=True))
        narrow(i, "d_vb", jnp.sum(g2.reshape(-1, 8, dim), axis=0))

    def to_w(i, at):
        w = mm_t(low_ref[at, :], join_ref[2])
        w_ref[at, :] = w
        narrow(i, "dot2", narrow(i, "dot2") + jnp.sum(ffn_ref[at, :] * w, axis=-1, keepdims=True))

    def score_grads(i, at):
        big_w = mm_t(w_ref[at, :].astype(BF), up)
        big_w_ref[at, :] = big_w
        gvals = per_adapter(act2_ref[at, :].astype(F32) * big_w) + narrow(i, "dot2")
        fprobs = narrow(i, "probs")
        gs = fprobs * (gvals - jnp.sum(gvals * fprobs, axis=-1, keepdims=True)) * fscale
        narrow(i, "gs", gs)
        narrow(i, "gs_sum", jnp.sum(gs, axis=-1, keepdims=True))

    def to_t(i, at):
        wide = two_pass(narrow(i, "gs"), member_t)
        weighed = (wide * act2_ref[at, :].astype(F32)).astype(BF)
        grad = wide * big_u_ref[at, :] + p_wide_ref[at, :] * big_w_ref[at, :]
        slope_ref[at, :] = (grad * slope_ref[at, :].astype(F32)).astype(BF)
        t_ref[at, :] = (mm(weighed, up) + narrow(i, "gs_sum") * ffn_ref[at, :]).astype(BF)

    def to_gq(i, at):
        gq = mm(t_ref[at, :], join_ref[1]).astype(BF)
        gq_ref[at, :] = gq
        narrow(i, "d_qb", jnp.sum(gq.astype(F32).reshape(-1, 8, dim), axis=0))

    def all_halves(*steps):
        for step in steps:
            for i, at in enumerate(everyone):
                step(i, at)

    all_halves(to_q, down, to_u, scores, mix, norm)
    stores = begin(((out_ref, out_hbm), (g2_ref, g2_hbm)), store_sems)
    all_halves(to_w, score_grads)
    sums_ref[2] = t_mm(mixed_ref[...], low_ref[...])
    all_halves(to_t)
    sums_ref[1] = t_mm(t_ref[...], q_ref[...])
    all_halves(to_gq)
    sums_ref[0] = t_mm(x_ref[...], gq_ref[...])
    row = lax.broadcasted_iota(jnp.int32, (8, 1), 0)
    d_qb, d_vb = (
        jnp.sum(sum(narrow(i, name) for i in range(seqs)), axis=0, keepdims=True) for name in ("d_qb", "d_vb")
    )
    bias_ref[...] = jnp.where(row == 0, d_qb, jnp.where(row == 1, d_vb, 0.0))
    if halves:
        core = lax.rem(spots_ref[0], 2)
        part = dim // 8
        for i, (ref, side) in enumerate(((grad_ref1, 1 - core), (grad_ref0, core))):
            for q in range(4):
                at = pl.ds(pl.multiple_of((2 * q + side) * part, part), part)
                put_rows(ref.at[q], [sums_ref[i, at, :] for i in range(3)], bias_ref[...])
            hbm = grad_hbm0 if i else grad_hbm1
            stores += begin(((ref, hbm),), store_sems.at[pl.ds(2 + i, 1)])
    else:
        stores += begin(((sums_ref, grad_hbm0), (bias_ref, grad_hbm1)), store_sems.at[pl.ds(2, 2)])
    for i, at in enumerate(everyone):
        total = mm_t(slope_ref[at, :], down_ref[...]) + mm_t(gq_ref[at, :], join_ref[0])
        g_ffn_ref[at, :] = (narrow(i, "gs_sum") * u_ref[at, :] + w_ref[at, :] + total).astype(BF)
    for store in stores:
        store.wait()


def joining(spots, halves, act, sources, adapt_down, up, join_sources, member, member_t, avail, xhat1, norms, cot):
    rows, dim = xhat1.shape
    if halves:
        grads = [jax.ShapeDtypeStruct((4, 3 * dim // 8 + 16, dim), BF)] * 2
    else:
        grads = [jax.ShapeDtypeStruct((3, dim, dim), F32), jax.ShapeDtypeStruct((8, dim), F32)]
    wide, low = pltpu.VMEM((rows, dim), F32), pltpu.VMEM((rows, dim), BF)
    height, blocks = join_sources[-1].shape[-2:][0], 32
    stage_shape = join_sources[0].shape if len(join_sources) == 1 else (blocks, height, dim)
    return pl.pallas_call(
        partial(joining_kernel, halves=halves, count=len(join_sources)),
        out_shape=[
            jax.ShapeDtypeStruct((rows, dim), BF),
            jax.ShapeDtypeStruct((rows, dim), F32),
            jax.ShapeDtypeStruct((rows, dim), BF),
        ] + grads,
        in_specs=[SMEM] + [VMEM] * 4 + [ANY] * (len(sources) + len(join_sources) + 5),
        out_specs=[ANY, ANY, VMEM, ANY, ANY],
        scratch_shapes=[
            pltpu.VMEM(act.shape, BF),
            pltpu.VMEM((act.shape[1], dim), BF),
            pltpu.VMEM(adapt_down.shape, BF),
            pltpu.VMEM(up.shape, BF),
            pltpu.VMEM((3, dim, dim), BF),
            wide,
            low,
            WEIGHT_SEMS,
            WEIGHT_SEMS,
            pltpu.SemaphoreType.DMA((4,)),
            pltpu.SemaphoreType.DMA((4,)),
        ] + [wide] * 6 + [pltpu.VMEM((3, dim, dim), F32)] + [low] * 8 + [
            low,
            wide,
            pltpu.VMEM(grads[0].shape if halves else (8, 128), BF),
            pltpu.VMEM(grads[1].shape if halves else (8, 128), BF),
            pltpu.VMEM((8, dim), F32),
            pltpu.VMEM(stage_shape, BF),
            pltpu.VMEM((8, dim), F32),
            pltpu.SemaphoreType.DMA,
        ],
        compiler_params=limit(60),
        cost_estimate=cost(2 * rows * dim * (15 * dim + act.shape[1]), 2 * dim * (8 * dim + 10 * rows), 2 * rows * dim),
    )(spots, member, member_t, avail, norms, act, xhat1, cot, adapt_down, up, *join_sources, *sources)


def ffn_back_kernel(spots_ref, g_ref, rstd_ref, norms_ref, slope_hbm, g2_hbm, xhat_hbm, *refs, count):
    refs, (out_sources, in_sources) = refs[sum(count) :], (refs[: count[0]], refs[count[0] : sum(count)])
    g1_hbm, low_hbm, g1_ref, low_ref, slope_ref, g2_ref, xhat_ref, w_out_ref, w_in_ref, pre_ref, out_sems, in_sems, slope_sems, sems, store_sems = refs
    units = w_out_ref.shape[0] // 4
    rows = g_ref.shape[0]
    everyone = [slice(i * rows // 2, (i + 1) * rows // 2) for i in range(2)]
    loads = []

    def issue(r):
        if r < 4:
            fetch(spots_ref, out_sources, w_out_ref, out_sems, [r])
            cols = pl.ds(r * units, units)
            loads.extend(begin(((slope_hbm.at[:, cols], slope_ref.at[:, cols]),), slope_sems.at[pl.ds(r, 1)]))
        elif r < 8:
            fetch(spots_ref, in_sources, w_in_ref, in_sems, [r - 4], side_by_side=True)
        elif r == 8:
            loads.extend(begin(((g2_hbm, g2_ref), (xhat_hbm, xhat_ref)), sems))

    issue(0)
    issue(1)
    for r in range(4):
        issue(r + 2)
        cols = slice(r * units, (r + 1) * units)
        arrive(w_out_ref, out_sems, r)
        loads[r].wait()
        for at in everyone:
            pre_ref[at, cols] = (mm_t(g_ref[at, :], w_out_ref[cols, :]) * slope_ref[at, cols].astype(F32)).astype(BF)
    for r in range(4, 8):
        issue(r + 2)
        arrive(w_in_ref, in_sems, r - 4, side_by_side=True)
        if r == 5:
            both = slice(0, 2 * units)
            for at in everyone:
                g1_ref[at, :] = mm_t(pre_ref[at, both], w_in_ref[:, both])
    for load in loads[4:]:
        load.wait()
    both = slice(2 * units, 4 * units)
    stores = []
    for at in everyone:
        total = mm_t(pre_ref[at, both], w_in_ref[:, both]) + g1_ref[at, :] + g2_ref[at, :]
        g1 = norm_back(total, norms_ref[0:1, :], xhat_ref[at, :], rstd_ref[at, :])
        g1_ref[at, :] = g1
        low_ref[at, :] = g1.astype(BF)
        stores += begin(((g1_ref.at[at], g1_hbm.at[at]), (low_ref.at[at], low_hbm.at[at])), store_sems.at[pl.ds(len(stores), 2)])
    for store in stores:
        store.wait()


def ffn_backward(spots, g_ffn, slope, out_sources, in_sources, g2, xhat, rstd, norms):
    rows, dim = xhat.shape
    planes = 4
    units = slope.shape[1] // planes
    return pl.pallas_call(
        partial(ffn_back_kernel, count=(len(out_sources), len(in_sources))),
        out_shape=[jax.ShapeDtypeStruct((rows, dim), F32), jax.ShapeDtypeStruct((rows, dim), BF)],
        in_specs=[SMEM] + [VMEM] * 3 + [ANY] * (len(out_sources) + len(in_sources) + 3),
        out_specs=[ANY, ANY],
        scratch_shapes=[
            pltpu.VMEM((rows, dim), F32), pltpu.VMEM((rows, dim), BF),
            pltpu.VMEM(slope.shape, BF), pltpu.VMEM((rows, dim), F32), pltpu.VMEM((rows, dim), F32),
            pltpu.VMEM((planes * units, dim), BF), pltpu.VMEM((dim, planes * units), BF), pltpu.VMEM(slope.shape, BF),
            WEIGHT_SEMS, WEIGHT_SEMS, WEIGHT_SEMS, pltpu.SemaphoreType.DMA((2,)),
            pltpu.SemaphoreType.DMA((4,)),
        ],
        compiler_params=limit(60),
        cost_estimate=cost(4 * rows * dim * units * planes, 2 * planes * units * (2 * dim + rows)),
    )(spots, g_ffn, rstd, norms, slope, g2, xhat, *out_sources, *in_sources)


def attention_back_heads(s, seq_len, q_ref, k_ref, v_ref, p_ref, g_ref, dq_ref, dk_ref, dv_ref, first_seq):
    dim = q_ref.shape[1]
    scale = 1.0 / math.sqrt(dim // HEADS)
    masks, first = head_masks()
    at = slice((s - first_seq) * seq_len, (s - first_seq + 1) * seq_len)
    for j in range(HEADS // 2):
        cols = slice(128 * j, 128 * (j + 1))
        q, k, v, g = q_ref[at, cols], k_ref[at, cols], v_ref[at, cols], g_ref[at, cols]
        dq, dk, dv = [], [], []
        for h in range(2):
            probs_low = p_ref[(s - first_seq) * HEADS + 2 * j + h]
            probs = probs_low.astype(F32)
            g_probs = mm_t(v, g * masks[h])
            g_scores = (probs * (g_probs - jnp.sum(g_probs * probs, axis=0, keepdims=True))).astype(BF)
            dv.append(mm(probs_low, g))
            dk.append(mm(g_scores, q))
            dq.append(t_mm(g_scores, k))
        dq_ref[at, cols] = (jnp.where(first, dq[0], dq[1]) * scale).astype(BF)
        dk_ref[at, cols] = jnp.where(first, dk[0], dk[1]).astype(BF)
        dv_ref[at, cols] = jnp.where(first, dv[0], dv[1]).astype(BF)


def load_heads(hbm, vmem, sems, first, count):
    seq_len = hbm[3].shape[1]
    rows, heads = pl.ds(first * seq_len, count * seq_len), pl.ds(first * HEADS, count * HEADS)
    pairs = [(hbm[i].at[rows], vmem[i]) for i in range(3)] + [(hbm[3].at[heads], vmem[3])]
    return begin(pairs, sems)


def attention_back_first_kernel(spots_ref, *refs):
    *refs, ctx_hbm, dq_ref, dk_ref, dv_ref, w_ref, g1_ref, ctx_ref, q_ref, k_ref, v_ref, p_ref, w_sems, sems, g_sems = refs
    g1_hbm, *sources, q_hbm, k_hbm, v_hbm, p_hbm = refs
    seq_len = p_ref.shape[1]
    rows, dim = g1_ref.shape
    loads = begin(((g1_hbm, g1_ref),), g_sems.at[pl.ds(0, 1)])
    fetch_stacked(spots_ref, sources, w_ref, w_sems, True)
    seqs = q_ref.shape[0] // seq_len
    loads += load_heads((q_hbm, k_hbm, v_hbm, p_hbm), (q_ref, k_ref, v_ref, p_ref), sems, 0, seqs)
    loads[0].wait()
    arrive_stacked(w_ref, w_sems, 3)
    ctx_ref[...] = mm_t(g1_ref[...], w_ref[3]).astype(BF)
    later = pl.ds(seqs * seq_len, rows - seqs * seq_len)
    store = begin(((ctx_ref.at[later], ctx_hbm),), g_sems.at[pl.ds(1, 1)])[0]
    for load in loads[1:]:
        load.wait()
    for s in range(seqs):
        attention_back_heads(s, seq_len, q_ref, k_ref, v_ref, p_ref, ctx_ref, dq_ref, dk_ref, dv_ref, 0)
    store.wait()


def attention_back_last_kernel(spots_ref, *refs):
    *refs, out_ref, g1_ref, ctx_ref, dq0_ref, dk0_ref, dv0_ref, w_ref, q_ref, k_ref, v_ref, p_ref, dq_ref, dk_ref, dv_ref, w_sems, sems, late_sems = refs
    g1_hbm, ctx_hbm, dq0_hbm, dk0_hbm, dv0_hbm, *sources, q_hbm, k_hbm, v_hbm, p_hbm = refs
    rows, dim = g1_ref.shape
    seq_len = p_ref.shape[1]
    first = dq0_ref.shape[0] // seq_len
    seqs = q_ref.shape[0] // seq_len
    loads = begin(((ctx_hbm, ctx_ref),), late_sems.at[pl.ds(0, 1)])
    loads += load_heads((q_hbm, k_hbm, v_hbm, p_hbm), (q_ref, k_ref, v_ref, p_ref), sems, first, seqs)
    for load in loads:
        load.wait()
    fetch_stacked(spots_ref, sources, w_ref, w_sems, False)
    pairs = ((dq0_hbm, dq0_ref), (dk0_hbm, dk0_ref), (dv0_hbm, dv0_ref), (g1_hbm, g1_ref))
    loads = begin(pairs, late_sems.at[pl.ds(1, 4)])
    for s in range(seqs):
        attention_back_heads(s, seq_len, q_ref, k_ref, v_ref, p_ref, ctx_ref, dq_ref, dk_ref, dv_ref, 0)
    for load in loads:
        load.wait()
    for m in range(3):
        arrive_stacked(w_ref, w_sems, m)
    for at, grads in ((slice(0, first * seq_len), (dq0_ref, dk0_ref, dv0_ref)), (slice(first * seq_len, rows), (dq_ref, dk_ref, dv_ref))):
        total = g1_ref[at, :]
        for m, grad in enumerate(grads):
            total = total + mm(grad[...], w_ref[m])
        out_ref[at, :] = total.astype(BF)


def attention_backward_first(spots, g1_low, sources, q, k, v, probs):
    rows, dim = g1_low.shape
    heads, seq_len = probs.shape[0] // 2, probs.shape[1]
    half, low = jax.ShapeDtypeStruct((rows // 2, dim), BF), pltpu.VMEM((rows // 2, dim), BF)
    return pl.pallas_call(
        attention_back_first_kernel,
        out_shape=[half, half, half, half],
        in_specs=[SMEM, ANY] + [ANY] * (len(sources) + 4),
        out_specs=[ANY] + [VMEM] * 3,
        scratch_shapes=[pltpu.VMEM((4, dim, dim), BF), pltpu.VMEM((rows, dim), BF), pltpu.VMEM((rows, dim), BF), low, low, low, pltpu.VMEM((heads,) + probs.shape[1:], BF),
                        WEIGHT_SEMS, pltpu.SemaphoreType.DMA((4,)), pltpu.SemaphoreType.DMA((2,))],
        compiler_params=limit(60),
        cost_estimate=cost(2 * rows * dim * (dim + 2 * seq_len), 2 * (dim * dim + 5 * rows * dim)),
    )(spots, g1_low, *sources, q, k, v, probs)


def attention_backward_last(spots, g1, halfway, sources, q, k, v, probs):
    rows, dim = g1.shape
    heads, seq_len = probs.shape[0] // 2, probs.shape[1]
    low = pltpu.VMEM((rows // 2, dim), BF)
    return pl.pallas_call(
        attention_back_last_kernel,
        out_shape=jax.ShapeDtypeStruct((rows, dim), BF),
        in_specs=[SMEM] + [ANY] * (len(sources) + 9),
        out_specs=VMEM,
        scratch_shapes=[pltpu.VMEM((rows, dim), F32), low, low, low, low, pltpu.VMEM((4, dim, dim), BF), low, low, low, pltpu.VMEM((heads,) + probs.shape[1:], BF), low, low, low,
                        WEIGHT_SEMS, pltpu.SemaphoreType.DMA((4,)), pltpu.SemaphoreType.DMA((5,))],
        compiler_params=limit(60),
        cost_estimate=cost(2 * rows * dim * (3 * dim + 2 * seq_len), 2 * (3 * dim * dim + 5 * rows * dim)),
    )(spots, g1, *halfway, *sources, q, k, v, probs)


def shards(
    tokens, lengths, adapter_mask, cotangent, att_query, att_key, att_value, att_out,
    norm1_gain, norm1_bias, ffn_in, ffn_bias, ffn_out, adapt_down, adapt_up, norm2_gain,
    norm2_bias, joining_query, joining_key, joining_value, joining_qbias, joining_vbias,
):
    groups = lax.axis_size("tensor")
    dp_size = lax.axis_size("dp")
    my_z = lax.axis_index("tensor")
    my_d = lax.axis_index("dp")
    seq_local, seq_len, dim = tokens.shape
    mine = seq_local // groups
    rows = mine * seq_len
    adapters, neck = adapt_up.shape[0], adapt_up.shape[1]
    own_rows = joining_query.shape[0]

    gather = Gather(dp_size, groups, my_d, my_z, mine)
    spots = gather.spots
    biases = lax.dynamic_update_slice(
        jnp.zeros((8, dim), BF), jnp.stack([joining_qbias, joining_vbias]), (0, (my_d * groups + my_z) * own_rows)
    )
    att_mats = [att_query.T, att_key.T, att_value.T, att_out]
    join_part = jnp.concatenate([joining_query, joining_key, joining_value, biases], axis=0)

    def my_slice(array):
        return lax.dynamic_slice_in_dim(array, my_z * mine, mine, 0)

    x = my_slice(tokens).reshape(rows, dim)
    shifts = jnp.arange(128, dtype=jnp.int32)
    bits = jnp.right_shift(my_slice(adapter_mask)[:, None], jnp.minimum(shifts, adapters)[None, :]) % 2
    avail = jnp.where(shifts[None, :] < adapters, bits, 0)[:, None, :]
    norms = jnp.stack([norm1_gain, norm1_bias, norm2_gain, norm2_bias])
    lens = my_slice(lengths)
    owner = jnp.arange(adapters * neck, dtype=jnp.int32) // neck
    member = (owner[:, None] == shifts[None, :]).astype(BF)
    member_t = (shifts[:, None] == owner[None, :]).astype(BF)
    kept = {}

    def attend(sources):
        kept["att"] = attention_forward(spots, lens, x, sources, norms, seq_len)
        return [kept["att"][4]]

    def feed(sources):
        kept["ffn"] = ffn_forward(spots, kept["att"][4], sources, ffn_bias, ffn_in.shape[1])
        return [kept["ffn"][0]]

    if gather.paired:
        own = [att_mats, [ffn_in], None, [ffn_out]]
        steps = [
            lambda got: [],
            lambda got: [],
            lambda got: attend(got[0] + own[0]),
            lambda got: feed(got[1] + own[1]),
            lambda got: [],
            lambda got: [],
        ]
        quarter = att_mats[3]
        for i in range(3):
            quarter = jnp.where(my_d // 2 == i, att_mats[i], quarter)
        half = gather.half_of(quarter)
        rounds = [(half, tie(quarter, half))]
        shards_in, shards_out = tie(ffn_in, half), tie(ffn_out, half)
        in_quarter, in_half, out_quarter, out_half = cut(spots, [shards_in, shards_out])
        rounds += [(in_half, in_quarter), (out_half, out_quarter)]
        join_part = tie(join_part, *rounds[0])
        theirs = send(join_part, CORE)
        even = lax.rem(my_d, 2) == 0
        pair = jnp.concatenate([jnp.where(even, join_part, theirs), jnp.where(even, theirs, join_part)], axis=0)
        rounds.insert(2, (join_part, pair, join_part, theirs))
        got = gather.all_rounds(rounds, [x, norms, lens, avail, member, member_t, spots], steps)
        att_sources, in_sources, out_sources = (got[i] + own[i] for i in (0, 1, 3))
        join_sources = got[2]
    else:
        att_pack = jnp.concatenate(att_mats, axis=0)
        att_sources = gather.whole(gather.part_of(att_pack), True)
        in_sources, out_sources = (gather.whole(gather.part_of(shard)) for shard in (ffn_in, ffn_out))
        join_sources = [lax.all_gather(join_part, ("dp", "tensor"), axis=0)]
    up = adapt_up.reshape(adapters * neck, dim)
    cot = cotangent.reshape(rows, dim)

    def rest(att, ffn, avail, cot):
        q, k, v, probs, low1, xhat1, rstd1 = att
        act, slope = ffn
        layer_out, g2, g_ffn, *grads = joining(
            spots, gather.paired, act, out_sources, adapt_down, up, join_sources, member, member_t, avail, xhat1, norms, cot
        )
        done = {}

        def between(start):
            gradient = g_ffn if start is None else tie(g_ffn, start)
            done["g1"], g1_low = ffn_backward(spots, gradient, slope, out_sources, in_sources, g2, xhat1, rstd1, norms)
            done["half"] = attention_backward_first(spots, g1_low, att_sources, q, k, v, probs)
            return done["half"][1]

        def at_last(start):
            halfway = done["half"] if start is None else [tie(done["half"][0], start)] + list(done["half"][1:])
            return attention_backward_last(spots, done["g1"], halfway, att_sources, q, k, v, probs)

        return layer_out, grads, between, at_last

    if gather.paired:
        layer_out, grads, between, at_last = rest(kept["att"], kept["ffn"], avail, cot)
        (d_q, d_k, d_v, d_bias), input_grad = reduce_grads(gather, grads, own_rows, between, at_last)
    else:
        outs = []
        for first in range(0, mine, 2):
            at = slice(first * seq_len, (first + 2) * seq_len)
            att = attention_forward(spots, lens[first : first + 2], x[at], att_sources, norms, seq_len)
            ffn = ffn_forward(spots, att[4], in_sources, ffn_bias, ffn_in.shape[1])
            outs.append(rest(att, ffn, avail[first : first + 2], cot[at]))
        layer_out = jnp.concatenate([out[0] for out in outs])
        grads = [sum(out[1][i] for out in outs) for i in range(2)]
        (d_q, d_k, d_v, d_bias), input_grad = reduce_grads(
            gather, grads, own_rows, lambda start: [out[2](None) for out in outs],
            lambda start: jnp.concatenate([out[3](None) for out in outs]),
        )
    d_bias = lax.dynamic_slice_in_dim(d_bias[:2], (my_d * groups + my_z) * own_rows, own_rows, 1)
    return (
        layer_out.reshape(mine, seq_len, dim),
        input_grad.reshape(mine, seq_len, dim),
        d_q, d_k, d_v, d_bias[0], d_bias[1],
    )


def solution(mesh):
    both = P(ALL, None)
    return jax.shard_map(
        shards,
        mesh=mesh,
        in_specs=(
            P("dp", None, None), P("dp"), P("dp"), P(ALL, None, None),
            P(None, "tensor"), P(None, "tensor"), P(None, "tensor"), P("tensor", None),
            P(), P(), P(None, "tensor"), P(), P("tensor", None), P(), P(), P(), P(),
            both, both, both, P(ALL), P(ALL),
        ),
        out_specs=(P(ALL, None, None), P(ALL, None, None), both, both, both, P(ALL), P(ALL)),
        check_vma=False,
    )
```

```python
from functools import partial
import math

import jax
import jax.numpy as jnp
from jax import lax
from jax.experimental import pallas as pl
from jax.experimental.pallas import tpu as pltpu
from jax.sharding import PartitionSpec as P

HEADS = 12
EPS = 1e-05
MASKED = -1e30
ALL = ("dp", "tensor")
BF = jnp.bfloat16
F32 = jnp.float32


def mm(left, right):
    return jnp.dot(left, right, preferred_element_type=F32)


def mm_t(left, right):
    return lax.dot_general(left, right, (((1,), (1,)), ((), ())), preferred_element_type=F32)


def t_mm(left, right):
    return lax.dot_general(left, right, (((0,), (0,)), ((), ())), preferred_element_type=F32)


def norm_parts(values):
    average = jnp.mean(values, axis=-1, keepdims=True)
    centered = values - average
    variance = jnp.mean(centered * centered, axis=-1, keepdims=True)
    rstd = lax.rsqrt(variance + EPS)
    return centered * rstd, rstd


def norm_back(grad, gain, xhat, rstd):
    scaled = grad * gain
    return rstd * (
        scaled
        - jnp.mean(scaled, axis=-1, keepdims=True)
        - xhat * jnp.mean(scaled * xhat, axis=-1, keepdims=True)
    )


def gelu_parts(pre):
    cdf = 0.5 * (1.0 + lax.erf(pre * (1.0 / math.sqrt(2.0))))
    pdf = jnp.exp(-0.5 * pre * pre) * (1.0 / math.sqrt(2.0 * math.pi))
    return pre * cdf, cdf + pre * pdf


def limit(mebibytes):
    return pltpu.CompilerParams(vmem_limit_bytes=mebibytes * 2**20)


VMEM = pl.BlockSpec(memory_space=pltpu.VMEM)
SMEM = pl.BlockSpec(memory_space=pltpu.SMEM)
LITTLE = limit(24)
FAR_XY = [(i, i ^ 6) for i in range(8)]
CORE = [(i, i ^ 1) for i in range(8)]
ALONG_X = [(i, i ^ 2) for i in range(8)]
ALONG_Y = [(i, i ^ 4) for i in range(8)]
SPLIT_XY = [(i, i ^ (4 if i & 1 else 2)) for i in range(8)]
CROSS_XY = [(i, i ^ (3 if i & 1 else 5)) for i in range(8)]


def send(array, pairs):
    return lax.ppermute(array, "dp", pairs)


def shift(array, by, groups):
    return lax.ppermute(array, "tensor", [(i, (i + by) % groups) for i in range(groups)])


def scoped(name, step, *args):
    with jax.named_scope(name):
        return step(*args)


def tie(array, *others):
    return lax.optimization_barrier((array,) + others)[0]


def fetch_blocks(spots_ref, sources, stage_ref, sem):
    if len(sources) == 1:
        pltpu.make_async_copy(sources[0], stage_ref, sem).start()
        return
    planes = planes_in_order(spots_ref)
    for k, (ref, first) in enumerate(views(sources)):
        for i, plane in enumerate(planes[1:] + planes[:1]):
            pltpu.make_async_copy(ref.at[first + i], stage_ref.at[spots_ref[k] * len(planes) + plane], sem).start()


def order_rows(stage_ref, join_ref, biases_ref):
    blocks = stage_ref.shape[0]
    rows = join_ref.shape[1] // blocks
    total = 0.0
    for b in range(0, blocks, 2):
        pair = [stage_ref[b + i].astype(F32) for i in range(2)]
        for m in range(3):
            both = jnp.concatenate([block[m * rows : (m + 1) * rows] for block in pair], axis=0)
            join_ref[m, b * rows : (b + 2) * rows, :] = both.astype(BF)
        total = total + pair[0][3 * rows :] + pair[1][3 * rows :]
    biases_ref[...] = total


def fetch(spots_ref, sources, out_ref, sems, which, side_by_side=False):
    planes = planes_in_order(spots_ref)
    dim = sources[-1].shape[-1]
    rows = sources[-1].shape[-2]

    def copy(source, r, at):
        if side_by_side:
            target = out_ref.at[at, pl.ds(r * dim, dim)]
        else:
            target = out_ref.at[pl.ds(r * rows + at.start, at.size)]
        pltpu.make_async_copy(source, target, sems.at[r]).start()

    for r in which:
        if len(sources) == 1:
            copy(sources[0].at[planes[r]], r, pl.ds(0, rows))
        elif r == 0:
            copy(sources[-1], r, pl.ds(0, rows))
        else:
            for k, (ref, first) in enumerate(views(sources[:-1])):
                part = ref.shape[1]
                copy(ref.at[first + r - 1], r, pl.ds(pl.multiple_of(spots_ref[k] * part, part), part))


def arrive(out_ref, sems, r, side_by_side=False):
    dim = out_ref.shape[0] if side_by_side else out_ref.shape[1]
    block = out_ref.at[:, pl.ds(r * dim, dim)] if side_by_side else out_ref.at[pl.ds(r * out_ref.shape[0] // 4, out_ref.shape[0] // 4)]
    pltpu.make_async_copy(block, block, sems.at[r]).wait()


def fetch_stacked(spots_ref, sources, out_ref, sems, last):
    groups, dim = out_ref.shape[0], out_ref.shape[1]
    chosen = range(groups - 1, groups) if last else range(groups - 1)
    if len(sources) == 1:
        for m in chosen:
            pltpu.make_async_copy(sources[0].at[m], out_ref.at[m], sems.at[m]).start()
        return
    own = sources[-groups:]
    pieces = views(sources[:-groups])
    width, rows = dim // groups, pieces[0][0].shape[1]
    per = width // rows
    my_z = spots_ref[8]
    for m in chosen:
        at = pl.ds(pl.multiple_of(my_z * width, width), width)
        pltpu.make_async_copy(own[m], out_ref.at[m, at], sems.at[m]).start()
    for k, (ref, first) in enumerate(pieces):
        e = spots_ref[k]
        m = lax.div(e, per)

        @pl.when((m == groups - 1) == last)
        def _():
            for i, plane in enumerate(planes_in_order(spots_ref)[1:]):
                at = pl.ds(pl.multiple_of(plane * width + lax.rem(e, per) * rows, rows), rows)
                pltpu.make_async_copy(ref.at[first + i], out_ref.at[m, at], sems.at[m]).start()


def arrive_stacked(out_ref, sems, m):
    pltpu.make_async_copy(out_ref.at[m], out_ref.at[m], sems.at[m]).wait()


def views(sources):
    if len(sources) == 8:
        return [(source, 0) for source in sources]
    both, near, far, swapped, swapped_far = sources
    count = far.shape[0]
    return [(both, 0), (both, count), (near, 0), (near, count), (far, 0), (swapped, 0), (swapped, count), (swapped_far, 0)]


def cut_kernel(spots_ref, *refs):
    count = (len(refs) - 1) // 3
    shards, outs, sems = refs[:count], refs[count:-1], refs[-1]
    pairs = []
    for i, shard in enumerate(shards):
        rows = outs[2 * i].shape[0]
        at = pl.ds(pl.multiple_of(lax.div(spots_ref[0], 2) * rows, rows), rows)
        pairs.append((shard.at[at], outs[2 * i]))
        at = pl.ds(pl.multiple_of(spots_ref[0] * (rows // 2), rows // 2), rows // 2)
        pairs.append((shard.at[at], outs[2 * i + 1]))
    for copy in begin(pairs, sems):
        copy.wait()


def cut(spots, shards):
    outs = []
    for shard in shards:
        rows, dim = shard.shape
        outs += [jax.ShapeDtypeStruct((rows // 4, dim), BF), jax.ShapeDtypeStruct((rows // 8, dim), BF)]
    return pl.pallas_call(
        cut_kernel,
        out_shape=outs,
        in_specs=[SMEM] + [ANY] * len(shards),
        out_specs=[VMEM] * len(outs),
        scratch_shapes=[pltpu.SemaphoreType.DMA((len(outs),))],
        compiler_params=limit(60),
    )(spots, *shards)


def merge_kernel(spots_ref, *refs, count):
    beside, across, beside2, across2, *own = refs[:count]
    outs = refs[count:]
    core = lax.rem(spots_ref[0], 2)
    rows = across.shape[0]
    blocks = 3 + len(own) // 2
    sides = [outs[0], outs[1]] if len(outs) == 2 else [outs[0].at[pl.ds(i * blocks, blocks)] for i in range(2)]
    parts = [pl.ds(pl.multiple_of(at * rows, rows), rows) for at in (core, 1 - core)]
    for side, at, last, mine in zip(sides, parts, (across, across2), own or (None, None)):
        side[core] = beside[at, :]
        side[1 - core] = beside2[at, :]
        side[2] = last[...]
        if mine is not None:
            side[3] = mine[...]


def merge(spots, arrays, split):
    rows, dim = arrays[1].shape
    blocks = 3 + (len(arrays) - 4) // 2
    outs = [blocks, blocks] if split else [2 * blocks]
    return pl.pallas_call(
        partial(merge_kernel, count=len(arrays)),
        out_shape=[jax.ShapeDtypeStruct((out, rows, dim), BF) for out in outs],
        in_specs=[SMEM] + [VMEM] * len(arrays),
        out_specs=[VMEM] * len(outs),
        compiler_params=limit(8),
    )(spots, *arrays)


def planes_in_order(spots_ref, groups=4):
    return [lax.rem(spots_ref[8] + step, groups) for step in (0, 1, groups - 1, 2)]


def begin(pairs, sems):
    copies = [pltpu.make_async_copy(source, target, sems.at[i]) for i, (source, target) in enumerate(pairs)]
    for one in copies:
        one.start()
    return copies


WEIGHT_SEMS = pltpu.SemaphoreType.DMA((4,))
ANY = pl.BlockSpec(memory_space=pltpu.HBM)


class Gather:
    def __init__(self, dp_size, groups, my_d, my_z, seqs):
        self.dp_size, self.groups, self.my_d, self.my_z = dp_size, groups, my_d, my_z
        self.paired = dp_size == 8 and groups == 4 and seqs == 2
        core = lax.rem(my_d, 2)
        even = [0, 1, 2, 3, 7, 5, 4, 6]
        odd = [0, 1, 4, 5, 7, 3, 2, 6]
        flips = jnp.where(core == 0, jnp.array(even, jnp.int32), jnp.array(odd, jnp.int32))
        self.spots = jnp.concatenate([jnp.bitwise_xor(my_d, flips), my_z[None]]).astype(jnp.int32)

    def all_parts(self, part):
        whole = lax.all_gather(part, ("dp", "tensor"), axis=0)
        return whole.reshape((self.dp_size, self.groups) + part.shape).transpose(1, 0, 2, 3)

    def part_of(self, shard):
        rows = shard.shape[0] // self.dp_size
        return lax.dynamic_slice_in_dim(shard, self.my_d * rows, rows, 0)

    def all_rounds(self, parts, early, steps):
        count = len(parts)
        gathered, spread = [], []
        ahead, done = self.planes(parts[0], 0), [rows for part in parts[1:] for rows in part[:2]] + early
        for r in range(count + 2):
            with jax.named_scope("round%d" % r):
                ready = list(lax.optimization_barrier((*ahead, *done)))
                ahead = ready[: len(ahead)]
                if r >= 1:
                    at = len(ahead)
                    if r <= count:
                        last = spread[r - 1]
                        last[1] = ready[at : at + len(last[1])]
                        at += len(last[1])
                    if 2 <= r <= count:
                        spread[r - 2][2] = ready[at]
                done = []
                if 1 <= r < count:
                    near_half = last[1][0] if len(last[1]) == 2 else last[1][0][: last[1][0].shape[0] // 2]
                    last.append(scoped("far", send, near_half, CROSS_XY))
                if r < count:
                    beside, across = ahead
                    ahead = []
                    if r + 1 < count:
                        ahead = self.planes([tie(rows, beside) for rows in parts[r + 1]], r + 1)
                    others = [scoped("others", send, beside, CORE), scoped("others", send, across, CORE)]
                    both = merge(self.spots, [beside, across, *others, *parts[r][2:]], r == count - 1)
                    near = [scoped("near", send, side, SPLIT_XY) for side in both]
                    spread.append([both, near])
                    done += near
                else:
                    ahead = []
                if 1 <= r <= count:
                    late = last[2:] if r == count else []
                    last.append([scoped("swap", send, array, CORE) for array in last[1][:-1]])
                    last[3].append(scoped("swap", send, tie(last[1][-1], *late), CORE))
                    done += (last[2:3] if r < count else []) + last[3]
                if r >= 2:
                    whole = spread[r - 2]
                    gathered.append([*whole[0], *whole[1], whole[2], *whole[3], scoped("swapfar", send, whole[2], CORE)])
                done += steps[r](gathered)
                if r == count - 1:
                    spread[r].append(scoped("far", send, tie(near[0], *done[len(near) :]), CROSS_XY))
        return gathered

    def planes(self, part, r):
        with jax.named_scope("planes%d" % r):
            groups = self.groups
            pairs = [
                (d * groups + z, d * groups + (z + (1 if d & 1 else groups - 1)) % groups)
                for d in range(self.dp_size)
                for z in range(groups)
            ]
            beside = scoped("beside", lax.ppermute, part[1], ("dp", "tensor"), pairs)
            return beside, scoped("across", shift, part[0], 2, groups)

    def half_of(self, quarter):
        rows = quarter.shape[0] // 2
        return jnp.where(lax.rem(self.my_d, 2) == 0, quarter[:rows], quarter[rows:])

    def quarter_of(self, shard):
        rows = 2 * shard.shape[0] // self.dp_size
        return lax.dynamic_slice_in_dim(shard, self.my_d // 2 * rows, rows, 0)

    def whole(self, part, stacked=False):
        whole = self.all_parts(part)
        dim = part.shape[1]
        if stacked:
            whole = whole.reshape(self.groups, 4, -1, dim).transpose(1, 0, 2, 3)
        return [whole.reshape(4, -1, dim)]


def reduce_grads(gather, grads, own_rows, between, at_last):
    groups, spots = gather.groups, gather.spots
    if not gather.paired:
        mats, bias = grads
        mats = lax.psum_scatter(mats, ("dp", "tensor"), scatter_dimension=1, tiled=True)
        middle = between(None)
        return (mats[0], mats[1], mats[2], lax.psum(bias, ("dp", "tensor"))), at_last(None)
    keep, away = grads
    rows, dim = keep.shape[1:]
    low = jax.ShapeDtypeStruct((rows, dim), BF)
    come = scoped("cores", send, away, CORE)
    to_x, to_y, to_far = pl.pallas_call(
        add_cores_kernel,
        out_shape=[low, low, low],
        in_specs=[SMEM, ANY, ANY],
        out_specs=[ANY] * 3,
        scratch_shapes=[pltpu.VMEM((3, rows, dim), BF)] * 3 + [pltpu.SemaphoreType.DMA((6,)), pltpu.SemaphoreType.DMA((3,))],
        compiler_params=limit(60),
    )(spots, keep, come)
    from_far = scoped("far", send, to_far, FAR_XY)
    from_x = scoped("x", send, to_x, ALONG_X)
    from_y = scoped("y", send, to_y, ALONG_Y)
    block = jax.ShapeDtypeStruct((3 * own_rows + 8, dim), BF)
    middle = between(to_far)
    mine, *goes = pl.pallas_call(
        add_plane_kernel,
        out_shape=[jax.ShapeDtypeStruct((3 * own_rows + 8, dim), F32)] + [block] * (groups - 1),
        in_specs=[SMEM] + [ANY] * 5,
        out_specs=[VMEM] * groups,
        scratch_shapes=[pltpu.VMEM((rows - 16, dim), F32), pltpu.VMEM((5, rows, dim), BF), pltpu.SemaphoreType.DMA((5,))],
        compiler_params=limit(60),
    )(spots, from_x, from_y, from_far, tie(keep, middle), come)
    after = at_last(mine)
    comes = [scoped("stack%d" % i, shift, go, i + 1, groups) for i, go in enumerate(goes)]
    part = jax.ShapeDtypeStruct((own_rows, dim), F32)
    sums = pl.pallas_call(
        add_stack_kernel,
        out_shape=[part, part, part, jax.ShapeDtypeStruct((8, dim), F32)],
        in_specs=[VMEM] * groups,
        out_specs=[VMEM] * 4,
        compiler_params=LITTLE,
    )(mine, *comes)
    return sums, after


def cost(flops, moved, exps=0):
    return pl.CostEstimate(flops=int(flops), bytes_accessed=int(moved), transcendentals=int(exps))


def head_masks():
    lane = lax.broadcasted_iota(jnp.int32, (1, 128), 1)
    first = (lane < 64).astype(F32)
    return [first.astype(BF), (1.0 - first).astype(BF)], lane < 64


def attention_kernel(spots_ref, len_ref, x_ref, norms_ref, *refs):
    *sources, q_hbm, k_hbm, v_hbm, p_hbm, low_ref, xhat_hbm, rstd_ref, w_ref, ctx_ref, q_ref, k_ref, v_ref, p_ref, xhat_ref, sems, store_sems = refs
    fetch_stacked(spots_ref, sources, w_ref, sems, False)
    fetch_stacked(spots_ref, sources, w_ref, sems, True)
    rows, dim = x_ref.shape
    for m in range(4):
        arrive_stacked(w_ref, sems, m)
    seq_len = p_ref.shape[1]
    x = x_ref[...]
    q_ref[...] = (mm_t(x, w_ref[0]).astype(BF).astype(F32) * (1.0 / math.sqrt(dim // HEADS))).astype(BF)
    k_ref[...] = mm_t(x, w_ref[1]).astype(BF)
    v_ref[...] = mm_t(x, w_ref[2]).astype(BF)
    stores = begin(((q_ref, q_hbm), (k_ref, k_hbm), (v_ref, v_hbm)), store_sems)
    masks, first = head_masks()
    key_at = lax.broadcasted_iota(jnp.int32, (seq_len, 1), 0)

    for s in range(rows // seq_len):
        at = slice(s * seq_len, (s + 1) * seq_len)
        valid = key_at < len_ref[s]
        for j in range(HEADS // 2):
            cols = slice(128 * j, 128 * (j + 1))
            q, k, v = q_ref[at, cols], k_ref[at, cols], v_ref[at, cols]
            parts = []
            for h in range(2):
                scores = jnp.where(valid, mm_t(k, q * masks[h]), MASKED)
                exps = jnp.exp(scores - jnp.max(scores, axis=0, keepdims=True))
                probs = (exps * (1.0 / jnp.sum(exps, axis=0, keepdims=True))).astype(BF)
                p_ref[s * HEADS + 2 * j + h] = probs
                parts.append(t_mm(probs, v))
            ctx_ref[at, cols] = jnp.where(first, parts[0], parts[1]).astype(BF)
        heads = pl.ds(s * HEADS, HEADS)
        stores += begin(((p_ref.at[heads], p_hbm.at[heads]),), store_sems.at[pl.ds(3 + s, 1)])
    xhat, rstd = norm_parts(x.astype(F32) + mm(ctx_ref[...], w_ref[3]))
    xhat_ref[...] = xhat
    stores += begin(((xhat_ref, xhat_hbm),), store_sems.at[pl.ds(3 + rows // seq_len, 1)])
    rstd_ref[...] = rstd
    low_ref[...] = (xhat * norms_ref[0:1, :] + norms_ref[1:2, :]).astype(BF)
    for store in stores:
        store.wait()


def attention_forward(spots, lengths, x, sources, norms, seq_len):
    rows, dim = x.shape
    seqs = rows // seq_len
    low = jax.ShapeDtypeStruct((rows, dim), BF)
    return pl.pallas_call(
        attention_kernel,
        out_shape=[low, low, low,
                   jax.ShapeDtypeStruct((seqs * HEADS, seq_len, seq_len), BF), low,
                   jax.ShapeDtypeStruct((rows, dim), F32), jax.ShapeDtypeStruct((rows, 1), F32)],
        in_specs=[SMEM] * 2 + [VMEM] * 2 + [ANY] * len(sources),
        out_specs=[ANY] * 4 + [VMEM, ANY, VMEM],
        scratch_shapes=[pltpu.VMEM((4, dim, dim), BF)] + [pltpu.VMEM((rows, dim), BF)] * 4 + [
            pltpu.VMEM((seqs * HEADS, seq_len, seq_len), BF), pltpu.VMEM((rows, dim), F32),
            WEIGHT_SEMS, pltpu.SemaphoreType.DMA((4 + seqs,)),
        ],
        compiler_params=limit(60),
        cost_estimate=cost(2 * rows * dim * (4 * dim + 2 * seq_len), 2 * (4 * dim * dim + 8 * rows * dim), rows * seq_len * HEADS),
    )(spots, lengths, x, norms, *sources)


def by_rows(rows, step, work, unroll=1):
    work(slice(0, rows))


def ffn_in_kernel(spots_ref, x_ref, bias_ref, *refs):
    *sources, act_hbm, slope_hbm, act_ref, slope_ref, w_ref, pre_ref, sems, store_sems = refs
    units = pre_ref.shape[1]
    order = planes_in_order(spots_ref)
    stores = []
    fetch(spots_ref, sources, w_ref, sems, [0, 1])
    for r in range(4):
        fetch(spots_ref, sources, w_ref, sems, [r + 2] if r < 2 else [])
        arrive(w_ref, sems, r)
        pre_ref[...] = mm(x_ref[...], w_ref[r * x_ref.shape[1] : (r + 1) * x_ref.shape[1], :])
        cols = slice(r * units, (r + 1) * units)
        act, slope = gelu_parts(pre_ref[...] + bias_ref[order[r]])
        act_ref[:, cols] = act.astype(BF)
        slope_ref[:, cols] = slope.astype(BF)
        pairs = [(act_ref, act_hbm), (slope_ref, slope_hbm)]
        stores += begin([(ref.at[:, cols], hbm.at[:, cols]) for ref, hbm in pairs], store_sems.at[pl.ds(2 * r, 2)])
    for store in stores:
        store.wait()


def ffn_forward(spots, x, sources, bias, units):
    rows, dim = x.shape
    planes = bias.shape[0] // units
    out = jax.ShapeDtypeStruct((rows, planes * units), BF)
    return pl.pallas_call(
        ffn_in_kernel,
        out_shape=[out, out],
        in_specs=[SMEM] + [VMEM] * 2 + [ANY] * len(sources),
        out_specs=[ANY] * 2,
        scratch_shapes=[
            pltpu.VMEM((rows, planes * units), BF), pltpu.VMEM((rows, planes * units), BF),
            pltpu.VMEM((planes * dim, units), BF), pltpu.VMEM((rows, units), F32), WEIGHT_SEMS, pltpu.SemaphoreType.DMA((8,)),
        ],
        compiler_params=limit(60),
        cost_estimate=cost(2 * rows * dim * units * planes, 2 * planes * units * (dim + 2 * rows), 2 * rows * units * planes),
    )(spots, x, bias.reshape(planes, 1, units), *sources)


def two_pass(values, table):
    high = values.astype(BF)
    return mm(high, table) + mm((values - high.astype(F32)).astype(BF), table)


def put_rows(ref, mats, bias):
    at = 0
    for mat in mats:
        ref[at : at + mat.shape[0], :] = mat.astype(BF)
        at += mat.shape[0]
    high = bias.astype(BF).astype(F32)
    ref[at : at + 16, :] = jnp.concatenate([high, bias - high], axis=0).astype(BF)


def sum_rows(arrays):
    total = arrays[0].astype(F32)
    for array in arrays[1:]:
        total = total + array.astype(F32)
    rows = total.shape[0] - 16
    return total[:rows], total[rows : rows + 8] + total[rows + 8 :]


def add_cores_kernel(spots_ref, keep_hbm, come_hbm, *refs):
    hbm, (sums_ref, keep_ref, come_ref, sems, store_sems) = refs[:3], refs[3:]
    quarter = lax.div(spots_ref[0], 2)
    pairs = []
    for i in range(3):
        q = jnp.bitwise_xor(quarter, i + 1)
        pairs += [(keep_hbm.at[q], keep_ref.at[i]), (come_hbm.at[q], come_ref.at[i])]
    copies = begin(pairs, sems)
    stores = []
    for i in range(3):
        copies[2 * i].wait()
        copies[2 * i + 1].wait()
        mats, bias = sum_rows([keep_ref[i], come_ref[i]])
        put_rows(sums_ref.at[i], [mats], bias)
        stores += begin(((sums_ref.at[i], hbm[i]),), store_sems.at[pl.ds(i, 1)])
    for store in stores:
        store.wait()


def fold_bias(bias):
    high = bias.astype(BF).astype(F32)
    row = lax.broadcasted_iota(jnp.int32, (8, 1), 0)
    return jnp.where(row < 4, high, pltpu.roll(bias - high, 4, 0))


def add_plane_kernel(spots_ref, *refs):
    parts, refs = refs[:3], refs[3:]
    keep_hbm, come_hbm, mine_ref, *go_refs, total_ref, arrays_ref, sems = refs
    quarter = lax.div(spots_ref[0], 2)
    sources = (keep_hbm.at[quarter], come_hbm.at[quarter], *parts)
    for copy in begin([(source, arrays_ref.at[i]) for i, source in enumerate(sources)], sems):
        copy.wait()
    total_ref[...], bias = sum_rows([arrays_ref[i] for i in range(5)])
    groups = len(go_refs) + 1
    width = total_ref.shape[0] // 3
    rows = width // groups

    def block(plane):
        at = [pl.multiple_of(i * width + plane * rows, 8) for i in range(3)]
        return jnp.concatenate([total_ref[pl.ds(a, rows), :] for a in at], axis=0)

    my_z = spots_ref[8]
    mine_ref[...] = jnp.concatenate([block(my_z), bias], axis=0)
    folded = fold_bias(bias)
    for i, ref in enumerate(go_refs):
        ref[...] = jnp.concatenate([block(lax.rem(my_z + i + 1, groups)), folded], axis=0).astype(BF)


def add_stack_kernel(mine_ref, *refs):
    come_refs, (q_ref, k_ref, v_ref, bias_ref) = refs[:-4], refs[-4:]
    total = mine_ref[...]
    rows = q_ref.shape[0]
    for ref in come_refs:
        come = ref[...].astype(F32)
        bias = come[3 * rows :]
        total = total + jnp.concatenate([come[: 3 * rows], bias + pltpu.roll(bias, 4, 0)], axis=0)
    q_ref[...], k_ref[...], v_ref[...] = (total[i * rows : (i + 1) * rows] for i in range(3))
    bias_ref[...] = total[3 * rows :]


def joining_kernel(
    spots_ref, member_ref, member_t_ref, avail_ref, norms_ref, act_hbm, xhat1_hbm, cot_hbm, *refs, halves, count
):
    gain1, bias1, gain2, bias2 = (norms_ref[i : i + 1, :] for i in range(4))
    down_hbm, up_hbm, *refs = refs
    join_sources, sources, refs = refs[:count], refs[count:-38], refs[-38:]
    stage_ref, biases_ref, stage_sem, refs = refs[-3], refs[-2], refs[-1], refs[:-3]
    out_hbm, g2_hbm, g_ffn_ref, grad_hbm0, grad_hbm1 = refs[:5]
    act_ref, w_out_ref, down_ref, up_ref, join_ref, xhat1_ref, cot_ref, act_sems, out_sems, sems, store_sems = refs[5:16]
    ffn_ref, u_ref, w_ref, big_u_ref, big_w_ref, p_wide_ref, sums_ref = refs[16:23]
    x_ref, act2_ref, slope_ref, q_ref, gq_ref, low_ref, mixed_ref, t_ref = refs[23:31]
    out_ref, g2_ref, bias_rows_ref, bias_ref = refs[31:35]
    rows, dim = out_ref.shape
    units = w_out_ref.shape[0] // 4
    seqs = avail_ref.shape[0]
    per = rows // seqs
    everyone = [slice(i * per, (i + 1) * per) for i in range(seqs)]
    fscale = 1.0 / math.sqrt(dim)
    member, member_t = member_ref[...], member_t_ref[...]
    loads = []

    def issue(r):
        if r < 4:
            fetch(spots_ref, sources, w_out_ref, out_sems, [r])
            cols = pl.ds(r * units, units)
            loads.extend(begin(((act_hbm.at[:, cols], act_ref.at[:, cols]),), act_sems.at[pl.ds(r, 1)]))
        elif r == 4:
            fetch_blocks(spots_ref, join_sources, stage_ref, stage_sem)
        elif r == 5:
            pairs = ((down_hbm, down_ref), (up_hbm, up_ref), (xhat1_hbm, xhat1_ref), (cot_hbm, cot_ref))
            loads.extend(begin(pairs, sems))

    issue(0)
    issue(1)
    for r in range(4):
        issue(r + 2)
        loads[r].wait()
        arrive(w_out_ref, out_sems, r)
        if r % 2 == 1:
            both = slice((r - 1) * units, (r + 1) * units)
            for at in everyone:
                term = mm(act_ref[at, both], w_out_ref[both, :])
                ffn_ref[at, :] = term if r == 1 else ffn_ref[at, :] + term
    loads = loads[4:]
    for at in everyone:
        x_ref[at, :] = ffn_ref[at, :].astype(BF)
    pltpu.make_async_copy(stage_ref, stage_ref, stage_sem).wait()
    order_rows(stage_ref, join_ref, biases_ref)
    qb, vb = biases_ref[0:1, :], biases_ref[1:2, :]
    for load in loads:
        load.wait()
    up = up_ref[...]
    halves_of = {}

    def narrow(i, name, value=None):
        if value is not None:
            halves_of[i, name] = value
        return halves_of[i, name]

    def per_adapter(values):
        high = values.astype(BF)
        return mm(high, member) + mm((values - high.astype(F32)).astype(BF), member)

    def to_q(i, at):
        q_ref[at, :] = (mm(x_ref[at, :], join_ref[0]) + qb).astype(BF)

    def down(i, at):
        act, slope = gelu_parts(mm(x_ref[at, :], down_ref[...]))
        act2_ref[at, :] = act.astype(BF)
        slope_ref[at, :] = slope.astype(BF)

    def to_u(i, at):
        u = mm_t(q_ref[at, :], join_ref[1])
        u_ref[at, :] = u
        narrow(i, "dot", jnp.sum(ffn_ref[at, :] * u, axis=-1, keepdims=True))

    def scores(i, at):
        big_u = mm_t(u_ref[at, :].astype(BF), up)
        big_u_ref[at, :] = big_u
        fscores = (per_adapter(act2_ref[at, :].astype(F32) * big_u) + narrow(i, "dot")) * fscale
        fscores = jnp.where(avail_ref[i] > 0, fscores, MASKED)
        fexp = jnp.exp(fscores - jnp.max(fscores, axis=-1, keepdims=True))
        narrow(i, "probs", fexp / jnp.sum(fexp, axis=-1, keepdims=True))

    def mix(i, at):
        p_wide = two_pass(narrow(i, "probs"), member_t)
        p_wide_ref[at, :] = p_wide
        weighed = (p_wide * act2_ref[at, :].astype(F32)).astype(BF)
        mixed_ref[at, :] = (ffn_ref[at, :] + mm(weighed, up)).astype(BF)

    def norm(i, at):
        normed1 = xhat1_ref[at, :] * gain1 + bias1
        xhat2, rstd2 = norm_parts(normed1 + mm(mixed_ref[at, :], join_ref[2]) + vb)
        out_ref[at, :] = (xhat2 * gain2 + bias2).astype(BF)
        g2 = norm_back(cot_ref[at, :].astype(F32), gain2, xhat2, rstd2)
        g2_ref[at, :] = g2
        low_ref[at, :] = g2.astype(BF)
        narrow(i, "dot2", jnp.sum(g2 * vb, axis=-1, keepdims=True))
        narrow(i, "d_vb", jnp.sum(g2.reshape(-1, 8, dim), axis=0))

    def to_w(i, at):
        w = mm_t(low_ref[at, :], join_ref[2])
        w_ref[at, :] = w
        narrow(i, "dot2", narrow(i, "dot2") + jnp.sum(ffn_ref[at, :] * w, axis=-1, keepdims=True))

    def score_grads(i, at):
        big_w = mm_t(w_ref[at, :].astype(BF), up)
        big_w_ref[at, :] = big_w
        gvals = per_adapter(act2_ref[at, :].astype(F32) * big_w) + narrow(i, "dot2")
        fprobs = narrow(i, "probs")
        gs = fprobs * (gvals - jnp.sum(gvals * fprobs, axis=-1, keepdims=True)) * fscale
        narrow(i, "gs", gs)
        narrow(i, "gs_sum", jnp.sum(gs, axis=-1, keepdims=True))

    def to_t(i, at):
        wide = two_pass(narrow(i, "gs"), member_t)
        weighed = (wide * act2_ref[at, :].astype(F32)).astype(BF)
        grad = wide * big_u_ref[at, :] + p_wide_ref[at, :] * big_w_ref[at, :]
        slope_ref[at, :] = (grad * slope_ref[at, :].astype(F32)).astype(BF)
        t_ref[at, :] = (mm(weighed, up) + narrow(i, "gs_sum") * ffn_ref[at, :]).astype(BF)

    def to_gq(i, at):
        gq = mm(t_ref[at, :], join_ref[1]).astype(BF)
        gq_ref[at, :] = gq
        narrow(i, "d_qb", jnp.sum(gq.astype(F32).reshape(-1, 8, dim), axis=0))

    def all_halves(*steps):
        for step in steps:
            for i, at in enumerate(everyone):
                step(i, at)

    all_halves(to_q, down, to_u, scores, mix, norm)
    stores = begin(((out_ref, out_hbm), (g2_ref, g2_hbm)), store_sems)
    all_halves(to_w, score_grads)
    sums_ref[2] = t_mm(mixed_ref[...], low_ref[...]).astype(sums_ref.dtype)
    all_halves(to_t)
    sums_ref[1] = t_mm(t_ref[...], q_ref[...]).astype(sums_ref.dtype)
    all_halves(to_gq)
    sums_ref[0] = t_mm(x_ref[...], gq_ref[...]).astype(sums_ref.dtype)
    row = lax.broadcasted_iota(jnp.int32, (8, 1), 0)
    d_qb, d_vb = (
        jnp.sum(sum(narrow(i, name) for i in range(seqs)), axis=0, keepdims=True) for name in ("d_qb", "d_vb")
    )
    bias_ref[...] = jnp.where(row == 0, d_qb, jnp.where(row == 1, d_vb, 0.0))
    if halves:
        core = lax.rem(spots_ref[0], 2)
        part = dim // 8
        put_rows(bias_rows_ref, [], bias_ref[...])
        for hbm, side, sem in ((grad_hbm1, 1 - core, store_sems.at[2]), (grad_hbm0, core, store_sems.at[3])):
            for q in range(4):
                at = pl.ds(pl.multiple_of((2 * q + side) * part, part), part)
                for i in range(3):
                    pltpu.make_async_copy(sums_ref.at[i, at], hbm.at[q, pl.ds(i * part, part)], sem).start()
                pltpu.make_async_copy(bias_rows_ref, hbm.at[q, pl.ds(3 * part, 16)], sem).start()
            stores.append(pltpu.make_async_copy(hbm, hbm, sem))
    else:
        stores += begin(((sums_ref, grad_hbm0), (bias_ref, grad_hbm1)), store_sems.at[pl.ds(2, 2)])
    for i, at in enumerate(everyone):
        total = mm_t(slope_ref[at, :], down_ref[...]) + mm_t(gq_ref[at, :], join_ref[0])
        g_ffn_ref[at, :] = (narrow(i, "gs_sum") * u_ref[at, :] + w_ref[at, :] + total).astype(BF)
    for store in stores:
        store.wait()


def joining(spots, halves, act, sources, adapt_down, up, join_sources, member, member_t, avail, xhat1, norms, cot):
    rows, dim = xhat1.shape
    if halves:
        grads = [jax.ShapeDtypeStruct((4, 3 * dim // 8 + 16, dim), BF)] * 2
    else:
        grads = [jax.ShapeDtypeStruct((3, dim, dim), F32), jax.ShapeDtypeStruct((8, dim), F32)]
    wide, low = pltpu.VMEM((rows, dim), F32), pltpu.VMEM((rows, dim), BF)
    height, blocks = join_sources[-1].shape[-2:][0], 32
    stage_shape = join_sources[0].shape if len(join_sources) == 1 else (blocks, height, dim)
    return pl.pallas_call(
        partial(joining_kernel, halves=halves, count=len(join_sources)),
        out_shape=[
            jax.ShapeDtypeStruct((rows, dim), BF),
            jax.ShapeDtypeStruct((rows, dim), F32),
            jax.ShapeDtypeStruct((rows, dim), BF),
        ] + grads,
        in_specs=[SMEM] + [VMEM] * 4 + [ANY] * (len(sources) + len(join_sources) + 5),
        out_specs=[ANY, ANY, VMEM, ANY, ANY],
        scratch_shapes=[
            pltpu.VMEM(act.shape, BF),
            pltpu.VMEM((act.shape[1], dim), BF),
            pltpu.VMEM(adapt_down.shape, BF),
            pltpu.VMEM(up.shape, BF),
            pltpu.VMEM((3, dim, dim), BF),
            wide,
            low,
            WEIGHT_SEMS,
            WEIGHT_SEMS,
            pltpu.SemaphoreType.DMA((4,)),
            pltpu.SemaphoreType.DMA((4,)),
        ] + [wide] * 6 + [pltpu.VMEM((3, dim, dim), BF if halves else F32)] + [low] * 8 + [
            low,
            wide,
            pltpu.VMEM((16, dim), BF),
            pltpu.VMEM((8, dim), F32),
            pltpu.VMEM(stage_shape, BF),
            pltpu.VMEM((8, dim), F32),
            pltpu.SemaphoreType.DMA,
        ],
        compiler_params=limit(60),
        cost_estimate=cost(2 * rows * dim * (15 * dim + act.shape[1]), 2 * dim * (8 * dim + 10 * rows), 2 * rows * dim),
    )(spots, member, member_t, avail, norms, act, xhat1, cot, adapt_down, up, *join_sources, *sources)


def ffn_back_kernel(spots_ref, g_ref, rstd_ref, norms_ref, slope_hbm, g2_hbm, xhat_hbm, *refs, count):
    refs, (out_sources, in_sources) = refs[sum(count) :], (refs[: count[0]], refs[count[0] : sum(count)])
    g1_hbm, low_hbm, g1_ref, low_ref, slope_ref, g2_ref, xhat_ref, w_out_ref, w_in_ref, pre_ref, out_sems, in_sems, slope_sems, sems, store_sems = refs
    units = w_out_ref.shape[0] // 4
    rows = g_ref.shape[0]
    everyone = [slice(i * rows // 2, (i + 1) * rows // 2) for i in range(2)]
    loads = []

    def issue(r):
        if r < 4:
            fetch(spots_ref, out_sources, w_out_ref, out_sems, [r])
            cols = pl.ds(r * units, units)
            loads.extend(begin(((slope_hbm.at[:, cols], slope_ref.at[:, cols]),), slope_sems.at[pl.ds(r, 1)]))
        elif r < 8:
            fetch(spots_ref, in_sources, w_in_ref, in_sems, [r - 4], side_by_side=True)
        elif r == 8:
            loads.extend(begin(((g2_hbm, g2_ref), (xhat_hbm, xhat_ref)), sems))

    issue(0)
    issue(1)
    for r in range(4):
        issue(r + 2)
        cols = slice(r * units, (r + 1) * units)
        arrive(w_out_ref, out_sems, r)
        loads[r].wait()
        for at in everyone:
            pre_ref[at, cols] = (mm_t(g_ref[at, :], w_out_ref[cols, :]) * slope_ref[at, cols].astype(F32)).astype(BF)
    for r in range(4, 8):
        issue(r + 2)
        arrive(w_in_ref, in_sems, r - 4, side_by_side=True)
        if r == 5:
            both = slice(0, 2 * units)
            for at in everyone:
                g1_ref[at, :] = mm_t(pre_ref[at, both], w_in_ref[:, both])
    for load in loads[4:]:
        load.wait()
    both = slice(2 * units, 4 * units)
    stores = []
    for at in everyone:
        total = mm_t(pre_ref[at, both], w_in_ref[:, both]) + g1_ref[at, :] + g2_ref[at, :]
        g1 = norm_back(total, norms_ref[0:1, :], xhat_ref[at, :], rstd_ref[at, :])
        g1_ref[at, :] = g1
        low_ref[at, :] = g1.astype(BF)
        stores += begin(((g1_ref.at[at], g1_hbm.at[at]), (low_ref.at[at], low_hbm.at[at])), store_sems.at[pl.ds(len(stores), 2)])
    for store in stores:
        store.wait()


def ffn_backward(spots, g_ffn, slope, out_sources, in_sources, g2, xhat, rstd, norms):
    rows, dim = xhat.shape
    planes = 4
    units = slope.shape[1] // planes
    return pl.pallas_call(
        partial(ffn_back_kernel, count=(len(out_sources), len(in_sources))),
        out_shape=[jax.ShapeDtypeStruct((rows, dim), F32), jax.ShapeDtypeStruct((rows, dim), BF)],
        in_specs=[SMEM] + [VMEM] * 3 + [ANY] * (len(out_sources) + len(in_sources) + 3),
        out_specs=[ANY, ANY],
        scratch_shapes=[
            pltpu.VMEM((rows, dim), F32), pltpu.VMEM((rows, dim), BF),
            pltpu.VMEM(slope.shape, BF), pltpu.VMEM((rows, dim), F32), pltpu.VMEM((rows, dim), F32),
            pltpu.VMEM((planes * units, dim), BF), pltpu.VMEM((dim, planes * units), BF), pltpu.VMEM(slope.shape, BF),
            WEIGHT_SEMS, WEIGHT_SEMS, WEIGHT_SEMS, pltpu.SemaphoreType.DMA((2,)),
            pltpu.SemaphoreType.DMA((4,)),
        ],
        compiler_params=limit(60),
        cost_estimate=cost(4 * rows * dim * units * planes, 2 * planes * units * (2 * dim + rows)),
    )(spots, g_ffn, rstd, norms, slope, g2, xhat, *out_sources, *in_sources)


def attention_back_heads(s, seq_len, q_ref, k_ref, v_ref, p_ref, g_ref, dq_ref, dk_ref, dv_ref, first_seq):
    dim = q_ref.shape[1]
    scale = 1.0 / math.sqrt(dim // HEADS)
    masks, first = head_masks()
    at = slice((s - first_seq) * seq_len, (s - first_seq + 1) * seq_len)
    for j in range(HEADS // 2):
        cols = slice(128 * j, 128 * (j + 1))
        q, k, v, g = q_ref[at, cols], k_ref[at, cols], v_ref[at, cols], g_ref[at, cols]
        dq, dk, dv = [], [], []
        for h in range(2):
            probs_low = p_ref[(s - first_seq) * HEADS + 2 * j + h]
            probs = probs_low.astype(F32)
            g_probs = mm_t(v, g * masks[h])
            g_scores = (probs * (g_probs - jnp.sum(g_probs * probs, axis=0, keepdims=True))).astype(BF)
            dv.append(mm(probs_low, g))
            dk.append(mm(g_scores, q))
            dq.append(t_mm(g_scores, k))
        dq_ref[at, cols] = (jnp.where(first, dq[0], dq[1]) * scale).astype(BF)
        dk_ref[at, cols] = jnp.where(first, dk[0], dk[1]).astype(BF)
        dv_ref[at, cols] = jnp.where(first, dv[0], dv[1]).astype(BF)


def load_heads(hbm, vmem, sems, first, count):
    seq_len = hbm[3].shape[1]
    rows, heads = pl.ds(first * seq_len, count * seq_len), pl.ds(first * HEADS, count * HEADS)
    pairs = [(hbm[i].at[rows], vmem[i]) for i in range(3)] + [(hbm[3].at[heads], vmem[3])]
    return begin(pairs, sems)


def attention_back_first_kernel(spots_ref, *refs):
    *refs, ctx_hbm, dq_ref, dk_ref, dv_ref, w_ref, g1_ref, ctx_ref, q_ref, k_ref, v_ref, p_ref, w_sems, sems, g_sems = refs
    g1_hbm, *sources, q_hbm, k_hbm, v_hbm, p_hbm = refs
    seq_len = p_ref.shape[1]
    rows, dim = g1_ref.shape
    loads = begin(((g1_hbm, g1_ref),), g_sems.at[pl.ds(0, 1)])
    fetch_stacked(spots_ref, sources, w_ref, w_sems, True)
    seqs = q_ref.shape[0] // seq_len
    loads += load_heads((q_hbm, k_hbm, v_hbm, p_hbm), (q_ref, k_ref, v_ref, p_ref), sems, 0, seqs)
    loads[0].wait()
    arrive_stacked(w_ref, w_sems, 3)
    ctx_ref[...] = mm_t(g1_ref[...], w_ref[3]).astype(BF)
    later = pl.ds(seqs * seq_len, rows - seqs * seq_len)
    store = begin(((ctx_ref.at[later], ctx_hbm),), g_sems.at[pl.ds(1, 1)])[0]
    for load in loads[1:]:
        load.wait()
    for s in range(seqs):
        attention_back_heads(s, seq_len, q_ref, k_ref, v_ref, p_ref, ctx_ref, dq_ref, dk_ref, dv_ref, 0)
    store.wait()


def attention_back_last_kernel(spots_ref, *refs):
    *refs, out_ref, g1_ref, ctx_ref, dq0_ref, dk0_ref, dv0_ref, w_ref, q_ref, k_ref, v_ref, p_ref, dq_ref, dk_ref, dv_ref, w_sems, sems, late_sems = refs
    g1_hbm, ctx_hbm, dq0_hbm, dk0_hbm, dv0_hbm, *sources, q_hbm, k_hbm, v_hbm, p_hbm = refs
    rows, dim = g1_ref.shape
    seq_len = p_ref.shape[1]
    first = dq0_ref.shape[0] // seq_len
    seqs = q_ref.shape[0] // seq_len
    loads = begin(((ctx_hbm, ctx_ref),), late_sems.at[pl.ds(0, 1)])
    loads += load_heads((q_hbm, k_hbm, v_hbm, p_hbm), (q_ref, k_ref, v_ref, p_ref), sems, first, seqs)
    for load in loads:
        load.wait()
    fetch_stacked(spots_ref, sources, w_ref, w_sems, False)
    pairs = ((dq0_hbm, dq0_ref), (dk0_hbm, dk0_ref), (dv0_hbm, dv0_ref), (g1_hbm, g1_ref))
    loads = begin(pairs, late_sems.at[pl.ds(1, 4)])
    for s in range(seqs):
        attention_back_heads(s, seq_len, q_ref, k_ref, v_ref, p_ref, ctx_ref, dq_ref, dk_ref, dv_ref, 0)
    for load in loads:
        load.wait()
    for m in range(3):
        arrive_stacked(w_ref, w_sems, m)
    for at, grads in ((slice(0, first * seq_len), (dq0_ref, dk0_ref, dv0_ref)), (slice(first * seq_len, rows), (dq_ref, dk_ref, dv_ref))):
        total = g1_ref[at, :]
        for m, grad in enumerate(grads):
            total = total + mm(grad[...], w_ref[m])
        out_ref[at, :] = total.astype(BF)


def attention_backward_first(spots, g1_low, sources, q, k, v, probs):
    rows, dim = g1_low.shape
    heads, seq_len = probs.shape[0] // 2, probs.shape[1]
    half, low = jax.ShapeDtypeStruct((rows // 2, dim), BF), pltpu.VMEM((rows // 2, dim), BF)
    return pl.pallas_call(
        attention_back_first_kernel,
        out_shape=[half, half, half, half],
        in_specs=[SMEM, ANY] + [ANY] * (len(sources) + 4),
        out_specs=[ANY] + [VMEM] * 3,
        scratch_shapes=[pltpu.VMEM((4, dim, dim), BF), pltpu.VMEM((rows, dim), BF), pltpu.VMEM((rows, dim), BF), low, low, low, pltpu.VMEM((heads,) + probs.shape[1:], BF),
                        WEIGHT_SEMS, pltpu.SemaphoreType.DMA((4,)), pltpu.SemaphoreType.DMA((2,))],
        compiler_params=limit(60),
        cost_estimate=cost(2 * rows * dim * (dim + 2 * seq_len), 2 * (dim * dim + 5 * rows * dim)),
    )(spots, g1_low, *sources, q, k, v, probs)


def attention_backward_last(spots, g1, halfway, sources, q, k, v, probs):
    rows, dim = g1.shape
    heads, seq_len = probs.shape[0] // 2, probs.shape[1]
    low = pltpu.VMEM((rows // 2, dim), BF)
    return pl.pallas_call(
        attention_back_last_kernel,
        out_shape=jax.ShapeDtypeStruct((rows, dim), BF),
        in_specs=[SMEM] + [ANY] * (len(sources) + 9),
        out_specs=VMEM,
        scratch_shapes=[pltpu.VMEM((rows, dim), F32), low, low, low, low, pltpu.VMEM((4, dim, dim), BF), low, low, low, pltpu.VMEM((heads,) + probs.shape[1:], BF), low, low, low,
                        WEIGHT_SEMS, pltpu.SemaphoreType.DMA((4,)), pltpu.SemaphoreType.DMA((5,))],
        compiler_params=limit(60),
        cost_estimate=cost(2 * rows * dim * (3 * dim + 2 * seq_len), 2 * (3 * dim * dim + 5 * rows * dim)),
    )(spots, g1, *halfway, *sources, q, k, v, probs)


def shards(
    tokens, lengths, adapter_mask, cotangent, att_query, att_key, att_value, att_out,
    norm1_gain, norm1_bias, ffn_in, ffn_bias, ffn_out, adapt_down, adapt_up, norm2_gain,
    norm2_bias, joining_query, joining_key, joining_value, joining_qbias, joining_vbias,
):
    groups = lax.axis_size("tensor")
    dp_size = lax.axis_size("dp")
    my_z = lax.axis_index("tensor")
    my_d = lax.axis_index("dp")
    seq_local, seq_len, dim = tokens.shape
    mine = seq_local // groups
    rows = mine * seq_len
    adapters, neck = adapt_up.shape[0], adapt_up.shape[1]
    own_rows = joining_query.shape[0]

    gather = Gather(dp_size, groups, my_d, my_z, mine)
    spots = gather.spots
    biases = lax.dynamic_update_slice(
        jnp.zeros((8, dim), BF), jnp.stack([joining_qbias, joining_vbias]), (0, (my_d * groups + my_z) * own_rows)
    )
    att_mats = [att_query.T, att_key.T, att_value.T, att_out]
    join_part = jnp.concatenate([joining_query, joining_key, joining_value, biases], axis=0)

    def my_slice(array):
        return lax.dynamic_slice_in_dim(array, my_z * mine, mine, 0)

    x = my_slice(tokens).reshape(rows, dim)
    shifts = jnp.arange(128, dtype=jnp.int32)
    bits = jnp.right_shift(my_slice(adapter_mask)[:, None], jnp.minimum(shifts, adapters)[None, :]) % 2
    avail = jnp.where(shifts[None, :] < adapters, bits, 0)[:, None, :]
    norms = jnp.stack([norm1_gain, norm1_bias, norm2_gain, norm2_bias])
    lens = my_slice(lengths)
    owner = jnp.arange(adapters * neck, dtype=jnp.int32) // neck
    member = (owner[:, None] == shifts[None, :]).astype(BF)
    member_t = (shifts[:, None] == owner[None, :]).astype(BF)
    kept = {}

    def attend(sources):
        kept["att"] = attention_forward(spots, lens, x, sources, norms, seq_len)
        return [kept["att"][4]]

    def feed(sources):
        kept["ffn"] = ffn_forward(spots, kept["att"][4], sources, ffn_bias, ffn_in.shape[1])
        return [kept["ffn"][0]]

    if gather.paired:
        own = [att_mats, [ffn_in], None, [ffn_out]]
        steps = [
            lambda got: [],
            lambda got: [],
            lambda got: attend(got[0] + own[0]),
            lambda got: feed(got[1] + own[1]),
            lambda got: [],
            lambda got: [],
        ]
        quarter = att_mats[3]
        for i in range(3):
            quarter = jnp.where(my_d // 2 == i, att_mats[i], quarter)
        half = gather.half_of(quarter)
        rounds = [(half, tie(quarter, half))]
        shards_in, shards_out = tie(ffn_in, half), tie(ffn_out, half)
        in_quarter, in_half, out_quarter, out_half = cut(spots, [shards_in, shards_out])
        rounds += [(in_half, in_quarter), (out_half, out_quarter)]
        join_part = tie(join_part, *rounds[0])
        theirs = send(join_part, CORE)
        even = lax.rem(my_d, 2) == 0
        pair = jnp.concatenate([jnp.where(even, join_part, theirs), jnp.where(even, theirs, join_part)], axis=0)
        rounds.insert(2, (join_part, pair, join_part, theirs))
        got = gather.all_rounds(rounds, [x, norms, lens, avail, member, member_t, spots], steps)
        att_sources, in_sources, out_sources = (got[i] + own[i] for i in (0, 1, 3))
        join_sources = got[2]
    else:
        att_pack = jnp.concatenate(att_mats, axis=0)
        att_sources = gather.whole(gather.part_of(att_pack), True)
        in_sources, out_sources = (gather.whole(gather.part_of(shard)) for shard in (ffn_in, ffn_out))
        join_sources = [lax.all_gather(join_part, ("dp", "tensor"), axis=0)]
    up = adapt_up.reshape(adapters * neck, dim)
    cot = cotangent.reshape(rows, dim)

    def rest(att, ffn, avail, cot):
        q, k, v, probs, low1, xhat1, rstd1 = att
        act, slope = ffn
        layer_out, g2, g_ffn, *grads = joining(
            spots, gather.paired, act, out_sources, adapt_down, up, join_sources, member, member_t, avail, xhat1, norms, cot
        )
        done = {}

        def between(start):
            gradient = g_ffn if start is None else tie(g_ffn, start)
            done["g1"], g1_low = ffn_backward(spots, gradient, slope, out_sources, in_sources, g2, xhat1, rstd1, norms)
            done["half"] = attention_backward_first(spots, g1_low, att_sources, q, k, v, probs)
            return done["half"][1]

        def at_last(start):
            halfway = done["half"] if start is None else [tie(done["half"][0], start)] + list(done["half"][1:])
            return attention_backward_last(spots, done["g1"], halfway, att_sources, q, k, v, probs)

        return layer_out, grads, between, at_last

    if gather.paired:
        layer_out, grads, between, at_last = rest(kept["att"], kept["ffn"], avail, cot)
        (d_q, d_k, d_v, d_bias), input_grad = reduce_grads(gather, grads, own_rows, between, at_last)
    else:
        outs = []
        for first in range(0, mine, 2):
            at = slice(first * seq_len, (first + 2) * seq_len)
            att = attention_forward(spots, lens[first : first + 2], x[at], att_sources, norms, seq_len)
            ffn = ffn_forward(spots, att[4], in_sources, ffn_bias, ffn_in.shape[1])
            outs.append(rest(att, ffn, avail[first : first + 2], cot[at]))
        layer_out = jnp.concatenate([out[0] for out in outs])
        grads = [sum(out[1][i] for out in outs) for i in range(2)]
        (d_q, d_k, d_v, d_bias), input_grad = reduce_grads(
            gather, grads, own_rows, lambda start: [out[2](None) for out in outs],
            lambda start: jnp.concatenate([out[3](None) for out in outs]),
        )
    d_bias = lax.dynamic_slice_in_dim(d_bias[:2], (my_d * groups + my_z) * own_rows, own_rows, 1)
    return (
        layer_out.reshape(mine, seq_len, dim),
        input_grad.reshape(mine, seq_len, dim),
        d_q, d_k, d_v, d_bias[0], d_bias[1],
    )


def solution(mesh):
    both = P(ALL, None)
    return jax.shard_map(
        shards,
        mesh=mesh,
        in_specs=(
            P("dp", None, None), P("dp"), P("dp"), P(ALL, None, None),
            P(None, "tensor"), P(None, "tensor"), P(None, "tensor"), P("tensor", None),
            P(), P(), P(None, "tensor"), P(), P("tensor", None), P(), P(), P(), P(),
            both, both, both, P(ALL), P(ALL),
        ),
        out_specs=(P(ALL, None, None), P(ALL, None, None), both, both, both, P(ALL), P(ALL)),
        check_vma=False,
    )
```

```python
from functools import partial
import math

import jax
import jax.numpy as jnp
from jax import lax
from jax.experimental import pallas as pl
from jax.experimental.pallas import tpu as pltpu
from jax.sharding import PartitionSpec as P

HEADS = 12
EPS = 1e-05
MASKED = -1e30
ALL = ("dp", "tensor")
BF = jnp.bfloat16
F32 = jnp.float32


def mm(left, right):
    return jnp.dot(left, right, preferred_element_type=F32)


def mm_t(left, right):
    return lax.dot_general(left, right, (((1,), (1,)), ((), ())), preferred_element_type=F32)


def t_mm(left, right):
    return lax.dot_general(left, right, (((0,), (0,)), ((), ())), preferred_element_type=F32)


def norm_parts(values):
    average = jnp.mean(values, axis=-1, keepdims=True)
    centered = values - average
    variance = jnp.mean(centered * centered, axis=-1, keepdims=True)
    rstd = lax.rsqrt(variance + EPS)
    return centered * rstd, rstd


def norm_back(grad, gain, xhat, rstd):
    scaled = grad * gain
    return rstd * (
        scaled
        - jnp.mean(scaled, axis=-1, keepdims=True)
        - xhat * jnp.mean(scaled * xhat, axis=-1, keepdims=True)
    )


def gelu_parts(pre):
    cdf = 0.5 * (1.0 + lax.erf(pre * (1.0 / math.sqrt(2.0))))
    pdf = jnp.exp(-0.5 * pre * pre) * (1.0 / math.sqrt(2.0 * math.pi))
    return pre * cdf, cdf + pre * pdf


def limit(mebibytes):
    return pltpu.CompilerParams(vmem_limit_bytes=mebibytes * 2**20)


VMEM = pl.BlockSpec(memory_space=pltpu.VMEM)
SMEM = pl.BlockSpec(memory_space=pltpu.SMEM)
LITTLE = limit(24)
FAR_XY = [(i, i ^ 6) for i in range(8)]
CORE = [(i, i ^ 1) for i in range(8)]
ALONG_X = [(i, i ^ 2) for i in range(8)]
ALONG_Y = [(i, i ^ 4) for i in range(8)]
SPLIT_XY = [(i, i ^ (4 if i & 1 else 2)) for i in range(8)]
CROSS_XY = [(i, i ^ (3 if i & 1 else 5)) for i in range(8)]


def send(array, pairs):
    return lax.ppermute(array, "dp", pairs)


def shift(array, by, groups):
    return lax.ppermute(array, "tensor", [(i, (i + by) % groups) for i in range(groups)])


def scoped(name, step, *args):
    with jax.named_scope(name):
        return step(*args)


def tie(array, *others):
    return lax.optimization_barrier((array,) + others)[0]


def fetch_blocks(spots_ref, sources, stage_ref, sem):
    if len(sources) == 1:
        pltpu.make_async_copy(sources[0], stage_ref, sem).start()
        return
    planes = planes_in_order(spots_ref)
    for k, (ref, first) in enumerate(views(sources)):
        for i, plane in enumerate(planes[1:] + planes[:1]):
            pltpu.make_async_copy(ref.at[first + i], stage_ref.at[spots_ref[k] * len(planes) + plane], sem).start()


def order_rows(stage_ref, join_ref, biases_ref):
    blocks = stage_ref.shape[0]
    rows = join_ref.shape[1] // blocks
    total = 0.0
    for b in range(0, blocks, 2):
        pair = [stage_ref[b + i].astype(F32) for i in range(2)]
        for m in range(3):
            both = jnp.concatenate([block[m * rows : (m + 1) * rows] for block in pair], axis=0)
            join_ref[m, b * rows : (b + 2) * rows, :] = both.astype(BF)
        total = total + pair[0][3 * rows :] + pair[1][3 * rows :]
    biases_ref[...] = total


def fetch(spots_ref, sources, out_ref, sems, which, side_by_side=False):
    planes = planes_in_order(spots_ref)
    dim = sources[-1].shape[-1]
    rows = sources[-1].shape[-2]

    def copy(source, r, at):
        if side_by_side:
            target = out_ref.at[at, pl.ds(r * dim, dim)]
        else:
            target = out_ref.at[pl.ds(r * rows + at.start, at.size)]
        pltpu.make_async_copy(source, target, sems.at[r]).start()

    for r in which:
        if len(sources) == 1:
            copy(sources[0].at[planes[r]], r, pl.ds(0, rows))
        elif r == 0:
            copy(sources[-1], r, pl.ds(0, rows))
        else:
            for k, (ref, first) in enumerate(views(sources[:-1])):
                part = ref.shape[1]
                copy(ref.at[first + r - 1], r, pl.ds(pl.multiple_of(spots_ref[k] * part, part), part))


def arrive(out_ref, sems, r, side_by_side=False):
    dim = out_ref.shape[0] if side_by_side else out_ref.shape[1]
    block = out_ref.at[:, pl.ds(r * dim, dim)] if side_by_side else out_ref.at[pl.ds(r * out_ref.shape[0] // 4, out_ref.shape[0] // 4)]
    pltpu.make_async_copy(block, block, sems.at[r]).wait()


def fetch_stacked(spots_ref, sources, out_ref, sems, last):
    groups, dim = out_ref.shape[0], out_ref.shape[1]
    chosen = range(groups - 1, groups) if last else range(groups - 1)
    if len(sources) == 1:
        for m in chosen:
            pltpu.make_async_copy(sources[0].at[m], out_ref.at[m], sems.at[m]).start()
        return
    own = sources[-groups:]
    pieces = views(sources[:-groups])
    width, rows = dim // groups, pieces[0][0].shape[1]
    per = width // rows
    my_z = spots_ref[8]
    for m in chosen:
        at = pl.ds(pl.multiple_of(my_z * width, width), width)
        pltpu.make_async_copy(own[m], out_ref.at[m, at], sems.at[m]).start()
    for k, (ref, first) in enumerate(pieces):
        e = spots_ref[k]
        m = lax.div(e, per)

        @pl.when((m == groups - 1) == last)
        def _():
            for i, plane in enumerate(planes_in_order(spots_ref)[1:]):
                at = pl.ds(pl.multiple_of(plane * width + lax.rem(e, per) * rows, rows), rows)
                pltpu.make_async_copy(ref.at[first + i], out_ref.at[m, at], sems.at[m]).start()


def arrive_stacked(out_ref, sems, m):
    pltpu.make_async_copy(out_ref.at[m], out_ref.at[m], sems.at[m]).wait()


def views(sources):
    if len(sources) == 8:
        return [(source, 0) for source in sources]
    both, near, far, swapped, swapped_far = sources
    count = far.shape[0]
    return [(both, 0), (both, count), (near, 0), (near, count), (far, 0), (swapped, 0), (swapped, count), (swapped_far, 0)]


def cut_kernel(spots_ref, *refs):
    count = (len(refs) - 1) // 3
    shards, outs, sems = refs[:count], refs[count:-1], refs[-1]
    pairs = []
    for i, shard in enumerate(shards):
        rows = outs[2 * i].shape[0]
        at = pl.ds(pl.multiple_of(lax.div(spots_ref[0], 2) * rows, rows), rows)
        pairs.append((shard.at[at], outs[2 * i]))
        at = pl.ds(pl.multiple_of(spots_ref[0] * (rows // 2), rows // 2), rows // 2)
        pairs.append((shard.at[at], outs[2 * i + 1]))
    for copy in begin(pairs, sems):
        copy.wait()


def cut(spots, shards):
    outs = []
    for shard in shards:
        rows, dim = shard.shape
        outs += [jax.ShapeDtypeStruct((rows // 4, dim), BF), jax.ShapeDtypeStruct((rows // 8, dim), BF)]
    return pl.pallas_call(
        cut_kernel,
        out_shape=outs,
        in_specs=[SMEM] + [ANY] * len(shards),
        out_specs=[VMEM] * len(outs),
        scratch_shapes=[pltpu.SemaphoreType.DMA((len(outs),))],
        compiler_params=limit(60),
    )(spots, *shards)


def merge_kernel(spots_ref, *refs, count):
    beside, across, beside2, across2, *own = refs[:count]
    outs = refs[count:]
    core = lax.rem(spots_ref[0], 2)
    rows = across.shape[0]
    blocks = 3 + len(own) // 2
    sides = [outs[0], outs[1]] if len(outs) == 2 else [outs[0].at[pl.ds(i * blocks, blocks)] for i in range(2)]
    parts = [pl.ds(pl.multiple_of(at * rows, rows), rows) for at in (core, 1 - core)]
    for side, at, last, mine in zip(sides, parts, (across, across2), own or (None, None)):
        side[core] = beside[at, :]
        side[1 - core] = beside2[at, :]
        side[2] = last[...]
        if mine is not None:
            side[3] = mine[...]


def merge(spots, arrays, split):
    rows, dim = arrays[1].shape
    blocks = 3 + (len(arrays) - 4) // 2
    outs = [blocks, blocks] if split else [2 * blocks]
    return pl.pallas_call(
        partial(merge_kernel, count=len(arrays)),
        out_shape=[jax.ShapeDtypeStruct((out, rows, dim), BF) for out in outs],
        in_specs=[SMEM] + [VMEM] * len(arrays),
        out_specs=[VMEM] * len(outs),
        compiler_params=limit(8),
    )(spots, *arrays)


def planes_in_order(spots_ref, groups=4):
    return [lax.rem(spots_ref[8] + step, groups) for step in (0, 1, groups - 1, 2)]


def begin(pairs, sems):
    copies = [pltpu.make_async_copy(source, target, sems.at[i]) for i, (source, target) in enumerate(pairs)]
    for one in copies:
        one.start()
    return copies


WEIGHT_SEMS = pltpu.SemaphoreType.DMA((4,))
ANY = pl.BlockSpec(memory_space=pltpu.HBM)


class Gather:
    def __init__(self, dp_size, groups, my_d, my_z, seqs):
        self.dp_size, self.groups, self.my_d, self.my_z = dp_size, groups, my_d, my_z
        self.paired = dp_size == 8 and groups == 4 and seqs == 2
        core = lax.rem(my_d, 2)
        even = [0, 1, 2, 3, 7, 5, 4, 6]
        odd = [0, 1, 4, 5, 7, 3, 2, 6]
        flips = jnp.where(core == 0, jnp.array(even, jnp.int32), jnp.array(odd, jnp.int32))
        self.spots = jnp.concatenate([jnp.bitwise_xor(my_d, flips), my_z[None]]).astype(jnp.int32)

    def all_parts(self, part):
        whole = lax.all_gather(part, ("dp", "tensor"), axis=0)
        return whole.reshape((self.dp_size, self.groups) + part.shape).transpose(1, 0, 2, 3)

    def part_of(self, shard):
        rows = shard.shape[0] // self.dp_size
        return lax.dynamic_slice_in_dim(shard, self.my_d * rows, rows, 0)

    def all_rounds(self, parts, early, steps):
        count = len(parts)
        gathered, spread = [], []
        ahead, done = self.planes(parts[0], 0), [rows for part in parts[1:] for rows in part[:2]] + early
        for r in range(count + 2):
            with jax.named_scope("round%d" % r):
                ready = list(lax.optimization_barrier((*ahead, *done))) if r < count else list(done)
                ahead = ready[: len(ahead)]
                if r >= 1:
                    at = len(ahead)
                    if r <= count:
                        last = spread[r - 1]
                        last[1] = ready[at : at + len(last[1])]
                        at += len(last[1])
                    if 2 <= r <= count:
                        spread[r - 2][2] = ready[at]
                done = []
                if 1 <= r < count:
                    near_half = last[1][0] if len(last[1]) == 2 else last[1][0][: last[1][0].shape[0] // 2]
                    last.append(scoped("far", send, near_half, CROSS_XY))
                if r < count:
                    beside, across = ahead
                    ahead = []
                    if r + 1 < count:
                        ahead = self.planes([tie(rows, beside) for rows in parts[r + 1]], r + 1)
                    others = [scoped("others", send, beside, CORE), scoped("others", send, across, CORE)]
                    both = merge(self.spots, [beside, across, *others, *parts[r][2:]], r == count - 1)
                    near = [scoped("near", send, side, SPLIT_XY) for side in both]
                    spread.append([both, near])
                    done += near
                else:
                    ahead = []
                if 1 <= r <= count:
                    late = []
                    last.append([scoped("swap", send, array, CORE) for array in last[1][:-1]])
                    last[3].append(scoped("swap", send, tie(last[1][-1], *late), CORE))
                    done += (last[2:3] if r < count else []) + last[3]
                if r >= 2:
                    whole = spread[r - 2]
                    gathered.append([*whole[0], *whole[1], whole[2], *whole[3], scoped("swapfar", send, whole[2], CORE)])
                done += steps[r](gathered)
                if r == count - 1:
                    spread[r].append(scoped("far", send, tie(near[0], *done[len(near) :]), CROSS_XY))
        return gathered

    def planes(self, part, r):
        with jax.named_scope("planes%d" % r):
            groups = self.groups
            pairs = [
                (d * groups + z, d * groups + (z + (1 if d & 1 else groups - 1)) % groups)
                for d in range(self.dp_size)
                for z in range(groups)
            ]
            beside = scoped("beside", lax.ppermute, part[1], ("dp", "tensor"), pairs)
            return beside, scoped("across", shift, part[0], 2, groups)

    def half_of(self, quarter):
        rows = quarter.shape[0] // 2
        return jnp.where(lax.rem(self.my_d, 2) == 0, quarter[:rows], quarter[rows:])

    def quarter_of(self, shard):
        rows = 2 * shard.shape[0] // self.dp_size
        return lax.dynamic_slice_in_dim(shard, self.my_d // 2 * rows, rows, 0)

    def whole(self, part, stacked=False):
        whole = self.all_parts(part)
        dim = part.shape[1]
        if stacked:
            whole = whole.reshape(self.groups, 4, -1, dim).transpose(1, 0, 2, 3)
        return [whole.reshape(4, -1, dim)]


def reduce_grads(gather, grads, own_rows, between, at_last):
    groups, spots = gather.groups, gather.spots
    if not gather.paired:
        mats, bias = grads
        mats = lax.psum_scatter(mats, ("dp", "tensor"), scatter_dimension=1, tiled=True)
        middle = between(None)
        return (mats[0], mats[1], mats[2], lax.psum(bias, ("dp", "tensor"))), at_last(None)
    keep, away = grads
    rows, dim = keep.shape[1:]
    low = jax.ShapeDtypeStruct((rows, dim), BF)
    come = scoped("cores", send, away, CORE)
    to_x, to_y, to_far = pl.pallas_call(
        add_cores_kernel,
        out_shape=[low, low, low],
        in_specs=[SMEM, ANY, ANY],
        out_specs=[ANY] * 3,
        scratch_shapes=[pltpu.VMEM((3, rows, dim), BF)] * 3 + [pltpu.SemaphoreType.DMA((6,)), pltpu.SemaphoreType.DMA((3,))],
        compiler_params=limit(60),
    )(spots, keep, come)
    from_far = scoped("far", send, to_far, FAR_XY)
    from_x = scoped("x", send, to_x, ALONG_X)
    from_y = scoped("y", send, to_y, ALONG_Y)
    block = jax.ShapeDtypeStruct((3 * own_rows + 8, dim), BF)
    middle = between(to_far)
    mine, *goes = pl.pallas_call(
        add_plane_kernel,
        out_shape=[jax.ShapeDtypeStruct((3 * own_rows + 8, dim), F32)] + [block] * (groups - 1),
        in_specs=[SMEM] + [ANY] * 5,
        out_specs=[VMEM] * groups,
        scratch_shapes=[pltpu.VMEM((rows - 16, dim), F32), pltpu.VMEM((5, rows, dim), BF), pltpu.SemaphoreType.DMA((5,))],
        compiler_params=limit(60),
    )(spots, from_x, from_y, from_far, tie(keep, middle), come)
    after = at_last(mine)
    comes = [scoped("stack%d" % i, shift, go, i + 1, groups) for i, go in enumerate(goes)]
    part = jax.ShapeDtypeStruct((own_rows, dim), F32)
    sums = pl.pallas_call(
        add_stack_kernel,
        out_shape=[part, part, part, jax.ShapeDtypeStruct((8, dim), F32)],
        in_specs=[VMEM] * groups,
        out_specs=[VMEM] * 4,
        compiler_params=LITTLE,
    )(mine, *comes)
    return sums, after


def cost(flops, moved, exps=0):
    return pl.CostEstimate(flops=int(flops), bytes_accessed=int(moved), transcendentals=int(exps))


def head_masks():
    lane = lax.broadcasted_iota(jnp.int32, (1, 128), 1)
    first = (lane < 64).astype(F32)
    return [first.astype(BF), (1.0 - first).astype(BF)], lane < 64


def attention_kernel(spots_ref, len_ref, x_ref, norms_ref, *refs):
    *sources, q_hbm, k_hbm, v_hbm, p_hbm, low_ref, xhat_hbm, rstd_ref, w_ref, ctx_ref, q_ref, k_ref, v_ref, p_ref, xhat_ref, sems, store_sems = refs
    fetch_stacked(spots_ref, sources, w_ref, sems, False)
    fetch_stacked(spots_ref, sources, w_ref, sems, True)
    rows, dim = x_ref.shape
    for m in range(4):
        arrive_stacked(w_ref, sems, m)
    seq_len = p_ref.shape[1]
    x = x_ref[...]
    q_ref[...] = (mm_t(x, w_ref[0]).astype(BF).astype(F32) * (1.0 / math.sqrt(dim // HEADS))).astype(BF)
    k_ref[...] = mm_t(x, w_ref[1]).astype(BF)
    v_ref[...] = mm_t(x, w_ref[2]).astype(BF)
    stores = begin(((q_ref, q_hbm), (k_ref, k_hbm), (v_ref, v_hbm)), store_sems)
    masks, first = head_masks()
    key_at = lax.broadcasted_iota(jnp.int32, (seq_len, 1), 0)

    for s in range(rows // seq_len):
        at = slice(s * seq_len, (s + 1) * seq_len)
        valid = key_at < len_ref[s]
        for j in range(HEADS // 2):
            cols = slice(128 * j, 128 * (j + 1))
            q, k, v = q_ref[at, cols], k_ref[at, cols], v_ref[at, cols]
            parts = []
            for h in range(2):
                scores = jnp.where(valid, mm_t(k, q * masks[h]), MASKED)
                exps = jnp.exp(scores - jnp.max(scores, axis=0, keepdims=True))
                probs = (exps * (1.0 / jnp.sum(exps, axis=0, keepdims=True))).astype(BF)
                p_ref[s * HEADS + 2 * j + h] = probs
                parts.append(t_mm(probs, v))
            ctx_ref[at, cols] = jnp.where(first, parts[0], parts[1]).astype(BF)
        heads = pl.ds(s * HEADS, HEADS)
        stores += begin(((p_ref.at[heads], p_hbm.at[heads]),), store_sems.at[pl.ds(3 + s, 1)])
    xhat, rstd = norm_parts(x.astype(F32) + mm(ctx_ref[...], w_ref[3]))
    xhat_ref[...] = xhat
    stores += begin(((xhat_ref, xhat_hbm),), store_sems.at[pl.ds(3 + rows // seq_len, 1)])
    rstd_ref[...] = rstd
    low_ref[...] = (xhat * norms_ref[0:1, :] + norms_ref[1:2, :]).astype(BF)
    for store in stores:
        store.wait()


def attention_forward(spots, lengths, x, sources, norms, seq_len):
    rows, dim = x.shape
    seqs = rows // seq_len
    low = jax.ShapeDtypeStruct((rows, dim), BF)
    return pl.pallas_call(
        attention_kernel,
        out_shape=[low, low, low,
                   jax.ShapeDtypeStruct((seqs * HEADS, seq_len, seq_len), BF), low,
                   jax.ShapeDtypeStruct((rows, dim), F32), jax.ShapeDtypeStruct((rows, 1), F32)],
        in_specs=[SMEM] * 2 + [VMEM] * 2 + [ANY] * len(sources),
        out_specs=[ANY] * 4 + [VMEM, ANY, VMEM],
        scratch_shapes=[pltpu.VMEM((4, dim, dim), BF)] + [pltpu.VMEM((rows, dim), BF)] * 4 + [
            pltpu.VMEM((seqs * HEADS, seq_len, seq_len), BF), pltpu.VMEM((rows, dim), F32),
            WEIGHT_SEMS, pltpu.SemaphoreType.DMA((4 + seqs,)),
        ],
        compiler_params=limit(60),
        cost_estimate=cost(2 * rows * dim * (4 * dim + 2 * seq_len), 2 * (4 * dim * dim + 8 * rows * dim), rows * seq_len * HEADS),
    )(spots, lengths, x, norms, *sources)


def by_rows(rows, step, work, unroll=1):
    work(slice(0, rows))


def ffn_in_kernel(spots_ref, x_ref, bias_ref, *refs):
    *sources, act_hbm, slope_hbm, act_ref, slope_ref, w_ref, pre_ref, sems, store_sems = refs
    units = pre_ref.shape[1]
    order = planes_in_order(spots_ref)
    stores = []
    fetch(spots_ref, sources, w_ref, sems, [0, 1])
    for r in range(4):
        fetch(spots_ref, sources, w_ref, sems, [r + 2] if r < 2 else [])
        arrive(w_ref, sems, r)
        pre_ref[...] = mm(x_ref[...], w_ref[r * x_ref.shape[1] : (r + 1) * x_ref.shape[1], :])
        cols = slice(r * units, (r + 1) * units)
        act, slope = gelu_parts(pre_ref[...] + bias_ref[order[r]])
        act_ref[:, cols] = act.astype(BF)
        slope_ref[:, cols] = slope.astype(BF)
        pairs = [(act_ref, act_hbm), (slope_ref, slope_hbm)]
        stores += begin([(ref.at[:, cols], hbm.at[:, cols]) for ref, hbm in pairs], store_sems.at[pl.ds(2 * r, 2)])
    for store in stores:
        store.wait()


def ffn_forward(spots, x, sources, bias, units):
    rows, dim = x.shape
    planes = bias.shape[0] // units
    out = jax.ShapeDtypeStruct((rows, planes * units), BF)
    return pl.pallas_call(
        ffn_in_kernel,
        out_shape=[out, out],
        in_specs=[SMEM] + [VMEM] * 2 + [ANY] * len(sources),
        out_specs=[ANY] * 2,
        scratch_shapes=[
            pltpu.VMEM((rows, planes * units), BF), pltpu.VMEM((rows, planes * units), BF),
            pltpu.VMEM((planes * dim, units), BF), pltpu.VMEM((rows, units), F32), WEIGHT_SEMS, pltpu.SemaphoreType.DMA((8,)),
        ],
        compiler_params=limit(60),
        cost_estimate=cost(2 * rows * dim * units * planes, 2 * planes * units * (dim + 2 * rows), 2 * rows * units * planes),
    )(spots, x, bias.reshape(planes, 1, units), *sources)


def two_pass(values, table):
    high = values.astype(BF)
    return mm(high, table) + mm((values - high.astype(F32)).astype(BF), table)


def put_rows(ref, mats, bias):
    at = 0
    for mat in mats:
        ref[at : at + mat.shape[0], :] = mat.astype(BF)
        at += mat.shape[0]
    high = bias.astype(BF).astype(F32)
    ref[at : at + 16, :] = jnp.concatenate([high, bias - high], axis=0).astype(BF)


def sum_rows(arrays):
    total = arrays[0].astype(F32)
    for array in arrays[1:]:
        total = total + array.astype(F32)
    rows = total.shape[0] - 16
    return total[:rows], total[rows : rows + 8] + total[rows + 8 :]


def add_cores_kernel(spots_ref, keep_hbm, come_hbm, *refs):
    hbm, (sums_ref, keep_ref, come_ref, sems, store_sems) = refs[:3], refs[3:]
    quarter = lax.div(spots_ref[0], 2)
    pairs = []
    for i in range(3):
        q = jnp.bitwise_xor(quarter, i + 1)
        pairs += [(keep_hbm.at[q], keep_ref.at[i]), (come_hbm.at[q], come_ref.at[i])]
    copies = begin(pairs, sems)
    stores = []
    for i in range(3):
        copies[2 * i].wait()
        copies[2 * i + 1].wait()
        mats, bias = sum_rows([keep_ref[i], come_ref[i]])
        put_rows(sums_ref.at[i], [mats], bias)
        stores += begin(((sums_ref.at[i], hbm[i]),), store_sems.at[pl.ds(i, 1)])
    for store in stores:
        store.wait()


def fold_bias(bias):
    high = bias.astype(BF).astype(F32)
    row = lax.broadcasted_iota(jnp.int32, (8, 1), 0)
    return jnp.where(row < 4, high, pltpu.roll(bias - high, 4, 0))


def add_plane_kernel(spots_ref, *refs):
    parts, refs = refs[:3], refs[3:]
    keep_hbm, come_hbm, mine_ref, *go_refs, total_ref, arrays_ref, sems = refs
    quarter = lax.div(spots_ref[0], 2)
    sources = (keep_hbm.at[quarter], come_hbm.at[quarter], *parts)
    for copy in begin([(source, arrays_ref.at[i]) for i, source in enumerate(sources)], sems):
        copy.wait()
    total_ref[...], bias = sum_rows([arrays_ref[i] for i in range(5)])
    groups = len(go_refs) + 1
    width = total_ref.shape[0] // 3
    rows = width // groups

    def block(plane):
        at = [pl.multiple_of(i * width + plane * rows, 8) for i in range(3)]
        return jnp.concatenate([total_ref[pl.ds(a, rows), :] for a in at], axis=0)

    my_z = spots_ref[8]
    mine_ref[...] = jnp.concatenate([block(my_z), bias], axis=0)
    folded = fold_bias(bias)
    for i, ref in enumerate(go_refs):
        ref[...] = jnp.concatenate([block(lax.rem(my_z + i + 1, groups)), folded], axis=0).astype(BF)


def add_stack_kernel(mine_ref, *refs):
    come_refs, (q_ref, k_ref, v_ref, bias_ref) = refs[:-4], refs[-4:]
    total = mine_ref[...]
    rows = q_ref.shape[0]
    for ref in come_refs:
        come = ref[...].astype(F32)
        bias = come[3 * rows :]
        total = total + jnp.concatenate([come[: 3 * rows], bias + pltpu.roll(bias, 4, 0)], axis=0)
    q_ref[...], k_ref[...], v_ref[...] = (total[i * rows : (i + 1) * rows] for i in range(3))
    bias_ref[...] = total[3 * rows :]


def joining_kernel(
    spots_ref, member_ref, member_t_ref, avail_ref, norms_ref, act_hbm, xhat1_hbm, cot_hbm, *refs, halves, count
):
    gain1, bias1, gain2, bias2 = (norms_ref[i : i + 1, :] for i in range(4))
    down_hbm, up_hbm, *refs = refs
    join_sources, sources, refs = refs[:count], refs[count:-38], refs[-38:]
    stage_ref, biases_ref, stage_sem, refs = refs[-3], refs[-2], refs[-1], refs[:-3]
    out_hbm, g2_hbm, g_ffn_ref, grad_hbm0, grad_hbm1 = refs[:5]
    act_ref, w_out_ref, down_ref, up_ref, join_ref, xhat1_ref, cot_ref, act_sems, out_sems, sems, store_sems = refs[5:16]
    ffn_ref, u_ref, w_ref, big_u_ref, big_w_ref, p_wide_ref, sums_ref = refs[16:23]
    x_ref, act2_ref, slope_ref, q_ref, gq_ref, low_ref, mixed_ref, t_ref = refs[23:31]
    out_ref, g2_ref, bias_rows_ref, bias_ref = refs[31:35]
    rows, dim = out_ref.shape
    units = w_out_ref.shape[0] // 4
    seqs = avail_ref.shape[0]
    per = rows // seqs
    everyone = [slice(i * per, (i + 1) * per) for i in range(seqs)]
    fscale = 1.0 / math.sqrt(dim)
    member, member_t = member_ref[...], member_t_ref[...]
    loads = []

    def issue(r):
        if r < 4:
            fetch(spots_ref, sources, w_out_ref, out_sems, [r])
            cols = pl.ds(r * units, units)
            loads.extend(begin(((act_hbm.at[:, cols], act_ref.at[:, cols]),), act_sems.at[pl.ds(r, 1)]))
        elif r == 4:
            fetch_blocks(spots_ref, join_sources, stage_ref, stage_sem)
        elif r == 5:
            pairs = ((down_hbm, down_ref), (up_hbm, up_ref), (xhat1_hbm, xhat1_ref), (cot_hbm, cot_ref))
            loads.extend(begin(pairs, sems))

    issue(0)
    issue(1)
    for r in range(4):
        issue(r + 2)
        loads[r].wait()
        arrive(w_out_ref, out_sems, r)
        if r % 2 == 1:
            both = slice((r - 1) * units, (r + 1) * units)
            for at in everyone:
                term = mm(act_ref[at, both], w_out_ref[both, :])
                ffn_ref[at, :] = term if r == 1 else ffn_ref[at, :] + term
    loads = loads[4:]
    for at in everyone:
        x_ref[at, :] = ffn_ref[at, :].astype(BF)
    pltpu.make_async_copy(stage_ref, stage_ref, stage_sem).wait()
    order_rows(stage_ref, join_ref, biases_ref)
    qb, vb = biases_ref[0:1, :], biases_ref[1:2, :]
    for load in loads:
        load.wait()
    up = up_ref[...]
    halves_of = {}

    def narrow(i, name, value=None):
        if value is not None:
            halves_of[i, name] = value
        return halves_of[i, name]

    def per_adapter(values):
        high = values.astype(BF)
        return mm(high, member) + mm((values - high.astype(F32)).astype(BF), member)

    def to_q(i, at):
        q_ref[at, :] = (mm(x_ref[at, :], join_ref[0]) + qb).astype(BF)

    def down(i, at):
        act, slope = gelu_parts(mm(x_ref[at, :], down_ref[...]))
        act2_ref[at, :] = act.astype(BF)
        slope_ref[at, :] = slope.astype(BF)

    def to_u(i, at):
        u = mm_t(q_ref[at, :], join_ref[1])
        u_ref[at, :] = u
        narrow(i, "dot", jnp.sum(ffn_ref[at, :] * u, axis=-1, keepdims=True))

    def scores(i, at):
        big_u = mm_t(u_ref[at, :].astype(BF), up)
        big_u_ref[at, :] = big_u
        fscores = (per_adapter(act2_ref[at, :].astype(F32) * big_u) + narrow(i, "dot")) * fscale
        fscores = jnp.where(avail_ref[i] > 0, fscores, MASKED)
        fexp = jnp.exp(fscores - jnp.max(fscores, axis=-1, keepdims=True))
        narrow(i, "probs", fexp / jnp.sum(fexp, axis=-1, keepdims=True))

    def mix(i, at):
        p_wide = two_pass(narrow(i, "probs"), member_t)
        p_wide_ref[at, :] = p_wide
        weighed = (p_wide * act2_ref[at, :].astype(F32)).astype(BF)
        mixed_ref[at, :] = (ffn_ref[at, :] + mm(weighed, up)).astype(BF)

    def norm(i, at):
        normed1 = xhat1_ref[at, :] * gain1 + bias1
        xhat2, rstd2 = norm_parts(normed1 + mm(mixed_ref[at, :], join_ref[2]) + vb)
        out_ref[at, :] = (xhat2 * gain2 + bias2).astype(BF)
        g2 = norm_back(cot_ref[at, :].astype(F32), gain2, xhat2, rstd2)
        g2_ref[at, :] = g2
        low_ref[at, :] = g2.astype(BF)
        narrow(i, "dot2", jnp.sum(g2 * vb, axis=-1, keepdims=True))
        narrow(i, "d_vb", jnp.sum(g2.reshape(-1, 8, dim), axis=0))

    def to_w(i, at):
        w = mm_t(low_ref[at, :], join_ref[2])
        w_ref[at, :] = w
        narrow(i, "dot2", narrow(i, "dot2") + jnp.sum(ffn_ref[at, :] * w, axis=-1, keepdims=True))

    def score_grads(i, at):
        big_w = mm_t(w_ref[at, :].astype(BF), up)
        big_w_ref[at, :] = big_w
        gvals = per_adapter(act2_ref[at, :].astype(F32) * big_w) + narrow(i, "dot2")
        fprobs = narrow(i, "probs")
        gs = fprobs * (gvals - jnp.sum(gvals * fprobs, axis=-1, keepdims=True)) * fscale
        narrow(i, "gs", gs)
        narrow(i, "gs_sum", jnp.sum(gs, axis=-1, keepdims=True))

    def to_t(i, at):
        wide = two_pass(narrow(i, "gs"), member_t)
        weighed = (wide * act2_ref[at, :].astype(F32)).astype(BF)
        grad = wide * big_u_ref[at, :] + p_wide_ref[at, :] * big_w_ref[at, :]
        slope_ref[at, :] = (grad * slope_ref[at, :].astype(F32)).astype(BF)
        t_ref[at, :] = (mm(weighed, up) + narrow(i, "gs_sum") * ffn_ref[at, :]).astype(BF)

    def to_gq(i, at):
        gq = mm(t_ref[at, :], join_ref[1]).astype(BF)
        gq_ref[at, :] = gq
        narrow(i, "d_qb", jnp.sum(gq.astype(F32).reshape(-1, 8, dim), axis=0))

    def all_halves(*steps):
        for step in steps:
            for i, at in enumerate(everyone):
                step(i, at)

    all_halves(to_q, down, to_u, scores, mix, norm)
    stores = begin(((out_ref, out_hbm), (g2_ref, g2_hbm)), store_sems)
    all_halves(to_w, score_grads)
    sums_ref[2] = t_mm(mixed_ref[...], low_ref[...]).astype(sums_ref.dtype)
    all_halves(to_t)
    sums_ref[1] = t_mm(t_ref[...], q_ref[...]).astype(sums_ref.dtype)
    all_halves(to_gq)
    sums_ref[0] = t_mm(x_ref[...], gq_ref[...]).astype(sums_ref.dtype)
    row = lax.broadcasted_iota(jnp.int32, (8, 1), 0)
    d_qb, d_vb = (
        jnp.sum(sum(narrow(i, name) for i in range(seqs)), axis=0, keepdims=True) for name in ("d_qb", "d_vb")
    )
    bias_ref[...] = jnp.where(row == 0, d_qb, jnp.where(row == 1, d_vb, 0.0))
    if halves:
        core = lax.rem(spots_ref[0], 2)
        part = dim // 8
        put_rows(bias_rows_ref, [], bias_ref[...])
        for hbm, side, sem in ((grad_hbm1, 1 - core, store_sems.at[2]), (grad_hbm0, core, store_sems.at[3])):
            for q in range(4):
                at = pl.ds(pl.multiple_of((2 * q + side) * part, part), part)
                for i in range(3):
                    pltpu.make_async_copy(sums_ref.at[i, at], hbm.at[q, pl.ds(i * part, part)], sem).start()
                pltpu.make_async_copy(bias_rows_ref, hbm.at[q, pl.ds(3 * part, 16)], sem).start()
            stores.append(pltpu.make_async_copy(hbm, hbm, sem))
    else:
        stores += begin(((sums_ref, grad_hbm0), (bias_ref, grad_hbm1)), store_sems.at[pl.ds(2, 2)])
    for i, at in enumerate(everyone):
        total = mm_t(slope_ref[at, :], down_ref[...]) + mm_t(gq_ref[at, :], join_ref[0])
        g_ffn_ref[at, :] = (narrow(i, "gs_sum") * u_ref[at, :] + w_ref[at, :] + total).astype(BF)
    for store in stores:
        store.wait()


def joining(spots, halves, act, sources, adapt_down, up, join_sources, member, member_t, avail, xhat1, norms, cot):
    rows, dim = xhat1.shape
    if halves:
        grads = [jax.ShapeDtypeStruct((4, 3 * dim // 8 + 16, dim), BF)] * 2
    else:
        grads = [jax.ShapeDtypeStruct((3, dim, dim), F32), jax.ShapeDtypeStruct((8, dim), F32)]
    wide, low = pltpu.VMEM((rows, dim), F32), pltpu.VMEM((rows, dim), BF)
    height, blocks = join_sources[-1].shape[-2:][0], 32
    stage_shape = join_sources[0].shape if len(join_sources) == 1 else (blocks, height, dim)
    return pl.pallas_call(
        partial(joining_kernel, halves=halves, count=len(join_sources)),
        out_shape=[
            jax.ShapeDtypeStruct((rows, dim), BF),
            jax.ShapeDtypeStruct((rows, dim), F32),
            jax.ShapeDtypeStruct((rows, dim), BF),
        ] + grads,
        in_specs=[SMEM] + [VMEM] * 4 + [ANY] * (len(sources) + len(join_sources) + 5),
        out_specs=[ANY, ANY, VMEM, ANY, ANY],
        scratch_shapes=[
            pltpu.VMEM(act.shape, BF),
            pltpu.VMEM((act.shape[1], dim), BF),
            pltpu.VMEM(adapt_down.shape, BF),
            pltpu.VMEM(up.shape, BF),
            pltpu.VMEM((3, dim, dim), BF),
            wide,
            low,
            WEIGHT_SEMS,
            WEIGHT_SEMS,
            pltpu.SemaphoreType.DMA((4,)),
            pltpu.SemaphoreType.DMA((4,)),
        ] + [wide] * 6 + [pltpu.VMEM((3, dim, dim), BF if halves else F32)] + [low] * 8 + [
            low,
            wide,
            pltpu.VMEM((16, dim), BF),
            pltpu.VMEM((8, dim), F32),
            pltpu.VMEM(stage_shape, BF),
            pltpu.VMEM((8, dim), F32),
            pltpu.SemaphoreType.DMA,
        ],
        compiler_params=limit(60),
        cost_estimate=cost(2 * rows * dim * (15 * dim + act.shape[1]), 2 * dim * (8 * dim + 10 * rows), 2 * rows * dim),
    )(spots, member, member_t, avail, norms, act, xhat1, cot, adapt_down, up, *join_sources, *sources)


def ffn_back_kernel(spots_ref, g_ref, rstd_ref, norms_ref, slope_hbm, g2_hbm, xhat_hbm, *refs, count):
    refs, (out_sources, in_sources) = refs[sum(count) :], (refs[: count[0]], refs[count[0] : sum(count)])
    g1_hbm, low_hbm, g1_ref, low_ref, slope_ref, g2_ref, xhat_ref, w_out_ref, w_in_ref, pre_ref, out_sems, in_sems, slope_sems, sems, store_sems = refs
    units = w_out_ref.shape[0] // 4
    rows = g_ref.shape[0]
    everyone = [slice(i * rows // 2, (i + 1) * rows // 2) for i in range(2)]
    loads = []

    def issue(r):
        if r < 4:
            fetch(spots_ref, out_sources, w_out_ref, out_sems, [r])
            cols = pl.ds(r * units, units)
            loads.extend(begin(((slope_hbm.at[:, cols], slope_ref.at[:, cols]),), slope_sems.at[pl.ds(r, 1)]))
        elif r < 8:
            fetch(spots_ref, in_sources, w_in_ref, in_sems, [r - 4], side_by_side=True)
        elif r == 8:
            loads.extend(begin(((g2_hbm, g2_ref), (xhat_hbm, xhat_ref)), sems))

    issue(0)
    issue(1)
    for r in range(4):
        issue(r + 2)
        cols = slice(r * units, (r + 1) * units)
        arrive(w_out_ref, out_sems, r)
        loads[r].wait()
        for at in everyone:
            pre_ref[at, cols] = (mm_t(g_ref[at, :], w_out_ref[cols, :]) * slope_ref[at, cols].astype(F32)).astype(BF)
    for r in range(4, 8):
        issue(r + 2)
        arrive(w_in_ref, in_sems, r - 4, side_by_side=True)
        if r == 5:
            both = slice(0, 2 * units)
            for at in everyone:
                g1_ref[at, :] = mm_t(pre_ref[at, both], w_in_ref[:, both])
    for load in loads[4:]:
        load.wait()
    both = slice(2 * units, 4 * units)
    stores = []
    for at in everyone:
        total = mm_t(pre_ref[at, both], w_in_ref[:, both]) + g1_ref[at, :] + g2_ref[at, :]
        g1 = norm_back(total, norms_ref[0:1, :], xhat_ref[at, :], rstd_ref[at, :])
        g1_ref[at, :] = g1
        low_ref[at, :] = g1.astype(BF)
        stores += begin(((g1_ref.at[at], g1_hbm.at[at]), (low_ref.at[at], low_hbm.at[at])), store_sems.at[pl.ds(len(stores), 2)])
    for store in stores:
        store.wait()


def ffn_backward(spots, g_ffn, slope, out_sources, in_sources, g2, xhat, rstd, norms):
    rows, dim = xhat.shape
    planes = 4
    units = slope.shape[1] // planes
    return pl.pallas_call(
        partial(ffn_back_kernel, count=(len(out_sources), len(in_sources))),
        out_shape=[jax.ShapeDtypeStruct((rows, dim), F32), jax.ShapeDtypeStruct((rows, dim), BF)],
        in_specs=[SMEM] + [VMEM] * 3 + [ANY] * (len(out_sources) + len(in_sources) + 3),
        out_specs=[ANY, ANY],
        scratch_shapes=[
            pltpu.VMEM((rows, dim), F32), pltpu.VMEM((rows, dim), BF),
            pltpu.VMEM(slope.shape, BF), pltpu.VMEM((rows, dim), F32), pltpu.VMEM((rows, dim), F32),
            pltpu.VMEM((planes * units, dim), BF), pltpu.VMEM((dim, planes * units), BF), pltpu.VMEM(slope.shape, BF),
            WEIGHT_SEMS, WEIGHT_SEMS, WEIGHT_SEMS, pltpu.SemaphoreType.DMA((2,)),
            pltpu.SemaphoreType.DMA((4,)),
        ],
        compiler_params=limit(60),
        cost_estimate=cost(4 * rows * dim * units * planes, 2 * planes * units * (2 * dim + rows)),
    )(spots, g_ffn, rstd, norms, slope, g2, xhat, *out_sources, *in_sources)


def attention_back_heads(s, seq_len, q_ref, k_ref, v_ref, p_ref, g_ref, dq_ref, dk_ref, dv_ref, first_seq):
    dim = q_ref.shape[1]
    scale = 1.0 / math.sqrt(dim // HEADS)
    masks = head_masks()[0]
    at = slice((s - first_seq) * seq_len, (s - first_seq + 1) * seq_len)
    for j in range(HEADS // 2):
        cols = slice(128 * j, 128 * (j + 1))
        q, k, v, g = q_ref[at, cols], k_ref[at, cols], v_ref[at, cols], g_ref[at, cols]
        split = [jnp.concatenate([array * mask for mask in masks], axis=0) for array in (q, k, g)]
        probs_low = [p_ref[(s - first_seq) * HEADS + 2 * j + h] for h in range(2)]
        g_scores = []
        for h in range(2):
            probs = probs_low[h].astype(F32)
            g_probs = mm_t(v, split[2][h * seq_len : (h + 1) * seq_len])
            g_scores.append((probs * (g_probs - jnp.sum(g_probs * probs, axis=0, keepdims=True))).astype(BF))
        dq_ref[at, cols] = (t_mm(jnp.concatenate(g_scores, axis=0), split[1]) * scale).astype(BF)
        dk_ref[at, cols] = mm(jnp.concatenate(g_scores, axis=1), split[0]).astype(BF)
        dv_ref[at, cols] = mm(jnp.concatenate(probs_low, axis=1), split[2]).astype(BF)


def load_heads(hbm, vmem, sems, first, count):
    seq_len = hbm[3].shape[1]
    rows, heads = pl.ds(first * seq_len, count * seq_len), pl.ds(first * HEADS, count * HEADS)
    pairs = [(hbm[i].at[rows], vmem[i]) for i in range(3)] + [(hbm[3].at[heads], vmem[3])]
    return begin(pairs, sems)


def attention_back_first_kernel(spots_ref, *refs):
    *refs, ctx_hbm, dq_ref, dk_ref, dv_ref, w_ref, g1_ref, ctx_ref, q_ref, k_ref, v_ref, p_ref, w_sems, sems, g_sems = refs
    g1_hbm, *sources, q_hbm, k_hbm, v_hbm, p_hbm = refs
    seq_len = p_ref.shape[1]
    rows, dim = g1_ref.shape
    loads = begin(((g1_hbm, g1_ref),), g_sems.at[pl.ds(0, 1)])
    fetch_stacked(spots_ref, sources, w_ref, w_sems, True)
    seqs = q_ref.shape[0] // seq_len
    loads += load_heads((q_hbm, k_hbm, v_hbm, p_hbm), (q_ref, k_ref, v_ref, p_ref), sems, 0, seqs)
    loads[0].wait()
    arrive_stacked(w_ref, w_sems, 3)
    ctx_ref[...] = mm_t(g1_ref[...], w_ref[3]).astype(BF)
    later = pl.ds(seqs * seq_len, rows - seqs * seq_len)
    store = begin(((ctx_ref.at[later], ctx_hbm),), g_sems.at[pl.ds(1, 1)])[0]
    for load in loads[1:]:
        load.wait()
    for s in range(seqs):
        attention_back_heads(s, seq_len, q_ref, k_ref, v_ref, p_ref, ctx_ref, dq_ref, dk_ref, dv_ref, 0)
    store.wait()


def attention_back_last_kernel(spots_ref, *refs):
    *refs, out_ref, g1_ref, ctx_ref, dq0_ref, dk0_ref, dv0_ref, w_ref, q_ref, k_ref, v_ref, p_ref, dq_ref, dk_ref, dv_ref, w_sems, sems, late_sems = refs
    g1_hbm, ctx_hbm, dq0_hbm, dk0_hbm, dv0_hbm, *sources, q_hbm, k_hbm, v_hbm, p_hbm = refs
    rows, dim = g1_ref.shape
    seq_len = p_ref.shape[1]
    first = dq0_ref.shape[0] // seq_len
    seqs = q_ref.shape[0] // seq_len
    loads = begin(((ctx_hbm, ctx_ref),), late_sems.at[pl.ds(0, 1)])
    loads += load_heads((q_hbm, k_hbm, v_hbm, p_hbm), (q_ref, k_ref, v_ref, p_ref), sems, first, seqs)
    for load in loads:
        load.wait()
    fetch_stacked(spots_ref, sources, w_ref, w_sems, False)
    pairs = ((dq0_hbm, dq0_ref), (dk0_hbm, dk0_ref), (dv0_hbm, dv0_ref), (g1_hbm, g1_ref))
    loads = begin(pairs, late_sems.at[pl.ds(1, 4)])
    for s in range(seqs):
        attention_back_heads(s, seq_len, q_ref, k_ref, v_ref, p_ref, ctx_ref, dq_ref, dk_ref, dv_ref, 0)
    for load in loads:
        load.wait()
    for m in range(3):
        arrive_stacked(w_ref, w_sems, m)
    for at, grads in ((slice(0, first * seq_len), (dq0_ref, dk0_ref, dv0_ref)), (slice(first * seq_len, rows), (dq_ref, dk_ref, dv_ref))):
        total = g1_ref[at, :]
        for m, grad in enumerate(grads):
            total = total + mm(grad[...], w_ref[m])
        out_ref[at, :] = total.astype(BF)


def attention_backward_first(spots, g1_low, sources, q, k, v, probs):
    rows, dim = g1_low.shape
    heads, seq_len = probs.shape[0] // 2, probs.shape[1]
    half, low = jax.ShapeDtypeStruct((rows // 2, dim), BF), pltpu.VMEM((rows // 2, dim), BF)
    return pl.pallas_call(
        attention_back_first_kernel,
        out_shape=[half, half, half, half],
        in_specs=[SMEM, ANY] + [ANY] * (len(sources) + 4),
        out_specs=[ANY] + [VMEM] * 3,
        scratch_shapes=[pltpu.VMEM((4, dim, dim), BF), pltpu.VMEM((rows, dim), BF), pltpu.VMEM((rows, dim), BF), low, low, low, pltpu.VMEM((heads,) + probs.shape[1:], BF),
                        WEIGHT_SEMS, pltpu.SemaphoreType.DMA((4,)), pltpu.SemaphoreType.DMA((2,))],
        compiler_params=limit(60),
        cost_estimate=cost(2 * rows * dim * (dim + 2 * seq_len), 2 * (dim * dim + 5 * rows * dim)),
    )(spots, g1_low, *sources, q, k, v, probs)


def attention_backward_last(spots, g1, halfway, sources, q, k, v, probs):
    rows, dim = g1.shape
    heads, seq_len = probs.shape[0] // 2, probs.shape[1]
    low = pltpu.VMEM((rows // 2, dim), BF)
    return pl.pallas_call(
        attention_back_last_kernel,
        out_shape=jax.ShapeDtypeStruct((rows, dim), BF),
        in_specs=[SMEM] + [ANY] * (len(sources) + 9),
        out_specs=VMEM,
        scratch_shapes=[pltpu.VMEM((rows, dim), F32), low, low, low, low, pltpu.VMEM((4, dim, dim), BF), low, low, low, pltpu.VMEM((heads,) + probs.shape[1:], BF), low, low, low,
                        WEIGHT_SEMS, pltpu.SemaphoreType.DMA((4,)), pltpu.SemaphoreType.DMA((5,))],
        compiler_params=limit(60),
        cost_estimate=cost(2 * rows * dim * (3 * dim + 2 * seq_len), 2 * (3 * dim * dim + 5 * rows * dim)),
    )(spots, g1, *halfway, *sources, q, k, v, probs)


def shards(
    tokens, lengths, adapter_mask, cotangent, att_query, att_key, att_value, att_out,
    norm1_gain, norm1_bias, ffn_in, ffn_bias, ffn_out, adapt_down, adapt_up, norm2_gain,
    norm2_bias, joining_query, joining_key, joining_value, joining_qbias, joining_vbias,
):
    groups = lax.axis_size("tensor")
    dp_size = lax.axis_size("dp")
    my_z = lax.axis_index("tensor")
    my_d = lax.axis_index("dp")
    seq_local, seq_len, dim = tokens.shape
    mine = seq_local // groups
    rows = mine * seq_len
    adapters, neck = adapt_up.shape[0], adapt_up.shape[1]
    own_rows = joining_query.shape[0]

    gather = Gather(dp_size, groups, my_d, my_z, mine)
    spots = gather.spots
    biases = lax.dynamic_update_slice(
        jnp.zeros((8, dim), BF), jnp.stack([joining_qbias, joining_vbias]), (0, (my_d * groups + my_z) * own_rows)
    )
    att_mats = [att_query.T, att_key.T, att_value.T, att_out]
    join_part = jnp.concatenate([joining_query, joining_key, joining_value, biases], axis=0)

    def my_slice(array):
        return lax.dynamic_slice_in_dim(array, my_z * mine, mine, 0)

    x = my_slice(tokens).reshape(rows, dim)
    shifts = jnp.arange(128, dtype=jnp.int32)
    bits = jnp.right_shift(my_slice(adapter_mask)[:, None], jnp.minimum(shifts, adapters)[None, :]) % 2
    avail = jnp.where(shifts[None, :] < adapters, bits, 0)[:, None, :]
    norms = jnp.stack([norm1_gain, norm1_bias, norm2_gain, norm2_bias])
    lens = my_slice(lengths)
    owner = jnp.arange(adapters * neck, dtype=jnp.int32) // neck
    member = (owner[:, None] == shifts[None, :]).astype(BF)
    member_t = (shifts[:, None] == owner[None, :]).astype(BF)
    kept = {}

    def attend(sources):
        kept["att"] = attention_forward(spots, lens, x, sources, norms, seq_len)
        return [kept["att"][4]]

    def feed(sources):
        kept["ffn"] = ffn_forward(spots, kept["att"][4], sources, ffn_bias, ffn_in.shape[1])
        return [kept["ffn"][0]]

    if gather.paired:
        own = [att_mats, [ffn_in], None, [ffn_out]]
        steps = [
            lambda got: [],
            lambda got: [],
            lambda got: attend(got[0] + own[0]),
            lambda got: feed(got[1] + own[1]),
            lambda got: [],
            lambda got: [],
        ]
        quarter = att_mats[3]
        for i in range(3):
            quarter = jnp.where(my_d // 2 == i, att_mats[i], quarter)
        half = gather.half_of(quarter)
        rounds = [(half, tie(quarter, half))]
        shards_in, shards_out = tie(ffn_in, half), tie(ffn_out, half)
        in_quarter, in_half, out_quarter, out_half = cut(spots, [shards_in, shards_out])
        rounds += [(in_half, in_quarter), (out_half, out_quarter)]
        join_part = tie(join_part, *rounds[0])
        theirs = send(join_part, CORE)
        even = lax.rem(my_d, 2) == 0
        pair = jnp.concatenate([jnp.where(even, join_part, theirs), jnp.where(even, theirs, join_part)], axis=0)
        rounds.insert(2, (join_part, pair, join_part, theirs))
        got = gather.all_rounds(rounds, [x, norms, lens, avail, member, member_t, spots], steps)
        att_sources, in_sources, out_sources = (got[i] + own[i] for i in (0, 1, 3))
        join_sources = got[2]
    else:
        att_pack = jnp.concatenate(att_mats, axis=0)
        att_sources = gather.whole(gather.part_of(att_pack), True)
        in_sources, out_sources = (gather.whole(gather.part_of(shard)) for shard in (ffn_in, ffn_out))
        join_sources = [lax.all_gather(join_part, ("dp", "tensor"), axis=0)]
    up = adapt_up.reshape(adapters * neck, dim)
    cot = cotangent.reshape(rows, dim)

    def rest(att, ffn, avail, cot):
        q, k, v, probs, low1, xhat1, rstd1 = att
        act, slope = ffn
        layer_out, g2, g_ffn, *grads = joining(
            spots, gather.paired, act, out_sources, adapt_down, up, join_sources, member, member_t, avail, xhat1, norms, cot
        )
        done = {}

        def between(start):
            gradient = g_ffn if start is None else tie(g_ffn, start)
            done["g1"], g1_low = ffn_backward(spots, gradient, slope, out_sources, in_sources, g2, xhat1, rstd1, norms)
            done["half"] = attention_backward_first(spots, g1_low, att_sources, q, k, v, probs)
            return done["half"][1]

        def at_last(start):
            halfway = done["half"] if start is None else [tie(done["half"][0], start)] + list(done["half"][1:])
            return attention_backward_last(spots, done["g1"], halfway, att_sources, q, k, v, probs)

        return layer_out, grads, between, at_last

    if gather.paired:
        layer_out, grads, between, at_last = rest(kept["att"], kept["ffn"], avail, cot)
        (d_q, d_k, d_v, d_bias), input_grad = reduce_grads(gather, grads, own_rows, between, at_last)
    else:
        outs = []
        for first in range(0, mine, 2):
            at = slice(first * seq_len, (first + 2) * seq_len)
            att = attention_forward(spots, lens[first : first + 2], x[at], att_sources, norms, seq_len)
            ffn = ffn_forward(spots, att[4], in_sources, ffn_bias, ffn_in.shape[1])
            outs.append(rest(att, ffn, avail[first : first + 2], cot[at]))
        layer_out = jnp.concatenate([out[0] for out in outs])
        grads = [sum(out[1][i] for out in outs) for i in range(2)]
        (d_q, d_k, d_v, d_bias), input_grad = reduce_grads(
            gather, grads, own_rows, lambda start: [out[2](None) for out in outs],
            lambda start: jnp.concatenate([out[3](None) for out in outs]),
        )
    d_bias = lax.dynamic_slice_in_dim(d_bias[:2], (my_d * groups + my_z) * own_rows, own_rows, 1)
    return (
        layer_out.reshape(mine, seq_len, dim),
        input_grad.reshape(mine, seq_len, dim),
        d_q, d_k, d_v, d_bias[0], d_bias[1],
    )


def solution(mesh):
    both = P(ALL, None)
    return jax.shard_map(
        shards,
        mesh=mesh,
        in_specs=(
            P("dp", None, None), P("dp"), P("dp"), P(ALL, None, None),
            P(None, "tensor"), P(None, "tensor"), P(None, "tensor"), P("tensor", None),
            P(), P(), P(None, "tensor"), P(), P("tensor", None), P(), P(), P(), P(),
            both, both, both, P(ALL), P(ALL),
        ),
        out_specs=(P(ALL, None, None), P(ALL, None, None), both, both, both, P(ALL), P(ALL)),
        check_vma=False,
    )
```

```python
from functools import partial
import math

import jax
import jax.numpy as jnp
from jax import lax
from jax.experimental import pallas as pl
from jax.experimental.pallas import tpu as pltpu
from jax.sharding import PartitionSpec as P

HEADS = 12
EPS = 1e-05
MASKED = -1e30
ALL = ("dp", "tensor")
BF = jnp.bfloat16
F32 = jnp.float32


def mm(left, right):
    return jnp.dot(left, right, preferred_element_type=F32)


def mm_t(left, right):
    return lax.dot_general(left, right, (((1,), (1,)), ((), ())), preferred_element_type=F32)


def t_mm(left, right):
    return lax.dot_general(left, right, (((0,), (0,)), ((), ())), preferred_element_type=F32)


def norm_parts(values):
    average = jnp.mean(values, axis=-1, keepdims=True)
    centered = values - average
    variance = jnp.mean(centered * centered, axis=-1, keepdims=True)
    rstd = lax.rsqrt(variance + EPS)
    return centered * rstd, rstd


def norm_back(grad, gain, xhat, rstd):
    scaled = grad * gain
    return rstd * (
        scaled
        - jnp.mean(scaled, axis=-1, keepdims=True)
        - xhat * jnp.mean(scaled * xhat, axis=-1, keepdims=True)
    )


def gelu_parts(pre):
    cdf = 0.5 * (1.0 + lax.erf(pre * (1.0 / math.sqrt(2.0))))
    pdf = jnp.exp(-0.5 * pre * pre) * (1.0 / math.sqrt(2.0 * math.pi))
    return pre * cdf, cdf + pre * pdf


def limit(mebibytes):
    return pltpu.CompilerParams(vmem_limit_bytes=mebibytes * 2**20)


VMEM = pl.BlockSpec(memory_space=pltpu.VMEM)
SMEM = pl.BlockSpec(memory_space=pltpu.SMEM)
LITTLE = limit(24)
FAR_XY = [(i, i ^ 6) for i in range(8)]
CORE = [(i, i ^ 1) for i in range(8)]
ALONG_X = [(i, i ^ 2) for i in range(8)]
ALONG_Y = [(i, i ^ 4) for i in range(8)]
SPLIT_XY = [(i, i ^ (4 if i & 1 else 2)) for i in range(8)]
CROSS_XY = [(i, i ^ (3 if i & 1 else 5)) for i in range(8)]


def send(array, pairs):
    return lax.ppermute(array, "dp", pairs)


def shift(array, by, groups):
    return lax.ppermute(array, "tensor", [(i, (i + by) % groups) for i in range(groups)])


def scoped(name, step, *args):
    with jax.named_scope(name):
        return step(*args)


def tie(array, *others):
    return lax.optimization_barrier((array,) + others)[0]


def fetch_blocks(spots_ref, sources, stage_ref, sem):
    if len(sources) == 1:
        pltpu.make_async_copy(sources[0], stage_ref, sem).start()
        return
    planes = planes_in_order(spots_ref)
    for k, (ref, first) in enumerate(views(sources)):
        for i, plane in enumerate(planes[1:] + planes[:1]):
            pltpu.make_async_copy(ref.at[first + i], stage_ref.at[spots_ref[k] * len(planes) + plane], sem).start()


def order_rows(stage_ref, join_ref, biases_ref):
    blocks = stage_ref.shape[0]
    rows = join_ref.shape[1] // blocks
    total = 0.0
    for b in range(0, blocks, 2):
        pair = [stage_ref[b + i].astype(F32) for i in range(2)]
        for m in range(3):
            both = jnp.concatenate([block[m * rows : (m + 1) * rows] for block in pair], axis=0)
            join_ref[m, b * rows : (b + 2) * rows, :] = both.astype(BF)
        total = total + pair[0][3 * rows :] + pair[1][3 * rows :]
    biases_ref[...] = total


def fetch(spots_ref, sources, out_ref, sems, which, side_by_side=False):
    planes = planes_in_order(spots_ref)
    dim = sources[-1].shape[-1]
    rows = sources[-1].shape[-2]

    def copy(source, r, at):
        if side_by_side:
            target = out_ref.at[at, pl.ds(r * dim, dim)]
        else:
            target = out_ref.at[pl.ds(r * rows + at.start, at.size)]
        pltpu.make_async_copy(source, target, sems.at[r]).start()

    for r in which:
        if len(sources) == 1:
            copy(sources[0].at[planes[r]], r, pl.ds(0, rows))
        elif r == 0:
            copy(sources[-1], r, pl.ds(0, rows))
        else:
            for k, (ref, first) in enumerate(views(sources[:-1])):
                part = ref.shape[1]
                copy(ref.at[first + r - 1], r, pl.ds(pl.multiple_of(spots_ref[k] * part, part), part))


def arrive(out_ref, sems, r, side_by_side=False):
    dim = out_ref.shape[0] if side_by_side else out_ref.shape[1]
    block = out_ref.at[:, pl.ds(r * dim, dim)] if side_by_side else out_ref.at[pl.ds(r * out_ref.shape[0] // 4, out_ref.shape[0] // 4)]
    pltpu.make_async_copy(block, block, sems.at[r]).wait()


def fetch_stacked(spots_ref, sources, out_ref, sems, last):
    groups, dim = out_ref.shape[0], out_ref.shape[1]
    chosen = range(groups - 1, groups) if last else range(groups - 1)
    if len(sources) == 1:
        for m in chosen:
            pltpu.make_async_copy(sources[0].at[m], out_ref.at[m], sems.at[m]).start()
        return
    own = sources[-groups:]
    pieces = views(sources[:-groups])
    width, rows = dim // groups, pieces[0][0].shape[1]
    per = width // rows
    my_z = spots_ref[8]
    for m in chosen:
        at = pl.ds(pl.multiple_of(my_z * width, width), width)
        pltpu.make_async_copy(own[m], out_ref.at[m, at], sems.at[m]).start()
    for k, (ref, first) in enumerate(pieces):
        e = spots_ref[k]
        m = lax.div(e, per)

        @pl.when((m == groups - 1) == last)
        def _():
            for i, plane in enumerate(planes_in_order(spots_ref)[1:]):
                at = pl.ds(pl.multiple_of(plane * width + lax.rem(e, per) * rows, rows), rows)
                pltpu.make_async_copy(ref.at[first + i], out_ref.at[m, at], sems.at[m]).start()


def arrive_stacked(out_ref, sems, m):
    pltpu.make_async_copy(out_ref.at[m], out_ref.at[m], sems.at[m]).wait()


def views(sources):
    if len(sources) == 8:
        return [(source, 0) for source in sources]
    both, near, far, swapped, swapped_far = sources
    count = far.shape[0]
    return [(both, 0), (both, count), (near, 0), (near, count), (far, 0), (swapped, 0), (swapped, count), (swapped_far, 0)]


def cut_kernel(spots_ref, *refs):
    count = (len(refs) - 1) // 3
    shards, outs, sems = refs[:count], refs[count:-1], refs[-1]
    pairs = []
    for i, shard in enumerate(shards):
        rows = outs[2 * i].shape[0]
        at = pl.ds(pl.multiple_of(lax.div(spots_ref[0], 2) * rows, rows), rows)
        pairs.append((shard.at[at], outs[2 * i]))
        at = pl.ds(pl.multiple_of(spots_ref[0] * (rows // 2), rows // 2), rows // 2)
        pairs.append((shard.at[at], outs[2 * i + 1]))
    for copy in begin(pairs, sems):
        copy.wait()


def cut(spots, shards):
    outs = []
    for shard in shards:
        rows, dim = shard.shape
        outs += [jax.ShapeDtypeStruct((rows // 4, dim), BF), jax.ShapeDtypeStruct((rows // 8, dim), BF)]
    return pl.pallas_call(
        cut_kernel,
        out_shape=outs,
        in_specs=[SMEM] + [ANY] * len(shards),
        out_specs=[VMEM] * len(outs),
        scratch_shapes=[pltpu.SemaphoreType.DMA((len(outs),))],
        compiler_params=limit(60),
    )(spots, *shards)


def merge_kernel(spots_ref, *refs, count):
    beside, across, beside2, across2, *own = refs[:count]
    outs = refs[count:]
    core = lax.rem(spots_ref[0], 2)
    rows = across.shape[0]
    blocks = 3 + len(own) // 2
    sides = [outs[0], outs[1]] if len(outs) == 2 else [outs[0].at[pl.ds(i * blocks, blocks)] for i in range(2)]
    parts = [pl.ds(pl.multiple_of(at * rows, rows), rows) for at in (core, 1 - core)]
    for side, at, last, mine in zip(sides, parts, (across, across2), own or (None, None)):
        side[core] = beside[at, :]
        side[1 - core] = beside2[at, :]
        side[2] = last[...]
        if mine is not None:
            side[3] = mine[...]


def merge(spots, arrays, split):
    rows, dim = arrays[1].shape
    blocks = 3 + (len(arrays) - 4) // 2
    outs = [blocks, blocks] if split else [2 * blocks]
    return pl.pallas_call(
        partial(merge_kernel, count=len(arrays)),
        out_shape=[jax.ShapeDtypeStruct((out, rows, dim), BF) for out in outs],
        in_specs=[SMEM] + [VMEM] * len(arrays),
        out_specs=[VMEM] * len(outs),
        compiler_params=limit(8),
    )(spots, *arrays)


def planes_in_order(spots_ref, groups=4):
    return [lax.rem(spots_ref[8] + step, groups) for step in (0, 1, groups - 1, 2)]


def begin(pairs, sems):
    copies = [pltpu.make_async_copy(source, target, sems.at[i]) for i, (source, target) in enumerate(pairs)]
    for one in copies:
        one.start()
    return copies


WEIGHT_SEMS = pltpu.SemaphoreType.DMA((4,))
ANY = pl.BlockSpec(memory_space=pltpu.HBM)


class Gather:
    def __init__(self, dp_size, groups, my_d, my_z, seqs):
        self.dp_size, self.groups, self.my_d, self.my_z = dp_size, groups, my_d, my_z
        self.paired = dp_size == 8 and groups == 4 and seqs == 2
        core = lax.rem(my_d, 2)
        even = [0, 1, 2, 3, 7, 5, 4, 6]
        odd = [0, 1, 4, 5, 7, 3, 2, 6]
        flips = jnp.where(core == 0, jnp.array(even, jnp.int32), jnp.array(odd, jnp.int32))
        self.spots = jnp.concatenate([jnp.bitwise_xor(my_d, flips), my_z[None]]).astype(jnp.int32)

    def all_parts(self, part):
        whole = lax.all_gather(part, ("dp", "tensor"), axis=0)
        return whole.reshape((self.dp_size, self.groups) + part.shape).transpose(1, 0, 2, 3)

    def part_of(self, shard):
        rows = shard.shape[0] // self.dp_size
        return lax.dynamic_slice_in_dim(shard, self.my_d * rows, rows, 0)

    def all_rounds(self, parts, early, steps):
        count = len(parts)
        gathered, spread = [], []
        ahead, done = self.planes(parts[0], 0), [rows for part in parts[1:] for rows in part[:2]] + early
        for r in range(count + 2):
            with jax.named_scope("round%d" % r):
                ready = list(lax.optimization_barrier((*ahead, *done))) if r < count else list(done)
                ahead = ready[: len(ahead)]
                if r >= 1:
                    at = len(ahead)
                    if r <= count:
                        last = spread[r - 1]
                        last[1] = ready[at : at + len(last[1])]
                        at += len(last[1])
                    if 2 <= r <= count:
                        spread[r - 2][2] = ready[at]
                done = []
                if 1 <= r < count:
                    near_half = last[1][0] if len(last[1]) == 2 else last[1][0][: last[1][0].shape[0] // 2]
                    last.append(scoped("far", send, near_half, CROSS_XY))
                if r < count:
                    beside, across = ahead
                    ahead = []
                    if r + 1 < count:
                        ahead = self.planes([tie(rows, beside) for rows in parts[r + 1]], r + 1)
                    others = [scoped("others", send, beside, CORE), scoped("others", send, across, CORE)]
                    both = merge(self.spots, [beside, across, *others, *parts[r][2:]], r == count - 1)
                    near = [scoped("near", send, side, SPLIT_XY) for side in both]
                    spread.append([both, near])
                    done += near
                else:
                    ahead = []
                if 1 <= r <= count:
                    late = []
                    last.append([scoped("swap", send, array, CORE) for array in last[1][:-1]])
                    last[3].append(scoped("swap", send, tie(last[1][-1], *late), CORE))
                    done += (last[2:3] if r < count else []) + last[3]
                if r >= 2:
                    whole = spread[r - 2]
                    gathered.append([*whole[0], *whole[1], whole[2], *whole[3], scoped("swapfar", send, whole[2], CORE)])
                done += steps[r](gathered)
                if r == count - 1:
                    spread[r].append(scoped("far", send, tie(near[0], *done[len(near) :]), CROSS_XY))
        return gathered

    def planes(self, part, r):
        with jax.named_scope("planes%d" % r):
            groups = self.groups
            pairs = [
                (d * groups + z, d * groups + (z + (1 if d & 1 else groups - 1)) % groups)
                for d in range(self.dp_size)
                for z in range(groups)
            ]
            beside = scoped("beside", lax.ppermute, part[1], ("dp", "tensor"), pairs)
            return beside, scoped("across", shift, part[0], 2, groups)

    def half_of(self, quarter):
        rows = quarter.shape[0] // 2
        return jnp.where(lax.rem(self.my_d, 2) == 0, quarter[:rows], quarter[rows:])

    def quarter_of(self, shard):
        rows = 2 * shard.shape[0] // self.dp_size
        return lax.dynamic_slice_in_dim(shard, self.my_d // 2 * rows, rows, 0)

    def whole(self, part, stacked=False):
        whole = self.all_parts(part)
        dim = part.shape[1]
        if stacked:
            whole = whole.reshape(self.groups, 4, -1, dim).transpose(1, 0, 2, 3)
        return [whole.reshape(4, -1, dim)]


def reduce_grads(gather, grads, own_rows, between, at_last):
    groups, spots = gather.groups, gather.spots
    if not gather.paired:
        mats, bias = grads
        mats = lax.psum_scatter(mats, ("dp", "tensor"), scatter_dimension=1, tiled=True)
        middle = between(None)
        return (mats[0], mats[1], mats[2], lax.psum(bias, ("dp", "tensor"))), at_last(None)
    keep, away = grads
    rows, dim = keep.shape[1:]
    low = jax.ShapeDtypeStruct((rows, dim), BF)
    come = scoped("cores", send, away, CORE)
    to_x, to_y, to_far = pl.pallas_call(
        add_cores_kernel,
        out_shape=[low, low, low],
        in_specs=[SMEM, ANY, ANY],
        out_specs=[ANY] * 3,
        scratch_shapes=[pltpu.VMEM((3, rows, dim), BF)] * 3 + [pltpu.SemaphoreType.DMA((6,)), pltpu.SemaphoreType.DMA((3,))],
        compiler_params=limit(60),
    )(spots, keep, come)
    from_far = scoped("far", send, to_far, FAR_XY)
    from_x = scoped("x", send, to_x, ALONG_X)
    from_y = scoped("y", send, to_y, ALONG_Y)
    block = jax.ShapeDtypeStruct((3 * own_rows + 8, dim), BF)
    middle = between(to_far)
    mine, *goes = pl.pallas_call(
        add_plane_kernel,
        out_shape=[jax.ShapeDtypeStruct((3 * own_rows + 8, dim), F32)] + [block] * (groups - 1),
        in_specs=[SMEM] + [ANY] * 5,
        out_specs=[VMEM] * groups,
        scratch_shapes=[pltpu.VMEM((rows - 16, dim), F32), pltpu.VMEM((5, rows, dim), BF), pltpu.SemaphoreType.DMA((5,))],
        compiler_params=limit(60),
    )(spots, from_x, from_y, from_far, tie(keep, middle), come)
    after = at_last(mine)
    comes = [scoped("stack%d" % i, shift, go, i + 1, groups) for i, go in enumerate(goes)]
    part = jax.ShapeDtypeStruct((own_rows, dim), F32)
    sums = pl.pallas_call(
        add_stack_kernel,
        out_shape=[part, part, part, jax.ShapeDtypeStruct((8, dim), F32)],
        in_specs=[VMEM] * groups,
        out_specs=[VMEM] * 4,
        compiler_params=LITTLE,
    )(mine, *comes)
    return sums, after


def cost(flops, moved, exps=0):
    return pl.CostEstimate(flops=int(flops), bytes_accessed=int(moved), transcendentals=int(exps))


def head_masks():
    lane = lax.broadcasted_iota(jnp.int32, (1, 128), 1)
    first = (lane < 64).astype(F32)
    return [first.astype(BF), (1.0 - first).astype(BF)], lane < 64


def attention_kernel(spots_ref, len_ref, x_ref, norms_ref, *refs):
    *sources, q_hbm, k_hbm, v_hbm, p_hbm, low_ref, xhat_hbm, rstd_ref, w_ref, ctx_ref, q_ref, k_ref, v_ref, p_ref, xhat_ref, sems, store_sems = refs
    fetch_stacked(spots_ref, sources, w_ref, sems, False)
    fetch_stacked(spots_ref, sources, w_ref, sems, True)
    rows, dim = x_ref.shape
    for m in range(4):
        arrive_stacked(w_ref, sems, m)
    seq_len = p_ref.shape[1]
    x = x_ref[...]
    q_ref[...] = (mm_t(x, w_ref[0]).astype(BF).astype(F32) * (1.0 / math.sqrt(dim // HEADS))).astype(BF)
    k_ref[...] = mm_t(x, w_ref[1]).astype(BF)
    v_ref[...] = mm_t(x, w_ref[2]).astype(BF)
    stores = begin(((q_ref, q_hbm), (k_ref, k_hbm), (v_ref, v_hbm)), store_sems)
    masks, first = head_masks()
    key_at = lax.broadcasted_iota(jnp.int32, (seq_len, 1), 0)

    for s in range(rows // seq_len):
        at = slice(s * seq_len, (s + 1) * seq_len)
        valid = key_at < len_ref[s]
        for j in range(HEADS // 2):
            cols = slice(128 * j, 128 * (j + 1))
            q, k, v = q_ref[at, cols], k_ref[at, cols], v_ref[at, cols]
            parts = []
            for h in range(2):
                scores = jnp.where(valid, mm_t(k, q * masks[h]), MASKED)
                exps = jnp.exp(scores - jnp.max(scores, axis=0, keepdims=True))
                probs = (exps * (1.0 / jnp.sum(exps, axis=0, keepdims=True))).astype(BF)
                p_ref[s * HEADS + 2 * j + h] = probs
                parts.append(t_mm(probs, v))
            ctx_ref[at, cols] = jnp.where(first, parts[0], parts[1]).astype(BF)
        heads = pl.ds(s * HEADS, HEADS)
        stores += begin(((p_ref.at[heads], p_hbm.at[heads]),), store_sems.at[pl.ds(3 + s, 1)])
    xhat, rstd = norm_parts(x.astype(F32) + mm(ctx_ref[...], w_ref[3]))
    xhat_ref[...] = xhat
    stores += begin(((xhat_ref, xhat_hbm),), store_sems.at[pl.ds(3 + rows // seq_len, 1)])
    rstd_ref[...] = rstd
    low_ref[...] = (xhat * norms_ref[0:1, :] + norms_ref[1:2, :]).astype(BF)
    for store in stores:
        store.wait()


def attention_forward(spots, lengths, x, sources, norms, seq_len):
    rows, dim = x.shape
    seqs = rows // seq_len
    low = jax.ShapeDtypeStruct((rows, dim), BF)
    return pl.pallas_call(
        attention_kernel,
        out_shape=[low, low, low,
                   jax.ShapeDtypeStruct((seqs * HEADS, seq_len, seq_len), BF), low,
                   jax.ShapeDtypeStruct((rows, dim), F32), jax.ShapeDtypeStruct((rows, 1), F32)],
        in_specs=[SMEM] * 2 + [VMEM] * 2 + [ANY] * len(sources),
        out_specs=[ANY] * 4 + [VMEM, ANY, VMEM],
        scratch_shapes=[pltpu.VMEM((4, dim, dim), BF)] + [pltpu.VMEM((rows, dim), BF)] * 4 + [
            pltpu.VMEM((seqs * HEADS, seq_len, seq_len), BF), pltpu.VMEM((rows, dim), F32),
            WEIGHT_SEMS, pltpu.SemaphoreType.DMA((4 + seqs,)),
        ],
        compiler_params=limit(60),
        cost_estimate=cost(2 * rows * dim * (4 * dim + 2 * seq_len), 2 * (4 * dim * dim + 8 * rows * dim), rows * seq_len * HEADS),
    )(spots, lengths, x, norms, *sources)


def by_rows(rows, step, work, unroll=1):
    work(slice(0, rows))


def ffn_in_kernel(spots_ref, x_ref, bias_ref, *refs):
    *sources, act_hbm, slope_hbm, act_ref, slope_ref, w_ref, pre_ref, sems, store_sems = refs
    units = pre_ref.shape[1]
    order = planes_in_order(spots_ref)
    stores = []
    fetch(spots_ref, sources, w_ref, sems, [0, 1])
    for r in range(4):
        fetch(spots_ref, sources, w_ref, sems, [r + 2] if r < 2 else [])
        arrive(w_ref, sems, r)
        pre_ref[...] = mm(x_ref[...], w_ref[r * x_ref.shape[1] : (r + 1) * x_ref.shape[1], :])
        cols = slice(r * units, (r + 1) * units)
        act, slope = gelu_parts(pre_ref[...] + bias_ref[order[r]])
        act_ref[:, cols] = act.astype(BF)
        slope_ref[:, cols] = slope.astype(BF)
        pairs = [(act_ref, act_hbm), (slope_ref, slope_hbm)]
        stores += begin([(ref.at[:, cols], hbm.at[:, cols]) for ref, hbm in pairs], store_sems.at[pl.ds(2 * r, 2)])
    for store in stores:
        store.wait()


def ffn_forward(spots, x, sources, bias, units):
    rows, dim = x.shape
    planes = bias.shape[0] // units
    out = jax.ShapeDtypeStruct((rows, planes * units), BF)
    return pl.pallas_call(
        ffn_in_kernel,
        out_shape=[out, out],
        in_specs=[SMEM] + [VMEM] * 2 + [ANY] * len(sources),
        out_specs=[ANY] * 2,
        scratch_shapes=[
            pltpu.VMEM((rows, planes * units), BF), pltpu.VMEM((rows, planes * units), BF),
            pltpu.VMEM((planes * dim, units), BF), pltpu.VMEM((rows, units), F32), WEIGHT_SEMS, pltpu.SemaphoreType.DMA((8,)),
        ],
        compiler_params=limit(60),
        cost_estimate=cost(2 * rows * dim * units * planes, 2 * planes * units * (dim + 2 * rows), 2 * rows * units * planes),
    )(spots, x, bias.reshape(planes, 1, units), *sources)


def two_pass(values, table):
    high = values.astype(BF)
    return mm(high, table) + mm((values - high.astype(F32)).astype(BF), table)


def put_rows(ref, mats, bias):
    at = 0
    for mat in mats:
        ref[at : at + mat.shape[0], :] = mat.astype(BF)
        at += mat.shape[0]
    high = bias.astype(BF).astype(F32)
    ref[at : at + 16, :] = jnp.concatenate([high, bias - high], axis=0).astype(BF)


def sum_rows(arrays):
    total = arrays[0].astype(F32)
    for array in arrays[1:]:
        total = total + array.astype(F32)
    rows = total.shape[0] - 16
    return total[:rows], total[rows : rows + 8] + total[rows + 8 :]


def add_cores_kernel(spots_ref, keep_hbm, come_hbm, *refs):
    hbm, (sums_ref, keep_ref, come_ref, sems, store_sems) = refs[:3], refs[3:]
    quarter = lax.div(spots_ref[0], 2)
    pairs = []
    for i in range(3):
        q = jnp.bitwise_xor(quarter, i + 1)
        pairs += [(keep_hbm.at[q], keep_ref.at[i]), (come_hbm.at[q], come_ref.at[i])]
    copies = begin(pairs, sems)
    stores = []
    for i in range(3):
        copies[2 * i].wait()
        copies[2 * i + 1].wait()
        mats, bias = sum_rows([keep_ref[i], come_ref[i]])
        put_rows(sums_ref.at[i], [mats], bias)
        stores += begin(((sums_ref.at[i], hbm[i]),), store_sems.at[pl.ds(i, 1)])
    for store in stores:
        store.wait()


def fold_bias(bias):
    high = bias.astype(BF).astype(F32)
    row = lax.broadcasted_iota(jnp.int32, (8, 1), 0)
    return jnp.where(row < 4, high, pltpu.roll(bias - high, 4, 0))


def add_plane_kernel(spots_ref, *refs):
    parts, refs = refs[:3], refs[3:]
    keep_hbm, come_hbm, mine_ref, *go_refs, total_ref, arrays_ref, sems = refs
    quarter = lax.div(spots_ref[0], 2)
    sources = (keep_hbm.at[quarter], come_hbm.at[quarter], *parts)
    for copy in begin([(source, arrays_ref.at[i]) for i, source in enumerate(sources)], sems):
        copy.wait()
    total_ref[...], bias = sum_rows([arrays_ref[i] for i in range(5)])
    groups = len(go_refs) + 1
    width = total_ref.shape[0] // 3
    rows = width // groups

    def block(plane):
        at = [pl.multiple_of(i * width + plane * rows, 8) for i in range(3)]
        return jnp.concatenate([total_ref[pl.ds(a, rows), :] for a in at], axis=0)

    my_z = spots_ref[8]
    mine_ref[...] = jnp.concatenate([block(my_z), bias], axis=0)
    folded = fold_bias(bias)
    for i, ref in enumerate(go_refs):
        ref[...] = jnp.concatenate([block(lax.rem(my_z + i + 1, groups)), folded], axis=0).astype(BF)


def add_stack_kernel(mine_ref, *refs):
    come_refs, (q_ref, k_ref, v_ref, bias_ref) = refs[:-4], refs[-4:]
    total = mine_ref[...]
    rows = q_ref.shape[0]
    for ref in come_refs:
        come = ref[...].astype(F32)
        bias = come[3 * rows :]
        total = total + jnp.concatenate([come[: 3 * rows], bias + pltpu.roll(bias, 4, 0)], axis=0)
    q_ref[...], k_ref[...], v_ref[...] = (total[i * rows : (i + 1) * rows] for i in range(3))
    bias_ref[...] = total[3 * rows :]


def joining_kernel(
    spots_ref, member_ref, member_t_ref, avail_ref, norms_ref, act_hbm, xhat1_hbm, cot_hbm, *refs, halves, count
):
    gain1, bias1, gain2, bias2 = (norms_ref[i : i + 1, :] for i in range(4))
    down_hbm, up_hbm, *refs = refs
    join_sources, sources, refs = refs[:count], refs[count:-38], refs[-38:]
    stage_ref, biases_ref, stage_sem, refs = refs[-3], refs[-2], refs[-1], refs[:-3]
    out_hbm, g2_hbm, g_ffn_ref, grad_hbm0, grad_hbm1 = refs[:5]
    act_ref, w_out_ref, down_ref, up_ref, join_ref, xhat1_ref, cot_ref, act_sems, out_sems, sems, store_sems = refs[5:16]
    ffn_ref, u_ref, w_ref, big_u_ref, big_w_ref, p_wide_ref, sums_ref = refs[16:23]
    x_ref, act2_ref, slope_ref, q_ref, gq_ref, low_ref, mixed_ref, t_ref = refs[23:31]
    out_ref, g2_ref, bias_rows_ref, bias_ref = refs[31:35]
    rows, dim = out_ref.shape
    units = w_out_ref.shape[0] // 4
    seqs = avail_ref.shape[0]
    per = rows // seqs
    everyone = [slice(i * per, (i + 1) * per) for i in range(seqs)]
    fscale = 1.0 / math.sqrt(dim)
    member, member_t = member_ref[...], member_t_ref[...]
    loads = []

    def issue(r):
        if r < 4:
            fetch(spots_ref, sources, w_out_ref, out_sems, [r])
            cols = pl.ds(r * units, units)
            loads.extend(begin(((act_hbm.at[:, cols], act_ref.at[:, cols]),), act_sems.at[pl.ds(r, 1)]))
        elif r == 4:
            fetch_blocks(spots_ref, join_sources, stage_ref, stage_sem)
        elif r == 5:
            pairs = ((down_hbm, down_ref), (up_hbm, up_ref), (xhat1_hbm, xhat1_ref), (cot_hbm, cot_ref))
            loads.extend(begin(pairs, sems))

    issue(0)
    issue(1)
    for r in range(4):
        issue(r + 2)
        loads[r].wait()
        arrive(w_out_ref, out_sems, r)
        if r % 2 == 1:
            both = slice((r - 1) * units, (r + 1) * units)
            for at in everyone:
                term = mm(act_ref[at, both], w_out_ref[both, :])
                ffn_ref[at, :] = term if r == 1 else ffn_ref[at, :] + term
    loads = loads[4:]
    for at in everyone:
        x_ref[at, :] = ffn_ref[at, :].astype(BF)
    pltpu.make_async_copy(stage_ref, stage_ref, stage_sem).wait()
    order_rows(stage_ref, join_ref, biases_ref)
    qb, vb = biases_ref[0:1, :], biases_ref[1:2, :]
    for load in loads:
        load.wait()
    up = up_ref[...]
    halves_of = {}

    def narrow(i, name, value=None):
        if value is not None:
            halves_of[i, name] = value
        return halves_of[i, name]

    def per_adapter(values):
        high = values.astype(BF)
        return mm(high, member) + mm((values - high.astype(F32)).astype(BF), member)

    def to_q(i, at):
        q_ref[at, :] = (mm(x_ref[at, :], join_ref[0]) + qb).astype(BF)

    def down(i, at):
        act, slope = gelu_parts(mm(x_ref[at, :], down_ref[...]))
        act2_ref[at, :] = act.astype(BF)
        slope_ref[at, :] = slope.astype(BF)

    def to_u(i, at):
        u = mm_t(q_ref[at, :], join_ref[1])
        u_ref[at, :] = u
        narrow(i, "dot", jnp.sum(ffn_ref[at, :] * u, axis=-1, keepdims=True))

    def scores(i, at):
        big_u = mm_t(u_ref[at, :].astype(BF), up)
        big_u_ref[at, :] = big_u
        fscores = (per_adapter(act2_ref[at, :].astype(F32) * big_u) + narrow(i, "dot")) * fscale
        fscores = jnp.where(avail_ref[i] > 0, fscores, MASKED)
        fexp = jnp.exp(fscores - jnp.max(fscores, axis=-1, keepdims=True))
        narrow(i, "probs", fexp / jnp.sum(fexp, axis=-1, keepdims=True))

    def mix(i, at):
        p_wide = two_pass(narrow(i, "probs"), member_t)
        p_wide_ref[at, :] = p_wide
        weighed = (p_wide * act2_ref[at, :].astype(F32)).astype(BF)
        mixed_ref[at, :] = (ffn_ref[at, :] + mm(weighed, up)).astype(BF)

    def norm(i, at):
        normed1 = xhat1_ref[at, :] * gain1 + bias1
        xhat2, rstd2 = norm_parts(normed1 + mm(mixed_ref[at, :], join_ref[2]) + vb)
        out_ref[at, :] = (xhat2 * gain2 + bias2).astype(BF)
        g2 = norm_back(cot_ref[at, :].astype(F32), gain2, xhat2, rstd2)
        g2_ref[at, :] = g2
        low_ref[at, :] = g2.astype(BF)
        narrow(i, "dot2", jnp.sum(g2 * vb, axis=-1, keepdims=True))
        narrow(i, "d_vb", jnp.sum(g2.reshape(-1, 8, dim), axis=0))

    def to_w(i, at):
        w = mm_t(low_ref[at, :], join_ref[2])
        w_ref[at, :] = w
        narrow(i, "dot2", narrow(i, "dot2") + jnp.sum(ffn_ref[at, :] * w, axis=-1, keepdims=True))

    def score_grads(i, at):
        big_w = mm_t(w_ref[at, :].astype(BF), up)
        big_w_ref[at, :] = big_w
        gvals = per_adapter(act2_ref[at, :].astype(F32) * big_w) + narrow(i, "dot2")
        fprobs = narrow(i, "probs")
        gs = fprobs * (gvals - jnp.sum(gvals * fprobs, axis=-1, keepdims=True)) * fscale
        narrow(i, "gs", gs)
        narrow(i, "gs_sum", jnp.sum(gs, axis=-1, keepdims=True))

    def to_t(i, at):
        wide = two_pass(narrow(i, "gs"), member_t)
        weighed = (wide * act2_ref[at, :].astype(F32)).astype(BF)
        grad = wide * big_u_ref[at, :] + p_wide_ref[at, :] * big_w_ref[at, :]
        slope_ref[at, :] = (grad * slope_ref[at, :].astype(F32)).astype(BF)
        t_ref[at, :] = (mm(weighed, up) + narrow(i, "gs_sum") * ffn_ref[at, :]).astype(BF)

    def to_gq(i, at):
        gq = mm(t_ref[at, :], join_ref[1]).astype(BF)
        gq_ref[at, :] = gq
        narrow(i, "d_qb", jnp.sum(gq.astype(F32).reshape(-1, 8, dim), axis=0))

    def all_halves(*steps):
        for step in steps:
            for i, at in enumerate(everyone):
                step(i, at)

    all_halves(to_q, down, to_u, scores, mix, norm)
    stores = begin(((out_ref, out_hbm), (g2_ref, g2_hbm)), store_sems)
    all_halves(to_w, score_grads)
    sums_ref[2] = t_mm(mixed_ref[...], low_ref[...]).astype(sums_ref.dtype)
    all_halves(to_t)
    sums_ref[1] = t_mm(t_ref[...], q_ref[...]).astype(sums_ref.dtype)
    all_halves(to_gq)
    sums_ref[0] = t_mm(x_ref[...], gq_ref[...]).astype(sums_ref.dtype)
    row = lax.broadcasted_iota(jnp.int32, (8, 1), 0)
    d_qb, d_vb = (
        jnp.sum(sum(narrow(i, name) for i in range(seqs)), axis=0, keepdims=True) for name in ("d_qb", "d_vb")
    )
    bias_ref[...] = jnp.where(row == 0, d_qb, jnp.where(row == 1, d_vb, 0.0))
    if halves:
        core = lax.rem(spots_ref[0], 2)
        part = dim // 8
        put_rows(bias_rows_ref, [], bias_ref[...])
        for hbm, side, sem in ((grad_hbm1, 1 - core, store_sems.at[2]), (grad_hbm0, core, store_sems.at[3])):
            for q in range(4):
                at = pl.ds(pl.multiple_of((2 * q + side) * part, part), part)
                for i in range(3):
                    pltpu.make_async_copy(sums_ref.at[i, at], hbm.at[q, pl.ds(i * part, part)], sem).start()
                pltpu.make_async_copy(bias_rows_ref, hbm.at[q, pl.ds(3 * part, 16)], sem).start()
            stores.append(pltpu.make_async_copy(hbm, hbm, sem))
    else:
        stores += begin(((sums_ref, grad_hbm0), (bias_ref, grad_hbm1)), store_sems.at[pl.ds(2, 2)])
    for i, at in enumerate(everyone):
        total = mm_t(slope_ref[at, :], down_ref[...]) + mm_t(gq_ref[at, :], join_ref[0])
        g_ffn_ref[at, :] = (narrow(i, "gs_sum") * u_ref[at, :] + w_ref[at, :] + total).astype(BF)
    for store in stores:
        store.wait()


def joining(spots, halves, act, sources, adapt_down, up, join_sources, member, member_t, avail, xhat1, norms, cot):
    rows, dim = xhat1.shape
    if halves:
        grads = [jax.ShapeDtypeStruct((4, 3 * dim // 8 + 16, dim), BF)] * 2
    else:
        grads = [jax.ShapeDtypeStruct((3, dim, dim), F32), jax.ShapeDtypeStruct((8, dim), F32)]
    wide, low = pltpu.VMEM((rows, dim), F32), pltpu.VMEM((rows, dim), BF)
    height, blocks = join_sources[-1].shape[-2:][0], 32
    stage_shape = join_sources[0].shape if len(join_sources) == 1 else (blocks, height, dim)
    return pl.pallas_call(
        partial(joining_kernel, halves=halves, count=len(join_sources)),
        out_shape=[
            jax.ShapeDtypeStruct((rows, dim), BF),
            jax.ShapeDtypeStruct((rows, dim), F32),
            jax.ShapeDtypeStruct((rows, dim), BF),
        ] + grads,
        in_specs=[SMEM] + [VMEM] * 4 + [ANY] * (len(sources) + len(join_sources) + 5),
        out_specs=[ANY, ANY, VMEM, ANY, ANY],
        scratch_shapes=[
            pltpu.VMEM(act.shape, BF),
            pltpu.VMEM((act.shape[1], dim), BF),
            pltpu.VMEM(adapt_down.shape, BF),
            pltpu.VMEM(up.shape, BF),
            pltpu.VMEM((3, dim, dim), BF),
            wide,
            low,
            WEIGHT_SEMS,
            WEIGHT_SEMS,
            pltpu.SemaphoreType.DMA((4,)),
            pltpu.SemaphoreType.DMA((4,)),
        ] + [wide] * 6 + [pltpu.VMEM((3, dim, dim), BF if halves else F32)] + [low] * 8 + [
            low,
            wide,
            pltpu.VMEM((16, dim), BF),
            pltpu.VMEM((8, dim), F32),
            pltpu.VMEM(stage_shape, BF),
            pltpu.VMEM((8, dim), F32),
            pltpu.SemaphoreType.DMA,
        ],
        compiler_params=limit(60),
        cost_estimate=cost(2 * rows * dim * (15 * dim + act.shape[1]), 2 * dim * (8 * dim + 10 * rows), 2 * rows * dim),
    )(spots, member, member_t, avail, norms, act, xhat1, cot, adapt_down, up, *join_sources, *sources)


def ffn_back_kernel(spots_ref, g_ref, rstd_ref, norms_ref, slope_hbm, g2_hbm, xhat_hbm, *refs, count):
    refs, (out_sources, in_sources) = refs[sum(count) :], (refs[: count[0]], refs[count[0] : sum(count)])
    g1_hbm, low_hbm, g1_ref, low_ref, slope_ref, g2_ref, xhat_ref, w_out_ref, w_in_ref, pre_ref, out_sems, in_sems, slope_sems, sems, store_sems = refs
    units = w_out_ref.shape[0] // 4
    rows = g_ref.shape[0]
    everyone = [slice(i * rows // 2, (i + 1) * rows // 2) for i in range(2)]
    loads = []

    def issue(r):
        if r < 4:
            fetch(spots_ref, out_sources, w_out_ref, out_sems, [r])
            cols = pl.ds(r * units, units)
            loads.extend(begin(((slope_hbm.at[:, cols], slope_ref.at[:, cols]),), slope_sems.at[pl.ds(r, 1)]))
        elif r < 8:
            fetch(spots_ref, in_sources, w_in_ref, in_sems, [r - 4], side_by_side=True)
        elif r == 8:
            loads.extend(begin(((g2_hbm, g2_ref), (xhat_hbm, xhat_ref)), sems))

    issue(0)
    issue(1)
    for r in range(4):
        issue(r + 2)
        cols = slice(r * units, (r + 1) * units)
        arrive(w_out_ref, out_sems, r)
        loads[r].wait()
        for at in everyone:
            pre_ref[at, cols] = (mm_t(g_ref[at, :], w_out_ref[cols, :]) * slope_ref[at, cols].astype(F32)).astype(BF)
    for r in range(4, 8):
        issue(r + 2)
        arrive(w_in_ref, in_sems, r - 4, side_by_side=True)
        if r == 5:
            both = slice(0, 2 * units)
            for at in everyone:
                g1_ref[at, :] = mm_t(pre_ref[at, both], w_in_ref[:, both])
    for load in loads[4:]:
        load.wait()
    both = slice(2 * units, 4 * units)
    stores = []
    for at in everyone:
        total = mm_t(pre_ref[at, both], w_in_ref[:, both]) + g1_ref[at, :] + g2_ref[at, :]
        g1 = norm_back(total, norms_ref[0:1, :], xhat_ref[at, :], rstd_ref[at, :])
        g1_ref[at, :] = g1
        low_ref[at, :] = g1.astype(BF)
        stores += begin(((g1_ref.at[at], g1_hbm.at[at]), (low_ref.at[at], low_hbm.at[at])), store_sems.at[pl.ds(len(stores), 2)])
    for store in stores:
        store.wait()


def ffn_backward(spots, g_ffn, slope, out_sources, in_sources, g2, xhat, rstd, norms):
    rows, dim = xhat.shape
    planes = 4
    units = slope.shape[1] // planes
    return pl.pallas_call(
        partial(ffn_back_kernel, count=(len(out_sources), len(in_sources))),
        out_shape=[jax.ShapeDtypeStruct((rows, dim), F32), jax.ShapeDtypeStruct((rows, dim), BF)],
        in_specs=[SMEM] + [VMEM] * 3 + [ANY] * (len(out_sources) + len(in_sources) + 3),
        out_specs=[ANY, ANY],
        scratch_shapes=[
            pltpu.VMEM((rows, dim), F32), pltpu.VMEM((rows, dim), BF),
            pltpu.VMEM(slope.shape, BF), pltpu.VMEM((rows, dim), F32), pltpu.VMEM((rows, dim), F32),
            pltpu.VMEM((planes * units, dim), BF), pltpu.VMEM((dim, planes * units), BF), pltpu.VMEM(slope.shape, BF),
            WEIGHT_SEMS, WEIGHT_SEMS, WEIGHT_SEMS, pltpu.SemaphoreType.DMA((2,)),
            pltpu.SemaphoreType.DMA((4,)),
        ],
        compiler_params=limit(60),
        cost_estimate=cost(4 * rows * dim * units * planes, 2 * planes * units * (2 * dim + rows)),
    )(spots, g_ffn, rstd, norms, slope, g2, xhat, *out_sources, *in_sources)


def attention_back_heads(s, seq_len, q_ref, k_ref, v_ref, p_ref, g_ref, dq_ref, dk_ref, dv_ref, first_seq):
    dim = q_ref.shape[1]
    scale = 1.0 / math.sqrt(dim // HEADS)
    masks = head_masks()[0]
    at = slice((s - first_seq) * seq_len, (s - first_seq + 1) * seq_len)
    for j in range(HEADS // 2):
        cols = slice(128 * j, 128 * (j + 1))
        q, k, v, g = q_ref[at, cols], k_ref[at, cols], v_ref[at, cols], g_ref[at, cols]
        split = [jnp.concatenate([array * mask for mask in masks], axis=0) for array in (q, k, g)]
        probs_low = [p_ref[(s - first_seq) * HEADS + 2 * j + h] for h in range(2)]
        g_scores = []
        for h in range(2):
            probs = probs_low[h].astype(F32)
            g_probs = mm_t(v, split[2][h * seq_len : (h + 1) * seq_len])
            g_scores.append((probs * (g_probs - jnp.sum(g_probs * probs, axis=0, keepdims=True))).astype(BF))
        dq_ref[at, cols] = (t_mm(jnp.concatenate(g_scores, axis=0), split[1]) * scale).astype(BF)
        dk_ref[at, cols] = mm(jnp.concatenate(g_scores, axis=1), split[0]).astype(BF)
        dv_ref[at, cols] = mm(jnp.concatenate(probs_low, axis=1), split[2]).astype(BF)


def load_heads(hbm, vmem, sems, first, count):
    seq_len = hbm[3].shape[1]
    rows, heads = pl.ds(first * seq_len, count * seq_len), pl.ds(first * HEADS, count * HEADS)
    pairs = [(hbm[i].at[rows], vmem[i]) for i in range(3)] + [(hbm[3].at[heads], vmem[3])]
    return begin(pairs, sems)


def input_rows(g1, grads, weights):
    total = g1
    for grad, weight in zip(grads, weights):
        total = total + mm(grad, weight)
    return total.astype(BF)


def attention_back_first_kernel(spots_ref, *refs):
    *refs, ctx_hbm, out_ref, w_ref, low_ref, g1_ref, ctx_ref, q_ref, k_ref, v_ref, p_ref, dq_ref, dk_ref, dv_ref, w_sems, sems, g_sems = refs
    low_hbm, g1_hbm, *sources, q_hbm, k_hbm, v_hbm, p_hbm = refs
    seq_len = p_ref.shape[1]
    rows, dim = low_ref.shape
    loads = begin(((low_hbm, low_ref),), g_sems.at[pl.ds(0, 1)])
    fetch_stacked(spots_ref, sources, w_ref, w_sems, True)
    seqs = q_ref.shape[0] // seq_len
    loads += load_heads((q_hbm, k_hbm, v_hbm, p_hbm), (q_ref, k_ref, v_ref, p_ref), sems, 0, seqs)
    loads[0].wait()
    arrive_stacked(w_ref, w_sems, 3)
    ctx_ref[...] = mm_t(low_ref[...], w_ref[3]).astype(BF)
    mine, later = pl.ds(0, seqs * seq_len), pl.ds(seqs * seq_len, rows - seqs * seq_len)
    store = begin(((ctx_ref.at[later], ctx_hbm),), g_sems.at[pl.ds(1, 1)])[0]
    for load in loads[1:]:
        load.wait()
    fetch_stacked(spots_ref, sources, w_ref, w_sems, False)
    load = begin(((g1_hbm.at[mine], g1_ref),), g_sems.at[pl.ds(2, 1)])[0]
    for s in range(seqs):
        attention_back_heads(s, seq_len, q_ref, k_ref, v_ref, p_ref, ctx_ref, dq_ref, dk_ref, dv_ref, 0)
    load.wait()
    for m in range(3):
        arrive_stacked(w_ref, w_sems, m)
    out_ref[...] = input_rows(g1_ref[...], (dq_ref[...], dk_ref[...], dv_ref[...]), (w_ref[0], w_ref[1], w_ref[2]))
    store.wait()


def attention_back_last_kernel(spots_ref, *refs):
    *refs, out_ref, g1_ref, ctx_ref, first_ref, w_ref, q_ref, k_ref, v_ref, p_ref, dq_ref, dk_ref, dv_ref, w_sems, sems, late_sems = refs
    g1_hbm, ctx_hbm, first_hbm, *sources, q_hbm, k_hbm, v_hbm, p_hbm = refs
    rows = out_ref.shape[0]
    seq_len = p_ref.shape[1]
    first = first_ref.shape[0] // seq_len
    seqs = q_ref.shape[0] // seq_len
    loads = begin(((ctx_hbm, ctx_ref),), late_sems.at[pl.ds(0, 1)])
    loads += load_heads((q_hbm, k_hbm, v_hbm, p_hbm), (q_ref, k_ref, v_ref, p_ref), sems, first, seqs)
    for load in loads:
        load.wait()
    fetch_stacked(spots_ref, sources, w_ref, w_sems, False)
    later = pl.ds(first * seq_len, seqs * seq_len)
    loads = begin(((g1_hbm.at[later], g1_ref), (first_hbm, first_ref)), late_sems.at[pl.ds(1, 2)])
    for s in range(seqs):
        attention_back_heads(s, seq_len, q_ref, k_ref, v_ref, p_ref, ctx_ref, dq_ref, dk_ref, dv_ref, 0)
    for load in loads:
        load.wait()
    for m in range(3):
        arrive_stacked(w_ref, w_sems, m)
    out_ref[: first * seq_len, :] = first_ref[...]
    out_ref[first * seq_len : rows, :] = input_rows(
        g1_ref[...], (dq_ref[...], dk_ref[...], dv_ref[...]), (w_ref[0], w_ref[1], w_ref[2])
    )


def attention_backward_first(spots, g1_low, g1, sources, q, k, v, probs):
    rows, dim = g1.shape
    heads, seq_len = probs.shape[0] // 2, probs.shape[1]
    half, low = jax.ShapeDtypeStruct((rows // 2, dim), BF), pltpu.VMEM((rows // 2, dim), BF)
    return pl.pallas_call(
        attention_back_first_kernel,
        out_shape=[half, half],
        in_specs=[SMEM] + [ANY] * (len(sources) + 6),
        out_specs=[ANY, VMEM],
        scratch_shapes=[pltpu.VMEM((4, dim, dim), BF), pltpu.VMEM((rows, dim), BF), pltpu.VMEM((rows // 2, dim), F32),
                        pltpu.VMEM((rows, dim), BF), low, low, low, pltpu.VMEM((heads,) + probs.shape[1:], BF), low, low, low,
                        WEIGHT_SEMS, pltpu.SemaphoreType.DMA((4,)), pltpu.SemaphoreType.DMA((3,))],
        compiler_params=limit(60),
        cost_estimate=cost(2 * rows * dim * (3 * dim + 2 * seq_len), 2 * (4 * dim * dim + 5 * rows * dim)),
    )(spots, g1_low, g1, *sources, q, k, v, probs)


def attention_backward_last(spots, g1, halfway, sources, q, k, v, probs):
    rows, dim = g1.shape
    heads, seq_len = probs.shape[0] // 2, probs.shape[1]
    low = pltpu.VMEM((rows // 2, dim), BF)
    return pl.pallas_call(
        attention_back_last_kernel,
        out_shape=jax.ShapeDtypeStruct((rows, dim), BF),
        in_specs=[SMEM] + [ANY] * (len(sources) + 7),
        out_specs=VMEM,
        scratch_shapes=[pltpu.VMEM((rows // 2, dim), F32), low, low, pltpu.VMEM((4, dim, dim), BF), low, low, low,
                        pltpu.VMEM((heads,) + probs.shape[1:], BF), low, low, low,
                        WEIGHT_SEMS, pltpu.SemaphoreType.DMA((4,)), pltpu.SemaphoreType.DMA((3,))],
        compiler_params=limit(60),
        cost_estimate=cost(2 * rows * dim * (2 * dim + 2 * seq_len), 2 * (3 * dim * dim + 4 * rows * dim)),
    )(spots, g1, *halfway, *sources, q, k, v, probs)


def shards(
    tokens, lengths, adapter_mask, cotangent, att_query, att_key, att_value, att_out,
    norm1_gain, norm1_bias, ffn_in, ffn_bias, ffn_out, adapt_down, adapt_up, norm2_gain,
    norm2_bias, joining_query, joining_key, joining_value, joining_qbias, joining_vbias,
):
    groups = lax.axis_size("tensor")
    dp_size = lax.axis_size("dp")
    my_z = lax.axis_index("tensor")
    my_d = lax.axis_index("dp")
    seq_local, seq_len, dim = tokens.shape
    mine = seq_local // groups
    rows = mine * seq_len
    adapters, neck = adapt_up.shape[0], adapt_up.shape[1]
    own_rows = joining_query.shape[0]

    gather = Gather(dp_size, groups, my_d, my_z, mine)
    spots = gather.spots
    biases = lax.dynamic_update_slice(
        jnp.zeros((8, dim), BF), jnp.stack([joining_qbias, joining_vbias]), (0, (my_d * groups + my_z) * own_rows)
    )
    att_mats = [att_query.T, att_key.T, att_value.T, att_out]
    join_part = jnp.concatenate([joining_query, joining_key, joining_value, biases], axis=0)

    def my_slice(array):
        return lax.dynamic_slice_in_dim(array, my_z * mine, mine, 0)

    x = my_slice(tokens).reshape(rows, dim)
    shifts = jnp.arange(128, dtype=jnp.int32)
    bits = jnp.right_shift(my_slice(adapter_mask)[:, None], jnp.minimum(shifts, adapters)[None, :]) % 2
    avail = jnp.where(shifts[None, :] < adapters, bits, 0)[:, None, :]
    norms = jnp.stack([norm1_gain, norm1_bias, norm2_gain, norm2_bias])
    lens = my_slice(lengths)
    owner = jnp.arange(adapters * neck, dtype=jnp.int32) // neck
    member = (owner[:, None] == shifts[None, :]).astype(BF)
    member_t = (shifts[:, None] == owner[None, :]).astype(BF)
    kept = {}

    def attend(sources):
        kept["att"] = attention_forward(spots, lens, x, sources, norms, seq_len)
        return [kept["att"][4]]

    def feed(sources):
        kept["ffn"] = ffn_forward(spots, kept["att"][4], sources, ffn_bias, ffn_in.shape[1])
        return [kept["ffn"][0]]

    if gather.paired:
        own = [att_mats, [ffn_in], None, [ffn_out]]
        steps = [
            lambda got: [],
            lambda got: [],
            lambda got: attend(got[0] + own[0]),
            lambda got: feed(got[1] + own[1]),
            lambda got: [],
            lambda got: [],
        ]
        quarter = att_mats[3]
        for i in range(3):
            quarter = jnp.where(my_d // 2 == i, att_mats[i], quarter)
        half = gather.half_of(quarter)
        rounds = [(half, tie(quarter, half))]
        shards_in, shards_out = tie(ffn_in, half), tie(ffn_out, half)
        in_quarter, in_half, out_quarter, out_half = cut(spots, [shards_in, shards_out])
        rounds += [(in_half, in_quarter), (out_half, out_quarter)]
        join_part = tie(join_part, *rounds[0])
        theirs = send(join_part, CORE)
        even = lax.rem(my_d, 2) == 0
        pair = jnp.concatenate([jnp.where(even, join_part, theirs), jnp.where(even, theirs, join_part)], axis=0)
        rounds.insert(2, (join_part, pair, join_part, theirs))
        got = gather.all_rounds(rounds, [x, norms, lens, avail, member, member_t, spots], steps)
        att_sources, in_sources, out_sources = (got[i] + own[i] for i in (0, 1, 3))
        join_sources = got[2]
    else:
        att_pack = jnp.concatenate(att_mats, axis=0)
        att_sources = gather.whole(gather.part_of(att_pack), True)
        in_sources, out_sources = (gather.whole(gather.part_of(shard)) for shard in (ffn_in, ffn_out))
        join_sources = [lax.all_gather(join_part, ("dp", "tensor"), axis=0)]
    up = adapt_up.reshape(adapters * neck, dim)
    cot = cotangent.reshape(rows, dim)

    def rest(att, ffn, avail, cot):
        q, k, v, probs, low1, xhat1, rstd1 = att
        act, slope = ffn
        layer_out, g2, g_ffn, *grads = joining(
            spots, gather.paired, act, out_sources, adapt_down, up, join_sources, member, member_t, avail, xhat1, norms, cot
        )
        done = {}

        def between(start):
            gradient = g_ffn if start is None else tie(g_ffn, start)
            done["g1"], g1_low = ffn_backward(spots, gradient, slope, out_sources, in_sources, g2, xhat1, rstd1, norms)
            done["half"] = attention_backward_first(spots, g1_low, done["g1"], att_sources, q, k, v, probs)
            return done["half"][0]

        def at_last(start):
            halfway = done["half"] if start is None else [tie(done["half"][0], start)] + list(done["half"][1:])
            return attention_backward_last(spots, done["g1"], halfway, att_sources, q, k, v, probs)

        return layer_out, grads, between, at_last

    if gather.paired:
        layer_out, grads, between, at_last = rest(kept["att"], kept["ffn"], avail, cot)
        (d_q, d_k, d_v, d_bias), input_grad = reduce_grads(gather, grads, own_rows, between, at_last)
    else:
        outs = []
        for first in range(0, mine, 2):
            at = slice(first * seq_len, (first + 2) * seq_len)
            att = attention_forward(spots, lens[first : first + 2], x[at], att_sources, norms, seq_len)
            ffn = ffn_forward(spots, att[4], in_sources, ffn_bias, ffn_in.shape[1])
            outs.append(rest(att, ffn, avail[first : first + 2], cot[at]))
        layer_out = jnp.concatenate([out[0] for out in outs])
        grads = [sum(out[1][i] for out in outs) for i in range(2)]
        (d_q, d_k, d_v, d_bias), input_grad = reduce_grads(
            gather, grads, own_rows, lambda start: [out[2](None) for out in outs],
            lambda start: jnp.concatenate([out[3](None) for out in outs]),
        )
    d_bias = lax.dynamic_slice_in_dim(d_bias[:2], (my_d * groups + my_z) * own_rows, own_rows, 1)
    return (
        layer_out.reshape(mine, seq_len, dim),
        input_grad.reshape(mine, seq_len, dim),
        d_q, d_k, d_v, d_bias[0], d_bias[1],
    )


def solution(mesh):
    both = P(ALL, None)
    return jax.shard_map(
        shards,
        mesh=mesh,
        in_specs=(
            P("dp", None, None), P("dp"), P("dp"), P(ALL, None, None),
            P(None, "tensor"), P(None, "tensor"), P(None, "tensor"), P("tensor", None),
            P(), P(), P(None, "tensor"), P(), P("tensor", None), P(), P(), P(), P(),
            both, both, both, P(ALL), P(ALL),
        ),
        out_specs=(P(ALL, None, None), P(ALL, None, None), both, both, both, P(ALL), P(ALL)),
        check_vma=False,
    )
```

```python
from functools import partial
import math

import jax
import jax.numpy as jnp
from jax import lax
from jax.experimental import pallas as pl
from jax.experimental.pallas import tpu as pltpu
from jax.sharding import PartitionSpec as P

HEADS = 12
EPS = 1e-05
MASKED = -1e30
ALL = ("dp", "tensor")
BF = jnp.bfloat16
F32 = jnp.float32


def mm(left, right):
    return jnp.dot(left, right, preferred_element_type=F32)


def mm_t(left, right):
    return lax.dot_general(left, right, (((1,), (1,)), ((), ())), preferred_element_type=F32)


def t_mm(left, right):
    return lax.dot_general(left, right, (((0,), (0,)), ((), ())), preferred_element_type=F32)


def norm_parts(values):
    average = jnp.mean(values, axis=-1, keepdims=True)
    centered = values - average
    variance = jnp.mean(centered * centered, axis=-1, keepdims=True)
    rstd = lax.rsqrt(variance + EPS)
    return centered * rstd, rstd


def norm_back(grad, gain, xhat, rstd):
    scaled = grad * gain
    return rstd * (
        scaled
        - jnp.mean(scaled, axis=-1, keepdims=True)
        - xhat * jnp.mean(scaled * xhat, axis=-1, keepdims=True)
    )


def gelu_parts(pre):
    cdf = 0.5 * (1.0 + lax.erf(pre * (1.0 / math.sqrt(2.0))))
    pdf = jnp.exp(-0.5 * pre * pre) * (1.0 / math.sqrt(2.0 * math.pi))
    return pre * cdf, cdf + pre * pdf


def limit(mebibytes):
    return pltpu.CompilerParams(vmem_limit_bytes=mebibytes * 2**20)


VMEM = pl.BlockSpec(memory_space=pltpu.VMEM)
SMEM = pl.BlockSpec(memory_space=pltpu.SMEM)
LITTLE = limit(24)
FAR_XY = [(i, i ^ 6) for i in range(8)]
CORE = [(i, i ^ 1) for i in range(8)]
ALONG_X = [(i, i ^ 2) for i in range(8)]
ALONG_Y = [(i, i ^ 4) for i in range(8)]
SPLIT_XY = [(i, i ^ (4 if i & 1 else 2)) for i in range(8)]
CROSS_XY = [(i, i ^ (3 if i & 1 else 5)) for i in range(8)]


def send(array, pairs):
    return lax.ppermute(array, "dp", pairs)


def shift(array, by, groups):
    return lax.ppermute(array, "tensor", [(i, (i + by) % groups) for i in range(groups)])


def scoped(name, step, *args):
    with jax.named_scope(name):
        return step(*args)


def tie(array, *others):
    return lax.optimization_barrier((array,) + others)[0]


def fetch_blocks(spots_ref, sources, stage_ref, sem):
    if len(sources) == 1:
        pltpu.make_async_copy(sources[0], stage_ref, sem).start()
        return
    planes = planes_in_order(spots_ref)
    for k, (ref, first) in enumerate(views(sources)):
        for i, plane in enumerate(planes[1:] + planes[:1]):
            pltpu.make_async_copy(ref.at[first + i], stage_ref.at[spots_ref[k] * len(planes) + plane], sem).start()


def order_rows(stage_ref, join_ref, biases_ref):
    blocks = stage_ref.shape[0]
    rows = join_ref.shape[1] // blocks
    total = 0.0
    for b in range(0, blocks, 2):
        pair = [stage_ref[b + i].astype(F32) for i in range(2)]
        for m in range(3):
            both = jnp.concatenate([block[m * rows : (m + 1) * rows] for block in pair], axis=0)
            join_ref[m, b * rows : (b + 2) * rows, :] = both.astype(BF)
        total = total + pair[0][3 * rows :] + pair[1][3 * rows :]
    biases_ref[...] = total


def fetch(spots_ref, sources, out_ref, sems, which, side_by_side=False):
    planes = planes_in_order(spots_ref)
    dim = sources[-1].shape[-1]
    rows = sources[-1].shape[-2]

    def copy(source, r, at):
        if side_by_side:
            target = out_ref.at[at, pl.ds(r * dim, dim)]
        else:
            target = out_ref.at[pl.ds(r * rows + at.start, at.size)]
        pltpu.make_async_copy(source, target, sems.at[r]).start()

    for r in which:
        if len(sources) == 1:
            copy(sources[0].at[planes[r]], r, pl.ds(0, rows))
        elif r == 0:
            copy(sources[-1], r, pl.ds(0, rows))
        else:
            for k, (ref, first) in enumerate(views(sources[:-1])):
                part = ref.shape[1]
                copy(ref.at[first + r - 1], r, pl.ds(pl.multiple_of(spots_ref[k] * part, part), part))


def arrive(out_ref, sems, r, side_by_side=False):
    dim = out_ref.shape[0] if side_by_side else out_ref.shape[1]
    block = out_ref.at[:, pl.ds(r * dim, dim)] if side_by_side else out_ref.at[pl.ds(r * out_ref.shape[0] // 4, out_ref.shape[0] // 4)]
    pltpu.make_async_copy(block, block, sems.at[r]).wait()


def fetch_stacked(spots_ref, sources, out_ref, sems, last):
    groups, dim = out_ref.shape[0], out_ref.shape[1]
    chosen = range(groups - 1, groups) if last else range(groups - 1)
    if len(sources) == 1:
        for m in chosen:
            pltpu.make_async_copy(sources[0].at[m], out_ref.at[m], sems.at[m]).start()
        return
    own = sources[-groups:]
    pieces = views(sources[:-groups])
    width, rows = dim // groups, pieces[0][0].shape[1]
    per = width // rows
    my_z = spots_ref[8]
    for m in chosen:
        at = pl.ds(pl.multiple_of(my_z * width, width), width)
        pltpu.make_async_copy(own[m], out_ref.at[m, at], sems.at[m]).start()
    for k, (ref, first) in enumerate(pieces):
        e = spots_ref[k]
        m = lax.div(e, per)

        @pl.when((m == groups - 1) == last)
        def _():
            for i, plane in enumerate(planes_in_order(spots_ref)[1:]):
                at = pl.ds(pl.multiple_of(plane * width + lax.rem(e, per) * rows, rows), rows)
                pltpu.make_async_copy(ref.at[first + i], out_ref.at[m, at], sems.at[m]).start()


def arrive_stacked(out_ref, sems, m):
    pltpu.make_async_copy(out_ref.at[m], out_ref.at[m], sems.at[m]).wait()


def views(sources):
    if len(sources) == 8:
        return [(source, 0) for source in sources]
    both, near, far, swapped, swapped_far = sources
    count = far.shape[0]
    return [(both, 0), (both, count), (near, 0), (near, count), (far, 0), (swapped, 0), (swapped, count), (swapped_far, 0)]


def cut_kernel(spots_ref, *refs):
    count = (len(refs) - 1) // 3
    shards, outs, sems = refs[:count], refs[count:-1], refs[-1]
    pairs = []
    for i, shard in enumerate(shards):
        rows = outs[2 * i].shape[0]
        at = pl.ds(pl.multiple_of(lax.div(spots_ref[0], 2) * rows, rows), rows)
        pairs.append((shard.at[at], outs[2 * i]))
        at = pl.ds(pl.multiple_of(spots_ref[0] * (rows // 2), rows // 2), rows // 2)
        pairs.append((shard.at[at], outs[2 * i + 1]))
    for copy in begin(pairs, sems):
        copy.wait()


def cut(spots, shards):
    outs = []
    for shard in shards:
        rows, dim = shard.shape
        outs += [jax.ShapeDtypeStruct((rows // 4, dim), BF), jax.ShapeDtypeStruct((rows // 8, dim), BF)]
    return pl.pallas_call(
        cut_kernel,
        out_shape=outs,
        in_specs=[SMEM] + [ANY] * len(shards),
        out_specs=[VMEM] * len(outs),
        scratch_shapes=[pltpu.SemaphoreType.DMA((len(outs),))],
        compiler_params=limit(60),
    )(spots, *shards)


def merge_kernel(spots_ref, *refs, count):
    beside, across, beside2, across2, *own = refs[:count]
    outs = refs[count:]
    core = lax.rem(spots_ref[0], 2)
    rows = across.shape[0]
    blocks = 3 + len(own) // 2
    sides = [outs[0], outs[1]] if len(outs) == 2 else [outs[0].at[pl.ds(i * blocks, blocks)] for i in range(2)]
    parts = [pl.ds(pl.multiple_of(at * rows, rows), rows) for at in (core, 1 - core)]
    for side, at, last, mine in zip(sides, parts, (across, across2), own or (None, None)):
        side[core] = beside[at, :]
        side[1 - core] = beside2[at, :]
        side[2] = last[...]
        if mine is not None:
            side[3] = mine[...]


def merge(spots, arrays, split):
    rows, dim = arrays[1].shape
    blocks = 3 + (len(arrays) - 4) // 2
    outs = [blocks, blocks] if split else [2 * blocks]
    return pl.pallas_call(
        partial(merge_kernel, count=len(arrays)),
        out_shape=[jax.ShapeDtypeStruct((out, rows, dim), BF) for out in outs],
        in_specs=[SMEM] + [VMEM] * len(arrays),
        out_specs=[VMEM] * len(outs),
        compiler_params=limit(8),
    )(spots, *arrays)


def planes_in_order(spots_ref, groups=4):
    return [lax.rem(spots_ref[8] + step, groups) for step in (0, 1, groups - 1, 2)]


def begin(pairs, sems):
    copies = [pltpu.make_async_copy(source, target, sems.at[i]) for i, (source, target) in enumerate(pairs)]
    for one in copies:
        one.start()
    return copies


WEIGHT_SEMS = pltpu.SemaphoreType.DMA((4,))
ANY = pl.BlockSpec(memory_space=pltpu.HBM)


class Gather:
    def __init__(self, dp_size, groups, my_d, my_z, seqs):
        self.dp_size, self.groups, self.my_d, self.my_z = dp_size, groups, my_d, my_z
        self.paired = dp_size == 8 and groups == 4 and seqs == 2
        core = lax.rem(my_d, 2)
        even = [0, 1, 2, 3, 7, 5, 4, 6]
        odd = [0, 1, 4, 5, 7, 3, 2, 6]
        flips = jnp.where(core == 0, jnp.array(even, jnp.int32), jnp.array(odd, jnp.int32))
        self.spots = jnp.concatenate([jnp.bitwise_xor(my_d, flips), my_z[None]]).astype(jnp.int32)

    def all_parts(self, part):
        whole = lax.all_gather(part, ("dp", "tensor"), axis=0)
        return whole.reshape((self.dp_size, self.groups) + part.shape).transpose(1, 0, 2, 3)

    def part_of(self, shard):
        rows = shard.shape[0] // self.dp_size
        return lax.dynamic_slice_in_dim(shard, self.my_d * rows, rows, 0)

    def all_rounds(self, parts, early, steps):
        count = len(parts)
        gathered, spread = [], []
        ahead, done = self.planes(parts[0], 0), [rows for part in parts[1:] for rows in part[:2]] + early
        for r in range(count + 2):
            with jax.named_scope("round%d" % r):
                ready = list(lax.optimization_barrier((*ahead, *done))) if r < count else list(done)
                ahead = ready[: len(ahead)]
                if r >= 1:
                    at = len(ahead)
                    if r <= count:
                        last = spread[r - 1]
                        last[1] = ready[at : at + len(last[1])]
                        at += len(last[1])
                    if 2 <= r <= count:
                        spread[r - 2][2] = ready[at]
                done = []
                if 1 <= r < count:
                    near_half = last[1][0] if len(last[1]) == 2 else last[1][0][: last[1][0].shape[0] // 2]
                    last.append(scoped("far", send, near_half, CROSS_XY))
                if r < count:
                    beside, across = ahead
                    ahead = []
                    if r + 1 < count:
                        ahead = self.planes([tie(rows, beside) for rows in parts[r + 1]], r + 1)
                    others = [scoped("others", send, beside, CORE), scoped("others", send, across, CORE)]
                    both = merge(self.spots, [beside, across, *others, *parts[r][2:]], r == count - 1)
                    near = [scoped("near", send, side, SPLIT_XY) for side in both]
                    spread.append([both, near])
                    done += near
                else:
                    ahead = []
                if 1 <= r <= count:
                    late = []
                    last.append([scoped("swap", send, array, CORE) for array in last[1][:-1]])
                    last[3].append(scoped("swap", send, tie(last[1][-1], *late), CORE))
                    done += (last[2:3] if r < count else []) + last[3]
                if r >= 2:
                    whole = spread[r - 2]
                    gathered.append([*whole[0], *whole[1], whole[2], *whole[3], scoped("swapfar", send, whole[2], CORE)])
                done += steps[r](gathered)
                if r == count - 1:
                    spread[r].append(scoped("far", send, tie(near[0], *done[len(near) :]), CROSS_XY))
        return gathered

    def planes(self, part, r):
        with jax.named_scope("planes%d" % r):
            groups = self.groups
            pairs = [
                (d * groups + z, d * groups + (z + (1 if d & 1 else groups - 1)) % groups)
                for d in range(self.dp_size)
                for z in range(groups)
            ]
            beside = scoped("beside", lax.ppermute, part[1], ("dp", "tensor"), pairs)
            return beside, scoped("across", shift, part[0], 2, groups)

    def half_of(self, quarter):
        rows = quarter.shape[0] // 2
        return jnp.where(lax.rem(self.my_d, 2) == 0, quarter[:rows], quarter[rows:])

    def quarter_of(self, shard):
        rows = 2 * shard.shape[0] // self.dp_size
        return lax.dynamic_slice_in_dim(shard, self.my_d // 2 * rows, rows, 0)

    def whole(self, part, stacked=False):
        whole = self.all_parts(part)
        dim = part.shape[1]
        if stacked:
            whole = whole.reshape(self.groups, 4, -1, dim).transpose(1, 0, 2, 3)
        return [whole.reshape(4, -1, dim)]


def reduce_grads(gather, grads, own_rows, between, at_last):
    groups, spots = gather.groups, gather.spots
    if not gather.paired:
        mats, bias = grads
        mats = lax.psum_scatter(mats, ("dp", "tensor"), scatter_dimension=1, tiled=True)
        middle = between(None)
        return (mats[0], mats[1], mats[2], lax.psum(bias, ("dp", "tensor"))), at_last(None)
    keep, away = grads
    rows, dim = keep.shape[1:]
    low = jax.ShapeDtypeStruct((rows, dim), BF)
    come = scoped("cores", send, away, CORE)
    to_x, to_y, to_far = pl.pallas_call(
        add_cores_kernel,
        out_shape=[low, low, low],
        in_specs=[SMEM, ANY, ANY],
        out_specs=[ANY] * 3,
        scratch_shapes=[pltpu.VMEM((3, rows, dim), BF)] * 3 + [pltpu.SemaphoreType.DMA((6,)), pltpu.SemaphoreType.DMA((3,))],
        compiler_params=limit(60),
    )(spots, keep, come)
    from_far = scoped("far", send, to_far, FAR_XY)
    from_x = scoped("x", send, to_x, ALONG_X)
    from_y = scoped("y", send, to_y, ALONG_Y)
    block = jax.ShapeDtypeStruct((3 * own_rows + 8, dim), BF)
    middle = between(to_far)
    mine, *goes = pl.pallas_call(
        add_plane_kernel,
        out_shape=[jax.ShapeDtypeStruct((3 * own_rows + 8, dim), F32)] + [block] * (groups - 1),
        in_specs=[SMEM] + [ANY] * 5,
        out_specs=[VMEM] * groups,
        scratch_shapes=[pltpu.VMEM((rows - 16, dim), F32), pltpu.VMEM((5, rows, dim), BF), pltpu.SemaphoreType.DMA((5,))],
        compiler_params=limit(60),
    )(spots, from_x, from_y, from_far, tie(keep, middle), come)
    after = at_last(mine)
    comes = [scoped("stack%d" % i, shift, go, i + 1, groups) for i, go in enumerate(goes)]
    part = jax.ShapeDtypeStruct((own_rows, dim), F32)
    sums = pl.pallas_call(
        add_stack_kernel,
        out_shape=[part, part, part, jax.ShapeDtypeStruct((8, dim), F32)],
        in_specs=[VMEM] * groups,
        out_specs=[VMEM] * 4,
        compiler_params=LITTLE,
    )(mine, *comes)
    return sums, after


def cost(flops, moved, exps=0):
    return pl.CostEstimate(flops=int(flops), bytes_accessed=int(moved), transcendentals=int(exps))


def head_masks():
    lane = lax.broadcasted_iota(jnp.int32, (1, 128), 1)
    first = (lane < 64).astype(F32)
    return [first.astype(BF), (1.0 - first).astype(BF)], lane < 64


def attention_kernel(spots_ref, len_ref, x_ref, norms_ref, *refs):
    *sources, q_hbm, k_hbm, v_hbm, p_hbm, low_ref, xhat_hbm, rstd_ref, w_ref, ctx_ref, q_ref, k_ref, v_ref, p_ref, xhat_ref, sems, store_sems = refs
    fetch_stacked(spots_ref, sources, w_ref, sems, False)
    fetch_stacked(spots_ref, sources, w_ref, sems, True)
    rows, dim = x_ref.shape
    for m in range(4):
        arrive_stacked(w_ref, sems, m)
    seq_len = p_ref.shape[1]
    x = x_ref[...]
    q_ref[...] = (mm_t(x, w_ref[0]).astype(BF).astype(F32) * (1.0 / math.sqrt(dim // HEADS))).astype(BF)
    k_ref[...] = mm_t(x, w_ref[1]).astype(BF)
    v_ref[...] = mm_t(x, w_ref[2]).astype(BF)
    stores = begin(((q_ref, q_hbm), (k_ref, k_hbm), (v_ref, v_hbm)), store_sems)
    masks, first = head_masks()
    key_at = lax.broadcasted_iota(jnp.int32, (seq_len, 1), 0)

    for s in range(rows // seq_len):
        at = slice(s * seq_len, (s + 1) * seq_len)
        valid = key_at < len_ref[s]
        for j in range(HEADS // 2):
            cols = slice(128 * j, 128 * (j + 1))
            q, k, v = q_ref[at, cols], k_ref[at, cols], v_ref[at, cols]
            parts = []
            for h in range(2):
                scores = jnp.where(valid, mm_t(k, q * masks[h]), MASKED)
                exps = jnp.exp(scores - jnp.max(scores, axis=0, keepdims=True))
                probs = (exps * (1.0 / jnp.sum(exps, axis=0, keepdims=True))).astype(BF)
                p_ref[s * HEADS + 2 * j + h] = probs
                parts.append(t_mm(probs, v))
            ctx_ref[at, cols] = jnp.where(first, parts[0], parts[1]).astype(BF)
        heads = pl.ds(s * HEADS, HEADS)
        stores += begin(((p_ref.at[heads], p_hbm.at[heads]),), store_sems.at[pl.ds(3 + s, 1)])
    xhat, rstd = norm_parts(x.astype(F32) + mm(ctx_ref[...], w_ref[3]))
    xhat_ref[...] = xhat
    stores += begin(((xhat_ref, xhat_hbm),), store_sems.at[pl.ds(3 + rows // seq_len, 1)])
    rstd_ref[...] = rstd
    low_ref[...] = (xhat * norms_ref[0:1, :] + norms_ref[1:2, :]).astype(BF)
    for store in stores:
        store.wait()


def attention_forward(spots, lengths, x, sources, norms, seq_len):
    rows, dim = x.shape
    seqs = rows // seq_len
    low = jax.ShapeDtypeStruct((rows, dim), BF)
    return pl.pallas_call(
        attention_kernel,
        out_shape=[low, low, low,
                   jax.ShapeDtypeStruct((seqs * HEADS, seq_len, seq_len), BF), low,
                   jax.ShapeDtypeStruct((rows, dim), F32), jax.ShapeDtypeStruct((rows, 1), F32)],
        in_specs=[SMEM] * 2 + [VMEM] * 2 + [ANY] * len(sources),
        out_specs=[ANY] * 4 + [VMEM, ANY, VMEM],
        scratch_shapes=[pltpu.VMEM((4, dim, dim), BF)] + [pltpu.VMEM((rows, dim), BF)] * 4 + [
            pltpu.VMEM((seqs * HEADS, seq_len, seq_len), BF), pltpu.VMEM((rows, dim), F32),
            WEIGHT_SEMS, pltpu.SemaphoreType.DMA((4 + seqs,)),
        ],
        compiler_params=limit(60),
        cost_estimate=cost(2 * rows * dim * (4 * dim + 2 * seq_len), 2 * (4 * dim * dim + 8 * rows * dim), rows * seq_len * HEADS),
    )(spots, lengths, x, norms, *sources)


def by_rows(rows, step, work, unroll=1):
    work(slice(0, rows))


def ffn_in_kernel(spots_ref, x_ref, bias_ref, *refs):
    *sources, act_hbm, slope_hbm, act_ref, slope_ref, w_ref, pre_ref, sems, store_sems = refs
    units = pre_ref.shape[1]
    order = planes_in_order(spots_ref)
    stores = []
    fetch(spots_ref, sources, w_ref, sems, [0, 1])
    for r in range(4):
        fetch(spots_ref, sources, w_ref, sems, [r + 2] if r < 2 else [])
        arrive(w_ref, sems, r)
        pre_ref[...] = mm(x_ref[...], w_ref[r * x_ref.shape[1] : (r + 1) * x_ref.shape[1], :])
        cols = slice(r * units, (r + 1) * units)
        act, slope = gelu_parts(pre_ref[...] + bias_ref[order[r]])
        act_ref[:, cols] = act.astype(BF)
        slope_ref[:, cols] = slope.astype(BF)
        pairs = [(act_ref, act_hbm), (slope_ref, slope_hbm)]
        stores += begin([(ref.at[:, cols], hbm.at[:, cols]) for ref, hbm in pairs], store_sems.at[pl.ds(2 * r, 2)])
    for store in stores:
        store.wait()


def ffn_forward(spots, x, sources, bias, units):
    rows, dim = x.shape
    planes = bias.shape[0] // units
    out = jax.ShapeDtypeStruct((rows, planes * units), BF)
    return pl.pallas_call(
        ffn_in_kernel,
        out_shape=[out, out],
        in_specs=[SMEM] + [VMEM] * 2 + [ANY] * len(sources),
        out_specs=[ANY] * 2,
        scratch_shapes=[
            pltpu.VMEM((rows, planes * units), BF), pltpu.VMEM((rows, planes * units), BF),
            pltpu.VMEM((planes * dim, units), BF), pltpu.VMEM((rows, units), F32), WEIGHT_SEMS, pltpu.SemaphoreType.DMA((8,)),
        ],
        compiler_params=limit(60),
        cost_estimate=cost(2 * rows * dim * units * planes, 2 * planes * units * (dim + 2 * rows), 2 * rows * units * planes),
    )(spots, x, bias.reshape(planes, 1, units), *sources)


def two_pass(values, table):
    high = values.astype(BF)
    return mm(high, table) + mm((values - high.astype(F32)).astype(BF), table)


def put_rows(ref, mats, bias):
    at = 0
    for mat in mats:
        ref[at : at + mat.shape[0], :] = mat.astype(BF)
        at += mat.shape[0]
    high = bias.astype(BF).astype(F32)
    ref[at : at + 16, :] = jnp.concatenate([high, bias - high], axis=0).astype(BF)


def sum_rows(arrays):
    total = arrays[0].astype(F32)
    for array in arrays[1:]:
        total = total + array.astype(F32)
    rows = total.shape[0] - 16
    return total[:rows], total[rows : rows + 8] + total[rows + 8 :]


def add_cores_kernel(spots_ref, keep_hbm, come_hbm, *refs):
    hbm, (sums_ref, keep_ref, come_ref, sems, store_sems) = refs[:3], refs[3:]
    quarter = lax.div(spots_ref[0], 2)
    pairs = []
    for i in range(3):
        q = jnp.bitwise_xor(quarter, i + 1)
        pairs += [(keep_hbm.at[q], keep_ref.at[i]), (come_hbm.at[q], come_ref.at[i])]
    copies = begin(pairs, sems)
    stores = []
    for i in range(3):
        copies[2 * i].wait()
        copies[2 * i + 1].wait()
        mats, bias = sum_rows([keep_ref[i], come_ref[i]])
        put_rows(sums_ref.at[i], [mats], bias)
        stores += begin(((sums_ref.at[i], hbm[i]),), store_sems.at[pl.ds(i, 1)])
    for store in stores:
        store.wait()


def fold_bias(bias):
    high = bias.astype(BF).astype(F32)
    row = lax.broadcasted_iota(jnp.int32, (8, 1), 0)
    return jnp.where(row < 4, high, pltpu.roll(bias - high, 4, 0))


def add_plane_kernel(spots_ref, *refs):
    parts, refs = refs[:3], refs[3:]
    keep_hbm, come_hbm, mine_ref, *go_refs, total_ref, arrays_ref, sems = refs
    quarter = lax.div(spots_ref[0], 2)
    sources = (keep_hbm.at[quarter], come_hbm.at[quarter], *parts)
    for copy in begin([(source, arrays_ref.at[i]) for i, source in enumerate(sources)], sems):
        copy.wait()
    total_ref[...], bias = sum_rows([arrays_ref[i] for i in range(5)])
    groups = len(go_refs) + 1
    width = total_ref.shape[0] // 3
    rows = width // groups

    def block(plane):
        at = [pl.multiple_of(i * width + plane * rows, 8) for i in range(3)]
        return jnp.concatenate([total_ref[pl.ds(a, rows), :] for a in at], axis=0)

    my_z = spots_ref[8]
    mine_ref[...] = jnp.concatenate([block(my_z), bias], axis=0)
    folded = fold_bias(bias)
    for i, ref in enumerate(go_refs):
        ref[...] = jnp.concatenate([block(lax.rem(my_z + i + 1, groups)), folded], axis=0).astype(BF)


def add_stack_kernel(mine_ref, *refs):
    come_refs, (q_ref, k_ref, v_ref, bias_ref) = refs[:-4], refs[-4:]
    total = mine_ref[...]
    rows = q_ref.shape[0]
    for ref in come_refs:
        come = ref[...].astype(F32)
        bias = come[3 * rows :]
        total = total + jnp.concatenate([come[: 3 * rows], bias + pltpu.roll(bias, 4, 0)], axis=0)
    q_ref[...], k_ref[...], v_ref[...] = (total[i * rows : (i + 1) * rows] for i in range(3))
    bias_ref[...] = total[3 * rows :]


def belongs(shape, unit_dim, adapter_dim, neck):
    unit, adapter = (lax.broadcasted_iota(jnp.int32, shape, d) for d in (unit_dim, adapter_dim))
    return jnp.where(jnp.logical_and(unit >= adapter * neck, unit < (adapter + 1) * neck), 1.0, 0.0).astype(BF)


def joining_kernel(
    spots_ref, mask_ref, norms_ref, act_hbm, xhat1_hbm, cot_hbm, *refs, halves, count, adapters
):
    gain1, bias1, gain2, bias2 = (norms_ref[i : i + 1, :] for i in range(4))
    down_hbm, up_hbm, *refs = refs
    join_sources, sources, refs = refs[:count], refs[count:-38], refs[-38:]
    stage_ref, biases_ref, stage_sem, refs = refs[-3], refs[-2], refs[-1], refs[:-3]
    out_hbm, g2_hbm, g_ffn_ref, grad_hbm0, grad_hbm1 = refs[:5]
    act_ref, w_out_ref, down_ref, up_ref, join_ref, xhat1_ref, cot_ref, act_sems, out_sems, sems, store_sems = refs[5:16]
    ffn_ref, u_ref, w_ref, big_u_ref, big_w_ref, p_wide_ref, sums_ref = refs[16:23]
    x_ref, act2_ref, slope_ref, q_ref, gq_ref, low_ref, mixed_ref, t_ref = refs[23:31]
    out_ref, g2_ref, bias_rows_ref, bias_ref = refs[31:35]
    rows, dim = out_ref.shape
    units = w_out_ref.shape[0] // 4
    seqs = mask_ref.shape[0]
    per = rows // seqs
    everyone = [slice(i * per, (i + 1) * per) for i in range(seqs)]
    fscale = 1.0 / math.sqrt(dim)
    member = belongs((dim, 128), 0, 1, dim // adapters)
    member_t = belongs((128, dim), 1, 0, dim // adapters)
    lane = lax.broadcasted_iota(jnp.int32, (1, 128), 1)
    loads = []

    def issue(r):
        if r < 4:
            fetch(spots_ref, sources, w_out_ref, out_sems, [r])
            cols = pl.ds(r * units, units)
            loads.extend(begin(((act_hbm.at[:, cols], act_ref.at[:, cols]),), act_sems.at[pl.ds(r, 1)]))
        elif r == 4:
            fetch_blocks(spots_ref, join_sources, stage_ref, stage_sem)
        elif r == 5:
            pairs = ((down_hbm, down_ref), (up_hbm, up_ref), (xhat1_hbm, xhat1_ref), (cot_hbm, cot_ref))
            loads.extend(begin(pairs, sems))

    issue(0)
    issue(1)
    for r in range(4):
        issue(r + 2)
        loads[r].wait()
        arrive(w_out_ref, out_sems, r)
        if r % 2 == 1:
            both = slice((r - 1) * units, (r + 1) * units)
            for at in everyone:
                term = mm(act_ref[at, both], w_out_ref[both, :])
                ffn_ref[at, :] = term if r == 1 else ffn_ref[at, :] + term
    loads = loads[4:]
    for at in everyone:
        x_ref[at, :] = ffn_ref[at, :].astype(BF)
    pltpu.make_async_copy(stage_ref, stage_ref, stage_sem).wait()
    order_rows(stage_ref, join_ref, biases_ref)
    qb, vb = biases_ref[0:1, :], biases_ref[1:2, :]
    for load in loads:
        load.wait()
    up = up_ref[...]
    halves_of = {}

    def narrow(i, name, value=None):
        if value is not None:
            halves_of[i, name] = value
        return halves_of[i, name]

    def per_adapter(values):
        high = values.astype(BF)
        return mm(high, member) + mm((values - high.astype(F32)).astype(BF), member)

    def to_q(i, at):
        q_ref[at, :] = (mm(x_ref[at, :], join_ref[0]) + qb).astype(BF)

    def down(i, at):
        act, slope = gelu_parts(mm(x_ref[at, :], down_ref[...]))
        act2_ref[at, :] = act.astype(BF)
        slope_ref[at, :] = slope.astype(BF)

    def to_u(i, at):
        u = mm_t(q_ref[at, :], join_ref[1])
        u_ref[at, :] = u
        narrow(i, "dot", jnp.sum(ffn_ref[at, :] * u, axis=-1, keepdims=True))

    def scores(i, at):
        big_u = mm_t(u_ref[at, :].astype(BF), up)
        big_u_ref[at, :] = big_u
        fscores = (per_adapter(act2_ref[at, :].astype(F32) * big_u) + narrow(i, "dot")) * fscale
        bit = lax.rem(lax.shift_right_logical(jnp.full_like(lane, mask_ref[i]), jnp.minimum(lane, adapters)), 2)
        fscores = jnp.where(jnp.logical_and(bit == 1, lane < adapters), fscores, MASKED)
        fexp = jnp.exp(fscores - jnp.max(fscores, axis=-1, keepdims=True))
        narrow(i, "probs", fexp / jnp.sum(fexp, axis=-1, keepdims=True))

    def mix(i, at):
        p_wide = two_pass(narrow(i, "probs"), member_t)
        p_wide_ref[at, :] = p_wide
        weighed = (p_wide * act2_ref[at, :].astype(F32)).astype(BF)
        mixed_ref[at, :] = (ffn_ref[at, :] + mm(weighed, up)).astype(BF)

    def norm(i, at):
        normed1 = xhat1_ref[at, :] * gain1 + bias1
        xhat2, rstd2 = norm_parts(normed1 + mm(mixed_ref[at, :], join_ref[2]) + vb)
        out_ref[at, :] = (xhat2 * gain2 + bias2).astype(BF)
        g2 = norm_back(cot_ref[at, :].astype(F32), gain2, xhat2, rstd2)
        g2_ref[at, :] = g2
        low_ref[at, :] = g2.astype(BF)
        narrow(i, "dot2", jnp.sum(g2 * vb, axis=-1, keepdims=True))
        narrow(i, "d_vb", jnp.sum(g2.reshape(-1, 8, dim), axis=0))

    def to_w(i, at):
        w = mm_t(low_ref[at, :], join_ref[2])
        w_ref[at, :] = w
        narrow(i, "dot2", narrow(i, "dot2") + jnp.sum(ffn_ref[at, :] * w, axis=-1, keepdims=True))

    def score_grads(i, at):
        big_w = mm_t(w_ref[at, :].astype(BF), up)
        big_w_ref[at, :] = big_w
        gvals = per_adapter(act2_ref[at, :].astype(F32) * big_w) + narrow(i, "dot2")
        fprobs = narrow(i, "probs")
        gs = fprobs * (gvals - jnp.sum(gvals * fprobs, axis=-1, keepdims=True)) * fscale
        narrow(i, "gs", gs)
        narrow(i, "gs_sum", jnp.sum(gs, axis=-1, keepdims=True))

    def to_t(i, at):
        wide = two_pass(narrow(i, "gs"), member_t)
        weighed = (wide * act2_ref[at, :].astype(F32)).astype(BF)
        grad = wide * big_u_ref[at, :] + p_wide_ref[at, :] * big_w_ref[at, :]
        slope_ref[at, :] = (grad * slope_ref[at, :].astype(F32)).astype(BF)
        t_ref[at, :] = (mm(weighed, up) + narrow(i, "gs_sum") * ffn_ref[at, :]).astype(BF)

    def to_gq(i, at):
        gq = mm(t_ref[at, :], join_ref[1]).astype(BF)
        gq_ref[at, :] = gq
        narrow(i, "d_qb", jnp.sum(gq.astype(F32).reshape(-1, 8, dim), axis=0))

    def all_halves(*steps):
        for step in steps:
            for i, at in enumerate(everyone):
                step(i, at)

    all_halves(to_q, down, to_u, scores, mix, norm)
    stores = begin(((out_ref, out_hbm), (g2_ref, g2_hbm)), store_sems)
    all_halves(to_w, score_grads)
    sums_ref[2] = t_mm(mixed_ref[...], low_ref[...]).astype(sums_ref.dtype)
    all_halves(to_t)
    sums_ref[1] = t_mm(t_ref[...], q_ref[...]).astype(sums_ref.dtype)
    all_halves(to_gq)
    sums_ref[0] = t_mm(x_ref[...], gq_ref[...]).astype(sums_ref.dtype)
    row = lax.broadcasted_iota(jnp.int32, (8, 1), 0)
    d_qb, d_vb = (
        jnp.sum(sum(narrow(i, name) for i in range(seqs)), axis=0, keepdims=True) for name in ("d_qb", "d_vb")
    )
    bias_ref[...] = jnp.where(row == 0, d_qb, jnp.where(row == 1, d_vb, 0.0))
    if halves:
        core = lax.rem(spots_ref[0], 2)
        part = dim // 8
        put_rows(bias_rows_ref, [], bias_ref[...])
        for hbm, side, sem in ((grad_hbm1, 1 - core, store_sems.at[2]), (grad_hbm0, core, store_sems.at[3])):
            for q in range(4):
                at = pl.ds(pl.multiple_of((2 * q + side) * part, part), part)
                for i in range(3):
                    pltpu.make_async_copy(sums_ref.at[i, at], hbm.at[q, pl.ds(i * part, part)], sem).start()
                pltpu.make_async_copy(bias_rows_ref, hbm.at[q, pl.ds(3 * part, 16)], sem).start()
            stores.append(pltpu.make_async_copy(hbm, hbm, sem))
    else:
        stores += begin(((sums_ref, grad_hbm0), (bias_ref, grad_hbm1)), store_sems.at[pl.ds(2, 2)])
    for i, at in enumerate(everyone):
        total = mm_t(slope_ref[at, :], down_ref[...]) + mm_t(gq_ref[at, :], join_ref[0])
        g_ffn_ref[at, :] = (narrow(i, "gs_sum") * u_ref[at, :] + w_ref[at, :] + total).astype(BF)
    for store in stores:
        store.wait()


def joining(spots, halves, act, sources, adapt_down, up, join_sources, masks, adapters, xhat1, norms, cot):
    rows, dim = xhat1.shape
    if halves:
        grads = [jax.ShapeDtypeStruct((4, 3 * dim // 8 + 16, dim), BF)] * 2
    else:
        grads = [jax.ShapeDtypeStruct((3, dim, dim), F32), jax.ShapeDtypeStruct((8, dim), F32)]
    wide, low = pltpu.VMEM((rows, dim), F32), pltpu.VMEM((rows, dim), BF)
    height, blocks = join_sources[-1].shape[-2:][0], 32
    stage_shape = join_sources[0].shape if len(join_sources) == 1 else (blocks, height, dim)
    return pl.pallas_call(
        partial(joining_kernel, halves=halves, count=len(join_sources), adapters=adapters),
        out_shape=[
            jax.ShapeDtypeStruct((rows, dim), BF),
            jax.ShapeDtypeStruct((rows, dim), F32),
            jax.ShapeDtypeStruct((rows, dim), BF),
        ] + grads,
        in_specs=[SMEM] * 2 + [VMEM] + [ANY] * (len(sources) + len(join_sources) + 5),
        out_specs=[ANY, ANY, VMEM, ANY, ANY],
        scratch_shapes=[
            pltpu.VMEM(act.shape, BF),
            pltpu.VMEM((act.shape[1], dim), BF),
            pltpu.VMEM(adapt_down.shape, BF),
            pltpu.VMEM(up.shape, BF),
            pltpu.VMEM((3, dim, dim), BF),
            wide,
            low,
            WEIGHT_SEMS,
            WEIGHT_SEMS,
            pltpu.SemaphoreType.DMA((4,)),
            pltpu.SemaphoreType.DMA((4,)),
        ] + [wide] * 6 + [pltpu.VMEM((3, dim, dim), BF if halves else F32)] + [low] * 8 + [
            low,
            wide,
            pltpu.VMEM((16, dim), BF),
            pltpu.VMEM((8, dim), F32),
            pltpu.VMEM(stage_shape, BF),
            pltpu.VMEM((8, dim), F32),
            pltpu.SemaphoreType.DMA,
        ],
        compiler_params=limit(60),
        cost_estimate=cost(2 * rows * dim * (15 * dim + act.shape[1]), 2 * dim * (8 * dim + 10 * rows), 2 * rows * dim),
    )(spots, masks, norms, act, xhat1, cot, adapt_down, up, *join_sources, *sources)


def ffn_back_kernel(spots_ref, g_ref, rstd_ref, norms_ref, slope_hbm, g2_hbm, xhat_hbm, *refs, count):
    refs, (out_sources, in_sources) = refs[sum(count) :], (refs[: count[0]], refs[count[0] : sum(count)])
    g1_hbm, low_hbm, g1_ref, low_ref, slope_ref, g2_ref, xhat_ref, w_out_ref, w_in_ref, pre_ref, out_sems, in_sems, slope_sems, sems, store_sems = refs
    units = w_out_ref.shape[0] // 4
    rows = g_ref.shape[0]
    everyone = [slice(i * rows // 2, (i + 1) * rows // 2) for i in range(2)]
    loads = []

    def issue(r):
        if r < 4:
            fetch(spots_ref, out_sources, w_out_ref, out_sems, [r])
            cols = pl.ds(r * units, units)
            loads.extend(begin(((slope_hbm.at[:, cols], slope_ref.at[:, cols]),), slope_sems.at[pl.ds(r, 1)]))
        elif r < 8:
            fetch(spots_ref, in_sources, w_in_ref, in_sems, [r - 4], side_by_side=True)
        elif r == 8:
            loads.extend(begin(((g2_hbm, g2_ref), (xhat_hbm, xhat_ref)), sems))

    issue(0)
    issue(1)
    for r in range(4):
        issue(r + 2)
        cols = slice(r * units, (r + 1) * units)
        arrive(w_out_ref, out_sems, r)
        loads[r].wait()
        for at in everyone:
            pre_ref[at, cols] = (mm_t(g_ref[at, :], w_out_ref[cols, :]) * slope_ref[at, cols].astype(F32)).astype(BF)
    for r in range(4, 8):
        issue(r + 2)
        arrive(w_in_ref, in_sems, r - 4, side_by_side=True)
        if r == 5:
            both = slice(0, 2 * units)
            for at in everyone:
                g1_ref[at, :] = mm_t(pre_ref[at, both], w_in_ref[:, both])
    for load in loads[4:]:
        load.wait()
    both = slice(2 * units, 4 * units)
    stores = []
    for at in everyone:
        total = mm_t(pre_ref[at, both], w_in_ref[:, both]) + g1_ref[at, :] + g2_ref[at, :]
        g1 = norm_back(total, norms_ref[0:1, :], xhat_ref[at, :], rstd_ref[at, :])
        g1_ref[at, :] = g1
        low_ref[at, :] = g1.astype(BF)
        stores += begin(((g1_ref.at[at], g1_hbm.at[at]), (low_ref.at[at], low_hbm.at[at])), store_sems.at[pl.ds(len(stores), 2)])
    for store in stores:
        store.wait()


def ffn_backward(spots, g_ffn, slope, out_sources, in_sources, g2, xhat, rstd, norms):
    rows, dim = xhat.shape
    planes = 4
    units = slope.shape[1] // planes
    return pl.pallas_call(
        partial(ffn_back_kernel, count=(len(out_sources), len(in_sources))),
        out_shape=[jax.ShapeDtypeStruct((rows, dim), F32), jax.ShapeDtypeStruct((rows, dim), BF)],
        in_specs=[SMEM] + [VMEM] * 3 + [ANY] * (len(out_sources) + len(in_sources) + 3),
        out_specs=[ANY, ANY],
        scratch_shapes=[
            pltpu.VMEM((rows, dim), F32), pltpu.VMEM((rows, dim), BF),
            pltpu.VMEM(slope.shape, BF), pltpu.VMEM((rows, dim), F32), pltpu.VMEM((rows, dim), F32),
            pltpu.VMEM((planes * units, dim), BF), pltpu.VMEM((dim, planes * units), BF), pltpu.VMEM(slope.shape, BF),
            WEIGHT_SEMS, WEIGHT_SEMS, WEIGHT_SEMS, pltpu.SemaphoreType.DMA((2,)),
            pltpu.SemaphoreType.DMA((4,)),
        ],
        compiler_params=limit(60),
        cost_estimate=cost(4 * rows * dim * units * planes, 2 * planes * units * (2 * dim + rows)),
    )(spots, g_ffn, rstd, norms, slope, g2, xhat, *out_sources, *in_sources)


def attention_back_heads(s, seq_len, q_ref, k_ref, v_ref, p_ref, g_ref, dq_ref, dk_ref, dv_ref, first_seq):
    dim = q_ref.shape[1]
    scale = 1.0 / math.sqrt(dim // HEADS)
    masks = head_masks()[0]
    at = slice((s - first_seq) * seq_len, (s - first_seq + 1) * seq_len)
    for j in range(HEADS // 2):
        cols = slice(128 * j, 128 * (j + 1))
        q, k, v, g = q_ref[at, cols], k_ref[at, cols], v_ref[at, cols], g_ref[at, cols]
        split = [jnp.concatenate([array * mask for mask in masks], axis=0) for array in (q, k, g)]
        probs_low = [p_ref[(s - first_seq) * HEADS + 2 * j + h] for h in range(2)]
        g_scores = []
        for h in range(2):
            probs = probs_low[h].astype(F32)
            g_probs = mm_t(v, split[2][h * seq_len : (h + 1) * seq_len])
            g_scores.append((probs * (g_probs - jnp.sum(g_probs * probs, axis=0, keepdims=True))).astype(BF))
        dq_ref[at, cols] = (t_mm(jnp.concatenate(g_scores, axis=0), split[1]) * scale).astype(BF)
        dk_ref[at, cols] = mm(jnp.concatenate(g_scores, axis=1), split[0]).astype(BF)
        dv_ref[at, cols] = mm(jnp.concatenate(probs_low, axis=1), split[2]).astype(BF)


def load_heads(hbm, vmem, sems, first, count):
    seq_len = hbm[3].shape[1]
    rows, heads = pl.ds(first * seq_len, count * seq_len), pl.ds(first * HEADS, count * HEADS)
    pairs = [(hbm[i].at[rows], vmem[i]) for i in range(3)] + [(hbm[3].at[heads], vmem[3])]
    return begin(pairs, sems)


def input_rows(g1, grads, weights):
    total = g1
    for grad, weight in zip(grads, weights):
        total = total + mm(grad, weight)
    return total.astype(BF)


def attention_back_first_kernel(spots_ref, *refs):
    *refs, ctx_hbm, out_ref, w_ref, low_ref, g1_ref, ctx_ref, q_ref, k_ref, v_ref, p_ref, dq_ref, dk_ref, dv_ref, w_sems, sems, g_sems = refs
    low_hbm, g1_hbm, *sources, q_hbm, k_hbm, v_hbm, p_hbm = refs
    seq_len = p_ref.shape[1]
    rows, dim = low_ref.shape
    loads = begin(((low_hbm, low_ref),), g_sems.at[pl.ds(0, 1)])
    fetch_stacked(spots_ref, sources, w_ref, w_sems, True)
    seqs = q_ref.shape[0] // seq_len
    loads += load_heads((q_hbm, k_hbm, v_hbm, p_hbm), (q_ref, k_ref, v_ref, p_ref), sems, 0, seqs)
    loads[0].wait()
    arrive_stacked(w_ref, w_sems, 3)
    ctx_ref[...] = mm_t(low_ref[...], w_ref[3]).astype(BF)
    mine, later = pl.ds(0, seqs * seq_len), pl.ds(seqs * seq_len, rows - seqs * seq_len)
    store = begin(((ctx_ref.at[later], ctx_hbm),), g_sems.at[pl.ds(1, 1)])[0]
    for load in loads[1:]:
        load.wait()
    fetch_stacked(spots_ref, sources, w_ref, w_sems, False)
    load = begin(((g1_hbm.at[mine], g1_ref),), g_sems.at[pl.ds(2, 1)])[0]
    for s in range(seqs):
        attention_back_heads(s, seq_len, q_ref, k_ref, v_ref, p_ref, ctx_ref, dq_ref, dk_ref, dv_ref, 0)
    load.wait()
    for m in range(3):
        arrive_stacked(w_ref, w_sems, m)
    out_ref[...] = input_rows(g1_ref[...], (dq_ref[...], dk_ref[...], dv_ref[...]), (w_ref[0], w_ref[1], w_ref[2]))
    store.wait()


def attention_back_last_kernel(spots_ref, *refs):
    *refs, out_ref, g1_ref, ctx_ref, first_ref, w_ref, q_ref, k_ref, v_ref, p_ref, dq_ref, dk_ref, dv_ref, w_sems, sems, late_sems = refs
    g1_hbm, ctx_hbm, first_hbm, *sources, q_hbm, k_hbm, v_hbm, p_hbm = refs
    rows = out_ref.shape[0]
    seq_len = p_ref.shape[1]
    first = first_ref.shape[0] // seq_len
    seqs = q_ref.shape[0] // seq_len
    loads = begin(((ctx_hbm, ctx_ref),), late_sems.at[pl.ds(0, 1)])
    loads += load_heads((q_hbm, k_hbm, v_hbm, p_hbm), (q_ref, k_ref, v_ref, p_ref), sems, first, seqs)
    for load in loads:
        load.wait()
    fetch_stacked(spots_ref, sources, w_ref, w_sems, False)
    later = pl.ds(first * seq_len, seqs * seq_len)
    loads = begin(((g1_hbm.at[later], g1_ref), (first_hbm, first_ref)), late_sems.at[pl.ds(1, 2)])
    for s in range(seqs):
        attention_back_heads(s, seq_len, q_ref, k_ref, v_ref, p_ref, ctx_ref, dq_ref, dk_ref, dv_ref, 0)
    for load in loads:
        load.wait()
    for m in range(3):
        arrive_stacked(w_ref, w_sems, m)
    out_ref[: first * seq_len, :] = first_ref[...]
    out_ref[first * seq_len : rows, :] = input_rows(
        g1_ref[...], (dq_ref[...], dk_ref[...], dv_ref[...]), (w_ref[0], w_ref[1], w_ref[2])
    )


def attention_backward_first(spots, g1_low, g1, sources, q, k, v, probs):
    rows, dim = g1.shape
    heads, seq_len = probs.shape[0] // 2, probs.shape[1]
    half, low = jax.ShapeDtypeStruct((rows // 2, dim), BF), pltpu.VMEM((rows // 2, dim), BF)
    return pl.pallas_call(
        attention_back_first_kernel,
        out_shape=[half, half],
        in_specs=[SMEM] + [ANY] * (len(sources) + 6),
        out_specs=[ANY, VMEM],
        scratch_shapes=[pltpu.VMEM((4, dim, dim), BF), pltpu.VMEM((rows, dim), BF), pltpu.VMEM((rows // 2, dim), F32),
                        pltpu.VMEM((rows, dim), BF), low, low, low, pltpu.VMEM((heads,) + probs.shape[1:], BF), low, low, low,
                        WEIGHT_SEMS, pltpu.SemaphoreType.DMA((4,)), pltpu.SemaphoreType.DMA((3,))],
        compiler_params=limit(60),
        cost_estimate=cost(2 * rows * dim * (3 * dim + 2 * seq_len), 2 * (4 * dim * dim + 5 * rows * dim)),
    )(spots, g1_low, g1, *sources, q, k, v, probs)


def attention_backward_last(spots, g1, halfway, sources, q, k, v, probs):
    rows, dim = g1.shape
    heads, seq_len = probs.shape[0] // 2, probs.shape[1]
    low = pltpu.VMEM((rows // 2, dim), BF)
    return pl.pallas_call(
        attention_back_last_kernel,
        out_shape=jax.ShapeDtypeStruct((rows, dim), BF),
        in_specs=[SMEM] + [ANY] * (len(sources) + 7),
        out_specs=VMEM,
        scratch_shapes=[pltpu.VMEM((rows // 2, dim), F32), low, low, pltpu.VMEM((4, dim, dim), BF), low, low, low,
                        pltpu.VMEM((heads,) + probs.shape[1:], BF), low, low, low,
                        WEIGHT_SEMS, pltpu.SemaphoreType.DMA((4,)), pltpu.SemaphoreType.DMA((3,))],
        compiler_params=limit(60),
        cost_estimate=cost(2 * rows * dim * (2 * dim + 2 * seq_len), 2 * (3 * dim * dim + 4 * rows * dim)),
    )(spots, g1, *halfway, *sources, q, k, v, probs)


def shards(
    tokens, lengths, adapter_mask, cotangent, att_query, att_key, att_value, att_out,
    norm1_gain, norm1_bias, ffn_in, ffn_bias, ffn_out, adapt_down, adapt_up, norm2_gain,
    norm2_bias, joining_query, joining_key, joining_value, joining_qbias, joining_vbias,
):
    groups = lax.axis_size("tensor")
    dp_size = lax.axis_size("dp")
    my_z = lax.axis_index("tensor")
    my_d = lax.axis_index("dp")
    seq_local, seq_len, dim = tokens.shape
    mine = seq_local // groups
    rows = mine * seq_len
    adapters, neck = adapt_up.shape[0], adapt_up.shape[1]
    own_rows = joining_query.shape[0]

    gather = Gather(dp_size, groups, my_d, my_z, mine)
    spots = gather.spots
    biases = lax.dynamic_update_slice(
        jnp.zeros((8, dim), BF), jnp.stack([joining_qbias, joining_vbias]), (0, (my_d * groups + my_z) * own_rows)
    )
    att_mats = [att_query.T, att_key.T, att_value.T, att_out]
    join_part = jnp.concatenate([joining_query, joining_key, joining_value, biases], axis=0)

    def my_slice(array):
        return lax.dynamic_slice_in_dim(array, my_z * mine, mine, 0)

    x = my_slice(tokens).reshape(rows, dim)
    masks = my_slice(adapter_mask)
    norms = jnp.stack([norm1_gain, norm1_bias, norm2_gain, norm2_bias])
    lens = my_slice(lengths)
    kept = {}

    def attend(sources):
        kept["att"] = attention_forward(spots, lens, x, sources, norms, seq_len)
        return [kept["att"][4]]

    def feed(sources):
        kept["ffn"] = ffn_forward(spots, kept["att"][4], sources, ffn_bias, ffn_in.shape[1])
        return [kept["ffn"][0]]

    if gather.paired:
        own = [att_mats, [ffn_in], None, [ffn_out]]
        steps = [
            lambda got: [],
            lambda got: [],
            lambda got: attend(got[0] + own[0]),
            lambda got: feed(got[1] + own[1]),
            lambda got: [],
            lambda got: [],
        ]
        quarter = att_mats[3]
        for i in range(3):
            quarter = jnp.where(my_d // 2 == i, att_mats[i], quarter)
        low = quarter.shape[0] // 2
        choices = [part for mat in att_mats for part in (mat[:low], mat[low:])]
        half = choices[7]
        for i in range(7):
            half = jnp.where(my_d == i, choices[i], half)
        rounds = [(half, tie(quarter, half))]
        shards_in, shards_out = tie(ffn_in, half), tie(ffn_out, half)
        in_quarter, in_half, out_quarter, out_half = cut(spots, [shards_in, shards_out])
        rounds += [(in_half, in_quarter), (out_half, out_quarter)]
        join_part = tie(join_part, *rounds[0])
        theirs = send(join_part, CORE)
        even = lax.rem(my_d, 2) == 0
        pair = jnp.concatenate([jnp.where(even, join_part, theirs), jnp.where(even, theirs, join_part)], axis=0)
        rounds.insert(2, (join_part, pair, join_part, theirs))
        got = gather.all_rounds(rounds, [spots, x, norms, lens, masks], steps)
        att_sources, in_sources, out_sources = (got[i] + own[i] for i in (0, 1, 3))
        join_sources = got[2]
    else:
        att_pack = jnp.concatenate(att_mats, axis=0)
        att_sources = gather.whole(gather.part_of(att_pack), True)
        in_sources, out_sources = (gather.whole(gather.part_of(shard)) for shard in (ffn_in, ffn_out))
        join_sources = [lax.all_gather(join_part, ("dp", "tensor"), axis=0)]
    up = adapt_up.reshape(adapters * neck, dim)
    cot = cotangent.reshape(rows, dim)

    def rest(att, ffn, masks, cot):
        q, k, v, probs, low1, xhat1, rstd1 = att
        act, slope = ffn
        layer_out, g2, g_ffn, *grads = joining(
            spots, gather.paired, act, out_sources, adapt_down, up, join_sources, masks, adapters, xhat1, norms, cot
        )
        done = {}

        def between(start):
            gradient = g_ffn if start is None else tie(g_ffn, start)
            done["g1"], g1_low = ffn_backward(spots, gradient, slope, out_sources, in_sources, g2, xhat1, rstd1, norms)
            done["half"] = attention_backward_first(spots, g1_low, done["g1"], att_sources, q, k, v, probs)
            return done["half"][0]

        def at_last(start):
            halfway = done["half"] if start is None else [tie(done["half"][0], start)] + list(done["half"][1:])
            return attention_backward_last(spots, done["g1"], halfway, att_sources, q, k, v, probs)

        return layer_out, grads, between, at_last

    if gather.paired:
        layer_out, grads, between, at_last = rest(kept["att"], kept["ffn"], masks, cot)
        (d_q, d_k, d_v, d_bias), input_grad = reduce_grads(gather, grads, own_rows, between, at_last)
    else:
        outs = []
        for first in range(0, mine, 2):
            at = slice(first * seq_len, (first + 2) * seq_len)
            att = attention_forward(spots, lens[first : first + 2], x[at], att_sources, norms, seq_len)
            ffn = ffn_forward(spots, att[4], in_sources, ffn_bias, ffn_in.shape[1])
            outs.append(rest(att, ffn, masks[first : first + 2], cot[at]))
        layer_out = jnp.concatenate([out[0] for out in outs])
        grads = [sum(out[1][i] for out in outs) for i in range(2)]
        (d_q, d_k, d_v, d_bias), input_grad = reduce_grads(
            gather, grads, own_rows, lambda start: [out[2](None) for out in outs],
            lambda start: jnp.concatenate([out[3](None) for out in outs]),
        )
    d_bias = lax.dynamic_slice_in_dim(d_bias[:2], (my_d * groups + my_z) * own_rows, own_rows, 1)
    return (
        layer_out.reshape(mine, seq_len, dim),
        input_grad.reshape(mine, seq_len, dim),
        d_q, d_k, d_v, d_bias[0], d_bias[1],
    )


def solution(mesh):
    both = P(ALL, None)
    return jax.shard_map(
        shards,
        mesh=mesh,
        in_specs=(
            P("dp", None, None), P("dp"), P("dp"), P(ALL, None, None),
            P(None, "tensor"), P(None, "tensor"), P(None, "tensor"), P("tensor", None),
            P(), P(), P(None, "tensor"), P(), P("tensor", None), P(), P(), P(), P(),
            both, both, both, P(ALL), P(ALL),
        ),
        out_specs=(P(ALL, None, None), P(ALL, None, None), both, both, both, P(ALL), P(ALL)),
        check_vma=False,
    )
```

```python
from functools import partial
import math

import jax
import jax.numpy as jnp
from jax import lax
from jax.experimental import pallas as pl
from jax.experimental.pallas import tpu as pltpu
from jax.sharding import PartitionSpec as P

HEADS = 12
EPS = 1e-05
MASKED = -1e30
ALL = ("dp", "tensor")
BF = jnp.bfloat16
F32 = jnp.float32


def mm(left, right):
    return jnp.dot(left, right, preferred_element_type=F32)


def mm_t(left, right):
    return lax.dot_general(left, right, (((1,), (1,)), ((), ())), preferred_element_type=F32)


def t_mm(left, right):
    return lax.dot_general(left, right, (((0,), (0,)), ((), ())), preferred_element_type=F32)


def norm_parts(values):
    average = jnp.mean(values, axis=-1, keepdims=True)
    centered = values - average
    variance = jnp.mean(centered * centered, axis=-1, keepdims=True)
    rstd = lax.rsqrt(variance + EPS)
    return centered * rstd, rstd


def norm_back(grad, gain, xhat, rstd):
    scaled = grad * gain
    return rstd * (
        scaled
        - jnp.mean(scaled, axis=-1, keepdims=True)
        - xhat * jnp.mean(scaled * xhat, axis=-1, keepdims=True)
    )


def gelu_parts(pre):
    cdf = 0.5 * (1.0 + lax.erf(pre * (1.0 / math.sqrt(2.0))))
    pdf = jnp.exp(-0.5 * pre * pre) * (1.0 / math.sqrt(2.0 * math.pi))
    return pre * cdf, cdf + pre * pdf


def limit(mebibytes):
    return pltpu.CompilerParams(vmem_limit_bytes=mebibytes * 2**20)


VMEM = pl.BlockSpec(memory_space=pltpu.VMEM)
SMEM = pl.BlockSpec(memory_space=pltpu.SMEM)
LITTLE = limit(24)
FAR_XY = [(i, i ^ 6) for i in range(8)]
CORE = [(i, i ^ 1) for i in range(8)]
ALONG_X = [(i, i ^ 2) for i in range(8)]
ALONG_Y = [(i, i ^ 4) for i in range(8)]
SPLIT_XY = [(i, i ^ (4 if i & 1 else 2)) for i in range(8)]
CROSS_XY = [(i, i ^ (3 if i & 1 else 5)) for i in range(8)]


def send(array, pairs):
    return lax.ppermute(array, "dp", pairs)


def shift(array, by, groups):
    return lax.ppermute(array, "tensor", [(i, (i + by) % groups) for i in range(groups)])


def scoped(name, step, *args):
    with jax.named_scope(name):
        return step(*args)


def tie(array, *others):
    return lax.optimization_barrier((array,) + others)[0]


def fetch_blocks(spots_ref, sources, stage_ref, sem):
    if len(sources) == 1:
        pltpu.make_async_copy(sources[0], stage_ref, sem).start()
        return
    planes = planes_in_order(spots_ref)
    for k, (ref, first) in enumerate(views(sources)):
        for i, plane in enumerate(planes[1:] + planes[:1]):
            pltpu.make_async_copy(ref.at[first + i], stage_ref.at[spots_ref[k] * len(planes) + plane], sem).start()


def order_rows(stage_ref, join_ref, biases_ref):
    blocks = stage_ref.shape[0]
    rows = join_ref.shape[1] // blocks
    total = 0.0
    for b in range(0, blocks, 2):
        pair = [stage_ref[b + i].astype(F32) for i in range(2)]
        for m in range(3):
            both = jnp.concatenate([block[m * rows : (m + 1) * rows] for block in pair], axis=0)
            join_ref[m, b * rows : (b + 2) * rows, :] = both.astype(BF)
        total = total + pair[0][3 * rows :] + pair[1][3 * rows :]
    biases_ref[...] = total


def fetch(spots_ref, sources, out_ref, sems, which, side_by_side=False):
    planes = planes_in_order(spots_ref)
    dim = sources[-1].shape[-1]
    rows = sources[-1].shape[-2]

    def copy(source, r, at):
        if side_by_side:
            target = out_ref.at[at, pl.ds(r * dim, dim)]
        else:
            target = out_ref.at[pl.ds(r * rows + at.start, at.size)]
        pltpu.make_async_copy(source, target, sems.at[r]).start()

    for r in which:
        if len(sources) == 1:
            copy(sources[0].at[planes[r]], r, pl.ds(0, rows))
        elif r == 0:
            copy(sources[-1], r, pl.ds(0, rows))
        else:
            for k, (ref, first) in enumerate(views(sources[:-1])):
                part = ref.shape[1]
                copy(ref.at[first + r - 1], r, pl.ds(pl.multiple_of(spots_ref[k] * part, part), part))


def arrive(out_ref, sems, r, side_by_side=False):
    dim = out_ref.shape[0] if side_by_side else out_ref.shape[1]
    block = out_ref.at[:, pl.ds(r * dim, dim)] if side_by_side else out_ref.at[pl.ds(r * out_ref.shape[0] // 4, out_ref.shape[0] // 4)]
    pltpu.make_async_copy(block, block, sems.at[r]).wait()


def fetch_stacked(spots_ref, sources, out_ref, sems, last):
    groups, dim = out_ref.shape[0], out_ref.shape[1]
    chosen = range(groups - 1, groups) if last else range(groups - 1)
    if len(sources) == 1:
        for m in chosen:
            pltpu.make_async_copy(sources[0].at[m], out_ref.at[m], sems.at[m]).start()
        return
    own = sources[-groups:]
    pieces = views(sources[:-groups])
    width, rows = dim // groups, pieces[0][0].shape[1]
    per = width // rows
    my_z = spots_ref[8]
    for m in chosen:
        at = pl.ds(pl.multiple_of(my_z * width, width), width)
        pltpu.make_async_copy(own[m], out_ref.at[m, at], sems.at[m]).start()
    for k, (ref, first) in enumerate(pieces):
        e = spots_ref[k]
        m = lax.div(e, per)

        @pl.when((m == groups - 1) == last)
        def _():
            for i, plane in enumerate(planes_in_order(spots_ref)[1:]):
                at = pl.ds(pl.multiple_of(plane * width + lax.rem(e, per) * rows, rows), rows)
                pltpu.make_async_copy(ref.at[first + i], out_ref.at[m, at], sems.at[m]).start()


def arrive_stacked(out_ref, sems, m):
    pltpu.make_async_copy(out_ref.at[m], out_ref.at[m], sems.at[m]).wait()


def views(sources):
    if len(sources) == 8:
        return [(source, 0) for source in sources]
    both, near, far, swapped, swapped_far = sources
    count = far.shape[0]
    return [(both, 0), (both, count), (near, 0), (near, count), (far, 0), (swapped, 0), (swapped, count), (swapped_far, 0)]


def cut_kernel(spots_ref, *refs):
    count = (len(refs) - 1) // 3
    shards, outs, sems = refs[:count], refs[count:-1], refs[-1]
    pairs = []
    for i, shard in enumerate(shards):
        rows = outs[2 * i].shape[0]
        at = pl.ds(pl.multiple_of(lax.div(spots_ref[0], 2) * rows, rows), rows)
        pairs.append((shard.at[at], outs[2 * i]))
        at = pl.ds(pl.multiple_of(spots_ref[0] * (rows // 2), rows // 2), rows // 2)
        pairs.append((shard.at[at], outs[2 * i + 1]))
    for copy in begin(pairs, sems):
        copy.wait()


def cut(spots, shards):
    outs = []
    for shard in shards:
        rows, dim = shard.shape
        outs += [jax.ShapeDtypeStruct((rows // 4, dim), BF), jax.ShapeDtypeStruct((rows // 8, dim), BF)]
    return pl.pallas_call(
        cut_kernel,
        out_shape=outs,
        in_specs=[SMEM] + [ANY] * len(shards),
        out_specs=[VMEM] * len(outs),
        scratch_shapes=[pltpu.SemaphoreType.DMA((len(outs),))],
        compiler_params=limit(60),
    )(spots, *shards)


def merge_kernel(spots_ref, *refs, count):
    beside, across, beside2, across2, *own = refs[:count]
    outs = refs[count:]
    core = lax.rem(spots_ref[0], 2)
    rows = across.shape[0]
    blocks = 3 + len(own) // 2
    sides = [outs[0], outs[1]] if len(outs) == 2 else [outs[0].at[pl.ds(i * blocks, blocks)] for i in range(2)]
    parts = [pl.ds(pl.multiple_of(at * rows, rows), rows) for at in (core, 1 - core)]
    for side, at, last, mine in zip(sides, parts, (across, across2), own or (None, None)):
        side[core] = beside[at, :]
        side[1 - core] = beside2[at, :]
        side[2] = last[...]
        if mine is not None:
            side[3] = mine[...]


def merge(spots, arrays, split):
    rows, dim = arrays[1].shape
    blocks = 3 + (len(arrays) - 4) // 2
    outs = [blocks, blocks] if split else [2 * blocks]
    return pl.pallas_call(
        partial(merge_kernel, count=len(arrays)),
        out_shape=[jax.ShapeDtypeStruct((out, rows, dim), BF) for out in outs],
        in_specs=[SMEM] + [VMEM] * len(arrays),
        out_specs=[VMEM] * len(outs),
        compiler_params=limit(8),
    )(spots, *arrays)


def planes_in_order(spots_ref, groups=4):
    return [lax.rem(spots_ref[8] + step, groups) for step in (0, 1, groups - 1, 2)]


def begin(pairs, sems):
    copies = [pltpu.make_async_copy(source, target, sems.at[i]) for i, (source, target) in enumerate(pairs)]
    for one in copies:
        one.start()
    return copies


WEIGHT_SEMS = pltpu.SemaphoreType.DMA((4,))
ANY = pl.BlockSpec(memory_space=pltpu.HBM)


class Gather:
    def __init__(self, dp_size, groups, my_d, my_z, seqs):
        self.dp_size, self.groups, self.my_d, self.my_z = dp_size, groups, my_d, my_z
        self.paired = dp_size == 8 and groups == 4 and seqs == 2
        core = lax.rem(my_d, 2)
        even = [0, 1, 2, 3, 7, 5, 4, 6]
        odd = [0, 1, 4, 5, 7, 3, 2, 6]
        flips = jnp.where(core == 0, jnp.array(even, jnp.int32), jnp.array(odd, jnp.int32))
        self.spots = jnp.concatenate([jnp.bitwise_xor(my_d, flips), my_z[None]]).astype(jnp.int32)

    def all_parts(self, part):
        whole = lax.all_gather(part, ("dp", "tensor"), axis=0)
        return whole.reshape((self.dp_size, self.groups) + part.shape).transpose(1, 0, 2, 3)

    def part_of(self, shard):
        rows = shard.shape[0] // self.dp_size
        return lax.dynamic_slice_in_dim(shard, self.my_d * rows, rows, 0)

    def all_rounds(self, parts, early, steps):
        count = len(parts)
        gathered, spread = [], []
        ahead, done = self.planes(parts[0], 0), [rows for part in parts[1:] for rows in part[:2]] + early
        for r in range(count + 2):
            with jax.named_scope("round%d" % r):
                ready = list(lax.optimization_barrier((*ahead, *done))) if r < count else list(done)
                ahead = ready[: len(ahead)]
                if r >= 1:
                    at = len(ahead)
                    if r <= count:
                        last = spread[r - 1]
                        last[1] = ready[at : at + len(last[1])]
                        at += len(last[1])
                    if 2 <= r <= count:
                        spread[r - 2][2] = ready[at]
                done = []
                if 1 <= r < count:
                    near_half = last[1][0] if len(last[1]) == 2 else last[1][0][: last[1][0].shape[0] // 2]
                    last.append(scoped("far", send, near_half, CROSS_XY))
                if r < count:
                    beside, across = ahead
                    ahead = []
                    if r + 1 < count:
                        ahead = self.planes([tie(rows, beside) for rows in parts[r + 1]], r + 1)
                    others = [scoped("others", send, beside, CORE), scoped("others", send, across, CORE)]
                    both = merge(self.spots, [beside, across, *others, *parts[r][2:]], r == count - 1)
                    near = [scoped("near", send, side, SPLIT_XY) for side in both]
                    spread.append([both, near])
                    done += near
                else:
                    ahead = []
                if 1 <= r <= count:
                    late = []
                    last.append([scoped("swap", send, array, CORE) for array in last[1][:-1]])
                    last[3].append(scoped("swap", send, tie(last[1][-1], *late), CORE))
                    done += (last[2:3] if r < count else []) + last[3]
                if r >= 2:
                    whole = spread[r - 2]
                    gathered.append([*whole[0], *whole[1], whole[2], *whole[3], scoped("swapfar", send, whole[2], CORE)])
                done += steps[r](gathered)
                if r == count - 1:
                    spread[r].append(scoped("far", send, tie(near[0], *done[len(near) :]), CROSS_XY))
        return gathered

    def planes(self, part, r):
        with jax.named_scope("planes%d" % r):
            groups = self.groups
            pairs = [
                (d * groups + z, d * groups + (z + (1 if d & 1 else groups - 1)) % groups)
                for d in range(self.dp_size)
                for z in range(groups)
            ]
            beside = scoped("beside", lax.ppermute, part[1], ("dp", "tensor"), pairs)
            return beside, scoped("across", shift, part[0], 2, groups)

    def half_of(self, quarter):
        rows = quarter.shape[0] // 2
        return jnp.where(lax.rem(self.my_d, 2) == 0, quarter[:rows], quarter[rows:])

    def quarter_of(self, shard):
        rows = 2 * shard.shape[0] // self.dp_size
        return lax.dynamic_slice_in_dim(shard, self.my_d // 2 * rows, rows, 0)

    def whole(self, part, stacked=False):
        whole = self.all_parts(part)
        dim = part.shape[1]
        if stacked:
            whole = whole.reshape(self.groups, 4, -1, dim).transpose(1, 0, 2, 3)
        return [whole.reshape(4, -1, dim)]


def reduce_grads(gather, grads, own_rows, between, at_last):
    groups, spots = gather.groups, gather.spots
    if not gather.paired:
        mats, bias = grads
        mats = lax.psum_scatter(mats, ("dp", "tensor"), scatter_dimension=1, tiled=True)
        middle = between(None)
        return (mats[0], mats[1], mats[2], lax.psum(bias, ("dp", "tensor"))), at_last(None)
    keep, away = grads
    rows, dim = keep.shape[1:]
    low = jax.ShapeDtypeStruct((rows, dim), BF)
    come = scoped("cores", send, away, CORE)
    to_x, to_y, to_far = pl.pallas_call(
        add_cores_kernel,
        out_shape=[low, low, low],
        in_specs=[SMEM, ANY, ANY],
        out_specs=[ANY] * 3,
        scratch_shapes=[pltpu.VMEM((3, rows, dim), BF)] * 3 + [pltpu.SemaphoreType.DMA((6,)), pltpu.SemaphoreType.DMA((3,))],
        compiler_params=limit(60),
    )(spots, keep, come)
    from_far = scoped("far", send, to_far, FAR_XY)
    from_x = scoped("x", send, to_x, ALONG_X)
    from_y = scoped("y", send, to_y, ALONG_Y)
    block = jax.ShapeDtypeStruct((3 * own_rows + 8, dim), BF)
    middle = between(to_far)
    mine, *goes = pl.pallas_call(
        add_plane_kernel,
        out_shape=[jax.ShapeDtypeStruct((3 * own_rows + 8, dim), F32)] + [block] * (groups - 1),
        in_specs=[SMEM] + [ANY] * 5,
        out_specs=[VMEM] * groups,
        scratch_shapes=[pltpu.VMEM((rows - 16, dim), F32), pltpu.VMEM((5, rows, dim), BF), pltpu.SemaphoreType.DMA((5,))],
        compiler_params=limit(60),
    )(spots, from_x, from_y, from_far, tie(keep, middle), come)
    after = at_last(mine)
    comes = [scoped("stack%d" % i, shift, go, i + 1, groups) for i, go in enumerate(goes)]
    part = jax.ShapeDtypeStruct((own_rows, dim), F32)
    sums = pl.pallas_call(
        add_stack_kernel,
        out_shape=[part, part, part, jax.ShapeDtypeStruct((8, dim), F32)],
        in_specs=[VMEM] * groups,
        out_specs=[VMEM] * 4,
        compiler_params=LITTLE,
    )(mine, *comes)
    return sums, after


def cost(flops, moved, exps=0):
    return pl.CostEstimate(flops=int(flops), bytes_accessed=int(moved), transcendentals=int(exps))


def head_masks():
    lane = lax.broadcasted_iota(jnp.int32, (1, 128), 1)
    first = (lane < 64).astype(F32)
    return [first.astype(BF), (1.0 - first).astype(BF)], lane < 64


def attention_kernel(spots_ref, len_ref, x_ref, norms_ref, *refs):
    *sources, q_hbm, k_hbm, v_hbm, p_hbm, low_ref, xhat_hbm, rstd_ref, w_ref, ctx_ref, q_ref, k_ref, v_ref, p_ref, xhat_ref, sems, store_sems = refs
    fetch_stacked(spots_ref, sources, w_ref, sems, False)
    fetch_stacked(spots_ref, sources, w_ref, sems, True)
    rows, dim = x_ref.shape
    for m in range(4):
        arrive_stacked(w_ref, sems, m)
    seq_len = p_ref.shape[1]
    x = x_ref[...]
    q_ref[...] = (mm_t(x, w_ref[0]).astype(BF).astype(F32) * (1.0 / math.sqrt(dim // HEADS))).astype(BF)
    k_ref[...] = mm_t(x, w_ref[1]).astype(BF)
    v_ref[...] = mm_t(x, w_ref[2]).astype(BF)
    stores = begin(((q_ref, q_hbm), (k_ref, k_hbm), (v_ref, v_hbm)), store_sems)
    masks, first = head_masks()
    key_at = lax.broadcasted_iota(jnp.int32, (seq_len, 1), 0)

    for s in range(rows // seq_len):
        at = slice(s * seq_len, (s + 1) * seq_len)
        valid = key_at < len_ref[s]
        for j in range(HEADS // 2):
            cols = slice(128 * j, 128 * (j + 1))
            q, k, v = q_ref[at, cols], k_ref[at, cols], v_ref[at, cols]
            parts = []
            for h in range(2):
                scores = jnp.where(valid, mm_t(k, q * masks[h]), MASKED)
                exps = jnp.exp(scores - jnp.max(scores, axis=0, keepdims=True))
                probs = (exps * (1.0 / jnp.sum(exps, axis=0, keepdims=True))).astype(BF)
                p_ref[s * HEADS + 2 * j + h] = probs
                parts.append(t_mm(probs, v))
            ctx_ref[at, cols] = jnp.where(first, parts[0], parts[1]).astype(BF)
        heads = pl.ds(s * HEADS, HEADS)
        stores += begin(((p_ref.at[heads], p_hbm.at[heads]),), store_sems.at[pl.ds(3 + s, 1)])
    xhat, rstd = norm_parts(x.astype(F32) + mm(ctx_ref[...], w_ref[3]))
    xhat_ref[...] = xhat
    stores += begin(((xhat_ref, xhat_hbm),), store_sems.at[pl.ds(3 + rows // seq_len, 1)])
    rstd_ref[...] = rstd
    low_ref[...] = (xhat * norms_ref[0:1, :] + norms_ref[1:2, :]).astype(BF)
    for store in stores:
        store.wait()


def attention_forward(spots, lengths, x, sources, norms, seq_len):
    rows, dim = x.shape
    seqs = rows // seq_len
    low = jax.ShapeDtypeStruct((rows, dim), BF)
    return pl.pallas_call(
        attention_kernel,
        out_shape=[low, low, low,
                   jax.ShapeDtypeStruct((seqs * HEADS, seq_len, seq_len), BF), low,
                   jax.ShapeDtypeStruct((rows, dim), F32), jax.ShapeDtypeStruct((rows, 1), F32)],
        in_specs=[SMEM] * 2 + [VMEM] * 2 + [ANY] * len(sources),
        out_specs=[ANY] * 4 + [VMEM, ANY, VMEM],
        scratch_shapes=[pltpu.VMEM((4, dim, dim), BF)] + [pltpu.VMEM((rows, dim), BF)] * 4 + [
            pltpu.VMEM((seqs * HEADS, seq_len, seq_len), BF), pltpu.VMEM((rows, dim), F32),
            WEIGHT_SEMS, pltpu.SemaphoreType.DMA((4 + seqs,)),
        ],
        compiler_params=limit(60),
        cost_estimate=cost(2 * rows * dim * (4 * dim + 2 * seq_len), 2 * (4 * dim * dim + 8 * rows * dim), rows * seq_len * HEADS),
    )(spots, lengths, x, norms, *sources)


def by_rows(rows, step, work, unroll=1):
    work(slice(0, rows))


def ffn_in_kernel(spots_ref, x_ref, bias_ref, *refs):
    *sources, act_hbm, slope_hbm, act_ref, slope_ref, w_ref, pre_ref, sems, store_sems = refs
    units = pre_ref.shape[1]
    order = planes_in_order(spots_ref)
    stores = []
    fetch(spots_ref, sources, w_ref, sems, [0, 1])
    for r in range(4):
        fetch(spots_ref, sources, w_ref, sems, [r + 2] if r < 2 else [])
        arrive(w_ref, sems, r)
        pre_ref[...] = mm(x_ref[...], w_ref[r * x_ref.shape[1] : (r + 1) * x_ref.shape[1], :])
        cols = slice(r * units, (r + 1) * units)
        act, slope = gelu_parts(pre_ref[...] + bias_ref[order[r]])
        act_ref[:, cols] = act.astype(BF)
        slope_ref[:, cols] = slope.astype(BF)
        pairs = [(act_ref, act_hbm), (slope_ref, slope_hbm)]
        stores += begin([(ref.at[:, cols], hbm.at[:, cols]) for ref, hbm in pairs], store_sems.at[pl.ds(2 * r, 2)])
    for store in stores:
        store.wait()


def ffn_forward(spots, x, sources, bias, units):
    rows, dim = x.shape
    planes = bias.shape[0] // units
    out = jax.ShapeDtypeStruct((rows, planes * units), BF)
    return pl.pallas_call(
        ffn_in_kernel,
        out_shape=[out, out],
        in_specs=[SMEM] + [VMEM] * 2 + [ANY] * len(sources),
        out_specs=[ANY] * 2,
        scratch_shapes=[
            pltpu.VMEM((rows, planes * units), BF), pltpu.VMEM((rows, planes * units), BF),
            pltpu.VMEM((planes * dim, units), BF), pltpu.VMEM((rows, units), F32), WEIGHT_SEMS, pltpu.SemaphoreType.DMA((8,)),
        ],
        compiler_params=limit(60),
        cost_estimate=cost(2 * rows * dim * units * planes, 2 * planes * units * (dim + 2 * rows), 2 * rows * units * planes),
    )(spots, x, bias.reshape(planes, 1, units), *sources)


def two_pass(values, table):
    high = values.astype(BF)
    return mm(high, table) + mm((values - high.astype(F32)).astype(BF), table)


def put_rows(ref, mats, bias):
    at = 0
    for mat in mats:
        ref[at : at + mat.shape[0], :] = mat.astype(BF)
        at += mat.shape[0]
    high = bias.astype(BF).astype(F32)
    ref[at : at + 16, :] = jnp.concatenate([high, bias - high], axis=0).astype(BF)


def sum_rows(arrays):
    total = arrays[0].astype(F32)
    for array in arrays[1:]:
        total = total + array.astype(F32)
    rows = total.shape[0] - 16
    return total[:rows], total[rows : rows + 8] + total[rows + 8 :]


def add_cores_kernel(spots_ref, keep_hbm, come_hbm, *refs):
    hbm, (sums_ref, keep_ref, come_ref, sems, store_sems) = refs[:3], refs[3:]
    quarter = lax.div(spots_ref[0], 2)
    pairs = []
    for i in range(3):
        q = jnp.bitwise_xor(quarter, i + 1)
        pairs += [(keep_hbm.at[q], keep_ref.at[i]), (come_hbm.at[q], come_ref.at[i])]
    copies = begin(pairs, sems)
    stores = []
    for i in range(3):
        copies[2 * i].wait()
        copies[2 * i + 1].wait()
        mats, bias = sum_rows([keep_ref[i], come_ref[i]])
        put_rows(sums_ref.at[i], [mats], bias)
        stores += begin(((sums_ref.at[i], hbm[i]),), store_sems.at[pl.ds(i, 1)])
    for store in stores:
        store.wait()


def fold_bias(bias):
    high = bias.astype(BF).astype(F32)
    row = lax.broadcasted_iota(jnp.int32, (8, 1), 0)
    return jnp.where(row < 4, high, pltpu.roll(bias - high, 4, 0))


def add_plane_kernel(spots_ref, *refs):
    parts, refs = refs[:3], refs[3:]
    keep_hbm, come_hbm, mine_ref, *go_refs, total_ref, arrays_ref, sems = refs
    quarter = lax.div(spots_ref[0], 2)
    sources = (keep_hbm.at[quarter], come_hbm.at[quarter], *parts)
    for copy in begin([(source, arrays_ref.at[i]) for i, source in enumerate(sources)], sems):
        copy.wait()
    total_ref[...], bias = sum_rows([arrays_ref[i] for i in range(5)])
    groups = len(go_refs) + 1
    width = total_ref.shape[0] // 3
    rows = width // groups

    def block(plane):
        at = [pl.multiple_of(i * width + plane * rows, 8) for i in range(3)]
        return jnp.concatenate([total_ref[pl.ds(a, rows), :] for a in at], axis=0)

    my_z = spots_ref[8]
    mine_ref[...] = jnp.concatenate([block(my_z), bias], axis=0)
    folded = fold_bias(bias)
    for i, ref in enumerate(go_refs):
        ref[...] = jnp.concatenate([block(lax.rem(my_z + i + 1, groups)), folded], axis=0).astype(BF)


def add_stack_kernel(mine_ref, *refs):
    come_refs, (q_ref, k_ref, v_ref, bias_ref) = refs[:-4], refs[-4:]
    total = mine_ref[...]
    rows = q_ref.shape[0]
    for ref in come_refs:
        come = ref[...].astype(F32)
        bias = come[3 * rows :]
        total = total + jnp.concatenate([come[: 3 * rows], bias + pltpu.roll(bias, 4, 0)], axis=0)
    q_ref[...], k_ref[...], v_ref[...] = (total[i * rows : (i + 1) * rows] for i in range(3))
    bias_ref[...] = total[3 * rows :]


def belongs(shape, unit_dim, adapter_dim, neck):
    unit, adapter = (lax.broadcasted_iota(jnp.int32, shape, d) for d in (unit_dim, adapter_dim))
    return jnp.where(jnp.logical_and(unit >= adapter * neck, unit < (adapter + 1) * neck), 1.0, 0.0).astype(BF)


def joining_kernel(
    spots_ref, mask_ref, norms_ref, act_hbm, xhat1_hbm, cot_hbm, *refs, halves, count, adapters
):
    gain1, bias1, gain2, bias2 = (norms_ref[i : i + 1, :] for i in range(4))
    down_hbm, up_hbm, *refs = refs
    join_sources, sources, refs = refs[:count], refs[count:-38], refs[-38:]
    stage_ref, biases_ref, stage_sem, refs = refs[-3], refs[-2], refs[-1], refs[:-3]
    out_hbm, g2_hbm, g_ffn_ref, grad_hbm0, grad_hbm1 = refs[:5]
    act_ref, w_out_ref, down_ref, up_ref, join_ref, xhat1_ref, cot_ref, act_sems, out_sems, sems, store_sems = refs[5:16]
    ffn_ref, u_ref, w_ref, big_u_ref, big_w_ref, p_wide_ref, sums_ref = refs[16:23]
    x_ref, act2_ref, slope_ref, q_ref, gq_ref, low_ref, mixed_ref, t_ref = refs[23:31]
    out_ref, g2_ref, bias_rows_ref, bias_ref = refs[31:35]
    rows, dim = out_ref.shape
    units = w_out_ref.shape[0] // 4
    seqs = mask_ref.shape[0]
    per = rows // seqs
    everyone = [slice(i * per, (i + 1) * per) for i in range(seqs)]
    fscale = 1.0 / math.sqrt(dim)
    member = belongs((dim, 128), 0, 1, dim // adapters)
    member_t = belongs((128, dim), 1, 0, dim // adapters)
    lane = lax.broadcasted_iota(jnp.int32, (1, 128), 1)
    loads = []

    def issue(r):
        if r < 4:
            fetch(spots_ref, sources, w_out_ref, out_sems, [r])
            cols = pl.ds(r * units, units)
            loads.extend(begin(((act_hbm.at[:, cols], act_ref.at[:, cols]),), act_sems.at[pl.ds(r, 1)]))
        elif r == 4:
            fetch_blocks(spots_ref, join_sources, stage_ref, stage_sem)
        elif r == 5:
            pairs = ((down_hbm, down_ref), (up_hbm, up_ref), (xhat1_hbm, xhat1_ref), (cot_hbm, cot_ref))
            loads.extend(begin(pairs, sems))

    issue(0)
    issue(1)
    issue(2)
    for r in range(4):
        issue(r + 3)
        loads[r].wait()
        arrive(w_out_ref, out_sems, r)
        if r % 2 == 1:
            both = slice((r - 1) * units, (r + 1) * units)
            for at in everyone:
                term = mm(act_ref[at, both], w_out_ref[both, :])
                ffn_ref[at, :] = term if r == 1 else ffn_ref[at, :] + term
    loads = loads[4:]
    for at in everyone:
        x_ref[at, :] = ffn_ref[at, :].astype(BF)
    pltpu.make_async_copy(stage_ref, stage_ref, stage_sem).wait()
    order_rows(stage_ref, join_ref, biases_ref)
    qb, vb = biases_ref[0:1, :], biases_ref[1:2, :]
    for load in loads:
        load.wait()
    up = up_ref[...]
    halves_of = {}

    def narrow(i, name, value=None):
        if value is not None:
            halves_of[i, name] = value
        return halves_of[i, name]

    def per_adapter(values):
        high = values.astype(BF)
        return mm(high, member) + mm((values - high.astype(F32)).astype(BF), member)

    def to_q(i, at):
        q_ref[at, :] = (mm(x_ref[at, :], join_ref[0]) + qb).astype(BF)

    def down(i, at):
        act, slope = gelu_parts(mm(x_ref[at, :], down_ref[...]))
        act2_ref[at, :] = act.astype(BF)
        slope_ref[at, :] = slope.astype(BF)

    def to_u(i, at):
        u = mm_t(q_ref[at, :], join_ref[1])
        u_ref[at, :] = u
        narrow(i, "dot", jnp.sum(ffn_ref[at, :] * u, axis=-1, keepdims=True))

    def scores(i, at):
        big_u = mm_t(u_ref[at, :].astype(BF), up)
        big_u_ref[at, :] = big_u
        fscores = (per_adapter(act2_ref[at, :].astype(F32) * big_u) + narrow(i, "dot")) * fscale
        bit = lax.rem(lax.shift_right_logical(jnp.full_like(lane, mask_ref[i]), jnp.minimum(lane, adapters)), 2)
        fscores = jnp.where(jnp.logical_and(bit == 1, lane < adapters), fscores, MASKED)
        fexp = jnp.exp(fscores - jnp.max(fscores, axis=-1, keepdims=True))
        narrow(i, "probs", fexp / jnp.sum(fexp, axis=-1, keepdims=True))

    def mix(i, at):
        p_wide = two_pass(narrow(i, "probs"), member_t)
        p_wide_ref[at, :] = p_wide
        weighed = (p_wide * act2_ref[at, :].astype(F32)).astype(BF)
        mixed_ref[at, :] = (ffn_ref[at, :] + mm(weighed, up)).astype(BF)

    def norm(i, at):
        normed1 = xhat1_ref[at, :] * gain1 + bias1
        xhat2, rstd2 = norm_parts(normed1 + mm(mixed_ref[at, :], join_ref[2]) + vb)
        out_ref[at, :] = (xhat2 * gain2 + bias2).astype(BF)
        g2 = norm_back(cot_ref[at, :].astype(F32), gain2, xhat2, rstd2)
        g2_ref[at, :] = g2
        low_ref[at, :] = g2.astype(BF)
        narrow(i, "dot2", jnp.sum(g2 * vb, axis=-1, keepdims=True))
        narrow(i, "d_vb", jnp.sum(g2.reshape(-1, 8, dim), axis=0))

    def to_w(i, at):
        w = mm_t(low_ref[at, :], join_ref[2])
        w_ref[at, :] = w
        narrow(i, "dot2", narrow(i, "dot2") + jnp.sum(ffn_ref[at, :] * w, axis=-1, keepdims=True))

    def score_grads(i, at):
        big_w = mm_t(w_ref[at, :].astype(BF), up)
        big_w_ref[at, :] = big_w
        gvals = per_adapter(act2_ref[at, :].astype(F32) * big_w) + narrow(i, "dot2")
        fprobs = narrow(i, "probs")
        gs = fprobs * (gvals - jnp.sum(gvals * fprobs, axis=-1, keepdims=True)) * fscale
        narrow(i, "gs", gs)
        narrow(i, "gs_sum", jnp.sum(gs, axis=-1, keepdims=True))

    def to_t(i, at):
        wide = two_pass(narrow(i, "gs"), member_t)
        weighed = (wide * act2_ref[at, :].astype(F32)).astype(BF)
        grad = wide * big_u_ref[at, :] + p_wide_ref[at, :] * big_w_ref[at, :]
        slope_ref[at, :] = (grad * slope_ref[at, :].astype(F32)).astype(BF)
        t_ref[at, :] = (mm(weighed, up) + narrow(i, "gs_sum") * ffn_ref[at, :]).astype(BF)

    def to_gq(i, at):
        gq = mm(t_ref[at, :], join_ref[1]).astype(BF)
        gq_ref[at, :] = gq
        narrow(i, "d_qb", jnp.sum(gq.astype(F32).reshape(-1, 8, dim), axis=0))

    def all_halves(*steps):
        for step in steps:
            for i, at in enumerate(everyone):
                step(i, at)

    all_halves(to_q, down, to_u, scores, mix, norm)
    stores = begin(((out_ref, out_hbm), (g2_ref, g2_hbm)), store_sems)
    all_halves(to_w, score_grads)
    sums_ref[2] = t_mm(mixed_ref[...], low_ref[...]).astype(sums_ref.dtype)
    all_halves(to_t)
    sums_ref[1] = t_mm(t_ref[...], q_ref[...]).astype(sums_ref.dtype)
    all_halves(to_gq)
    sums_ref[0] = t_mm(x_ref[...], gq_ref[...]).astype(sums_ref.dtype)
    row = lax.broadcasted_iota(jnp.int32, (8, 1), 0)
    d_qb, d_vb = (
        jnp.sum(sum(narrow(i, name) for i in range(seqs)), axis=0, keepdims=True) for name in ("d_qb", "d_vb")
    )
    bias_ref[...] = jnp.where(row == 0, d_qb, jnp.where(row == 1, d_vb, 0.0))
    if halves:
        core = lax.rem(spots_ref[0], 2)
        part = dim // 8
        put_rows(bias_rows_ref, [], bias_ref[...])
        for hbm, side, sem in ((grad_hbm1, 1 - core, store_sems.at[2]), (grad_hbm0, core, store_sems.at[3])):
            for q in range(4):
                at = pl.ds(pl.multiple_of((2 * q + side) * part, part), part)
                for i in range(3):
                    pltpu.make_async_copy(sums_ref.at[i, at], hbm.at[q, pl.ds(i * part, part)], sem).start()
                pltpu.make_async_copy(bias_rows_ref, hbm.at[q, pl.ds(3 * part, 16)], sem).start()
            stores.append(pltpu.make_async_copy(hbm, hbm, sem))
    else:
        stores += begin(((sums_ref, grad_hbm0), (bias_ref, grad_hbm1)), store_sems.at[pl.ds(2, 2)])
    for i, at in enumerate(everyone):
        total = mm_t(slope_ref[at, :], down_ref[...]) + mm_t(gq_ref[at, :], join_ref[0])
        g_ffn_ref[at, :] = (narrow(i, "gs_sum") * u_ref[at, :] + w_ref[at, :] + total).astype(BF)
    for store in stores:
        store.wait()


def joining(spots, halves, act, sources, adapt_down, up, join_sources, masks, adapters, xhat1, norms, cot):
    rows, dim = xhat1.shape
    if halves:
        grads = [jax.ShapeDtypeStruct((4, 3 * dim // 8 + 16, dim), BF)] * 2
    else:
        grads = [jax.ShapeDtypeStruct((3, dim, dim), F32), jax.ShapeDtypeStruct((8, dim), F32)]
    wide, low = pltpu.VMEM((rows, dim), F32), pltpu.VMEM((rows, dim), BF)
    height, blocks = join_sources[-1].shape[-2:][0], 32
    stage_shape = join_sources[0].shape if len(join_sources) == 1 else (blocks, height, dim)
    return pl.pallas_call(
        partial(joining_kernel, halves=halves, count=len(join_sources), adapters=adapters),
        out_shape=[
            jax.ShapeDtypeStruct((rows, dim), BF),
            jax.ShapeDtypeStruct((rows, dim), F32),
            jax.ShapeDtypeStruct((rows, dim), BF),
        ] + grads,
        in_specs=[SMEM] * 2 + [VMEM] + [ANY] * (len(sources) + len(join_sources) + 5),
        out_specs=[ANY, ANY, VMEM, ANY, ANY],
        scratch_shapes=[
            pltpu.VMEM(act.shape, BF),
            pltpu.VMEM((act.shape[1], dim), BF),
            pltpu.VMEM(adapt_down.shape, BF),
            pltpu.VMEM(up.shape, BF),
            pltpu.VMEM((3, dim, dim), BF),
            wide,
            low,
            WEIGHT_SEMS,
            WEIGHT_SEMS,
            pltpu.SemaphoreType.DMA((4,)),
            pltpu.SemaphoreType.DMA((4,)),
        ] + [wide] * 6 + [pltpu.VMEM((3, dim, dim), BF if halves else F32)] + [low] * 8 + [
            low,
            wide,
            pltpu.VMEM((16, dim), BF),
            pltpu.VMEM((8, dim), F32),
            pltpu.VMEM(stage_shape, BF),
            pltpu.VMEM((8, dim), F32),
            pltpu.SemaphoreType.DMA,
        ],
        compiler_params=limit(60),
        cost_estimate=cost(2 * rows * dim * (15 * dim + act.shape[1]), 2 * dim * (8 * dim + 10 * rows), 2 * rows * dim),
    )(spots, masks, norms, act, xhat1, cot, adapt_down, up, *join_sources, *sources)


def ffn_back_kernel(spots_ref, g_ref, rstd_ref, norms_ref, slope_hbm, g2_hbm, xhat_hbm, *refs, count):
    refs, (out_sources, in_sources) = refs[sum(count) :], (refs[: count[0]], refs[count[0] : sum(count)])
    g1_hbm, low_hbm, g1_ref, low_ref, slope_ref, g2_ref, xhat_ref, w_out_ref, w_in_ref, pre_ref, out_sems, in_sems, slope_sems, sems, store_sems = refs
    units = w_out_ref.shape[0] // 4
    rows = g_ref.shape[0]
    everyone = [slice(i * rows // 2, (i + 1) * rows // 2) for i in range(2)]
    loads = []

    def issue(r):
        if r < 4:
            fetch(spots_ref, out_sources, w_out_ref, out_sems, [r])
            cols = pl.ds(r * units, units)
            loads.extend(begin(((slope_hbm.at[:, cols], slope_ref.at[:, cols]),), slope_sems.at[pl.ds(r, 1)]))
        elif r < 8:
            fetch(spots_ref, in_sources, w_in_ref, in_sems, [r - 4], side_by_side=True)
        elif r == 8:
            loads.extend(begin(((g2_hbm, g2_ref), (xhat_hbm, xhat_ref)), sems))

    issue(0)
    issue(1)
    for r in range(4):
        issue(r + 2)
        cols = slice(r * units, (r + 1) * units)
        arrive(w_out_ref, out_sems, r)
        loads[r].wait()
        for at in everyone:
            pre_ref[at, cols] = (mm_t(g_ref[at, :], w_out_ref[cols, :]) * slope_ref[at, cols].astype(F32)).astype(BF)
    for r in range(4, 8):
        issue(r + 2)
        arrive(w_in_ref, in_sems, r - 4, side_by_side=True)
        if r == 5:
            both = slice(0, 2 * units)
            for at in everyone:
                g1_ref[at, :] = mm_t(pre_ref[at, both], w_in_ref[:, both])
    for load in loads[4:]:
        load.wait()
    both = slice(2 * units, 4 * units)
    stores = []
    for at in everyone:
        total = mm_t(pre_ref[at, both], w_in_ref[:, both]) + g1_ref[at, :] + g2_ref[at, :]
        g1 = norm_back(total, norms_ref[0:1, :], xhat_ref[at, :], rstd_ref[at, :])
        g1_ref[at, :] = g1
        low_ref[at, :] = g1.astype(BF)
        stores += begin(((g1_ref.at[at], g1_hbm.at[at]), (low_ref.at[at], low_hbm.at[at])), store_sems.at[pl.ds(len(stores), 2)])
    for store in stores:
        store.wait()


def ffn_backward(spots, g_ffn, slope, out_sources, in_sources, g2, xhat, rstd, norms):
    rows, dim = xhat.shape
    planes = 4
    units = slope.shape[1] // planes
    return pl.pallas_call(
        partial(ffn_back_kernel, count=(len(out_sources), len(in_sources))),
        out_shape=[jax.ShapeDtypeStruct((rows, dim), F32), jax.ShapeDtypeStruct((rows, dim), BF)],
        in_specs=[SMEM] + [VMEM] * 3 + [ANY] * (len(out_sources) + len(in_sources) + 3),
        out_specs=[ANY, ANY],
        scratch_shapes=[
            pltpu.VMEM((rows, dim), F32), pltpu.VMEM((rows, dim), BF),
            pltpu.VMEM(slope.shape, BF), pltpu.VMEM((rows, dim), F32), pltpu.VMEM((rows, dim), F32),
            pltpu.VMEM((planes * units, dim), BF), pltpu.VMEM((dim, planes * units), BF), pltpu.VMEM(slope.shape, BF),
            WEIGHT_SEMS, WEIGHT_SEMS, WEIGHT_SEMS, pltpu.SemaphoreType.DMA((2,)),
            pltpu.SemaphoreType.DMA((4,)),
        ],
        compiler_params=limit(60),
        cost_estimate=cost(4 * rows * dim * units * planes, 2 * planes * units * (2 * dim + rows)),
    )(spots, g_ffn, rstd, norms, slope, g2, xhat, *out_sources, *in_sources)


def attention_back_heads(s, seq_len, q_ref, k_ref, v_ref, p_ref, g_ref, dq_ref, dk_ref, dv_ref, first_seq):
    dim = q_ref.shape[1]
    scale = 1.0 / math.sqrt(dim // HEADS)
    masks = head_masks()[0]
    at = slice((s - first_seq) * seq_len, (s - first_seq + 1) * seq_len)
    for j in range(HEADS // 2):
        cols = slice(128 * j, 128 * (j + 1))
        q, k, v, g = q_ref[at, cols], k_ref[at, cols], v_ref[at, cols], g_ref[at, cols]
        split = [jnp.concatenate([array * mask for mask in masks], axis=0) for array in (q, k, g)]
        probs_low = [p_ref[(s - first_seq) * HEADS + 2 * j + h] for h in range(2)]
        g_scores = []
        for h in range(2):
            probs = probs_low[h].astype(F32)
            g_probs = mm_t(v, split[2][h * seq_len : (h + 1) * seq_len])
            g_scores.append((probs * (g_probs - jnp.sum(g_probs * probs, axis=0, keepdims=True))).astype(BF))
        dq_ref[at, cols] = (t_mm(jnp.concatenate(g_scores, axis=0), split[1]) * scale).astype(BF)
        dk_ref[at, cols] = mm(jnp.concatenate(g_scores, axis=1), split[0]).astype(BF)
        dv_ref[at, cols] = mm(jnp.concatenate(probs_low, axis=1), split[2]).astype(BF)


def load_heads(hbm, vmem, sems, first, count):
    seq_len = hbm[3].shape[1]
    rows, heads = pl.ds(first * seq_len, count * seq_len), pl.ds(first * HEADS, count * HEADS)
    pairs = [(hbm[i].at[rows], vmem[i]) for i in range(3)] + [(hbm[3].at[heads], vmem[3])]
    return begin(pairs, sems)


def input_rows(g1, grads, weights):
    total = g1
    for grad, weight in zip(grads, weights):
        total = total + mm(grad, weight)
    return total.astype(BF)


def attention_back_first_kernel(spots_ref, *refs):
    *refs, ctx_hbm, out_ref, w_ref, low_ref, g1_ref, ctx_ref, q_ref, k_ref, v_ref, p_ref, dq_ref, dk_ref, dv_ref, w_sems, sems, g_sems = refs
    low_hbm, g1_hbm, *sources, q_hbm, k_hbm, v_hbm, p_hbm = refs
    seq_len = p_ref.shape[1]
    rows, dim = low_ref.shape
    loads = begin(((low_hbm, low_ref),), g_sems.at[pl.ds(0, 1)])
    fetch_stacked(spots_ref, sources, w_ref, w_sems, True)
    seqs = q_ref.shape[0] // seq_len
    loads += load_heads((q_hbm, k_hbm, v_hbm, p_hbm), (q_ref, k_ref, v_ref, p_ref), sems, 0, seqs)
    loads[0].wait()
    arrive_stacked(w_ref, w_sems, 3)
    ctx_ref[...] = mm_t(low_ref[...], w_ref[3]).astype(BF)
    mine, later = pl.ds(0, seqs * seq_len), pl.ds(seqs * seq_len, rows - seqs * seq_len)
    store = begin(((ctx_ref.at[later], ctx_hbm),), g_sems.at[pl.ds(1, 1)])[0]
    for load in loads[1:]:
        load.wait()
    fetch_stacked(spots_ref, sources, w_ref, w_sems, False)
    load = begin(((g1_hbm.at[mine], g1_ref),), g_sems.at[pl.ds(2, 1)])[0]
    for s in range(seqs):
        attention_back_heads(s, seq_len, q_ref, k_ref, v_ref, p_ref, ctx_ref, dq_ref, dk_ref, dv_ref, 0)
    load.wait()
    for m in range(3):
        arrive_stacked(w_ref, w_sems, m)
    out_ref[...] = input_rows(g1_ref[...], (dq_ref[...], dk_ref[...], dv_ref[...]), (w_ref[0], w_ref[1], w_ref[2]))
    store.wait()


def attention_back_last_kernel(spots_ref, *refs):
    *refs, out_ref, g1_ref, ctx_ref, first_ref, w_ref, q_ref, k_ref, v_ref, p_ref, dq_ref, dk_ref, dv_ref, w_sems, sems, late_sems = refs
    g1_hbm, ctx_hbm, first_hbm, *sources, q_hbm, k_hbm, v_hbm, p_hbm = refs
    rows = out_ref.shape[0]
    seq_len = p_ref.shape[1]
    first = first_ref.shape[0] // seq_len
    seqs = q_ref.shape[0] // seq_len
    loads = begin(((ctx_hbm, ctx_ref),), late_sems.at[pl.ds(0, 1)])
    loads += load_heads((q_hbm, k_hbm, v_hbm, p_hbm), (q_ref, k_ref, v_ref, p_ref), sems, first, seqs)
    for load in loads:
        load.wait()
    fetch_stacked(spots_ref, sources, w_ref, w_sems, False)
    later = pl.ds(first * seq_len, seqs * seq_len)
    loads = begin(((g1_hbm.at[later], g1_ref), (first_hbm, first_ref)), late_sems.at[pl.ds(1, 2)])
    for s in range(seqs):
        attention_back_heads(s, seq_len, q_ref, k_ref, v_ref, p_ref, ctx_ref, dq_ref, dk_ref, dv_ref, 0)
    for load in loads:
        load.wait()
    for m in range(3):
        arrive_stacked(w_ref, w_sems, m)
    out_ref[: first * seq_len, :] = first_ref[...]
    out_ref[first * seq_len : rows, :] = input_rows(
        g1_ref[...], (dq_ref[...], dk_ref[...], dv_ref[...]), (w_ref[0], w_ref[1], w_ref[2])
    )


def attention_backward_first(spots, g1_low, g1, sources, q, k, v, probs):
    rows, dim = g1.shape
    heads, seq_len = probs.shape[0] // 2, probs.shape[1]
    half, low = jax.ShapeDtypeStruct((rows // 2, dim), BF), pltpu.VMEM((rows // 2, dim), BF)
    return pl.pallas_call(
        attention_back_first_kernel,
        out_shape=[half, half],
        in_specs=[SMEM] + [ANY] * (len(sources) + 6),
        out_specs=[ANY, VMEM],
        scratch_shapes=[pltpu.VMEM((4, dim, dim), BF), pltpu.VMEM((rows, dim), BF), pltpu.VMEM((rows // 2, dim), F32),
                        pltpu.VMEM((rows, dim), BF), low, low, low, pltpu.VMEM((heads,) + probs.shape[1:], BF), low, low, low,
                        WEIGHT_SEMS, pltpu.SemaphoreType.DMA((4,)), pltpu.SemaphoreType.DMA((3,))],
        compiler_params=limit(60),
        cost_estimate=cost(2 * rows * dim * (3 * dim + 2 * seq_len), 2 * (4 * dim * dim + 5 * rows * dim)),
    )(spots, g1_low, g1, *sources, q, k, v, probs)


def attention_backward_last(spots, g1, halfway, sources, q, k, v, probs):
    rows, dim = g1.shape
    heads, seq_len = probs.shape[0] // 2, probs.shape[1]
    low = pltpu.VMEM((rows // 2, dim), BF)
    return pl.pallas_call(
        attention_back_last_kernel,
        out_shape=jax.ShapeDtypeStruct((rows, dim), BF),
        in_specs=[SMEM] + [ANY] * (len(sources) + 7),
        out_specs=VMEM,
        scratch_shapes=[pltpu.VMEM((rows // 2, dim), F32), low, low, pltpu.VMEM((4, dim, dim), BF), low, low, low,
                        pltpu.VMEM((heads,) + probs.shape[1:], BF), low, low, low,
                        WEIGHT_SEMS, pltpu.SemaphoreType.DMA((4,)), pltpu.SemaphoreType.DMA((3,))],
        compiler_params=limit(60),
        cost_estimate=cost(2 * rows * dim * (2 * dim + 2 * seq_len), 2 * (3 * dim * dim + 4 * rows * dim)),
    )(spots, g1, *halfway, *sources, q, k, v, probs)


def shards(
    tokens, lengths, adapter_mask, cotangent, att_query, att_key, att_value, att_out,
    norm1_gain, norm1_bias, ffn_in, ffn_bias, ffn_out, adapt_down, adapt_up, norm2_gain,
    norm2_bias, joining_query, joining_key, joining_value, joining_qbias, joining_vbias,
):
    groups = lax.axis_size("tensor")
    dp_size = lax.axis_size("dp")
    my_z = lax.axis_index("tensor")
    my_d = lax.axis_index("dp")
    seq_local, seq_len, dim = tokens.shape
    mine = seq_local // groups
    rows = mine * seq_len
    adapters, neck = adapt_up.shape[0], adapt_up.shape[1]
    own_rows = joining_query.shape[0]

    gather = Gather(dp_size, groups, my_d, my_z, mine)
    spots = gather.spots
    biases = lax.dynamic_update_slice(
        jnp.zeros((8, dim), BF), jnp.stack([joining_qbias, joining_vbias]), (0, (my_d * groups + my_z) * own_rows)
    )
    att_mats = [att_query.T, att_key.T, att_value.T, att_out]
    join_part = jnp.concatenate([joining_query, joining_key, joining_value, biases], axis=0)

    def my_slice(array):
        return lax.dynamic_slice_in_dim(array, my_z * mine, mine, 0)

    x = my_slice(tokens).reshape(rows, dim)
    masks = my_slice(adapter_mask)
    norms = jnp.stack([norm1_gain, norm1_bias, norm2_gain, norm2_bias])
    lens = my_slice(lengths)
    kept = {}

    def attend(sources):
        kept["att"] = attention_forward(spots, lens, x, sources, norms, seq_len)
        return [kept["att"][4]]

    def feed(sources):
        kept["ffn"] = ffn_forward(spots, kept["att"][4], sources, ffn_bias, ffn_in.shape[1])
        return [kept["ffn"][0]]

    if gather.paired:
        own = [att_mats, [ffn_in], None, [ffn_out]]
        steps = [
            lambda got: [],
            lambda got: [],
            lambda got: attend(got[0] + own[0]),
            lambda got: feed(got[1] + own[1]),
            lambda got: [],
            lambda got: [],
        ]
        quarter = att_mats[3]
        for i in range(3):
            quarter = jnp.where(my_d // 2 == i, att_mats[i], quarter)
        low = quarter.shape[0] // 2
        choices = [part for mat in att_mats for part in (mat[:low], mat[low:])]
        half = choices[7]
        for i in range(7):
            half = jnp.where(my_d == i, choices[i], half)
        rounds = [(half, tie(quarter, half))]
        shards_in, shards_out = tie(ffn_in, half), tie(ffn_out, half)
        in_quarter, in_half, out_quarter, out_half = cut(spots, [shards_in, shards_out])
        rounds += [(in_half, in_quarter), (out_half, out_quarter)]
        join_part = tie(join_part, *rounds[0])
        theirs = send(join_part, CORE)
        even = lax.rem(my_d, 2) == 0
        pair = jnp.concatenate([jnp.where(even, join_part, theirs), jnp.where(even, theirs, join_part)], axis=0)
        rounds.insert(2, (join_part, pair, join_part, theirs))
        got = gather.all_rounds(rounds, [spots, x, norms, lens, masks], steps)
        att_sources, in_sources, out_sources = (got[i] + own[i] for i in (0, 1, 3))
        join_sources = got[2]
    else:
        att_pack = jnp.concatenate(att_mats, axis=0)
        att_sources = gather.whole(gather.part_of(att_pack), True)
        in_sources, out_sources = (gather.whole(gather.part_of(shard)) for shard in (ffn_in, ffn_out))
        join_sources = [lax.all_gather(join_part, ("dp", "tensor"), axis=0)]
    up = adapt_up.reshape(adapters * neck, dim)
    cot = cotangent.reshape(rows, dim)

    def rest(att, ffn, masks, cot):
        q, k, v, probs, low1, xhat1, rstd1 = att
        act, slope = ffn
        layer_out, g2, g_ffn, *grads = joining(
            spots, gather.paired, act, out_sources, adapt_down, up, join_sources, masks, adapters, xhat1, norms, cot
        )
        done = {}

        def between(start):
            gradient = g_ffn if start is None else tie(g_ffn, start)
            done["g1"], g1_low = ffn_backward(spots, gradient, slope, out_sources, in_sources, g2, xhat1, rstd1, norms)
            done["half"] = attention_backward_first(spots, g1_low, done["g1"], att_sources, q, k, v, probs)
            return done["half"][0]

        def at_last(start):
            halfway = done["half"] if start is None else [tie(done["half"][0], start)] + list(done["half"][1:])
            return attention_backward_last(spots, done["g1"], halfway, att_sources, q, k, v, probs)

        return layer_out, grads, between, at_last

    if gather.paired:
        layer_out, grads, between, at_last = rest(kept["att"], kept["ffn"], masks, cot)
        (d_q, d_k, d_v, d_bias), input_grad = reduce_grads(gather, grads, own_rows, between, at_last)
    else:
        outs = []
        for first in range(0, mine, 2):
            at = slice(first * seq_len, (first + 2) * seq_len)
            att = attention_forward(spots, lens[first : first + 2], x[at], att_sources, norms, seq_len)
            ffn = ffn_forward(spots, att[4], in_sources, ffn_bias, ffn_in.shape[1])
            outs.append(rest(att, ffn, masks[first : first + 2], cot[at]))
        layer_out = jnp.concatenate([out[0] for out in outs])
        grads = [sum(out[1][i] for out in outs) for i in range(2)]
        (d_q, d_k, d_v, d_bias), input_grad = reduce_grads(
            gather, grads, own_rows, lambda start: [out[2](None) for out in outs],
            lambda start: jnp.concatenate([out[3](None) for out in outs]),
        )
    d_bias = lax.dynamic_slice_in_dim(d_bias[:2], (my_d * groups + my_z) * own_rows, own_rows, 1)
    return (
        layer_out.reshape(mine, seq_len, dim),
        input_grad.reshape(mine, seq_len, dim),
        d_q, d_k, d_v, d_bias[0], d_bias[1],
    )


def solution(mesh):
    both = P(ALL, None)
    return jax.shard_map(
        shards,
        mesh=mesh,
        in_specs=(
            P("dp", None, None), P("dp"), P("dp"), P(ALL, None, None),
            P(None, "tensor"), P(None, "tensor"), P(None, "tensor"), P("tensor", None),
            P(), P(), P(None, "tensor"), P(), P("tensor", None), P(), P(), P(), P(),
            both, both, both, P(ALL), P(ALL),
        ),
        out_specs=(P(ALL, None, None), P(ALL, None, None), both, both, both, P(ALL), P(ALL)),
        check_vma=False,
    )
```
